32 devices in a mesh: grp: 2 (over x), slab: 16 (over z, y, core).
Axes of the slice: x: 2, y: 2, z: 4, core: 2. Of those that a mesh axis runs over, the one named last changes fastest.
Arguments:
- volume: float32 [2048, 16, 1024], P('slab', 'grp'), parts along dimension 1, may hold values from -6 to 6
- sinogram: bfloat16 [2048, 16, 1024], P('slab', 'grp'), parts along dimension 1, may hold values from -6 to 6
- weights: bfloat16 [8, 128, 128], replicated, may hold values from -0.21875 to 0.21875
- coverage: int32 [16, 6], replicated, may hold values 0 or 1
- offsets: int32 [16, 6], replicated, may hold values from 0 to 7
Outputs:
- gradient: float32 [2048, 16, 1024], P('slab', 'grp'), parts along dimension 1
- residual: bfloat16 [2048, 16, 1024], P('slab', 'grp'), parts along dimension 1
The draws below stay inside these ranges and needn't reach their ends.
There are 2 independent parts, one for each index of `grp`. The reference program is written for one: setup_inputs(seed, part) draws one part's arguments, and reference() takes and returns one part's arrays. A program takes and returns all parts, laid end to end along the dimension named above; an argument that names none is the same for every part. Nothing has to cross between parts.
All inputs are finite; a program needn't handle non-finite values.
Results may differ from the reference program's by a relative error of at most 0.0034.
Values may be sent and summed in bfloat16 or wider, within the bound.
No kernel may reach another device: no remote copies, remote signals or barrier semaphores. Data moves between devices by JAX's collectives and lax.ppermute only.
A program may use at most 128 MiB of HBM per device.

```python
import jax
import jax.numpy as jnp

SZ = 128
SY = 8
NX = 1024
ROWS = 64
VIEWS = 2
SPAN = 6
NB = 8
GROUP = 128
NZ = 2048
NV = 2048
N_SLAB = 16


def set_ends(entries, stream_key, least, largest):
    place = [jax.random.randint(jax.random.fold_in(stream_key, axis), (), 0, length) for axis, length in enumerate(entries.shape)]
    longest = entries.shape.index(max(entries.shape))
    next_to = place[:longest] + [(place[longest] + 1) % entries.shape[longest]] + place[longest + 1:]
    return entries.at[tuple(place)].set(least).at[tuple(next_to)].set(largest)


def steps_of(own_key, dims, pieces, smallest, top_value):
    def one(dim, blocks):
        steps = jax.random.uniform(jax.random.fold_in(jax.random.fold_in(own_key, 6), dim), (blocks,), jnp.float32, smallest / len(pieces), top_value / len(pieces))
        return jnp.repeat(jnp.exp(steps), dims[dim] // blocks).reshape((-1,) + (1,) * (len(dims) - dim - 1))

    gain = one(*pieces[0])
    for cut in pieces[1:]:
        gain = gain * one(*cut)
    return gain


def noise(rng, dims, spread, most, shards=(), held_as=jnp.bfloat16):
    factor_of = steps_of(rng, dims, shards, -0.22, 0.18) if shards else 1.0
    array = jax.random.normal(rng, dims, jnp.float32) * spread * factor_of
    return jnp.minimum(jnp.maximum(array, -most), most).astype(held_as)


def setup_inputs(seed: int = 0, part: int = 0) -> dict:
    keys = jax.random.split(jax.random.key(seed), 6)
    own_keys = jax.random.split(jax.random.fold_in(keys[5], part), 6)
    return {
        "volume": noise(own_keys[0], (NZ, SY, NX), 1.0, 6.0, ((0, 16),), jnp.float32),
        "sinogram": noise(own_keys[1], (NV, SY, NX), 1.0, 6.0, ((0, 16),)),
        "weights": noise(keys[2], (NB, GROUP, SZ), (SZ * SPAN) ** -0.5, 0.21875),
        "coverage": set_ends((jax.random.randint(keys[3], (N_SLAB, SPAN), 0, 4) < 3).astype(jnp.int32), jax.random.fold_in(keys[3], 1), 0, 1),
        "offsets": set_ends(jax.random.randint(keys[4], (N_SLAB, SPAN), 0, NB), jax.random.fold_in(keys[4], 1), 0, NB - 1).astype(jnp.int32),
    }


def tv_from(full):
    base = full[:-1, :-1, :-1]
    diff_z = full[1:, :-1, :-1] - base
    diff_y = full[:-1, 1:, :-1] - base
    diff_x = full[:-1, :-1, 1:] - base
    scale = 1.0 / jnp.sqrt(diff_z * diff_z + diff_y * diff_y + diff_x * diff_x + 0.25)
    flux_z = diff_z * scale
    flux_y = diff_y * scale
    flux_x = diff_x * scale
    total = flux_z[:-1, 1:, 1:] - flux_z[1:, 1:, 1:]
    total = total + flux_y[1:, :-1, 1:] - flux_y[1:, 1:, 1:]
    total = total + flux_x[1:, 1:, :-1] - flux_x[1:, 1:, 1:]
    return total

def reference(volume, sinogram, weights, coverage, offsets):
    slabs = N_SLAB
    group = VIEWS * ROWS
    lowvol = volume.astype(jnp.bfloat16).astype(jnp.float32).reshape(slabs, SZ, SY * NX)
    wfull = weights.astype(jnp.float32)
    projection = jnp.zeros((slabs, group, SY * NX), jnp.float32)
    for k in range(SPAN):
        shifted = jnp.concatenate([lowvol[k:], jnp.zeros((k, SZ, SY * NX), jnp.float32)], axis=0)
        chosen = wfull[offsets[:, k]]
        term = jnp.einsum('ncs,nsp->ncp', chosen, shifted)
        projection = projection + coverage[:, k].astype(jnp.float32)[:, None, None] * term
    sino = sinogram.astype(jnp.float32).reshape(slabs, group, SY * NX)
    residual = (projection - sino).astype(jnp.bfloat16)
    resid_wide = residual.astype(jnp.float32)
    backproj = jnp.zeros((slabs, SZ, SY * NX), jnp.float32)
    for k in range(SPAN):
        count = slabs - k
        chosen = wfull[offsets[:count, k]]
        term = jnp.einsum('ncs,ncp->nsp', chosen, resid_wide[:count])
        term = coverage[:count, k].astype(jnp.float32)[:, None, None] * term
        backproj = backproj + jnp.concatenate([jnp.zeros((k, SZ, SY * NX), jnp.float32), term], axis=0)
    tvgrad = tv_from(jnp.pad(volume, 1))
    gradient = backproj.reshape(volume.shape) + 0.5 * tvgrad
    return (gradient, residual.reshape(sinogram.shape))
```

```python
import functools

import jax
import jax.numpy as jnp
from jax import lax
from jax.experimental import pallas as pl
from jax.experimental.pallas import tpu as pltpu
from jax.sharding import PartitionSpec as P

G = 4
CHUNKS = 2
F32 = jnp.float32
BF16 = jnp.bfloat16
VMEM_LIMIT = 40 * 1024 * 1024


def moved(value, steps):
    count = lax.axis_size("slab")
    first, last = max(0, -steps), min(count, count - steps)
    return lax.ppermute(value, "slab", [(source, source + steps) for source in range(first, last)])


def exchanged(value):
    count = lax.axis_size("slab")
    sets = [list(range(first, first + G)) for first in range(0, count, G)]
    return lax.all_to_all(value, "slab", 0, 0, axis_index_groups=sets, tiled=True)


def params(*semantics):
    return pltpu.CompilerParams(vmem_limit_bytes=VMEM_LIMIT)


def cost(flops, nbytes):
    return pl.CostEstimate(flops=int(flops), bytes_accessed=int(nbytes), transcendentals=0)


def cast_kernel(vol_ref, *out_refs):
    depth = out_refs[0].shape[1]
    per = 2
    for c in range(CHUNKS):
        for q in range(G):
            row = per * q + c
            out_refs[c][q] = vol_ref[pl.ds(row, depth, stride=8), :].astype(BF16)


def cast_rows(volume):
    depth, rows, cols = volume.shape
    tile = 128
    shape = jax.ShapeDtypeStruct((G, depth, cols), BF16)
    return pl.pallas_call(
        cast_kernel,
        grid=(cols // tile,),
        in_specs=[pl.BlockSpec((depth * rows, tile), lambda i: (0, i))],
        out_specs=[pl.BlockSpec((G, depth, tile), lambda i: (0, 0, i))] * CHUNKS,
        out_shape=[shape] * CHUNKS,
        compiler_params=params(),
        cost_estimate=cost(volume.size, volume.size * 6),
    )(volume.reshape(depth * rows, cols))


def split_kernel(in_ref, *refs):
    out_refs, wide = refs[:-1], refs[-1]
    depth = out_refs[0].shape[1]
    wide[...] = in_ref[...].astype(F32).reshape(wide.shape)
    for c in range(CHUNKS):
        for q in range(G):
            out_refs[c][q] = wide[pl.ds(2 * q + c, depth, stride=8), :].astype(BF16)


def split_rows(array):
    depth, rows, cols = array.shape
    tile = 128
    shape = jax.ShapeDtypeStruct((G, depth, cols), BF16)
    return pl.pallas_call(
        split_kernel,
        grid=(cols // tile,),
        in_specs=[pl.BlockSpec((depth, rows, tile), lambda i: (0, 0, i))],
        out_specs=[pl.BlockSpec((G, depth, tile), lambda i: (0, 0, i))] * CHUNKS,
        out_shape=[shape] * CHUNKS,
        scratch_shapes=[pltpu.VMEM((depth * rows, tile), F32)],
        compiler_params=params(),
        cost_estimate=cost(array.size, array.size * 4),
    )(array)


def join_kernel(*refs):
    in_refs, out_ref, wide = refs[:-2], refs[-2], refs[-1]
    depth = in_refs[0].shape[1]
    for c in range(CHUNKS):
        for q in range(G):
            wide[pl.ds(2 * q + c, depth, stride=8), :] = in_refs[c][q].astype(F32)
    out_ref[...] = wide[...].reshape(out_ref.shape).astype(out_ref.dtype)


def join_rows(chunks, rows):
    _, depth, cols = chunks[0].shape
    tile = 128
    return pl.pallas_call(
        join_kernel,
        grid=(cols // tile,),
        in_specs=[pl.BlockSpec((G, depth, tile), lambda i: (0, 0, i))] * CHUNKS,
        out_specs=pl.BlockSpec((depth, rows, tile), lambda i: (0, 0, i)),
        out_shape=jax.ShapeDtypeStruct((depth, rows, cols), BF16),
        scratch_shapes=[pltpu.VMEM((depth * rows, tile), F32)],
        compiler_params=params(),
        cost_estimate=cost(depth * rows * cols, depth * rows * cols * 4),
    )(*chunks)


def finish_kernel(tv_ref, *refs):
    in_refs, out_ref, wide = refs[:-2], refs[-2], refs[-1]
    depth = in_refs[0].shape[1]
    for c in range(CHUNKS):
        for q in range(G):
            wide[pl.ds(2 * q + c, depth, stride=8), :] = in_refs[c][q].astype(F32)
    out_ref[...] = tv_ref[...] + wide[...].reshape(out_ref.shape)


def finish(tv, chunks):
    depth, rows, cols = tv.shape
    tile = 128
    whole = pl.BlockSpec((depth, rows, tile), lambda i: (0, 0, i))
    return pl.pallas_call(
        finish_kernel,
        grid=(cols // tile,),
        in_specs=[whole] + [pl.BlockSpec((G, depth, tile), lambda i: (0, 0, i))] * CHUNKS,
        out_specs=whole,
        out_shape=jax.ShapeDtypeStruct((depth, rows, cols), F32),
        scratch_shapes=[pltpu.VMEM((depth * rows, tile), F32)],
        compiler_params=params(),
        cost_estimate=cost(depth * rows * cols, depth * rows * cols * 10),
    )(tv, *chunks)


def band_kernel(slabs, span, here_ref, cover_ref, offset_ref, w_ref, proj_ref, back_ref):
    side = w_ref.shape[1]
    first = (here_ref[0] // G) * G
    last_level = first + G >= slabs
    zero = jnp.zeros((side, side), BF16)

    def block(i, j, k, extra):
        safe = jnp.clip(i, 0, slabs - 1)
        inside = jnp.logical_and(jnp.logical_and(i >= 0, j < slabs), extra)
        live = jnp.logical_and(inside, cover_ref[safe, k] == 1)
        value = w_ref[offset_ref[safe, k]]
        return jnp.where(live, value, zero)

    for r in range(G + 1):
        for s in range(2 * G + 1):
            k = s - r
            value = zero
            if 0 <= k < span:
                extra = last_level if r == G else True
                value = block(first - 1 + r, first - 1 + s, k, extra)
            proj_ref[pl.ds(r * side, side), pl.ds(s * side, side)] = value
    for r in range(G):
        for s in range(2 * G + 1):
            k = (r + G + 1) - s
            value = zero
            if 0 <= k < span:
                value = block(first - G - 1 + s, first + r, k, True).astype(F32).T.astype(BF16)
            back_ref[pl.ds(r * side, side), pl.ds(s * side, side)] = value


def bands(here, coverage, offsets, weights):
    slabs, span = coverage.shape
    side = weights.shape[1]
    smem = pl.BlockSpec(memory_space=pltpu.SMEM)
    vmem = pl.BlockSpec(memory_space=pltpu.VMEM)
    return pl.pallas_call(
        functools.partial(band_kernel, slabs, span),
        in_specs=[smem, smem, smem, vmem],
        out_specs=[vmem, vmem],
        out_shape=[
            jax.ShapeDtypeStruct(((G + 1) * side, (2 * G + 1) * side), BF16),
            jax.ShapeDtypeStruct((G * side, (2 * G + 1) * side), BF16),
        ],
        compiler_params=params(),
        cost_estimate=cost(1e6, 4e6),
    )(here, coverage, offsets, weights)


def project_kernel(band_ref, low_ref, own_ref, high_ref, slow_ref, sown_ref, r_ref, last_ref, down_ref):
    side = low_ref.shape[0]
    n = G * side
    total = jnp.dot(band_ref[:, side : side + n], own_ref[...], preferred_element_type=F32)
    total += jnp.dot(band_ref[:, side + n :], high_ref[...], preferred_element_type=F32)
    total += jnp.dot(band_ref[:, :side], low_ref[...], preferred_element_type=F32)
    first = (total[:side] - slow_ref[...].astype(F32)).astype(BF16)
    rest = (total[side:] - sown_ref[...].astype(F32)).astype(BF16)
    r_ref[:side] = first
    r_ref[side:] = rest[: n - side]
    down_ref[...] = first
    last_ref[...] = rest[n - side :]


def project(band, low, own, high, slow, sown):
    side, cols = low.shape
    n = G * side
    tile = 256
    one = pl.BlockSpec((side, tile), lambda i: (0, i))
    many = pl.BlockSpec((n, tile), lambda i: (0, i))
    return pl.pallas_call(
        project_kernel,
        grid=(cols // tile,),
        in_specs=[pl.BlockSpec(band.shape, lambda i: (0, 0)), one, many, many, one, many],
        out_specs=[many, one, one],
        out_shape=[
            jax.ShapeDtypeStruct((n, cols), BF16),
            jax.ShapeDtypeStruct((side, cols), BF16),
            jax.ShapeDtypeStruct((side, cols), BF16),
        ],
        compiler_params=params(),
        cost_estimate=cost(2 * band.size * cols, 6e6),
    )(band, low, own, high, slow, sown)


def back_kernel(band_ref, low_ref, own_ref, high_ref, out_ref):
    side = high_ref.shape[0]
    n = G * side
    total = jnp.dot(band_ref[:, n : 2 * n], own_ref[...], preferred_element_type=F32)
    total += jnp.dot(band_ref[:, :n], low_ref[...], preferred_element_type=F32)
    total += jnp.dot(band_ref[:, 2 * n :], high_ref[...], preferred_element_type=F32)
    out_ref[...] = total.astype(BF16)


def back(band, low, own, high):
    side, cols = high.shape
    n = G * side
    tile = 256
    one = pl.BlockSpec((side, tile), lambda i: (0, i))
    many = pl.BlockSpec((n, tile), lambda i: (0, i))
    return pl.pallas_call(
        back_kernel,
        grid=(cols // tile,),
        in_specs=[pl.BlockSpec(band.shape, lambda i: (0, 0)), many, many, one],
        out_specs=many,
        out_shape=jax.ShapeDtypeStruct((n, cols), BF16),
        compiler_params=params(),
        cost_estimate=cost(2 * band.size * cols, 6e6),
    )(band, low, own, high)


def tv_kernel(low_ref, high_ref, next_ref, vol_ref, out_ref, flux_ref):
    step = pl.program_id(0)
    steps = pl.num_programs(0)
    deep, rows, cols = vol_ref.shape
    row = lax.broadcasted_iota(jnp.int32, (rows, cols), 0)
    col = lax.broadcasted_iota(jnp.int32, (rows, cols), 1)

    def up_y(v):
        return jnp.where(row == rows - 1, 0.0, pltpu.roll(v, rows - 1, 0))

    def up_x(v):
        return jnp.where(col == cols - 1, 0.0, pltpu.roll(v, cols - 1, 1))

    def scale_of(cur, above):
        dz = above - cur
        dy = up_y(cur) - cur
        dx = up_x(cur) - cur
        return dz, dy, dx, 0.5 * lax.rsqrt(dz * dz + dy * dy + dx * dx + 0.25)

    def edge(v):
        return 0.5 * v * lax.rsqrt(v * v + 0.25)

    @pl.when(step == 0)
    def _():
        dz, _, _, scale = scale_of(low_ref[0], vol_ref[0])
        flux_ref[...] = dz * scale

    def one(z, cur, above, below_flux):
        dz, dy, dx, scale = scale_of(cur, above)
        fz, fy, fx = dz * scale, dy * scale, dx * scale
        fy_low = jnp.where(row == 0, edge(cur), pltpu.roll(fy, 1, 0))
        fx_low = jnp.where(col == 0, edge(cur), pltpu.roll(fx, 1, 1))
        out_ref[z] = (below_flux - fz) + (fy_low - fy) + (fx_low - fx)
        return fz

    def body(z, flux):
        return one(z, vol_ref[z], vol_ref[z + 1], flux)

    flux = lax.fori_loop(0, deep - 1, body, flux_ref[...])
    above = jnp.where(step == steps - 1, high_ref[0], next_ref[0])
    flux_ref[...] = one(deep - 1, vol_ref[deep - 1], above, flux)


def half_tv(volume, low, high):
    depth, rows, cols = volume.shape
    deep = 16
    steps = depth // deep
    edge = pl.BlockSpec((1, rows, cols), lambda i: (0, 0, 0))
    body = pl.BlockSpec((deep, rows, cols), lambda i: (i, 0, 0))
    after = pl.BlockSpec((1, rows, cols), lambda i: (jnp.minimum((i + 1) * deep, depth - 1), 0, 0))
    return pl.pallas_call(
        tv_kernel,
        grid=(steps,),
        in_specs=[edge, edge, after, body],
        out_specs=body,
        out_shape=jax.ShapeDtypeStruct(volume.shape, F32),
        scratch_shapes=[pltpu.VMEM((rows, cols), F32)],
        compiler_params=params(),
        cost_estimate=cost(volume.size * 40, volume.size * 8),
    )(low, high, volume, volume)


def local(volume, sinogram, weights, coverage, offsets):
    slabs = lax.axis_size("slab")
    here = lax.axis_index("slab").astype(jnp.int32)
    depth, rows, cols = volume.shape
    last_level = here >= slabs - G

    vol_rows = cast_rows(volume)
    band_p, band_b = bands(here.reshape(1), coverage, offsets, weights)
    sino_rows = split_rows(sinogram)

    own = [exchanged(v).reshape(G * depth, cols) for v in vol_rows]
    high = [moved(v, -G) for v in own]
    low = [moved(v[(G - 1) * depth :], G) for v in own]
    sown = [exchanged(s).reshape(G * depth, cols) for s in sino_rows]
    slow = [moved(s[(G - 1) * depth :], G) for s in sown]

    below = moved(volume[-1:], 1)
    above = moved(volume[:1], -1)
    tv = half_tv(volume, below, above)

    resid_back, back_back = [], []
    for c in range(CHUNKS):
        resid, last, down = project(band_p, low[c], own[c], high[c], slow[c], sown[c])
        r_low = moved(resid, G)
        r_high = moved(down, -G)
        r_high = jnp.where(last_level, last, r_high)
        mine = jnp.concatenate([resid[depth:], r_high], axis=0)
        resid_back.append(exchanged(mine.reshape(G, depth, cols)))
        backproj = back(band_b, r_low, resid, r_high)
        back_back.append(exchanged(backproj.reshape(G, depth, cols)))

    residual = join_rows(resid_back, rows)
    gradient = finish(tv, back_back)
    return (gradient, residual)


def solution(mesh):
    placed = (P("slab", "grp", None), P("slab", "grp", None), P(), P(), P())
    return jax.shard_map(
        local,
        mesh=mesh,
        in_specs=placed,
        out_specs=(P("slab", "grp", None), P("slab", "grp", None)),
        check_vma=False,
    )
```

```python
import functools

import jax
import jax.numpy as jnp
from jax import lax
from jax.experimental import pallas as pl
from jax.experimental.pallas import tpu as pltpu
from jax.sharding import PartitionSpec as P

G = 4
CHUNKS = 2
F32 = jnp.float32
BF16 = jnp.bfloat16
MIB = 1024 * 1024
SMEM = pl.BlockSpec(memory_space=pltpu.SMEM)
VMEM = pl.BlockSpec(memory_space=pltpu.VMEM)
ANY = pl.BlockSpec(memory_space=pl.ANY)


def moved(value, steps, only=None):
    count = lax.axis_size("slab")
    first, last = max(0, -steps), min(count, count - steps)
    pairs = [(i, i + steps) for i in range(first, last) if only is None or i % G == only]
    return lax.ppermute(value, "slab", pairs)


def swapped(value, bits):
    count = lax.axis_size("slab")
    return lax.ppermute(value, "slab", [(i, i ^ bits) for i in range(count)])


def exchanged(value):
    count = lax.axis_size("slab")
    sets = [list(range(first, first + G)) for first in range(0, count, G)]
    return lax.all_to_all(value, "slab", 0, 0, axis_index_groups=sets, tiled=True)


def call(kernel, us, nbytes, vmem=16, **how):
    return pl.pallas_call(
        kernel,
        compiler_params=pltpu.CompilerParams(vmem_limit_bytes=vmem * MIB),
        cost_estimate=pl.CostEstimate(flops=int(us * 1.15e9), bytes_accessed=int(nbytes), transcendentals=0),
        **how,
    )


def cast_kernel(chunk, vol_ref, out_ref):
    depth = out_ref.shape[1]
    for p in range(G):
        out_ref[p] = vol_ref[pl.ds(2 * p + chunk, depth, stride=8), :].astype(BF16)


def cast_rows(volume, chunk):
    depth, rows, cols = volume.shape
    tile = 128
    return call(
        functools.partial(cast_kernel, chunk),
        2,
        5 * MIB,
        grid=(cols // tile,),
        in_specs=[pl.BlockSpec((depth * rows, tile), lambda i: (0, i))],
        out_specs=pl.BlockSpec((G, depth, tile), lambda i: (0, 0, i)),
        out_shape=jax.ShapeDtypeStruct((G, depth, cols), BF16),
    )(volume.reshape(depth * rows, cols))


def split_kernel(here_ref, own_ref, got_ref, *refs):
    out_refs, wide = refs[:-1], refs[-1]
    depth = out_refs[0].shape[0]
    place = lax.rem(here_ref[0], G)

    @pl.when(place == G - 1)
    def _():
        wide[...] = got_ref[...].astype(F32).reshape(wide.shape)

    @pl.when(place != G - 1)
    def _():
        wide[...] = own_ref[...].astype(F32).reshape(wide.shape)

    for c in range(CHUNKS):
        for m in range(G):
            row = 2 * jnp.bitwise_xor(place, m) + c
            out_refs[c * G + m][...] = wide[pl.ds(row, depth, stride=8), :].astype(BF16)


def split_rows(here, own, got):
    depth, rows, cols = own.shape
    tile = 128
    block = pl.BlockSpec((depth, rows, tile), lambda i: (0, 0, i))
    return call(
        split_kernel,
        4,
        6 * MIB,
        grid=(cols // tile,),
        in_specs=[SMEM, block, block],
        out_specs=[pl.BlockSpec((depth, tile), lambda i: (0, i))] * (CHUNKS * G),
        out_shape=[jax.ShapeDtypeStruct((depth, cols), BF16)] * (CHUNKS * G),
        scratch_shapes=[pltpu.VMEM((depth * rows, tile), F32)],
    )(here, own, got)


def last_kernel(slabs, here_ref, cover_ref, offset_ref, w_ref, v0_ref, v1_ref, sino_ref, r_ref, b_ref, v, s, r, b, wide):
    depth, rows, cols = sino_ref.shape
    tile = 128

    @pl.when(here_ref[0] == slabs - 1)
    def _():
        pltpu.sync_copy(v0_ref, v.at[0])
        pltpu.sync_copy(v1_ref, v.at[1])
        pltpu.sync_copy(sino_ref, s)
        block = w_ref[offset_ref[slabs - 1, 0]]
        block = jnp.where(cover_ref[slabs - 1, 0] == 1, block, jnp.zeros_like(block))
        turned = block.astype(F32).T.astype(BF16)

        def column(j, _):
            at = pl.ds(pl.multiple_of(j * tile, tile), tile)
            wide[...] = s[:, :, at].astype(F32).reshape(wide.shape)
            for row in range(rows):
                p, c = row // CHUNKS, row % CHUNKS
                seen = jnp.dot(block, v[c, p, :, at], preferred_element_type=F32)
                resid = (seen - wide[pl.ds(row, depth, stride=rows), :]).astype(BF16)
                r[row, :, at] = resid
                b[row, :, at] = jnp.dot(turned, resid, preferred_element_type=F32)
            return 0

        lax.fori_loop(0, cols // tile, column, 0)
        pltpu.sync_copy(r, r_ref)
        pltpu.sync_copy(b, b_ref)


def last_group(here, coverage, offsets, weights, v0, v1, sinogram):
    slabs = coverage.shape[0]
    depth, rows, cols = sinogram.shape
    return call(
        functools.partial(last_kernel, slabs),
        1,
        MIB,
        in_specs=[SMEM, SMEM, SMEM, VMEM, ANY, ANY, ANY],
        out_specs=[ANY, ANY],
        out_shape=[
            jax.ShapeDtypeStruct((rows, depth, cols), BF16),
            jax.ShapeDtypeStruct((rows, depth, cols), F32),
        ],
        scratch_shapes=[
            pltpu.VMEM((CHUNKS,) + v0.shape, BF16),
            pltpu.VMEM(sinogram.shape, BF16),
            pltpu.VMEM((rows, depth, cols), BF16),
            pltpu.VMEM((rows, depth, cols), F32),
            pltpu.VMEM((depth * rows, 128), F32),
        ],
    )(here, coverage, offsets, weights, v0, v1, sinogram)


def join_kernel(slabs, here_ref, *refs):
    in_refs, last_ref, out_ref, wide, held = refs[:-4], refs[-4], refs[-3], refs[-2], refs[-1]
    depth = in_refs[0].shape[0]
    rows, tile = held.shape[0], held.shape[2]
    place = lax.rem(here_ref[0], G)
    last = here_ref[0] == slabs - 1

    @pl.when(last)
    def _():
        at = pl.ds(pl.multiple_of(pl.program_id(0) * tile, tile), tile)
        pltpu.sync_copy(last_ref.at[:, :, at], held)
        for row in range(rows):
            wide[pl.ds(row, depth, stride=rows), :] = held[row].astype(F32)

    @pl.when(jnp.logical_not(last))
    def _():
        for c in range(CHUNKS):
            for m in range(G):
                row = 2 * jnp.bitwise_xor(place, m) + c
                wide[pl.ds(row, depth, stride=rows), :] = in_refs[c * G + m][...].astype(F32)

    out_ref[...] = wide[...].reshape(out_ref.shape).astype(out_ref.dtype)


def join_rows(here, slabs, blocks, last):
    rows, depth, cols = last.shape
    tile = 128
    return call(
        functools.partial(join_kernel, slabs),
        4,
        4 * MIB,
        grid=(cols // tile,),
        in_specs=[SMEM] + [pl.BlockSpec((depth, tile), lambda i: (0, i))] * len(blocks) + [ANY],
        out_specs=pl.BlockSpec((depth, rows, tile), lambda i: (0, 0, i)),
        out_shape=jax.ShapeDtypeStruct((depth, rows, cols), BF16),
        scratch_shapes=[pltpu.VMEM((depth * rows, tile), F32), pltpu.VMEM((rows, depth, tile), BF16)],
    )(here, *blocks, last)


def finish_kernel(slabs, here_ref, tv_ref, b0_ref, b1_ref, last_ref, out_ref, wide, held):
    depth = b0_ref.shape[1]
    rows, tile = held.shape[0], held.shape[2]
    last = here_ref[0] == slabs - 1
    for p in range(G):
        wide[pl.ds(2 * p, depth, stride=rows), :] = b0_ref[p].astype(F32)
        wide[pl.ds(2 * p + 1, depth, stride=rows), :] = b1_ref[p].astype(F32)

    @pl.when(last)
    def _():
        at = pl.ds(pl.multiple_of(pl.program_id(0) * tile, tile), tile)
        pltpu.sync_copy(last_ref.at[:, :, at], held)
        for row in range(rows):
            spot = pl.ds(row, depth, stride=rows)
            wide[spot, :] = wide[spot, :] + held[row]

    out_ref[...] = tv_ref[...] + wide[...].reshape(out_ref.shape)


def finish(here, slabs, tv, chunks, last):
    depth, rows, cols = tv.shape
    tile = 128
    whole = pl.BlockSpec((depth, rows, tile), lambda i: (0, 0, i))
    return call(
        functools.partial(finish_kernel, slabs),
        5,
        10 * MIB,
        grid=(cols // tile,),
        in_specs=[SMEM, whole] + [pl.BlockSpec((G, depth, tile), lambda i: (0, 0, i))] * CHUNKS + [ANY],
        out_specs=whole,
        out_shape=jax.ShapeDtypeStruct((depth, rows, cols), F32),
        scratch_shapes=[pltpu.VMEM((depth * rows, tile), F32), pltpu.VMEM((rows, depth, tile), F32)],
    )(here, tv, *chunks, last)


def band_kernel(slabs, span, here_ref, cover_ref, offset_ref, w_ref, proj_ref, back_ref):
    side = w_ref.shape[1]
    first = (here_ref[0] // G) * G
    zero = jnp.zeros((side, side), BF16)

    def block(i, j, k):
        safe = jnp.clip(i, 0, slabs - 1)
        inside = jnp.logical_and(i >= 0, j < slabs)
        live = jnp.logical_and(inside, cover_ref[safe, k] == 1)
        return jnp.where(live, w_ref[offset_ref[safe, k]], zero)

    for r in range(G):
        for s in range(2 * G + 1):
            at = (pl.ds(r * side, side), pl.ds(s * side, side))
            k = s - r
            proj_ref[at] = block(first - 1 + r, first - 1 + s, k) if 0 <= k < span else zero
            k = (r + G + 1) - s
            value = zero
            if 0 <= k < span:
                value = block(first - G - 1 + s, first + r, k).astype(F32).T.astype(BF16)
            back_ref[at] = value


def bands(here, coverage, offsets, weights):
    slabs, span = coverage.shape
    side = weights.shape[1]
    shape = jax.ShapeDtypeStruct((G * side, (2 * G + 1) * side), BF16)
    return call(
        functools.partial(band_kernel, slabs, span),
        1.5,
        3 * MIB,
        in_specs=[SMEM, SMEM, SMEM, VMEM],
        out_specs=[VMEM, VMEM],
        out_shape=[shape, shape],
    )(here, coverage, offsets, weights)


def project_kernel(here_ref, band_ref, low_ref, own_ref, high_ref, *refs):
    s_refs, (_, r_ref, down_ref, total) = refs[:G], refs[G:]
    side = low_ref.shape[0]
    n = G * side
    place = lax.rem(here_ref[0], G)
    sums = jnp.dot(band_ref[:, side : side + n], own_ref[...], preferred_element_type=F32)
    sums += jnp.dot(band_ref[:, side + n :], high_ref[...], preferred_element_type=F32)
    sums += jnp.dot(band_ref[:, :side], low_ref[...], preferred_element_type=F32)
    total[...] = sums
    for m in range(G):
        spot = lax.rem(jnp.bitwise_xor(place, m) + 1, G)
        at = pl.ds(pl.multiple_of(spot * side, side), side)
        r_ref[at, :] = (total[at, :] - s_refs[m][...].astype(F32)).astype(BF16)
    down_ref[...] = r_ref[:side]


def project(here, band, low, own, high, sinos, token):
    side, cols = low.shape
    n = G * side
    tile = 256
    one = pl.BlockSpec((side, tile), lambda i: (0, i))
    many = pl.BlockSpec((n, tile), lambda i: (0, i))
    return call(
        project_kernel,
        4,
        6 * MIB,
        grid=(cols // tile,),
        in_specs=[SMEM, pl.BlockSpec(band.shape, lambda i: (0, 0)), one, many, many] + [one] * G + [ANY],
        out_specs=[many, one],
        out_shape=[jax.ShapeDtypeStruct((n, cols), BF16), jax.ShapeDtypeStruct((side, cols), BF16)],
        scratch_shapes=[pltpu.VMEM((n, tile), F32)],
    )(here, band, low, own, high, *sinos, token)


def deal_kernel(here_ref, r_ref, high_ref, *out_refs):
    side = high_ref.shape[0]
    place = lax.rem(here_ref[0], G)
    for m in range(G):
        to = jnp.bitwise_xor(place, m)

        @pl.when(to == G - 1)
        def _():
            out_refs[m][...] = high_ref[...]

        @pl.when(to != G - 1)
        def _():
            spot = lax.rem(to + 1, G)
            out_refs[m][...] = r_ref[pl.ds(pl.multiple_of(spot * side, side), side), :]


def deal(here, resid, high):
    return call(
        deal_kernel,
        1,
        2 * MIB,
        in_specs=[SMEM, VMEM, VMEM],
        out_specs=[VMEM] * G,
        out_shape=[jax.ShapeDtypeStruct(high.shape, BF16)] * G,
    )(here, resid, high)


def back_kernel(band_ref, low_ref, own_ref, high_ref, out_ref):
    side = high_ref.shape[0]
    n = G * side
    total = jnp.dot(band_ref[:, n : 2 * n], own_ref[...], preferred_element_type=F32)
    total += jnp.dot(band_ref[:, :n], low_ref[...], preferred_element_type=F32)
    total += jnp.dot(band_ref[:, 2 * n :], high_ref[...], preferred_element_type=F32)
    out_ref[...] = total.astype(BF16)


def back(band, low, own, high):
    side, cols = high.shape
    n = G * side
    tile = 256
    one = pl.BlockSpec((side, tile), lambda i: (0, i))
    many = pl.BlockSpec((n, tile), lambda i: (0, i))
    return call(
        back_kernel,
        4,
        6 * MIB,
        grid=(cols // tile,),
        in_specs=[pl.BlockSpec(band.shape, lambda i: (0, 0)), many, many, one],
        out_specs=many,
        out_shape=jax.ShapeDtypeStruct((n, cols), BF16),
    )(band, low, own, high)


def tv_kernel(low_ref, high_ref, next_ref, vol_ref, out_ref, flux_ref):
    step = pl.program_id(0)
    steps = pl.num_programs(0)
    deep, rows, cols = vol_ref.shape
    row = lax.broadcasted_iota(jnp.int32, (rows, cols), 0)
    col = lax.broadcasted_iota(jnp.int32, (rows, cols), 1)

    def up_y(v):
        return jnp.where(row == rows - 1, 0.0, pltpu.roll(v, rows - 1, 0))

    def up_x(v):
        return jnp.where(col == cols - 1, 0.0, pltpu.roll(v, cols - 1, 1))

    def scale_of(cur, above):
        dz = above - cur
        dy = up_y(cur) - cur
        dx = up_x(cur) - cur
        return dz, dy, dx, 0.5 * lax.rsqrt(dz * dz + dy * dy + dx * dx + 0.25)

    def edge(v):
        return 0.5 * v * lax.rsqrt(v * v + 0.25)

    @pl.when(step == 0)
    def _():
        dz, _, _, scale = scale_of(low_ref[0], vol_ref[0])
        flux_ref[...] = dz * scale

    def one(z, cur, above, below_flux):
        dz, dy, dx, scale = scale_of(cur, above)
        fz, fy, fx = dz * scale, dy * scale, dx * scale
        sides = edge(cur)
        fy_low = jnp.where(row == 0, sides, pltpu.roll(fy, 1, 0))
        fx_low = jnp.where(col == 0, sides, pltpu.roll(fx, 1, 1))
        out_ref[z] = (below_flux - fz) + (fy_low - fy) + (fx_low - fx)
        return fz

    def body(z, flux):
        return one(z, vol_ref[z], vol_ref[z + 1], flux)

    flux = lax.fori_loop(0, deep - 1, body, flux_ref[...], unroll=5)
    above = jnp.where(step == steps - 1, high_ref[0], next_ref[0])
    flux_ref[...] = one(deep - 1, vol_ref[deep - 1], above, flux)


def half_tv(volume, low, high):
    depth, rows, cols = volume.shape
    deep = 16
    steps = depth // deep
    edge = pl.BlockSpec((1, rows, cols), lambda i: (0, 0, 0))
    body = pl.BlockSpec((deep, rows, cols), lambda i: (i, 0, 0))
    after = pl.BlockSpec((1, rows, cols), lambda i: (jnp.minimum((i + 1) * deep, depth - 1), 0, 0))
    return call(
        tv_kernel,
        10,
        8 * MIB,
        grid=(steps,),
        in_specs=[edge, edge, after, body],
        out_specs=body,
        out_shape=jax.ShapeDtypeStruct(volume.shape, F32),
        scratch_shapes=[pltpu.VMEM((rows, cols), F32)],
    )(low, high, volume, volume)


def local(volume, sinogram, weights, coverage, offsets):
    slabs = lax.axis_size("slab")
    here = lax.axis_index("slab").astype(jnp.int32).reshape(1)
    depth, rows, cols = volume.shape
    whole = (G * depth, cols)

    got = moved(sinogram, G, only=G - 1)
    vol_rows = [cast_rows(volume, c) for c in range(CHUNKS)]
    band_p, band_b = bands(here, coverage, offsets, weights)
    below = moved(volume[-1:], 1)
    above = moved(volume[:1], -1)
    r_last, b_last = last_group(here, coverage, offsets, weights, *vol_rows, sinogram)

    own = [exchanged(v).reshape(whole) for v in vol_rows]
    high = [moved(v, -G) for v in own]
    low = [moved(v[(G - 1) * depth :], G) for v in own]
    sino = split_rows(here, sinogram, got)
    sinos = []
    for c in range(CHUNKS):
        mine = sino[c * G : (c + 1) * G]
        sinos.append([mine[0]] + [swapped(mine[m], m) for m in range(1, G)])
    tv = half_tv(volume, below, above)

    resid_blocks, back_rows = [], []
    for c in range(CHUNKS):
        token = tv if c else band_b
        resid, down = project(here, band_p, low[c], own[c], high[c], sinos[c], token)
        r_low = moved(resid, G)
        r_high = moved(down, -G)
        dealt = deal(here, resid, r_high)
        resid_blocks += [dealt[0]] + [swapped(dealt[m], m) for m in range(1, G)]
        backproj = back(band_b, r_low, resid, r_high)
        back_rows.append(exchanged(backproj.reshape(G, depth, cols)))

    residual = join_rows(here, slabs, resid_blocks, r_last)
    gradient = finish(here, slabs, tv, back_rows, b_last)
    return (gradient, residual)


def solution(mesh):
    placed = (P("slab", "grp", None), P("slab", "grp", None), P(), P(), P())
    return jax.shard_map(
        local,
        mesh=mesh,
        in_specs=placed,
        out_specs=(P("slab", "grp", None), P("slab", "grp", None)),
        check_vma=False,
    )
```

```python
import functools

import jax
import jax.numpy as jnp
from jax import lax
from jax.experimental import pallas as pl
from jax.experimental.pallas import tpu as pltpu
from jax.sharding import PartitionSpec as P

G = 4
CHUNKS = 2
F32 = jnp.float32
BF16 = jnp.bfloat16
MIB = 1024 * 1024
LANES = 128
SMEM = pl.BlockSpec(memory_space=pltpu.SMEM)
VMEM = pl.BlockSpec(memory_space=pltpu.VMEM)
ANY = pl.BlockSpec(memory_space=pl.ANY)


def moved(value, steps, only=None):
    count = lax.axis_size("slab")
    first, last = max(0, -steps), min(count, count - steps)
    pairs = [(i, i + steps) for i in range(first, last) if only is None or i % G == only]
    return lax.ppermute(value, "slab", pairs)


def swapped(value, bits):
    count = lax.axis_size("slab")
    return lax.ppermute(value, "slab", [(i, i ^ bits) for i in range(count)])


def dealt_out(blocks):
    got = {m: swapped(blocks[m], m) for m in reversed(range(1, G))}
    return [blocks[0]] + [got[m] for m in range(1, G)]


def exchanged(array):
    count = lax.axis_size("slab")
    sets = [list(range(first, first + G)) for first in range(0, count, G)]
    return lax.all_to_all(array, "slab", 0, 0, axis_index_groups=sets, tiled=True)


def call(kernel, *, results, vmem=16, **how):
    return pl.pallas_call(
        kernel,
        out_shape=results,
        compiler_params=pltpu.CompilerParams(vmem_limit_bytes=vmem * MIB),
        cost_estimate=pl.CostEstimate(flops=1000, bytes_accessed=1000, transcendentals=0),
        **how,
    )


def value(shape, dtype):
    return jax.ShapeDtypeStruct(shape, dtype)


def far(array):
    return pltpu.with_memory_space_constraint(array, pltpu.HBM)


def across(shape, tile):
    block = shape[:-1] + (tile,)
    return pl.BlockSpec(block, lambda i: (0,) * (len(shape) - 1) + (i,))


def lanes(array, tile, parts):
    block = array.shape[:-1] + (tile,)
    zeros = (0,) * (len(block) - 1)
    return [pl.BlockSpec(block, lambda i, j=j: zeros + (i * parts + j,)) for j in range(parts)]


def row_of(place, m, chunk):
    return CHUNKS * jnp.bitwise_xor(place, m) + chunk


def cast_kernel(chunk, parts, *refs):
    vol_refs, out_ref = refs[:parts], refs[-1]
    depth = out_ref.shape[1]
    for j, vol_ref in enumerate(vol_refs):
        for p in range(G):
            spot = pl.ds(CHUNKS * p + chunk, depth, stride=CHUNKS * G)
            out_ref[p, :, j * LANES : (j + 1) * LANES] = vol_ref[spot, :].astype(BF16)


def cast_rows(volume, chunk, *tokens):
    depth, rows, cols = volume.shape
    flat = far(volume.reshape(depth * rows, cols))
    parts = 4
    return call(
        functools.partial(cast_kernel, chunk, parts),
        grid=(cols // (LANES * parts),),
        in_specs=lanes(flat, LANES, parts) + [ANY] * len(tokens),
        out_specs=across((G, depth, cols), LANES * parts),
        results=value((G, depth, cols), BF16),
    )(*[flat] * parts, *tokens)


def split_kernel(here_ref, own_ref, got_ref, *refs):
    out_refs, wide = refs[:-1], refs[-1]
    depth, rows, cols = own_ref.shape
    place = lax.rem(here_ref[0], G)

    def fill(ref):
        for j in range(cols // LANES):
            wide[j] = ref[:, :, j * LANES : (j + 1) * LANES].astype(F32).reshape(wide.shape[1:])

    @pl.when(place == G - 1)
    def _():
        fill(got_ref)

    @pl.when(place != G - 1)
    def _():
        fill(own_ref)

    for j in range(cols // LANES):
        at = pl.ds(j * LANES, LANES)
        for c in range(CHUNKS):
            for m in range(G):
                spot = pl.ds(row_of(place, m, c), depth, stride=rows)
                out_refs[c * G + m][:, at] = wide.at[j][spot, :].astype(BF16)


def split_rows(here, own, got):
    depth, rows, cols = own.shape
    tile = 512
    block = across(own.shape, tile)
    return call(
        split_kernel,
        grid=(cols // tile,),
        in_specs=[SMEM, block, block],
        out_specs=[across((depth, cols), tile)] * (CHUNKS * G),
        results=[value((depth, cols), BF16)] * (CHUNKS * G),
        scratch_shapes=[pltpu.VMEM((tile // LANES, depth * rows, LANES), F32)],
    )(here, far(own), got)


def last_kernel(slabs, here_ref, cover_ref, offset_ref, w_ref, *refs):
    v_refs, (sino_ref, r_ref, b_ref, v, s, r, b, wide) = refs[:CHUNKS], refs[CHUNKS:]
    depth, rows, cols = sino_ref.shape

    @pl.when(here_ref[0] == slabs - 1)
    def _():
        for i, v_ref in enumerate(v_refs):
            pltpu.sync_copy(v_ref, v.at[i])
        pltpu.sync_copy(sino_ref, s)
        block = w_ref[offset_ref[slabs - 1, 0]]
        block = jnp.where(cover_ref[slabs - 1, 0] == 1, block, jnp.zeros_like(block))
        turned = block.astype(F32).T.astype(BF16)

        def column(j, _):
            at = pl.ds(pl.multiple_of(j * LANES, LANES), LANES)
            wide[...] = s[:, :, at].astype(F32).reshape(wide.shape)
            for c in range(CHUNKS):
                for p in range(G):
                    row = CHUNKS * p + c
                    seen = jnp.dot(block, v[c, p, :, at], preferred_element_type=F32)
                    resid = (seen - wide[pl.ds(row, depth, stride=rows), :]).astype(BF16)
                    r[row, :, at] = resid
                    b[row, :, at] = jnp.dot(turned, resid, preferred_element_type=F32)
            return 0

        lax.fori_loop(0, cols // LANES, column, 0)
        pltpu.sync_copy(r, r_ref)
        pltpu.sync_copy(b, b_ref)


def last_group(here, coverage, offsets, weights, vols, sinogram):
    slabs = coverage.shape[0]
    depth, rows, cols = sinogram.shape
    return call(
        functools.partial(last_kernel, slabs),
        in_specs=[SMEM, SMEM, SMEM, VMEM] + [ANY] * (CHUNKS + 1),
        out_specs=[ANY, ANY],
        results=[pltpu.HBM((rows, depth, cols), BF16), pltpu.HBM((rows, depth, cols), F32)],
        scratch_shapes=[
            pltpu.VMEM((CHUNKS, G, depth, cols), BF16),
            pltpu.VMEM(sinogram.shape, BF16),
            pltpu.VMEM((rows, depth, cols), BF16),
            pltpu.VMEM((rows, depth, cols), F32),
            pltpu.VMEM((depth * rows, LANES), F32),
        ],
    )(here, coverage, offsets, weights, *vols, far(sinogram))


def join_kernel(slabs, here_ref, *refs):
    in_refs, (last_ref, out_ref, wide, held) = refs[: CHUNKS * G], refs[CHUNKS * G :]
    depth, rows, cols = out_ref.shape
    place = lax.rem(here_ref[0], G)
    last = here_ref[0] == slabs - 1

    @pl.when(last)
    def _():
        at = pl.ds(pl.multiple_of(pl.program_id(0) * cols, cols), cols)
        pltpu.sync_copy(last_ref.at[:, :, at], held)
        for j in range(cols // LANES):
            for row in range(rows):
                value = held[row, :, j * LANES : (j + 1) * LANES].astype(F32)
                wide.at[j][pl.ds(row, depth, stride=rows), :] = value

    @pl.when(jnp.logical_not(last))
    def _():
        for j in range(cols // LANES):
            at = pl.ds(j * LANES, LANES)
            for c in range(CHUNKS):
                for m in range(G):
                    spot = pl.ds(row_of(place, m, c), depth, stride=rows)
                    wide.at[j][spot, :] = in_refs[c * G + m][:, at].astype(F32)

    for j in range(cols // LANES):
        out_ref[:, :, j * LANES : (j + 1) * LANES] = wide[j].reshape(depth, rows, LANES).astype(out_ref.dtype)


def join_rows(here, slabs, blocks, last):
    rows, depth, cols = last.shape
    tile = 512
    return call(
        functools.partial(join_kernel, slabs),
        grid=(cols // tile,),
        in_specs=[SMEM] + [across((depth, cols), tile)] * len(blocks) + [ANY],
        out_specs=across((depth, rows, cols), tile),
        results=value((depth, rows, cols), BF16),
        scratch_shapes=[
            pltpu.VMEM((tile // LANES, depth * rows, LANES), F32),
            pltpu.VMEM((rows, depth, tile), BF16),
        ],
    )(here, *blocks, far(last))


def finish_kernel(slabs, here_ref, tv_ref, *refs):
    in_refs, (last_ref, out_ref, wide, held) = refs[:CHUNKS], refs[CHUNKS:]
    depth, rows, cols = out_ref.shape
    for j in range(cols // LANES):
        at = pl.ds(j * LANES, LANES)
        for c in range(CHUNKS):
            for p in range(G):
                spot = pl.ds(CHUNKS * p + c, depth, stride=rows)
                wide.at[j][spot, :] = in_refs[c][p, :, at].astype(F32)

    @pl.when(here_ref[0] == slabs - 1)
    def _():
        at = pl.ds(pl.multiple_of(pl.program_id(0) * cols, cols), cols)
        pltpu.sync_copy(last_ref.at[:, :, at], held)
        for j in range(cols // LANES):
            for row in range(rows):
                spot = pl.ds(row, depth, stride=rows)
                wide.at[j][spot, :] = wide.at[j][spot, :] + held[row, :, j * LANES : (j + 1) * LANES]

    for j in range(cols // LANES):
        at = pl.ds(j * LANES, LANES)
        out_ref[:, :, at] = tv_ref[:, :, at] + wide[j].reshape(depth, rows, LANES)


def finish(here, slabs, tv, blocks, last):
    depth, rows, cols = tv.shape
    tile = 256
    whole = across(tv.shape, tile)
    return call(
        functools.partial(finish_kernel, slabs),
        grid=(cols // tile,),
        in_specs=[SMEM, whole] + [across(blocks[0].shape, tile)] * len(blocks) + [ANY],
        out_specs=whole,
        results=value((depth, rows, cols), F32),
        scratch_shapes=[
            pltpu.VMEM((tile // LANES, depth * rows, LANES), F32),
            pltpu.VMEM((rows, depth, tile), F32),
        ],
    )(here, far(tv), *blocks, far(last))


def band_kernel(slabs, span, here_ref, cover_ref, offset_ref, w_ref, proj_ref, back_ref, turned):
    side = w_ref.shape[1]
    place = lax.rem(here_ref[0], G)
    first = here_ref[0] - place
    zero = jnp.zeros((side, side), BF16)
    for i in range(w_ref.shape[0]):
        turned[i] = w_ref[i].astype(F32).T.astype(BF16)

    def block(ref, i, j):
        k = j - i
        known, step = jnp.clip(i, 0, slabs - 1), jnp.clip(k, 0, span - 1)
        inside = (i >= 0) & (i < slabs) & (j >= 0) & (j < slabs) & (k >= 0) & (k < span)
        live = inside & (cover_ref[known, step] == 1)
        return jnp.where(live, ref[offset_ref[known, step]], zero)

    def group(m):
        to = jnp.bitwise_xor(place, m)
        return first + jnp.where(to == G - 1, -1, to)

    seen = [first + s for s in range(2 * G)] + [first - 1]
    seeing = [group(m) for m in range(G)] + [group(m) - G for m in range(G)] + [first + G - 1]
    for r in range(G):
        for s in range(2 * G + 1):
            at = (pl.ds(r * side, side), pl.ds(s * side, side))
            proj_ref[at] = block(w_ref, group(r), seen[s])
            back_ref[at] = block(turned, seeing[s], first + r)


def bands(here, coverage, offsets, weights):
    slabs, span = coverage.shape
    side = weights.shape[1]
    shape = (G * side, (2 * G + 1) * side)
    return call(
        functools.partial(band_kernel, slabs, span),
        in_specs=[SMEM, SMEM, SMEM, pl.BlockSpec(weights.shape, lambda i: (0, 0, 0))],
        grid=(1,),
        out_specs=[pl.BlockSpec(shape, lambda i: (0, 0))] * 2,
        results=[value(shape, BF16)] * 2,
        scratch_shapes=[pltpu.VMEM(weights.shape, BF16)],
    )(here, coverage, offsets, weights)


def project_kernel(here_ref, band_ref, own_ref, high_ref, low_ref, *refs):
    sinos, (r_ref, down_ref) = refs[:G], refs[-2:]
    side = low_ref.shape[0]
    seen = jnp.concatenate([own_ref[...], high_ref[...], low_ref[...]], axis=0)
    total = jnp.dot(band_ref[...], seen, preferred_element_type=F32)
    for m in range(G):
        at = pl.ds(m * side, side)
        r_ref[at, :] = (total[m * side : (m + 1) * side] - sinos[m][...].astype(F32)).astype(BF16)
    spot = jnp.bitwise_xor(lax.rem(here_ref[0], G), G - 1)
    down_ref[...] = r_ref[pl.ds(pl.multiple_of(spot * side, side), side), :]


def project(here, band, own, high, low, sinos, *tokens):
    side, cols = low.shape
    tile = 512
    one = across((side, cols), tile)
    many = across(own.shape, tile)
    return call(
        project_kernel,
        grid=(cols // tile,),
        in_specs=[SMEM, pl.BlockSpec(band.shape, lambda i: (0, 0)), many, many] + [one] * (G + 1) + [ANY] * len(tokens),
        out_specs=[many, one],
        results=[value(own.shape, BF16), value((side, cols), BF16)],
    )(here, band, own, high, low, *sinos, *tokens)


def deal_kernel(here_ref, r_ref, high_ref, *out_refs):
    side = high_ref.shape[0]
    place = lax.rem(here_ref[0], G)
    for m in range(G):
        last = jnp.bitwise_xor(place, m) == G - 1
        out_refs[m][...] = jnp.where(last, high_ref[...], r_ref[m * side : (m + 1) * side])


def deal(here, resid, high):
    side, cols = high.shape
    tile = 512
    one = across((side, cols), tile)
    return call(
        deal_kernel,
        grid=(cols // tile,),
        in_specs=[SMEM, across(resid.shape, tile), one],
        out_specs=[one] * G,
        results=[value((side, cols), BF16)] * G,
    )(here, resid, high)


def back_kernel(band_ref, own_ref, low_ref, high_ref, out_ref):
    seeing = jnp.concatenate([own_ref[...], low_ref[...], high_ref[...]], axis=0)
    total = jnp.dot(band_ref[...], seeing, preferred_element_type=F32)
    out_ref[...] = total.astype(BF16).reshape(out_ref.shape)


def back(band, own, low, high):
    side, cols = high.shape
    tile = 512
    many = across(own.shape, tile)
    return call(
        back_kernel,
        grid=(cols // tile,),
        in_specs=[pl.BlockSpec(band.shape, lambda i: (0, 0)), many, many, across((side, cols), tile)],
        out_specs=across((G, side, cols), tile),
        results=value((G, side, cols), BF16),
    )(band, own, low, high)


def tv_kernel(low_ref, high_ref, next_ref, vol_ref, out_ref, flux_ref):
    step = pl.program_id(0)
    steps = pl.num_programs(0)
    deep, rows, cols = vol_ref.shape
    row = lax.broadcasted_iota(jnp.int32, (rows, cols), 0)
    col = lax.broadcasted_iota(jnp.int32, (rows, cols), 1)

    def up_y(v):
        return jnp.where(row == rows - 1, 0.0, pltpu.roll(v, rows - 1, 0))

    def up_x(v):
        return jnp.where(col == cols - 1, 0.0, pltpu.roll(v, cols - 1, 1))

    def scale_of(cur, above):
        dz = above - cur
        dy = up_y(cur) - cur
        dx = up_x(cur) - cur
        return dz, dy, dx, 0.5 * lax.rsqrt(dz * dz + dy * dy + dx * dx + 0.25)

    def edge(v):
        return 0.5 * v * lax.rsqrt(v * v + 0.25)

    @pl.when(step == 0)
    def _():
        dz, _, _, scale = scale_of(low_ref[0], vol_ref[0])
        flux_ref[...] = dz * scale

    def one(z, cur, above, below_flux):
        dz, dy, dx, scale = scale_of(cur, above)
        fz, fy, fx = dz * scale, dy * scale, dx * scale
        sides = edge(cur)
        fy_low = jnp.where(row == 0, sides, pltpu.roll(fy, 1, 0))
        fx_low = jnp.where(col == 0, sides, pltpu.roll(fx, 1, 1))
        out_ref[z] = (below_flux - fz) + (fy_low - fy) + (fx_low - fx)
        return fz

    def body(z, flux):
        return one(z, vol_ref[z], vol_ref[z + 1], flux)

    flux = lax.fori_loop(0, deep - 1, body, flux_ref[...], unroll=5)
    above = jnp.where(step == steps - 1, high_ref[0], next_ref[0])
    flux_ref[...] = one(deep - 1, vol_ref[deep - 1], above, flux)


def half_tv(volume, low, high):
    depth, rows, cols = volume.shape
    deep = 16
    steps = depth // deep
    edge = pl.BlockSpec((1, rows, cols), lambda i: (0, 0, 0))
    body = pl.BlockSpec((deep, rows, cols), lambda i: (i, 0, 0))
    after = pl.BlockSpec((1, rows, cols), lambda i: (jnp.minimum((i + 1) * deep, depth - 1), 0, 0))
    return call(
        tv_kernel,
        grid=(steps,),
        in_specs=[edge, edge, after, body],
        out_specs=body,
        results=pltpu.HBM(volume.shape, F32),
        scratch_shapes=[pltpu.VMEM((rows, cols), F32)],
    )(low, high, far(volume), far(volume))


def local(volume, sinogram, weights, coverage, offsets):
    slabs = lax.axis_size("slab")
    here = lax.axis_index("slab").astype(jnp.int32).reshape(1)
    depth, rows, cols = volume.shape

    vols0 = cast_rows(volume, 0)
    got = moved(lax.optimization_barrier((sinogram, vols0))[0], G, only=G - 1)
    own0 = exchanged(vols0)
    band_p, band_b = bands(here, coverage, offsets, weights)
    below = moved(volume[-1:], 1)
    above = moved(volume[:1], -1)
    vols1 = cast_rows(volume, 1, own0)
    own1 = exchanged(vols1)
    r_last, b_last = last_group(here, coverage, offsets, weights, [vols0, vols1], sinogram)
    sino = split_rows(here, sinogram, got)
    sinos = [dealt_out(sino[c * G : (c + 1) * G]) for c in range(CHUNKS)]
    tv = half_tv(volume, below, above)

    resid_blocks, back_rows = [], []
    for c, own in enumerate((own0, own1)):
        own = own.reshape(G * depth, cols)
        high = moved(own, -G)
        low = moved(own[(G - 1) * depth :], G)
        resid, down = project(here, band_p, own, high, low, sinos[c], *([tv] if c else []))
        r_low = moved(resid, G)
        r_high = moved(down, -G)
        resid_blocks += dealt_out(deal(here, resid, r_high))
        back_rows.append(exchanged(back(band_b, resid, r_low, r_high)))

    residual = join_rows(here, slabs, resid_blocks, r_last)
    gradient = finish(here, slabs, tv, back_rows, b_last)
    return (gradient, residual)


def solution(mesh):
    placed = (P("slab", "grp", None), P("slab", "grp", None), P(), P(), P())
    return jax.shard_map(
        local,
        mesh=mesh,
        in_specs=placed,
        out_specs=(P("slab", "grp", None), P("slab", "grp", None)),
        check_vma=False,
    )
```

```python
import functools

import jax
import jax.numpy as jnp
from jax import lax
from jax.experimental import pallas as pl
from jax.experimental.pallas import tpu as pltpu
from jax.sharding import PartitionSpec as P

G = 4
CHUNKS = 2
F32 = jnp.float32
BF16 = jnp.bfloat16
MIB = 1024 * 1024
LANES = 128
OTHERS = (0, 2, 3)
SMEM = pl.BlockSpec(memory_space=pltpu.SMEM)
VMEM = pl.BlockSpec(memory_space=pltpu.VMEM)
ANY = pl.BlockSpec(memory_space=pl.ANY)


def moved(value, steps, only=None):
    count = lax.axis_size("slab")
    first, last = max(0, -steps), min(count, count - steps)
    pairs = [(i, i + steps) for i in range(first, last) if only is None or i % G == only]
    return lax.ppermute(value, "slab", pairs)


def swapped(value, bits):
    count = lax.axis_size("slab")
    return lax.ppermute(value, "slab", [(i, i ^ bits) for i in range(count)])


def exchanged(blocks):
    return [block if m == 0 else swapped(block, m) for m, block in blocks]


def call(kernel, us, *, results, vmem=16, **how):
    return pl.pallas_call(
        kernel,
        out_shape=results,
        compiler_params=pltpu.CompilerParams(vmem_limit_bytes=vmem * MIB),
        cost_estimate=pl.CostEstimate(flops=int(us * 1.15e9), bytes_accessed=1000, transcendentals=0),
        **how,
    )


def value(shape, dtype):
    return jax.ShapeDtypeStruct(shape, dtype)


def far(array):
    return pltpu.with_memory_space_constraint(array, pltpu.HBM)


def across(shape, tile):
    block = shape[:-1] + (tile,)
    return pl.BlockSpec(block, lambda i: (0,) * (len(shape) - 1) + (i,))


def lanes(array, tile, parts):
    block = array.shape[:-1] + (tile,)
    zeros = (0,) * (len(block) - 1)
    return [pl.BlockSpec(block, lambda i, j=j: zeros + (i * parts + j,)) for j in range(parts)]


def row_of(place, m, chunk):
    return CHUNKS * jnp.bitwise_xor(place, m) + chunk


def cast_kernel(parts, here_ref, *refs):
    vol_refs, out_refs = refs[:parts], refs[parts:]
    rows = CHUNKS * G
    depth = vol_refs[0].shape[0] // rows
    place = lax.rem(here_ref[0], G)
    for j, vol_ref in enumerate(vol_refs):
        at = pl.ds(j * LANES, LANES)
        ends = jnp.concatenate([vol_ref[:rows, :], vol_ref[(depth - 1) * rows :, :]], axis=0).astype(BF16)
        for c in range(CHUNKS):
            for m in range(G):
                out_ref = out_refs[c * G + m]
                spot = pl.ds(row_of(place, m, c), depth, stride=rows)
                out_ref[:depth, at] = vol_ref[spot, :].astype(BF16)
                if out_ref.shape[0] > depth:
                    out_ref[depth:, at] = ends


def cast_rows(here, volume):
    depth, rows, cols = volume.shape
    flat = far(volume.reshape(depth * rows, cols))
    parts = 2
    shapes = [(depth + (2 * rows if c == 0 and m % 2 else 0), cols) for c in range(CHUNKS) for m in range(G)]
    return call(
        functools.partial(cast_kernel, parts),
        3.5,
        grid=(cols // (LANES * parts),),
        in_specs=[SMEM] + lanes(flat, LANES, parts),
        out_specs=[across(shape, LANES * parts) for shape in shapes],
        results=[value(shape, BF16) for shape in shapes],
    )(here, *[flat] * parts)


def pack_kernel(here_ref, *refs):
    in_refs, (all_ref, last_ref) = refs[:G], refs[-2:]
    side = in_refs[0].shape[0]
    for m in range(G):
        all_ref[m * side : (m + 1) * side] = in_refs[m][:side]
    spot = jnp.bitwise_xor(lax.rem(here_ref[0], G), G - 1)
    last_ref[:side] = all_ref[pl.ds(pl.multiple_of(spot * side, side), side), :]
    if last_ref.shape[0] > side:
        all_ref[G * side :] = in_refs[G - 1][side:]
        last_ref[side:] = in_refs[G - 1][side:]


def pack(here, blocks, *tokens):
    side, cols = blocks[0].shape
    more = blocks[G - 1].shape[0] - side
    tile = 512
    shapes = [(G * side + more, cols), (side + more, cols)]
    return call(
        pack_kernel,
        1,
        grid=(cols // tile,),
        in_specs=[SMEM] + [across(block.shape, tile) for block in blocks] + [ANY] * len(tokens),
        out_specs=[across(shape, tile) for shape in shapes],
        results=[value(shape, BF16) for shape in shapes],
    )(here, *blocks, *tokens)


def blocks_of(refs, depth):
    both, rest = refs[0], refs[1:]
    found = []
    for c in range(CHUNKS):
        found.append((c, 1, both.at[c * depth : (c + 1) * depth]))
        for n, m in enumerate(OTHERS):
            found.append((c, m, rest[c * len(OTHERS) + n]))
    return found


def split_kernel(here_ref, own_ref, got_ref, *refs):
    out_refs, wide = refs[-CHUNKS * len(OTHERS) - 2 : -1], refs[-1]
    depth, rows, cols = own_ref.shape
    place = lax.rem(here_ref[0], G)

    def fill(ref):
        for j in range(cols // LANES):
            wide[j] = ref[:, :, j * LANES : (j + 1) * LANES].astype(F32).reshape(wide.shape[1:])

    @pl.when(place == G - 1)
    def _():
        fill(got_ref)

    @pl.when(place != G - 1)
    def _():
        fill(own_ref)

    for j in range(cols // LANES):
        at = pl.ds(j * LANES, LANES)
        for c, m, ref in blocks_of(out_refs, depth):
            spot = pl.ds(row_of(place, m, c), depth, stride=rows)
            ref[:, at] = wide.at[j][spot, :].astype(BF16)


def split_rows(here, own, got, *tokens):
    depth, rows, cols = own.shape
    tile = 512
    block = across(own.shape, tile)
    both, one = (CHUNKS * depth, cols), (depth, cols)
    count = CHUNKS * len(OTHERS)
    return call(
        split_kernel,
        4,
        grid=(cols // tile,),
        in_specs=[SMEM, block, block] + [ANY] * len(tokens),
        out_specs=[across(both, tile)] + [across(one, tile)] * count,
        results=[pltpu.HBM(both, BF16)] + [pltpu.HBM(one, BF16)] * count,
        scratch_shapes=[pltpu.VMEM((tile // LANES, depth * rows, LANES), F32)],
    )(here, far(own), got, *tokens)


def last_kernel(slabs, here_ref, cover_ref, offset_ref, w_ref, *refs):
    v_refs, (sino_ref, r_ref, b_ref, v, s, r, b, wide) = refs[: CHUNKS * G], refs[CHUNKS * G :]
    depth, rows, cols = sino_ref.shape

    @pl.when(here_ref[0] == slabs - 1)
    def _():
        for i, v_ref in enumerate(v_refs):
            pltpu.sync_copy(v_ref.at[:depth], v.at[i])
        pltpu.sync_copy(sino_ref, s)
        block = w_ref[offset_ref[slabs - 1, 0]]
        block = jnp.where(cover_ref[slabs - 1, 0] == 1, block, jnp.zeros_like(block))
        turned = block.astype(F32).T.astype(BF16)

        def column(j, _):
            at = pl.ds(pl.multiple_of(j * LANES, LANES), LANES)
            wide[...] = s[:, :, at].astype(F32).reshape(wide.shape)
            for c in range(CHUNKS):
                for m in range(G):
                    row = CHUNKS * ((G - 1) ^ m) + c
                    seen = jnp.dot(block, v[c * G + m, :, at], preferred_element_type=F32)
                    resid = (seen - wide[pl.ds(row, depth, stride=rows), :]).astype(BF16)
                    r[row, :, at] = resid
                    b[row, :, at] = jnp.dot(turned, resid, preferred_element_type=F32)
            return 0

        lax.fori_loop(0, cols // LANES, column, 0)
        pltpu.sync_copy(r, r_ref)
        pltpu.sync_copy(b, b_ref)


def last_group(here, coverage, offsets, weights, vols, sinogram):
    slabs = coverage.shape[0]
    depth, rows, cols = sinogram.shape
    return call(
        functools.partial(last_kernel, slabs),
        0.3,
        in_specs=[SMEM, SMEM, SMEM, VMEM] + [ANY] * (CHUNKS * G + 1),
        out_specs=[ANY, ANY],
        results=[pltpu.HBM((rows, depth, cols), BF16), pltpu.HBM((rows, depth, cols), F32)],
        scratch_shapes=[
            pltpu.VMEM((CHUNKS * G, depth, cols), BF16),
            pltpu.VMEM(sinogram.shape, BF16),
            pltpu.VMEM((rows, depth, cols), BF16),
            pltpu.VMEM((rows, depth, cols), F32),
            pltpu.VMEM((depth * rows, LANES), F32),
        ],
    )(here, coverage, offsets, weights, *vols, far(sinogram))


def join_kernel(slabs, here_ref, *refs):
    in_refs, (last_ref, out_ref, wide, held) = refs[:-4], refs[-4:]
    depth, rows, cols = out_ref.shape
    place = lax.rem(here_ref[0], G)
    last = here_ref[0] == slabs - 1

    @pl.when(last)
    def _():
        at = pl.ds(pl.multiple_of(pl.program_id(0) * cols, cols), cols)
        pltpu.sync_copy(last_ref.at[:, :, at], held)
        for j in range(cols // LANES):
            for row in range(rows):
                value = held[row, :, j * LANES : (j + 1) * LANES].astype(F32)
                wide.at[j][pl.ds(row, depth, stride=rows), :] = value

    @pl.when(jnp.logical_not(last))
    def _():
        for j in range(cols // LANES):
            at = pl.ds(j * LANES, LANES)
            for c, m, ref in blocks_of(in_refs, depth):
                spot = pl.ds(row_of(place, m, c), depth, stride=rows)
                wide.at[j][spot, :] = ref[:, at].astype(F32)

    for j in range(cols // LANES):
        out_ref[:, :, j * LANES : (j + 1) * LANES] = wide[j].reshape(depth, rows, LANES).astype(out_ref.dtype)


def join_rows(here, slabs, blocks, last):
    rows, depth, cols = last.shape
    tile = 512
    return call(
        functools.partial(join_kernel, slabs),
        2.6,
        grid=(cols // tile,),
        in_specs=[SMEM] + [across(block.shape, tile) for block in blocks] + [ANY],
        out_specs=across((depth, rows, cols), tile),
        results=value((depth, rows, cols), BF16),
        scratch_shapes=[
            pltpu.VMEM((tile // LANES, depth * rows, LANES), F32),
            pltpu.VMEM((rows, depth, tile), BF16),
        ],
    )(here, *blocks, far(last))


def finish_kernel(slabs, here_ref, tv_ref, *refs):
    in_refs, (last_ref, out_ref, wide, held) = refs[:-4], refs[-4:]
    place = lax.rem(here_ref[0], G)
    depth, rows, cols = out_ref.shape
    for j in range(cols // LANES):
        at = pl.ds(j * LANES, LANES)
        for c, m, ref in blocks_of(in_refs, depth):
            spot = pl.ds(row_of(place, m, c), depth, stride=rows)
            wide.at[j][spot, :] = ref[:, at].astype(F32)

    @pl.when(here_ref[0] == slabs - 1)
    def _():
        at = pl.ds(pl.multiple_of(pl.program_id(0) * cols, cols), cols)
        pltpu.sync_copy(last_ref.at[:, :, at], held)
        for j in range(cols // LANES):
            for row in range(rows):
                spot = pl.ds(row, depth, stride=rows)
                wide.at[j][spot, :] = wide.at[j][spot, :] + held[row, :, j * LANES : (j + 1) * LANES]

    for j in range(cols // LANES):
        at = pl.ds(j * LANES, LANES)
        out_ref[:, :, at] = tv_ref[:, :, at] + wide[j].reshape(depth, rows, LANES)


def finish(here, slabs, tv, blocks, last):
    depth, rows, cols = tv.shape
    tile = 256
    whole = across(tv.shape, tile)
    return call(
        functools.partial(finish_kernel, slabs),
        5,
        grid=(cols // tile,),
        in_specs=[SMEM, whole] + [across(block.shape, tile) for block in blocks] + [ANY],
        out_specs=whole,
        results=value((depth, rows, cols), F32),
        scratch_shapes=[
            pltpu.VMEM((tile // LANES, depth * rows, LANES), F32),
            pltpu.VMEM((rows, depth, tile), F32),
        ],
    )(here, far(tv), *blocks, far(last))


def band_kernel(slabs, span, here_ref, cover_ref, offset_ref, w_ref, *refs):
    proj_ref, back_ref, turned = refs[-3:]
    side = w_ref.shape[1]
    place = lax.rem(here_ref[0], G)
    first = here_ref[0] - place
    zero = jnp.zeros((side, side), BF16)
    for i in range(w_ref.shape[0]):
        turned[i] = w_ref[i].astype(F32).T.astype(BF16)

    def block(ref, i, j):
        k = j - i
        known, step = jnp.clip(i, 0, slabs - 1), jnp.clip(k, 0, span - 1)
        inside = (i >= 0) & (i < slabs) & (j >= 0) & (j < slabs) & (k >= 0) & (k < span)
        live = inside & (cover_ref[known, step] == 1)
        return jnp.where(live, ref[offset_ref[known, step]], zero)

    def slab(m):
        return first + jnp.bitwise_xor(place, m)

    def group(m):
        to = jnp.bitwise_xor(place, m)
        return first + jnp.where(to == G - 1, -1, to)

    seen = [slab(m) for m in range(G)] + [slab(m) + G for m in range(G)] + [first - 1]
    seeing = [group(m) for m in range(G)] + [group(m) - G for m in range(G)] + [first + G - 1]
    for r in range(G):
        for s in range(2 * G + 1):
            at = (pl.ds(r * side, side), pl.ds(s * side, side))
            proj_ref[at] = block(w_ref, group(r), seen[s])
            back_ref[at] = block(turned, seeing[s], slab(r))


def bands(here, coverage, offsets, weights, *tokens):
    slabs, span = coverage.shape
    side = weights.shape[1]
    shape = (G * side, (2 * G + 1) * side)
    return call(
        functools.partial(band_kernel, slabs, span),
        1.6,
        in_specs=[SMEM, SMEM, SMEM, pl.BlockSpec(weights.shape, lambda i: (0, 0, 0))] + [ANY] * len(tokens),
        grid=(1,),
        out_specs=[pl.BlockSpec(shape, lambda i: (0, 0))] * 2,
        results=[pltpu.HBM(shape, BF16)] * 2,
        scratch_shapes=[pltpu.VMEM(weights.shape, BF16)],
    )(here, coverage, offsets, weights, *tokens)


def project_kernel(here_ref, band_ref, own_ref, high_ref, low_ref, *refs):
    (both_ref, *rest), (r_ref, down_ref) = refs[:G], refs[-2:]
    side = down_ref.shape[0]
    n = G * side
    sinos = {1: both_ref, **dict(zip(OTHERS, rest))}
    seen = jnp.concatenate([own_ref[:n], high_ref[:n], low_ref[:side]], axis=0)
    total = jnp.dot(band_ref[...], seen, preferred_element_type=F32)
    for m in range(G):
        at = pl.ds(m * side, side)
        r_ref[at, :] = (total[m * side : (m + 1) * side] - sinos[m][...].astype(F32)).astype(BF16)
    spot = jnp.bitwise_xor(lax.rem(here_ref[0], G), G - 1)
    down_ref[...] = r_ref[pl.ds(pl.multiple_of(spot * side, side), side), :]


def project(here, chunk, band, own, high, low, sinos, *tokens):
    n, side = band.shape[0], band.shape[0] // G
    cols = own.shape[1]
    tile = 512
    one = across((side, cols), tile)
    return call(
        project_kernel,
        3,
        grid=(cols // tile,),
        in_specs=[SMEM, pl.BlockSpec(band.shape, lambda i: (0, 0))]
        + [across(array.shape, tile) for array in (own, high, low)]
        + [pl.BlockSpec((side, tile), lambda i: (chunk, i))]
        + [one] * len(OTHERS)
        + [ANY] * len(tokens),
        out_specs=[across((n, cols), tile), one],
        results=[value((n, cols), BF16), value((side, cols), BF16)],
    )(here, band, own, high, low, *sinos, *tokens)


def deal_kernel(chunk, here_ref, r_ref, high_ref, *refs):
    out_refs = refs[-G:]
    side = high_ref.shape[0]
    place = lax.rem(here_ref[0], G)

    def block(m):
        last = jnp.bitwise_xor(place, m) == G - 1
        return jnp.where(last, high_ref[...], r_ref[m * side : (m + 1) * side])

    put_blocks(chunk, block, out_refs, refs[0], side)


def put_blocks(chunk, block, out_refs, before_ref, side):
    both, rest = out_refs[0], out_refs[1:]
    if chunk:
        both[:side] = before_ref[...]
        both[side:] = block(1)
    else:
        both[...] = block(1)
    for n, m in enumerate(OTHERS):
        rest[n][...] = block(m)


def block_results(chunk, side, cols, tile):
    first = (CHUNKS * side if chunk else side, cols)
    shapes = [first] + [(side, cols)] * len(OTHERS)
    return dict(out_specs=[across(s, tile) for s in shapes], results=[value(s, BF16) for s in shapes])


def deal(here, chunk, resid, high, *before):
    side, cols = high.shape
    tile = 512
    one = across((side, cols), tile)
    return call(
        functools.partial(deal_kernel, chunk),
        1,
        grid=(cols // tile,),
        in_specs=[SMEM, across(resid.shape, tile), one] + [one] * len(before),
        **block_results(chunk, side, cols, tile),
    )(here, resid, high, *before)


def back_kernel(chunk, band_ref, own_ref, low_ref, high_ref, *refs):
    side = high_ref.shape[0]
    seeing = jnp.concatenate([own_ref[...], low_ref[...], high_ref[...]], axis=0)
    total = jnp.dot(band_ref[...], seeing, preferred_element_type=F32)
    put_blocks(chunk, lambda m: total[m * side : (m + 1) * side].astype(BF16), refs[-G:], refs[0], side)


def back(chunk, band, own, low, high, before, *tokens):
    side, cols = high.shape
    tile = 512
    one = across((side, cols), tile)
    many = across(own.shape, tile)
    return call(
        functools.partial(back_kernel, chunk),
        3,
        grid=(cols // tile,),
        in_specs=[pl.BlockSpec(band.shape, lambda i: (0, 0)), many, many, one]
        + [one] * len(before)
        + [ANY] * len(tokens),
        **block_results(chunk, side, cols, tile),
    )(band, own, low, high, *before, *tokens)


def tv_kernel(here_ref, near_ref, next_level_ref, far_ref, last_level_ref, next_ref, vol_ref, *refs):
    out_ref, flux_ref = refs[-2:]
    step = pl.program_id(0)
    steps = pl.num_programs(0)
    deep, rows, cols = vol_ref.shape
    place = lax.rem(here_ref[0], G)
    row = lax.broadcasted_iota(jnp.int32, (rows, cols), 0)

    def low_slice():
        inside = jnp.where(place == 2, far_ref[...], near_ref[...])
        return jnp.where(place == 0, last_level_ref[...], inside)[rows:].astype(F32)

    def high_slice():
        inside = jnp.where(place == 1, far_ref[...], near_ref[...])
        return jnp.where(place == G - 1, next_level_ref[...], inside)[:rows].astype(F32)

    col = lax.broadcasted_iota(jnp.int32, (rows, cols), 1)

    def up_y(v):
        return jnp.where(row == rows - 1, 0.0, pltpu.roll(v, rows - 1, 0))

    def up_x(v):
        return jnp.where(col == cols - 1, 0.0, pltpu.roll(v, cols - 1, 1))

    def scale_of(cur, above):
        dz = above - cur
        dy = up_y(cur) - cur
        dx = up_x(cur) - cur
        return dz, dy, dx, 0.5 * lax.rsqrt(dz * dz + dy * dy + dx * dx + 0.25)

    def edge(v):
        return 0.5 * v * lax.rsqrt(v * v + 0.25)

    @pl.when(step == 0)
    def _():
        dz, _, _, scale = scale_of(low_slice(), vol_ref[0])
        flux_ref[...] = dz * scale

    def one(z, cur, above, below_flux):
        dz, dy, dx, scale = scale_of(cur, above)
        fz, fy, fx = dz * scale, dy * scale, dx * scale
        sides = edge(cur)
        fy_low = jnp.where(row == 0, sides, pltpu.roll(fy, 1, 0))
        fx_low = jnp.where(col == 0, sides, pltpu.roll(fx, 1, 1))
        out_ref[z] = (below_flux - fz) + (fy_low - fy) + (fx_low - fx)
        return fz

    def body(z, flux):
        return one(z, vol_ref[z], vol_ref[z + 1], flux)

    flux = lax.fori_loop(0, deep - 1, body, flux_ref[...], unroll=5)
    above = jnp.where(step == steps - 1, high_slice(), next_ref[0])
    flux_ref[...] = one(deep - 1, vol_ref[deep - 1], above, flux)


def half_tv(here, volume, ends, *tokens):
    depth, rows, cols = volume.shape
    deep = 16
    steps = depth // deep
    edges = [pl.BlockSpec((2 * rows, cols), lambda i, last=end.shape[0] // (2 * rows) - 1: (last, 0)) for end in ends]
    body = pl.BlockSpec((deep, rows, cols), lambda i: (i, 0, 0))
    after = pl.BlockSpec((1, rows, cols), lambda i: (jnp.minimum((i + 1) * deep, depth - 1), 0, 0))
    return call(
        tv_kernel,
        7,
        grid=(steps,),
        in_specs=[SMEM] + edges + [after, body] + [ANY] * len(tokens),
        out_specs=body,
        results=pltpu.HBM(volume.shape, F32),
        scratch_shapes=[pltpu.VMEM((rows, cols), F32)],
    )(here, *ends, far(volume), far(volume), *tokens)


def local(volume, sinogram, weights, coverage, offsets):
    slabs = lax.axis_size("slab")
    here = lax.axis_index("slab").astype(jnp.int32).reshape(1)

    vols = cast_rows(here, volume)
    vols0, vols1 = vols[:G], vols[G:]
    got = moved(lax.optimization_barrier((sinogram, vols0[0]))[0], G, only=G - 1)
    blocks0 = exchanged(enumerate(vols0))
    own0, edge0 = pack(here, blocks0)
    band_p, band_b = bands(here, coverage, offsets, weights, own0)
    sino = split_rows(here, sinogram, got, own0)
    own1, edge1 = pack(here, exchanged(enumerate(vols1)), sino[0])
    r_last, b_last = last_group(here, coverage, offsets, weights, vols, sinogram)
    sino_core = swapped(sino[0], 1)
    high0, high1 = moved(own0, -G), moved(own1, -G)
    low0, low1 = moved(edge0, G), moved(edge1, G)

    def residuals(c, own, high, low, *tokens):
        sinos = exchanged(zip(OTHERS, sino[1 + c * len(OTHERS) :]))
        resid, down = project(here, c, band_p, own, high, low, [sino_core] + sinos, *tokens)
        return resid, moved(resid, G), moved(down, -G)

    resid0, from_low0, from_high0 = residuals(0, own0, high0, low0, low1)
    tv = half_tv(here, volume, [blocks0[1], high0, blocks0[3], low0], resid0)
    dealt0 = deal(here, 0, resid0, from_high0)
    resid1, from_low1, from_high1 = residuals(1, own1, high1, low1, dealt0[0], tv)
    dealt1 = deal(here, 1, resid1, from_high1, dealt0[0])
    resid_blocks0 = exchanged(zip(OTHERS, dealt0[1:]))
    resid_blocks1 = exchanged(zip(OTHERS, dealt1[1:]))
    resid_blocks = [swapped(dealt1[0], 1)] + resid_blocks0 + resid_blocks1

    backs0 = back(0, band_b, resid0, from_low0, from_high0, [], dealt1[1], *resid_blocks0)
    back_blocks0 = exchanged(zip(OTHERS, backs0[1:]))
    backs1 = back(1, band_b, resid1, from_low1, from_high1, [backs0[0]], *resid_blocks1, *back_blocks0)
    back_blocks = [swapped(backs1[0], 1)] + back_blocks0 + exchanged(zip(OTHERS, backs1[1:]))

    residual = join_rows(here, slabs, resid_blocks, r_last)
    gradient = finish(here, slabs, tv, back_blocks, b_last)
    return (gradient, residual)


def solution(mesh):
    placed = (P("slab", "grp", None), P("slab", "grp", None), P(), P(), P())
    return jax.shard_map(
        local,
        mesh=mesh,
        in_specs=placed,
        out_specs=(P("slab", "grp", None), P("slab", "grp", None)),
        check_vma=False,
    )
```

```python
import functools

import jax
import jax.numpy as jnp
from jax import lax
from jax.experimental import pallas as pl
from jax.experimental.pallas import tpu as pltpu
from jax.sharding import PartitionSpec as P

G = 4
CHUNKS = 2
F32 = jnp.float32
BF16 = jnp.bfloat16
MIB = 1024 * 1024
LANES = 128
SMEM = pl.BlockSpec(memory_space=pltpu.SMEM)
VMEM = pl.BlockSpec(memory_space=pltpu.VMEM)
ANY = pl.BlockSpec(memory_space=pl.ANY)


def moved(value, steps, only=None):
    count = lax.axis_size("slab")
    first, last = max(0, -steps), min(count, count - steps)
    pairs = [(i, i + steps) for i in range(first, last) if only is None or i % G == only]
    return lax.ppermute(value, "slab", pairs)


def swapped(value, bits):
    count = lax.axis_size("slab")
    return lax.ppermute(value, "slab", [(i, i ^ bits) for i in range(count)])


def direct(chunk, groups, arrays, skip=()):
    found = []
    for group, array in zip(groups, arrays):
        (m,) = group
        if m not in skip:
            found.append((chunk, m, array if m == 0 else swapped(array, m), 0))
    return found


def in_two(chunk, pair, after=None):
    side = pair.shape[0] // 2
    over = swapped(pair, 2)
    if after is not None:
        over = lax.optimization_barrier((over, after))[0]
    return [(chunk, 2, over, 0), (chunk, 3, swapped(over[side:], 1), 0)]


def call(kernel, us, *, results, vmem=16, **how):
    return pl.pallas_call(
        kernel,
        out_shape=results,
        compiler_params=pltpu.CompilerParams(vmem_limit_bytes=vmem * MIB),
        cost_estimate=pl.CostEstimate(flops=int(us * 1.15e9), bytes_accessed=1000, transcendentals=0),
        **how,
    )


def value(shape, dtype):
    return jax.ShapeDtypeStruct(shape, dtype)


def far(array):
    return pltpu.with_memory_space_constraint(array, pltpu.HBM)


def across(shape, tile):
    block = shape[:-1] + (tile,)
    return pl.BlockSpec(block, lambda i: (0,) * (len(shape) - 1) + (i,))


def lanes(array, tile, parts):
    block = array.shape[:-1] + (tile,)
    zeros = (0,) * (len(block) - 1)
    return [pl.BlockSpec(block, lambda i, j=j: zeros + (i * parts + j,)) for j in range(parts)]


def piece_specs(pieces, side, tile):
    return [pl.BlockSpec((side, tile), lambda i, at=at: (at, i)) for _, _, _, at in pieces]


def keys_of(pieces):
    return [(chunk, m) for chunk, m, _, _ in pieces]


def arrays_of(pieces):
    return [array for _, _, array, _ in pieces]


def group_results(groups, side, cols, tile, space=None):
    shapes = [(len(group) * side, cols) for group in groups]
    results = [space(shape, BF16) if space else value(shape, BF16) for shape in shapes]
    return dict(out_specs=[across(shape, tile) for shape in shapes], results=results)


def row_of(place, m, chunk):
    return CHUNKS * jnp.bitwise_xor(place, m) + chunk


CAST_GROUPS = ((0, (0,)), (0, (1,)), (0, (2,)), (0, (3,)), (1, (0,)), (1, (1,)), (1, (2, 3)))


def cast_kernel(parts, here_ref, *refs):
    vol_refs, out_refs = refs[:parts], refs[parts:]
    rows = CHUNKS * G
    depth = vol_refs[0].shape[0] // rows
    place = lax.rem(here_ref[0], G)
    for j, vol_ref in enumerate(vol_refs):
        at = pl.ds(j * LANES, LANES)
        ends = jnp.concatenate([vol_ref[:rows, :], vol_ref[(depth - 1) * rows :, :]], axis=0).astype(BF16)
        for (c, group), out_ref in zip(CAST_GROUPS, out_refs):
            for n, m in enumerate(group):
                spot = pl.ds(row_of(place, m, c), depth, stride=rows)
                out_ref[n * depth : (n + 1) * depth, at] = vol_ref[spot, :].astype(BF16)
            if out_ref.shape[0] > len(group) * depth:
                out_ref[len(group) * depth :, at] = ends


def cast_rows(here, volume):
    depth, rows, cols = volume.shape
    flat = far(volume.reshape(depth * rows, cols))
    parts = 2
    shapes = [(len(g) * depth + (2 * rows if c == 0 and g[0] % 2 else 0), cols) for c, g in CAST_GROUPS]
    return call(
        functools.partial(cast_kernel, parts),
        3.5,
        grid=(cols // (LANES * parts),),
        in_specs=[SMEM] + lanes(flat, LANES, parts),
        out_specs=[across(shape, LANES * parts) for shape in shapes],
        results=[value(shape, BF16) for shape in shapes],
    )(here, *[flat] * parts)


def pack_kernel(here_ref, *refs):
    in_refs, (all_ref, last_ref) = refs[:G], refs[-2:]
    side = in_refs[0].shape[0]
    for m in range(G):
        all_ref[m * side : (m + 1) * side] = in_refs[m][:side]
    spot = jnp.bitwise_xor(lax.rem(here_ref[0], G), G - 1)
    last_ref[:side] = all_ref[pl.ds(pl.multiple_of(spot * side, side), side), :]
    if last_ref.shape[0] > side:
        all_ref[G * side :] = in_refs[G - 1][side:]
        last_ref[side:] = in_refs[G - 1][side:]


def pack(here, pieces, more, *tokens):
    pieces = sorted(pieces, key=lambda piece: piece[1])
    side, cols = pieces[0][2].shape
    tile = 512
    shapes = [(G * side + more, cols), (side + more, cols)]
    specs = piece_specs(pieces, side, tile)
    if more:
        specs = [across(array.shape, tile) for array in arrays_of(pieces)]
    return call(
        pack_kernel,
        1,
        grid=(cols // tile,),
        in_specs=[SMEM] + specs + [ANY] * len(tokens),
        out_specs=[across(shape, tile) for shape in shapes],
        results=[value(shape, BF16) for shape in shapes],
    )(here, *arrays_of(pieces), *tokens)


SPLIT_GROUPS = (((0, 1), (1, 1)), ((0, 0),), ((0, 2),), ((0, 3),), ((1, 0),), ((1, 2), (1, 3)))


def split_kernel(here_ref, own_ref, got_ref, *refs):
    out_refs, wide = refs[-len(SPLIT_GROUPS) - 1 : -1], refs[-1]
    depth, rows, cols = own_ref.shape
    place = lax.rem(here_ref[0], G)

    def fill(ref):
        for j in range(cols // LANES):
            wide[j] = ref[:, :, j * LANES : (j + 1) * LANES].astype(F32).reshape(wide.shape[1:])

    @pl.when(place == G - 1)
    def _():
        fill(got_ref)

    @pl.when(place != G - 1)
    def _():
        fill(own_ref)

    for j in range(cols // LANES):
        at = pl.ds(j * LANES, LANES)
        for group, out_ref in zip(SPLIT_GROUPS, out_refs):
            for n, (c, m) in enumerate(group):
                spot = pl.ds(row_of(place, m, c), depth, stride=rows)
                out_ref[n * depth : (n + 1) * depth, at] = wide.at[j][spot, :].astype(BF16)


def split_rows(here, own, got, *tokens):
    depth, rows, cols = own.shape
    tile = 512
    block = across(own.shape, tile)
    return call(
        split_kernel,
        4,
        grid=(cols // tile,),
        in_specs=[SMEM, block, block] + [ANY] * len(tokens),
        scratch_shapes=[pltpu.VMEM((tile // LANES, depth * rows, LANES), F32)],
        **group_results(SPLIT_GROUPS, depth, cols, tile, pltpu.HBM),
    )(here, far(own), got, *tokens)


def patch_kernel(slabs, here_ref, cover_ref, offset_ref, *refs):
    w_ref, *refs = refs
    end_refs, (vol_ref, sino_ref, *v_refs), (r_ref, tv_ref) = refs[:4], refs[4 : 6 + len(CAST_GROUPS)], refs[-10:-8]
    v, s, r, wide, tv, slices, fixed, sem = refs[-8:]
    depth, rows, cols = sino_ref.shape
    place = lax.rem(here_ref[0], G)
    near, next_level, far_end, last_level = (ref[...] for ref in end_refs)
    low = jnp.where(place == 0, last_level, jnp.where(place == 2, far_end, near))[rows:].astype(F32)
    high = jnp.where(place == G - 1, next_level, jnp.where(place == 1, far_end, near))[:rows].astype(F32)

    for n, z in enumerate((0, depth - 2)):
        pltpu.make_async_copy(vol_ref.at[z : z + 2], slices.at[2 * n : 2 * n + 2], sem.at[n]).start()
    for n, z in enumerate((0, depth - 2)):
        pltpu.make_async_copy(vol_ref.at[z : z + 2], slices.at[2 * n : 2 * n + 2], sem.at[n]).wait()
    fixed[0] = tv_slice(slices[0], slices[1], tv_below(low, slices[0]))[0]
    fixed[1] = tv_slice(slices[3], high, tv_below(slices[2], slices[3]))[0]
    for n, z in enumerate((0, depth - 1)):
        pltpu.make_async_copy(fixed.at[n], tv_ref.at[z], sem.at[n]).start()
    for n, z in enumerate((0, depth - 1)):
        pltpu.make_async_copy(fixed.at[n], tv_ref.at[z], sem.at[n]).wait()

    @pl.when(here_ref[0] == slabs - 1)
    def _():
        for i, (ref, (_, group)) in enumerate(zip(v_refs, CAST_GROUPS)):
            for n, m in enumerate(group):
                at = CAST_GROUPS[i][0] * G + m
                pltpu.make_async_copy(ref.at[n * depth : (n + 1) * depth], v.at[at], sem.at[5 + at]).start()
        pltpu.make_async_copy(sino_ref, s, sem.at[3]).start()
        pltpu.make_async_copy(tv_ref, tv, sem.at[4]).start()
        pltpu.make_async_copy(sino_ref, s, sem.at[3]).wait()
        pltpu.make_async_copy(tv_ref, tv, sem.at[4]).wait()
        for at in range(CHUNKS * G):
            pltpu.make_async_copy(v_refs[0].at[:depth], v.at[at], sem.at[5 + at]).wait()
        block = w_ref[offset_ref[slabs - 1, 0]]
        block = jnp.where(cover_ref[slabs - 1, 0] == 1, block, jnp.zeros_like(block))
        turned = block.astype(F32).T.astype(BF16)

        def column(j, _):
            at = pl.ds(pl.multiple_of(j * LANES, LANES), LANES)
            wide[0] = s[:, :, at].astype(F32).reshape(wide.shape[1:])
            wide[1] = tv[:, :, at].reshape(wide.shape[1:])
            for c in range(CHUNKS):
                for m in range(G):
                    spot = pl.ds(CHUNKS * ((G - 1) ^ m) + c, depth, stride=rows)
                    seen = jnp.dot(block, v[c * G + m, :, at], preferred_element_type=F32)
                    resid = (seen - wide.at[0][spot, :]).astype(BF16)
                    wide.at[0][spot, :] = resid.astype(F32)
                    wide.at[1][spot, :] += jnp.dot(turned, resid, preferred_element_type=F32)
            r[:, :, at] = wide[0].reshape(depth, rows, LANES).astype(BF16)
            tv[:, :, at] = wide[1].reshape(depth, rows, LANES)
            return 0

        lax.fori_loop(0, cols // LANES, column, 0)
        pltpu.make_async_copy(r, r_ref, sem.at[3]).start()
        pltpu.make_async_copy(tv, tv_ref, sem.at[4]).start()
        pltpu.make_async_copy(r, r_ref, sem.at[3]).wait()
        pltpu.make_async_copy(tv, tv_ref, sem.at[4]).wait()


def patch(here, coverage, offsets, weights, ends, volume, sinogram, vols, tv, *tokens):
    slabs = coverage.shape[0]
    depth, rows, cols = sinogram.shape
    edges = [pl.BlockSpec((2 * rows, cols), lambda i, last=end.shape[0] // (2 * rows) - 1: (last, 0)) for end in ends]
    return call(
        functools.partial(patch_kernel, slabs),
        3,
        vmem=32,
        grid=(1,),
        in_specs=[SMEM, SMEM, SMEM, pl.BlockSpec(weights.shape, lambda i: (0, 0, 0))]
        + edges
        + [ANY] * (3 + len(vols) + len(tokens)),
        out_specs=[ANY, ANY],
        results=[pltpu.HBM(sinogram.shape, BF16), pltpu.HBM(volume.shape, F32)],
        input_output_aliases={10 + len(vols): 1},
        scratch_shapes=[
            pltpu.VMEM((CHUNKS * G, depth, cols), BF16),
            pltpu.VMEM(sinogram.shape, BF16),
            pltpu.VMEM(sinogram.shape, BF16),
            pltpu.VMEM((2, depth * rows, LANES), F32),
            pltpu.VMEM(volume.shape, F32),
            pltpu.VMEM((4, rows, cols), F32),
            pltpu.VMEM((2, rows, cols), F32),
            pltpu.SemaphoreType.DMA((5 + CHUNKS * G,)),
        ],
    )(here, coverage, offsets, weights, *ends, far(volume), far(sinogram), *vols, far(tv), *tokens)


def join_kernel(slabs, keys, here_ref, *refs):
    in_refs, (last_ref, out_ref, wide) = refs[: len(keys)], refs[-3:]
    depth, rows, cols = out_ref.shape
    place = lax.rem(here_ref[0], G)
    last = here_ref[0] == slabs - 1

    @pl.when(last)
    def _():
        at = pl.ds(pl.multiple_of(pl.program_id(0) * cols, cols), cols)
        pltpu.sync_copy(last_ref.at[:, :, at], out_ref)

    @pl.when(jnp.logical_not(last))
    def _():
        for j in range(cols // LANES):
            at = pl.ds(j * LANES, LANES)
            for (c, m), ref in zip(keys, in_refs):
                spot = pl.ds(row_of(place, m, c), depth, stride=rows)
                wide.at[j][spot, :] = ref[:, at].astype(F32)
            out_ref[:, :, at] = wide[j].reshape(depth, rows, LANES).astype(out_ref.dtype)


def join_rows(here, slabs, pieces, last):
    depth, rows, cols = last.shape
    tile = 512
    return call(
        functools.partial(join_kernel, slabs, keys_of(pieces)),
        2.6,
        grid=(cols // tile,),
        in_specs=[SMEM] + piece_specs(pieces, depth, tile) + [ANY],
        out_specs=across((depth, rows, cols), tile),
        results=value((depth, rows, cols), BF16),
        scratch_shapes=[pltpu.VMEM((tile // LANES, depth * rows, LANES), F32)],
    )(here, *arrays_of(pieces), far(last))


def finish_kernel(keys, here_ref, tv_ref, *refs):
    in_refs, (out_ref, wide) = refs[: len(keys)], refs[-2:]
    depth, rows, cols = out_ref.shape
    place = lax.rem(here_ref[0], G)
    for j in range(cols // LANES):
        at = pl.ds(j * LANES, LANES)
        for (c, m), ref in zip(keys, in_refs):
            spot = pl.ds(row_of(place, m, c), depth, stride=rows)
            wide.at[j][spot, :] = ref[:, at].astype(F32)
        out_ref[:, :, at] = tv_ref[:, :, at] + wide[j].reshape(depth, rows, LANES)


def finish(here, tv, pieces):
    depth, rows, cols = tv.shape
    tile = 256
    whole = across(tv.shape, tile)
    return call(
        functools.partial(finish_kernel, keys_of(pieces)),
        5,
        grid=(cols // tile,),
        in_specs=[SMEM, whole] + piece_specs(pieces, depth, tile),
        out_specs=whole,
        results=value((depth, rows, cols), F32),
        scratch_shapes=[pltpu.VMEM((tile // LANES, depth * rows, LANES), F32)],
    )(here, far(tv), *arrays_of(pieces))


def band_kernel(slabs, span, here_ref, cover_ref, offset_ref, w_ref, *refs):
    proj_ref, back_ref, turned = refs[-3:]
    side = w_ref.shape[1]
    place = lax.rem(here_ref[0], G)
    first = here_ref[0] - place
    zero = jnp.zeros((side, side), BF16)
    for i in range(w_ref.shape[0]):
        turned[i] = w_ref[i].astype(F32).T.astype(BF16)

    def block(ref, i, j):
        k = j - i
        known, step = jnp.clip(i, 0, slabs - 1), jnp.clip(k, 0, span - 1)
        inside = (i >= 0) & (i < slabs) & (j >= 0) & (j < slabs) & (k >= 0) & (k < span)
        live = inside & (cover_ref[known, step] == 1)
        return jnp.where(live, ref[offset_ref[known, step]], zero)

    def slab(m):
        return first + jnp.bitwise_xor(place, m)

    def group(m):
        to = jnp.bitwise_xor(place, m)
        return first + jnp.where(to == G - 1, -1, to)

    seen = [slab(m) for m in range(G)] + [slab(m) + G for m in range(G)] + [first - 1]
    seeing = [group(m) for m in range(G)] + [group(m) - G for m in range(G)] + [first + G - 1]
    for r in range(G):
        for s in range(2 * G + 1):
            at = (pl.ds(r * side, side), pl.ds(s * side, side))
            proj_ref[at] = block(w_ref, group(r), seen[s])
            back_ref[at] = block(turned, seeing[s], slab(r))


def bands(here, coverage, offsets, weights, *tokens):
    slabs, span = coverage.shape
    side = weights.shape[1]
    shape = (G * side, (2 * G + 1) * side)
    return call(
        functools.partial(band_kernel, slabs, span),
        1.6,
        in_specs=[SMEM, SMEM, SMEM, pl.BlockSpec(weights.shape, lambda i: (0, 0, 0))] + [ANY] * len(tokens),
        grid=(1,),
        out_specs=[pl.BlockSpec(shape, lambda i: (0, 0))] * 2,
        results=[pltpu.HBM(shape, BF16)] * 2,
        scratch_shapes=[pltpu.VMEM(weights.shape, BF16)],
    )(here, coverage, offsets, weights, *tokens)


def project_kernel(keys, here_ref, band_ref, own_ref, high_ref, low_ref, *refs):
    sinos, (r_ref, down_ref) = dict(zip(keys, refs)), refs[-2:]
    side = down_ref.shape[0]
    n = G * side
    seen = jnp.concatenate([own_ref[:n], high_ref[:n], low_ref[:side]], axis=0)
    total = jnp.dot(band_ref[...], seen, preferred_element_type=F32)
    for (_, m), ref in sinos.items():
        at = slice(m * side, (m + 1) * side)
        r_ref[at, :] = (total[at] - ref[...].astype(F32)).astype(BF16)
    spot = jnp.bitwise_xor(lax.rem(here_ref[0], G), G - 1)
    down_ref[...] = r_ref[pl.ds(pl.multiple_of(spot * side, side), side), :]


def project(here, band, own, high, low, pieces, *tokens):
    n, side = band.shape[0], band.shape[0] // G
    cols = own.shape[1]
    tile = 512
    one = across((side, cols), tile)
    return call(
        functools.partial(project_kernel, keys_of(pieces)),
        3,
        grid=(cols // tile,),
        in_specs=[SMEM, pl.BlockSpec(band.shape, lambda i: (0, 0))]
        + [across(array.shape, tile) for array in (own, high, low)]
        + piece_specs(pieces, side, tile)
        + [ANY] * len(tokens),
        out_specs=[across((n, cols), tile), one],
        results=[value((n, cols), BF16), value((side, cols), BF16)],
    )(here, band, own, high, low, *arrays_of(pieces), *tokens)


def put_groups(groups, block, out_refs, before_ref, side):
    for group, out_ref in zip(groups, out_refs):
        for n, m in enumerate(group):
            out_ref[n * side : (n + 1) * side] = before_ref[...] if m is None else block(m)


def deal_kernel(groups, here_ref, r_ref, high_ref, *refs):
    side = high_ref.shape[0]
    place = lax.rem(here_ref[0], G)

    def block(m):
        last = jnp.bitwise_xor(place, m) == G - 1
        return jnp.where(last, high_ref[...], r_ref[m * side : (m + 1) * side])

    put_groups(groups, block, refs[-len(groups) :], refs[0], side)


def deal(here, groups, resid, high, before, *tokens):
    side, cols = high.shape
    tile = 512
    one = across((side, cols), tile)
    return call(
        functools.partial(deal_kernel, groups),
        1,
        grid=(cols // tile,),
        in_specs=[SMEM, across(resid.shape, tile), one] + [one] * len(before) + [ANY] * len(tokens),
        **group_results(groups, side, cols, tile),
    )(here, resid, high, *before, *tokens)


def back_kernel(groups, band_ref, own_ref, low_ref, high_ref, *refs):
    side = high_ref.shape[0]
    seeing = jnp.concatenate([own_ref[...], low_ref[...], high_ref[...]], axis=0)
    total = jnp.dot(band_ref[...], seeing, preferred_element_type=F32)
    put_groups(groups, lambda m: total[m * side : (m + 1) * side].astype(BF16), refs[-len(groups) :], refs[0], side)


def back(groups, band, own, low, high, before, *tokens):
    side, cols = high.shape
    tile = 512
    one = across((side, cols), tile)
    many = across(own.shape, tile)
    return call(
        functools.partial(back_kernel, groups),
        3,
        grid=(cols // tile,),
        in_specs=[pl.BlockSpec(band.shape, lambda i: (0, 0)), many, many, one]
        + [one] * len(before)
        + [ANY] * len(tokens),
        **group_results(groups, side, cols, tile),
    )(band, own, low, high, *before, *tokens)


def tv_flux(cur, above):
    rows, cols = cur.shape
    row = lax.broadcasted_iota(jnp.int32, (rows, cols), 0)
    col = lax.broadcasted_iota(jnp.int32, (rows, cols), 1)
    dz = above - cur
    dy = jnp.where(row == rows - 1, 0.0, pltpu.roll(cur, rows - 1, 0)) - cur
    dx = jnp.where(col == cols - 1, 0.0, pltpu.roll(cur, cols - 1, 1)) - cur
    scale = 0.5 * lax.rsqrt(dz * dz + dy * dy + dx * dx + 0.25)
    return dz * scale, dy * scale, dx * scale


def tv_below(cur, above):
    return tv_flux(cur, above)[0]


def tv_slice(cur, above, below_flux):
    rows, cols = cur.shape
    row = lax.broadcasted_iota(jnp.int32, (rows, cols), 0)
    col = lax.broadcasted_iota(jnp.int32, (rows, cols), 1)
    fz, fy, fx = tv_flux(cur, above)
    sides = 0.5 * cur * lax.rsqrt(cur * cur + 0.25)
    fy_low = jnp.where(row == 0, sides, pltpu.roll(fy, 1, 0))
    fx_low = jnp.where(col == 0, sides, pltpu.roll(fx, 1, 1))
    return (below_flux - fz) + (fy_low - fy) + (fx_low - fx), fz


def tv_kernel(next_ref, vol_ref, *refs):
    out_ref, flux_ref = refs[-2:]
    deep = vol_ref.shape[0]

    @pl.when(pl.program_id(0) == 0)
    def _():
        flux_ref[...] = jnp.zeros_like(flux_ref)

    def body(z, flux):
        out_ref[z], flux = tv_slice(vol_ref[z], vol_ref[z + 1], flux)
        return flux

    flux = lax.fori_loop(0, deep - 1, body, flux_ref[...], unroll=5)
    out_ref[deep - 1], flux_ref[...] = tv_slice(vol_ref[deep - 1], next_ref[0], flux)


def half_tv(volume, *tokens):
    depth, rows, cols = volume.shape
    deep = 16
    body = pl.BlockSpec((deep, rows, cols), lambda i: (i, 0, 0))
    after = pl.BlockSpec((1, rows, cols), lambda i: (jnp.minimum((i + 1) * deep, depth - 1), 0, 0))
    return call(
        tv_kernel,
        9,
        grid=(depth // deep,),
        in_specs=[after, body] + [ANY] * len(tokens),
        out_specs=body,
        results=pltpu.HBM(volume.shape, F32),
        scratch_shapes=[pltpu.VMEM((rows, cols), F32)],
    )(far(volume), far(volume), *tokens)


def local(volume, sinogram, weights, coverage, offsets):
    slabs = lax.axis_size("slab")
    here = lax.axis_index("slab").astype(jnp.int32).reshape(1)
    depth, rows, cols = volume.shape
    single = ((0,), (1,), (2,), (3,))

    vols = cast_rows(here, volume)
    got = moved(lax.optimization_barrier((sinogram, vols[0]))[0], G, only=G - 1)
    pieces0 = direct(0, single, vols[:G])
    tv = half_tv(volume, vols[0])
    own0, edge0 = pack(here, pieces0, 2 * rows, tv)
    high0, low0 = moved(own0, -G), moved(edge0, G)

    band_p, band_b = bands(here, coverage, offsets, weights, own0)
    sino = split_rows(here, sinogram, got, own0)
    pieces1 = direct(1, ((0,), (1,)), vols[G : G + 2]) + in_two(1, vols[G + 2], sino[0])
    own1, edge1 = pack(here, pieces1, 0, sino[0])
    high1, low1 = moved(own1, -G), moved(edge1, G)

    sino_core = swapped(sino[0], 1)
    sinos0 = [(0, 1, sino_core, 0)] + direct(0, ((0,), (2,), (3,)), sino[1:4])

    resid0, down0 = project(here, band_p, own0, high0, low0, sinos0, own1, low1)
    from_low0, from_high0 = moved(resid0, G), moved(down0, -G)
    ends = [pieces0[1][2], high0, pieces0[3][2], low0]
    r_last, tv = patch(here, coverage, offsets, weights, ends, volume, sinogram, vols, tv, resid0)
    dealt0 = deal(here, ((0,), (1,), (2, 3)), resid0, from_high0, [], r_last)
    over0 = swapped(dealt0[2], 2)

    sinos1 = [(1, 1, sino_core, 1)] + direct(1, ((0,),), sino[4:5]) + in_two(1, sino[5], dealt0[0])
    resid1, down1 = project(here, band_p, own1, high1, low1, sinos1, dealt0[0])
    from_low1, from_high1 = moved(resid1, G), moved(down1, -G)
    backs0 = back(((0,), (1,), (2, 3)), band_b, resid0, from_low0, from_high0, [], over0)
    back_pieces = direct(0, ((0,),), backs0[:1]) + in_two(0, backs0[2])
    dealt1 = deal(here, ((0,), (None, 1), (2, 3)), resid1, from_high1, [dealt0[1]], backs0[0])
    over1 = swapped(dealt1[2], 2)
    backs1 = back(((0,), (None, 1), (2,), (3,)), band_b, resid1, from_low1, from_high1, [backs0[1]], back_pieces[2][2])

    far_core = swapped(jnp.concatenate([over0[depth:], over1[depth:]], axis=0), 1)
    near_core = swapped(dealt1[1], 1)
    resid_pieces = []
    for c, (dealt, over) in enumerate(((dealt0, over0), (dealt1, over1))):
        resid_pieces += [(c, 0, dealt[0], 0), (c, 1, near_core, c), (c, 2, over, 0), (c, 3, far_core, c)]
    residual = join_rows(here, slabs, resid_pieces, r_last)

    back_core = swapped(backs1[1], 1)
    back_pieces += [(0, 1, back_core, 0), (1, 1, back_core, 1)]
    back_pieces += direct(1, ((0,), (2,), (3,)), [backs1[0], backs1[2], backs1[3]])
    gradient = finish(here, tv, back_pieces)
    return (gradient, residual)


def solution(mesh):
    placed = (P("slab", "grp", None), P("slab", "grp", None), P(), P(), P())
    return jax.shard_map(
        local,
        mesh=mesh,
        in_specs=placed,
        out_specs=(P("slab", "grp", None), P("slab", "grp", None)),
        check_vma=False,
    )
```

```python
import functools

import jax
import jax.numpy as jnp
from jax import lax
from jax.experimental import pallas as pl
from jax.experimental.pallas import tpu as pltpu
from jax.sharding import PartitionSpec as P

G = 4
CHUNKS = 2
ROWS = 2
TILE = 256
F32 = jnp.float32
BF16 = jnp.bfloat16
MIB = 1024 * 1024
LANES = 128
SMEM = pl.BlockSpec(memory_space=pltpu.SMEM)
VMEM = pl.BlockSpec(memory_space=pltpu.VMEM)
ANY = pl.BlockSpec(memory_space=pl.ANY)


def moved(value, steps, only=None):
    count = lax.axis_size("slab")
    first, last = max(0, -steps), min(count, count - steps)
    pairs = [(i, i + steps) for i in range(first, last) if only is None or i % G == only]
    return lax.ppermute(value, "slab", pairs)


def swapped(value, bits):
    count = lax.axis_size("slab")
    return lax.ppermute(value, "slab", [(i, i ^ bits) for i in range(count)])


def direct(chunk, groups, arrays):
    return [(chunk, m, array if m == 0 else swapped(array, m), 0) for (m,), array in zip(groups, arrays)]


def in_two(chunk, pair, after=None):
    side = pair.shape[0] // 2
    over = swapped(pair, 2)
    if after is not None:
        over = lax.optimization_barrier((over, after))[0]
    return [(chunk, 2, over, 0), (chunk, 3, swapped(over[side:], 1), 0)]


def call(kernel, us, *, results, vmem=16, **how):
    return pl.pallas_call(
        kernel,
        out_shape=results,
        compiler_params=pltpu.CompilerParams(vmem_limit_bytes=vmem * MIB),
        cost_estimate=pl.CostEstimate(flops=int(us * 1.15e9), bytes_accessed=1000, transcendentals=0),
        **how,
    )


def value(shape, dtype):
    return jax.ShapeDtypeStruct(shape, dtype)


def far(array):
    return pltpu.with_memory_space_constraint(array, pltpu.HBM)


def across(shape, tile):
    block = shape[:-1] + (tile,)
    return pl.BlockSpec(block, lambda i: (0,) * (len(shape) - 1) + (i,))


def lanes(array, tile, parts):
    block = array.shape[:-1] + (tile,)
    zeros = (0,) * (len(block) - 1)
    return [pl.BlockSpec(block, lambda i, j=j: zeros + (i * parts + j,)) for j in range(parts)]


def piece_specs(pieces, side, tile):
    return [pl.BlockSpec((side, tile), lambda i, at=at: (at, i)) for _, _, _, at in pieces]


def keys_of(pieces):
    return [(chunk, m) for chunk, m, _, _ in pieces]


def arrays_of(pieces):
    return [array for _, _, array, _ in pieces]


def group_results(groups, side, cols, tile, space=None):
    shapes = [(len(group) * side, cols) for group in groups]
    results = [space(shape, BF16) if space else value(shape, BF16) for shape in shapes]
    return dict(out_specs=[across(shape, tile) for shape in shapes], results=results)


def rows_of(place, m):
    first = ROWS * jnp.bitwise_xor(place, m)
    return [(h * TILE, first + h) for h in range(ROWS)]


def wide_tile(rows_deep):
    return pltpu.VMEM((TILE // LANES, rows_deep, LANES), F32)


def chunk_tiles(chunk, cols):
    count = cols // CHUNKS // TILE
    return chunk * count, count


def cast_kernel(groups, sent, here_ref, *refs):
    parts = TILE // LANES
    vol_refs, refs = refs[:parts], refs[parts:]
    sem = refs[-1]
    sent_refs = refs[-1 - CHUNKS : -1] if sent else ()
    out_refs = refs[-1 - len(sent_refs) - len(groups) :]
    step = pl.program_id(0)
    rows = ROWS * G
    depth = vol_refs[0].shape[0] // rows
    place = lax.rem(here_ref[0], G)

    def copies():
        width = sent_refs[0].shape[2]
        return [
            pltpu.make_async_copy(refs[2].at[:, :, c * width : (c + 1) * width], sent_refs[c], sem.at[c])
            for c in range(CHUNKS)
        ]

    if sent:

        @pl.when(step == 0)
        def _():
            for copy in copies():
                copy.start()

    for j, vol_ref in enumerate(vol_refs):
        for group, out_ref in zip(groups, out_refs):
            for n, m in enumerate(group):
                for start, row in rows_of(place, m):
                    at = pl.ds(start + j * LANES, LANES)
                    out_ref[n * depth : (n + 1) * depth, at] = vol_ref[pl.ds(row, depth, stride=rows), :].astype(BF16)
    if sent:
        both = jnp.concatenate([refs[0][...], refs[1][...]], axis=0).astype(BF16)
        for group, out_ref in zip(groups, out_refs):
            if group[0] % 2:
                out_ref[depth:, :] = both
    if sent:

        @pl.when(step == pl.num_programs(0) - 1)
        def _():
            for copy in copies():
                copy.wait()


def cast_rows(here, volume, chunk, groups, sinogram=None, *tokens):
    depth, rows, cols = volume.shape
    flat = far(volume.reshape(depth * rows, cols))
    first, count = chunk_tiles(chunk, cols)
    parts, width = TILE // LANES, ROWS * TILE
    sent = sinogram is not None
    shapes = [(len(g) * depth + (2 * rows if sent and g[0] % 2 else 0), cols) for g in groups]
    out_specs = [across(shape, width) for shape in shapes]
    results = [value(shape, BF16) for shape in shapes]
    in_specs = [SMEM]
    in_specs += [pl.BlockSpec((depth * rows, LANES), lambda i, j=j: (0, (first + i) * parts + j)) for j in range(parts)]
    args = []
    if sent:
        args = [flat, flat, far(sinogram)]
        in_specs += [pl.BlockSpec((rows, width), lambda i, z=z: (z, i)) for z in (0, depth - 1)] + [ANY]
        out_specs += [ANY] * CHUNKS
        results += [pltpu.HBM((depth, rows, cols // CHUNKS), BF16)] * CHUNKS
    return call(
        functools.partial(cast_kernel, groups, sent),
        2,
        grid=(count,),
        in_specs=in_specs + [ANY] * len(tokens),
        out_specs=out_specs,
        results=results,
        scratch_shapes=[pltpu.SemaphoreType.DMA((CHUNKS,))],
    )(here, *[flat] * parts, *args, *tokens)


def pack_kernel(cuts, here_ref, *refs):
    in_refs, (*part_refs, last_ref) = refs[:G], refs[-len(cuts) - 1 :]
    side = in_refs[0].shape[0]
    spot = jnp.bitwise_xor(lax.rem(here_ref[0], G), G - 1)
    last = in_refs[0][...]
    for m in range(1, G):
        last = jnp.where(spot == m, in_refs[m][:side], last)
    last_ref[:side] = last
    for part, part_ref in zip(cuts, part_refs):
        for n, m in enumerate(part):
            part_ref[n * side : (n + 1) * side] = in_refs[m][:side]
    if last_ref.shape[0] > side:
        last_ref[side:] = in_refs[G - 1][side:]
        part_refs[-1][len(cuts[-1]) * side :] = in_refs[G - 1][side:]


def pack(here, pieces, cuts, more, *tokens):
    pieces = sorted(pieces, key=lambda piece: piece[1])
    side, cols = pieces[0][2].shape
    tile = 512
    shapes = [(len(part) * side, cols) for part in cuts] + [(side + more, cols)]
    shapes[-2] = (shapes[-2][0] + more, cols)
    specs = piece_specs(pieces, side, tile)
    if more:
        specs = [across(array.shape, tile) for array in arrays_of(pieces)]
    return call(
        functools.partial(pack_kernel, cuts),
        1,
        grid=(cols // tile,),
        in_specs=[SMEM] + specs + [ANY] * len(tokens),
        out_specs=[across(shape, tile) for shape in shapes],
        results=[value(shape, BF16) for shape in shapes],
    )(here, *arrays_of(pieces), *tokens)


def split_kernel(groups, here_ref, own_ref, got_ref, *refs):
    out_refs, wide = refs[-len(groups) - 1 : -1], refs[-1]
    depth, rows, cols = own_ref.shape
    place = lax.rem(here_ref[0], G)

    def fill(ref):
        for j in range(cols // LANES):
            wide[j] = ref[:, :, j * LANES : (j + 1) * LANES].astype(F32).reshape(wide.shape[1:])

    @pl.when(place == G - 1)
    def _():
        fill(got_ref)

    @pl.when(place != G - 1)
    def _():
        fill(own_ref)

    for j in range(cols // LANES):
        for group, out_ref in zip(groups, out_refs):
            for n, m in enumerate(group):
                for start, row in rows_of(place, m):
                    at = pl.ds(start + j * LANES, LANES)
                    out_ref[n * depth : (n + 1) * depth, at] = wide.at[j][pl.ds(row, depth, stride=rows), :].astype(BF16)


def split_rows(here, own, got, chunk, groups, *tokens):
    depth, rows, cols = own.shape
    first, count = chunk_tiles(chunk, cols)
    block = (depth, rows, TILE)
    return call(
        functools.partial(split_kernel, groups),
        2,
        grid=(count,),
        in_specs=[SMEM, pl.BlockSpec(block, lambda i: (0, 0, first + i)), pl.BlockSpec(block, lambda i: (0, 0, i))]
        + [ANY] * len(tokens),
        scratch_shapes=[wide_tile(depth * rows)],
        **group_results(groups, depth, cols, ROWS * TILE, pltpu.HBM),
    )(here, far(own), got, *tokens)


def patch_kernel(slabs, here_ref, cover_ref, offset_ref, *refs):
    w_ref, *refs = refs
    end_refs, (vol_ref, sino_ref), (r_ref, tv_ref) = refs[:4], refs[4:6], refs[-10:-8]
    vol, s, r, wide, tv, slices, fixed, sem = refs[-8:]
    depth, rows, cols = sino_ref.shape
    place = lax.rem(here_ref[0], G)
    near, next_level, far_end, last_level = (ref[...] for ref in end_refs)
    low = jnp.where(place == 0, last_level, jnp.where(place == 2, far_end, near))[rows:].astype(F32)
    high = jnp.where(place == G - 1, next_level, jnp.where(place == 1, far_end, near))[:rows].astype(F32)

    for n, z in enumerate((0, depth - 2)):
        pltpu.make_async_copy(vol_ref.at[z : z + 2], slices.at[2 * n : 2 * n + 2], sem.at[n]).start()
    for n, z in enumerate((0, depth - 2)):
        pltpu.make_async_copy(vol_ref.at[z : z + 2], slices.at[2 * n : 2 * n + 2], sem.at[n]).wait()
    fixed[0] = tv_slice(slices[0], slices[1], tv_below(low, slices[0]))[0]
    fixed[1] = tv_slice(slices[3], high, tv_below(slices[2], slices[3]))[0]
    for n, z in enumerate((0, depth - 1)):
        pltpu.make_async_copy(fixed.at[n], tv_ref.at[z], sem.at[n]).start()
    for n, z in enumerate((0, depth - 1)):
        pltpu.make_async_copy(fixed.at[n], tv_ref.at[z], sem.at[n]).wait()

    @pl.when(here_ref[0] == slabs - 1)
    def _():
        pltpu.make_async_copy(vol_ref, vol, sem.at[2]).start()
        pltpu.make_async_copy(sino_ref, s, sem.at[3]).start()
        pltpu.make_async_copy(tv_ref, tv, sem.at[4]).start()
        pltpu.make_async_copy(vol_ref, vol, sem.at[2]).wait()
        pltpu.make_async_copy(sino_ref, s, sem.at[3]).wait()
        pltpu.make_async_copy(tv_ref, tv, sem.at[4]).wait()
        block = w_ref[offset_ref[slabs - 1, 0]]
        block = jnp.where(cover_ref[slabs - 1, 0] == 1, block, jnp.zeros_like(block))
        turned = block.astype(F32).T.astype(BF16)

        def column(j, _):
            at = pl.ds(pl.multiple_of(j * LANES, LANES), LANES)
            for n, ref in enumerate((s, tv, vol)):
                wide[n] = ref[:, :, at].astype(F32).reshape(wide.shape[1:])
            for row in range(rows):
                spot = pl.ds(row, depth, stride=rows)
                seen = jnp.dot(block, wide.at[2][spot, :].astype(BF16), preferred_element_type=F32)
                resid = (seen - wide.at[0][spot, :]).astype(BF16)
                wide.at[0][spot, :] = resid.astype(F32)
                wide.at[1][spot, :] += jnp.dot(turned, resid, preferred_element_type=F32)
            r[:, :, at] = wide[0].reshape(depth, rows, LANES).astype(BF16)
            tv[:, :, at] = wide[1].reshape(depth, rows, LANES)
            return 0

        lax.fori_loop(0, cols // LANES, column, 0)
        pltpu.make_async_copy(r, r_ref, sem.at[3]).start()
        pltpu.make_async_copy(tv, tv_ref, sem.at[4]).start()
        pltpu.make_async_copy(r, r_ref, sem.at[3]).wait()
        pltpu.make_async_copy(tv, tv_ref, sem.at[4]).wait()


def patch(here, coverage, offsets, weights, ends, volume, sinogram, tv, *tokens):
    slabs = coverage.shape[0]
    depth, rows, cols = sinogram.shape
    edges = [pl.BlockSpec((2 * rows, cols), lambda i, last=end.shape[0] // (2 * rows) - 1: (last, 0)) for end in ends]
    return call(
        functools.partial(patch_kernel, slabs),
        3,
        vmem=32,
        grid=(1,),
        in_specs=[SMEM, SMEM, SMEM, pl.BlockSpec(weights.shape, lambda i: (0, 0, 0))]
        + edges
        + [ANY] * (3 + len(tokens)),
        out_specs=[ANY, ANY],
        results=[pltpu.HBM(sinogram.shape, BF16), pltpu.HBM(volume.shape, F32)],
        input_output_aliases={10: 1},
        scratch_shapes=[
            pltpu.VMEM(volume.shape, F32),
            pltpu.VMEM(sinogram.shape, BF16),
            pltpu.VMEM(sinogram.shape, BF16),
            pltpu.VMEM((3, depth * rows, LANES), F32),
            pltpu.VMEM(volume.shape, F32),
            pltpu.VMEM((4, rows, cols), F32),
            pltpu.VMEM((2, rows, cols), F32),
            pltpu.SemaphoreType.DMA((5,)),
        ],
    )(here, coverage, offsets, weights, *ends, far(volume), far(sinogram), far(tv), *tokens)


def join_kernel(slabs, first, keys, here_ref, *refs):
    in_refs, (base_ref, out_ref, wide) = refs[: len(keys)], refs[-3:]
    depth, rows, cols = out_ref.shape
    place = lax.rem(here_ref[0], G)
    last = here_ref[0] == slabs - 1

    @pl.when(last)
    def _():
        at = pl.ds(pl.multiple_of((first + pl.program_id(0)) * cols, cols), cols)
        pltpu.sync_copy(base_ref.at[:, :, at], out_ref)

    @pl.when(jnp.logical_not(last))
    def _():
        for j in range(cols // LANES):
            for m, ref in zip(keys, in_refs):
                for start, row in rows_of(place, m):
                    value = ref[:, start + j * LANES : start + (j + 1) * LANES].astype(F32)
                    wide.at[j][pl.ds(row, depth, stride=rows), :] = value
            out_ref[:, :, j * LANES : (j + 1) * LANES] = wide[j].reshape(depth, rows, LANES).astype(out_ref.dtype)


def join_rows(here, slabs, chunk, pieces, base, *tokens):
    depth, rows, cols = base.shape
    first, count = chunk_tiles(chunk, cols)
    return call(
        functools.partial(join_kernel, slabs, first, [m for _, m, _, _ in pieces]),
        1.5,
        grid=(count,),
        in_specs=[SMEM] + piece_specs(pieces, depth, ROWS * TILE) + [ANY] * (len(tokens) + 1),
        out_specs=pl.BlockSpec((depth, rows, TILE), lambda i: (0, 0, first + i)),
        results=pltpu.HBM(base.shape, BF16),
        input_output_aliases={1 + len(pieces) + len(tokens): 0},
        scratch_shapes=[wide_tile(depth * rows)],
    )(here, *arrays_of(pieces), *tokens, far(base))


def finish_kernel(keys, here_ref, tv_ref, *refs):
    in_refs, (out_ref, wide) = refs[: len(keys)], refs[-2:]
    depth, rows, cols = out_ref.shape
    place = lax.rem(here_ref[0], G)
    for j in range(cols // LANES):
        for m, ref in zip(keys, in_refs):
            for start, row in rows_of(place, m):
                value = ref[:, start + j * LANES : start + (j + 1) * LANES].astype(F32)
                wide.at[j][pl.ds(row, depth, stride=rows), :] = value
        at = pl.ds(j * LANES, LANES)
        out_ref[:, :, at] = tv_ref[:, :, at] + wide[j].reshape(depth, rows, LANES)


def finish(here, chunk, tv, pieces, *tokens):
    depth, rows, cols = tv.shape
    first, count = chunk_tiles(chunk, cols)
    part = pl.BlockSpec((depth, rows, TILE), lambda i: (0, 0, first + i))
    return call(
        functools.partial(finish_kernel, [m for _, m, _, _ in pieces]),
        2.6,
        grid=(count,),
        in_specs=[SMEM, part] + piece_specs(pieces, depth, ROWS * TILE) + [ANY] * len(tokens),
        out_specs=part,
        results=pltpu.HBM(tv.shape, F32),
        input_output_aliases={1: 0},
        scratch_shapes=[wide_tile(depth * rows)],
    )(here, far(tv), *arrays_of(pieces), *tokens)


def band_kernel(slabs, span, here_ref, cover_ref, offset_ref, w_ref, *refs):
    proj_ref, back_ref, turned = refs[-3:]
    side = w_ref.shape[1]
    place = lax.rem(here_ref[0], G)
    first = here_ref[0] - place
    zero = jnp.zeros((side, side), BF16)
    for i in range(w_ref.shape[0]):
        turned[i] = w_ref[i].astype(F32).T.astype(BF16)

    def block(ref, i, j):
        k = j - i
        known, step = jnp.clip(i, 0, slabs - 1), jnp.clip(k, 0, span - 1)
        inside = (i >= 0) & (i < slabs) & (j >= 0) & (j < slabs) & (k >= 0) & (k < span)
        live = inside & (cover_ref[known, step] == 1)
        return jnp.where(live, ref[offset_ref[known, step]], zero)

    def slab(m):
        return first + jnp.bitwise_xor(place, m)

    def group(m):
        to = jnp.bitwise_xor(place, m)
        return first + jnp.where(to == G - 1, -1, to)

    seen = [slab(m) for m in range(G)] + [slab(m) + G for m in range(G)] + [first - 1]
    seeing = [group(m) for m in range(G)] + [group(m) - G for m in range(G)] + [first + G - 1]
    for r in range(G):
        for s in range(2 * G + 1):
            at = (pl.ds(r * side, side), pl.ds(s * side, side))
            proj_ref[at] = block(w_ref, group(r), seen[s])
            back_ref[at] = block(turned, seeing[s], slab(r))


def bands(here, coverage, offsets, weights, *tokens):
    slabs, span = coverage.shape
    side = weights.shape[1]
    shape = (G * side, (2 * G + 1) * side)
    return call(
        functools.partial(band_kernel, slabs, span),
        1.6,
        in_specs=[SMEM, SMEM, SMEM, pl.BlockSpec(weights.shape, lambda i: (0, 0, 0))] + [ANY] * len(tokens),
        grid=(1,),
        out_specs=[pl.BlockSpec(shape, lambda i: (0, 0))] * 2,
        results=[pltpu.HBM(shape, BF16)] * 2,
        scratch_shapes=[pltpu.VMEM(weights.shape, BF16)],
    )(here, coverage, offsets, weights, *tokens)


def project_kernel(sources, keys, here_ref, band_ref, *refs):
    seen_refs, refs = refs[:sources], refs[sources:]
    sinos, (r_ref, down_ref) = dict(zip(keys, refs)), refs[-2:]
    side = down_ref.shape[0]
    seen = jnp.concatenate([ref[: ref.shape[0] // side * side] for ref in seen_refs], axis=0)
    total = jnp.dot(band_ref[...], seen, preferred_element_type=F32)
    for (_, m), ref in sinos.items():
        at = slice(m * side, (m + 1) * side)
        r_ref[at, :] = (total[at] - ref[...].astype(F32)).astype(BF16)
    spot = jnp.bitwise_xor(lax.rem(here_ref[0], G), G - 1)
    down_ref[...] = r_ref[pl.ds(pl.multiple_of(spot * side, side), side), :]


def project(here, band, sources, pieces, *tokens):
    n, side = band.shape[0], band.shape[0] // G
    cols = sources[0].shape[1]
    tile = 512
    one = across((side, cols), tile)
    return call(
        functools.partial(project_kernel, len(sources), keys_of(pieces)),
        3,
        grid=(cols // tile,),
        in_specs=[SMEM, pl.BlockSpec(band.shape, lambda i: (0, 0))]
        + [across(array.shape, tile) for array in sources]
        + piece_specs(pieces, side, tile)
        + [ANY] * len(tokens),
        out_specs=[across((n, cols), tile), one],
        results=[value((n, cols), BF16), value((side, cols), BF16)],
    )(here, band, *sources, *arrays_of(pieces), *tokens)


def put_groups(groups, block, out_refs, before_ref, side):
    for group, out_ref in zip(groups, out_refs):
        for n, m in enumerate(group):
            out_ref[n * side : (n + 1) * side] = before_ref[...] if m is None else block(m)


def deal_kernel(groups, here_ref, r_ref, high_ref, *refs):
    side = high_ref.shape[0]
    place = lax.rem(here_ref[0], G)

    def block(m):
        last = jnp.bitwise_xor(place, m) == G - 1
        return jnp.where(last, high_ref[...], r_ref[m * side : (m + 1) * side])

    put_groups(groups, block, refs[-len(groups) :], refs[0], side)


def deal(here, groups, resid, high, before, *tokens):
    side, cols = high.shape
    tile = 512
    one = across((side, cols), tile)
    return call(
        functools.partial(deal_kernel, groups),
        1,
        grid=(cols // tile,),
        in_specs=[SMEM, across(resid.shape, tile), one] + [one] * len(before) + [ANY] * len(tokens),
        **group_results(groups, side, cols, tile),
    )(here, resid, high, *before, *tokens)


def back_kernel(groups, band_ref, own_ref, low_ref, high_ref, *refs):
    side = high_ref.shape[0]
    seeing = jnp.concatenate([own_ref[...], low_ref[...], high_ref[...]], axis=0)
    total = jnp.dot(band_ref[...], seeing, preferred_element_type=F32)
    put_groups(groups, lambda m: total[m * side : (m + 1) * side].astype(BF16), refs[-len(groups) :], refs[0], side)


def back(groups, band, own, low, high, before, *tokens):
    side, cols = high.shape
    tile = 512
    one = across((side, cols), tile)
    many = across(own.shape, tile)
    return call(
        functools.partial(back_kernel, groups),
        3,
        grid=(cols // tile,),
        in_specs=[pl.BlockSpec(band.shape, lambda i: (0, 0)), many, many, one]
        + [one] * len(before)
        + [ANY] * len(tokens),
        **group_results(groups, side, cols, tile),
    )(band, own, low, high, *before, *tokens)


def tv_flux(cur, above):
    rows, cols = cur.shape
    row = lax.broadcasted_iota(jnp.int32, (rows, cols), 0)
    col = lax.broadcasted_iota(jnp.int32, (rows, cols), 1)
    dz = above - cur
    dy = jnp.where(row == rows - 1, 0.0, pltpu.roll(cur, rows - 1, 0)) - cur
    dx = jnp.where(col == cols - 1, 0.0, pltpu.roll(cur, cols - 1, 1)) - cur
    scale = 0.5 * lax.rsqrt(dz * dz + dy * dy + dx * dx + 0.25)
    return dz * scale, dy * scale, dx * scale


def tv_below(cur, above):
    return tv_flux(cur, above)[0]


def tv_slice(cur, above, below_flux):
    rows, cols = cur.shape
    row = lax.broadcasted_iota(jnp.int32, (rows, cols), 0)
    col = lax.broadcasted_iota(jnp.int32, (rows, cols), 1)
    fz, fy, fx = tv_flux(cur, above)
    sides = 0.5 * cur * lax.rsqrt(cur * cur + 0.25)
    fy_low = jnp.where(row == 0, sides, pltpu.roll(fy, 1, 0))
    fx_low = jnp.where(col == 0, sides, pltpu.roll(fx, 1, 1))
    return (below_flux - fz) + (fy_low - fy) + (fx_low - fx), fz


def tv_kernel(last_ref, next_ref, vol_ref, *refs):
    out_ref, done_ref, flux_ref = refs[-3:]
    deep = vol_ref.shape[0]

    @pl.when(pl.program_id(0) == 0)
    def _():
        flux_ref[...] = tv_below(last_ref[0], vol_ref[0])

    def body(z, flux):
        out_ref[z], flux = tv_slice(vol_ref[z], vol_ref[z + 1], flux)
        return flux

    flux = lax.fori_loop(0, deep - 1, body, flux_ref[...], unroll=5)
    out_ref[deep - 1], flux_ref[...] = tv_slice(vol_ref[deep - 1], next_ref[0], flux)
    done_ref[...] = flux_ref[:, : done_ref.shape[1]]


def half_tv(volume, half, base, *tokens):
    depth, rows, cols = volume.shape
    deep = 16
    steps = depth // deep // 2
    first = half * steps
    body = pl.BlockSpec((deep, rows, cols), lambda i: (first + i, 0, 0))
    before = pl.BlockSpec((1, rows, cols), lambda i: (max(first * deep - 1, 0), 0, 0))
    after = pl.BlockSpec((1, rows, cols), lambda i: (jnp.minimum((first + i + 1) * deep, depth - 1), 0, 0))
    bases = [] if base is None else [far(base)]
    return call(
        tv_kernel,
        5,
        grid=(steps,),
        in_specs=[before, after, body] + [ANY] * (len(bases) + len(tokens)),
        out_specs=[body, pl.BlockSpec((rows, LANES), lambda i: (0, 0))],
        results=[pltpu.HBM(volume.shape, F32), value((rows, LANES), F32)],
        input_output_aliases={3: 0} if bases else {},
        scratch_shapes=[pltpu.VMEM((rows, cols), F32)],
    )(*[far(volume)] * 3, *bases, *tokens)


def local(volume, sinogram, weights, coverage, offsets):
    slabs = lax.axis_size("slab")
    here = lax.axis_index("slab").astype(jnp.int32).reshape(1)
    rows = volume.shape[1]
    single = ((0,), (1,), (2,), (3,))
    paired = ((0,), (1,), (2, 3))

    def in_steps(chunk, blocks, after):
        return direct(chunk, paired[:2], blocks[:2]) + in_two(chunk, blocks[2], after)

    *vols0, sent0, sent1 = cast_rows(here, volume, 0, single, sinogram)
    got0 = moved(sent0, G, only=G - 1)
    pieces0 = direct(0, single, vols0)
    tv, tv_done = half_tv(volume, 0, None, vols0[0])
    vols1 = cast_rows(here, volume, 1, paired, None, tv_done)
    own0, edge0 = pack(here, pieces0, ((0, 1, 2, 3),), 2 * rows, vols1[0])
    high0, low0 = moved(own0, -G), moved(edge0, G)
    sino0 = split_rows(here, sinogram, got0, 0, single, own0)
    got1 = moved(lax.optimization_barrier((sent1, sino0[0]))[0], G, only=G - 1)
    sinos0 = direct(0, single, sino0)
    own1, own1_more, edge1 = pack(here, in_steps(1, vols1, sino0[0]), ((0, 1), (2, 3)), 0, sino0[0])
    high1, low1 = moved(own1, -G), moved(edge1, G)
    sino1 = split_rows(here, sinogram, got1, 1, paired, own1)
    band_p, band_b = bands(here, coverage, offsets, weights, own0)

    resid0, down0 = project(here, band_p, [own0, high0, low0], sinos0, low1, sino1[0])
    from_low0, from_high0 = moved(resid0, G), moved(down0, -G)
    high1_more = moved(lax.optimization_barrier((own1_more, resid0))[0], -G)
    tv, tv_done = half_tv(volume, 1, tv, resid0)
    dealt0 = deal(here, paired, resid0, from_high0, [], tv_done)
    sinos1 = in_steps(1, sino1, dealt0[0])
    resid1, down1 = project(here, band_p, [own1, own1_more, high1, high1_more, low1], sinos1, dealt0[0])
    from_low1, from_high1 = moved(resid1, G), moved(down1, -G)
    resid_pieces0 = in_steps(0, dealt0, resid1)

    backs0 = back(paired, band_b, resid0, from_low0, from_high0, [], resid_pieces0[2][2])
    dealt1 = deal(here, paired, resid1, from_high1, [], backs0[0])
    back_pieces0 = in_steps(0, backs0, dealt1[0])
    ends = [pieces0[1][2], high0, pieces0[3][2], low0]
    r_last, tv = patch(here, coverage, offsets, weights, ends, volume, sinogram, tv, dealt1[0])
    resid_pieces1 = in_steps(1, dealt1, r_last)
    settled = arrays_of(resid_pieces0[1:] + resid_pieces1[1:] + back_pieces0[1:])
    backs1 = back(single, band_b, resid1, from_low1, from_high1, [], r_last, *settled)
    back_pieces1 = direct(1, single, backs1)

    gradient = finish(here, 0, tv, back_pieces0, backs1[0])
    residual = join_rows(here, slabs, 0, resid_pieces0, r_last, backs1[0])
    residual = join_rows(here, slabs, 1, resid_pieces1, residual)
    gradient = finish(here, 1, gradient, back_pieces1)
    return (gradient, residual)


def solution(mesh):
    placed = (P("slab", "grp", None), P("slab", "grp", None), P(), P(), P())
    return jax.shard_map(
        local,
        mesh=mesh,
        in_specs=placed,
        out_specs=(P("slab", "grp", None), P("slab", "grp", None)),
        check_vma=False,
    )
```

```python
import functools

import jax
import jax.numpy as jnp
from jax import lax
from jax.experimental import pallas as pl
from jax.experimental.pallas import tpu as pltpu
from jax.sharding import PartitionSpec as P

G = 4
CHUNKS = 2
ROWS = 2
TILE = 256
F32 = jnp.float32
BF16 = jnp.bfloat16
MIB = 1024 * 1024
LANES = 128
SMEM = pl.BlockSpec(memory_space=pltpu.SMEM)
VMEM = pl.BlockSpec(memory_space=pltpu.VMEM)
ANY = pl.BlockSpec(memory_space=pl.ANY)


def moved(value, steps, only=None):
    count = lax.axis_size("slab")
    first, last = max(0, -steps), min(count, count - steps)
    pairs = [(i, i + steps) for i in range(first, last) if only is None or i % G == only]
    return lax.ppermute(value, "slab", pairs)


def swapped(value, bits):
    count = lax.axis_size("slab")
    return lax.ppermute(value, "slab", [(i, i ^ bits) for i in range(count)])


def direct(arrays):
    return [array if m == 0 else swapped(array, m) for m, array in enumerate(arrays)]


def call(kernel, us, *, results, vmem=16, **how):
    return pl.pallas_call(
        kernel,
        out_shape=results,
        compiler_params=pltpu.CompilerParams(vmem_limit_bytes=vmem * MIB),
        cost_estimate=pl.CostEstimate(flops=int(us * 1.15e9), bytes_accessed=1000, transcendentals=0),
        **how,
    )


def value(shape, dtype):
    return jax.ShapeDtypeStruct(shape, dtype)


def far(array):
    return pltpu.with_memory_space_constraint(array, pltpu.HBM)


def across(shape, tile):
    block = shape[:-1] + (tile,)
    return pl.BlockSpec(block, lambda i: (0,) * (len(shape) - 1) + (i,))


def piece_specs(pieces, side, tile):
    return [pl.BlockSpec((side, tile), lambda i, at=at: (at, i)) for _, at in pieces]


def arrays_of(pieces):
    return [array for array, _ in pieces]


def rows_of(place, m):
    first = ROWS * jnp.bitwise_xor(place, m)
    return [(h * TILE, first + h) for h in range(ROWS)]


def wide_tile(rows_deep):
    return pltpu.VMEM((TILE // LANES, rows_deep, LANES), F32)


def chunk_tiles(chunk, cols):
    count = cols // CHUNKS // TILE
    return chunk * count, count


CAST_GROUPS = ((0, (0,)), (0, (1,)), (0, (2,)), (0, (3,)), (1, (0,)), (1, (1,)), (1, (2, 3)))


def cast_kernel(count, here_ref, *refs):
    parts = TILE // LANES
    vol_refs, (top_ref, end_ref, sino_ref), out_refs = refs[:parts], refs[parts : parts + 3], refs[parts + 3 :]
    block_refs, sent_refs = out_refs[:-CHUNKS], out_refs[-CHUNKS:]
    step = pl.program_id(0)
    rows = ROWS * G
    depth = vol_refs[0].shape[0] // rows
    place = lax.rem(here_ref[0], G)

    for c in range(CHUNKS):

        @pl.when(step // count == c)
        def _():
            sent_refs[c][...] = sino_ref[...]
            for j, vol_ref in enumerate(vol_refs):
                for (chunk, group), out_ref in zip(CAST_GROUPS, block_refs):
                    if chunk != c:
                        continue
                    for n, m in enumerate(group):
                        for start, row in rows_of(place, m):
                            at = pl.ds(start + j * LANES, LANES)
                            block = vol_ref[pl.ds(row, depth, stride=rows), :].astype(BF16)
                            out_ref[n * depth : (n + 1) * depth, at] = block
            if c == 0:
                both = jnp.concatenate([top_ref[...], end_ref[...]], axis=0).astype(BF16)
                for (chunk, group), out_ref in zip(CAST_GROUPS, block_refs):
                    if chunk == 0 and group[0] % 2:
                        out_ref[depth:, :] = both


def cast_rows(here, volume, sinogram):
    depth, rows, cols = volume.shape
    flat = far(volume.reshape(depth * rows, cols))
    _, count = chunk_tiles(0, cols)
    parts, width = TILE // LANES, ROWS * TILE

    def step_of(chunk):
        return lambda i: jnp.clip(i - chunk * count, 0, count - 1)

    shapes = [(len(g) * depth + (2 * rows if c == 0 and g[0] % 2 else 0), cols) for c, g in CAST_GROUPS]
    out_specs = [
        pl.BlockSpec((shape[0], width), lambda i, at=step_of(c): (0, at(i))) for (c, _), shape in zip(CAST_GROUPS, shapes)
    ]
    out_specs += [pl.BlockSpec((depth, rows, TILE), lambda i, at=step_of(c): (0, 0, at(i))) for c in range(CHUNKS)]
    results = [value(shape, BF16) for shape in shapes] + [value((depth, rows, cols // CHUNKS), BF16)] * CHUNKS
    in_specs = [SMEM]
    in_specs += [pl.BlockSpec((depth * rows, LANES), lambda i, j=j: (0, i * parts + j)) for j in range(parts)]
    in_specs += [pl.BlockSpec((rows, width), lambda i, z=z, at=step_of(0): (z, at(i))) for z in (0, depth - 1)]
    in_specs += [pl.BlockSpec((depth, rows, TILE), lambda i: (0, 0, i))]
    return call(
        functools.partial(cast_kernel, count),
        4,
        grid=(CHUNKS * count,),
        in_specs=in_specs,
        out_specs=out_specs,
        results=results,
    )(here, *[flat] * parts, flat, flat, far(sinogram))


def last_block(here_ref, blocks):
    spot = jnp.bitwise_xor(lax.rem(here_ref[0], G), G - 1)
    last = blocks[0]
    for m in range(1, G):
        last = jnp.where(spot == m, blocks[m], last)
    return last


def pack_kernel(here_ref, *refs):
    in_refs, (all_ref, last_ref) = refs[:G], refs[-2:]
    side = in_refs[0].shape[0]
    for m in range(G):
        all_ref[m * side : (m + 1) * side] = in_refs[m][:side]
    last_ref[:side] = last_block(here_ref, [ref[:side] for ref in in_refs])
    all_ref[G * side :] = in_refs[G - 1][side:]
    last_ref[side:] = in_refs[G - 1][side:]


def pack(here, blocks, *tokens):
    side, cols = blocks[0].shape
    more = blocks[G - 1].shape[0] - side
    tile = 512
    shapes = [(G * side + more, cols), (side + more, cols)]
    return call(
        pack_kernel,
        1,
        grid=(cols // tile,),
        in_specs=[SMEM] + [across(block.shape, tile) for block in blocks] + [ANY] * len(tokens),
        out_specs=[across(shape, tile) for shape in shapes],
        results=[value(shape, BF16) for shape in shapes],
    )(here, *blocks, *tokens)


def split_kernel(with_resid, here_ref, own_ref, got_ref, *refs):
    out_refs, wide = refs[-G - 1 : -1], refs[-1]
    depth, rows, cols = own_ref.shape
    place = lax.rem(here_ref[0], G)

    def fill(ref):
        for j in range(cols // LANES):
            wide[j] = ref[:, :, j * LANES : (j + 1) * LANES].astype(F32).reshape(wide.shape[1:])

    @pl.when(place == G - 1)
    def _():
        fill(got_ref)

    @pl.when(place != G - 1)
    def _():
        fill(own_ref)

    for m, out_ref in enumerate(out_refs):
        for j in range(cols // LANES):
            for start, row in rows_of(place, m):
                at = pl.ds(start + j * LANES, LANES)
                out_ref[:depth, at] = wide.at[j][pl.ds(row, depth, stride=rows), :].astype(BF16)
        if with_resid:
            out_ref[depth:] = refs[0][m * depth : (m + 1) * depth]


def split_rows(here, own, got, chunk, resid, *tokens):
    depth, rows, cols = own.shape
    first, count = chunk_tiles(chunk, cols)
    block = (depth, rows, TILE)
    width = ROWS * TILE
    extra = [] if resid is None else [resid]
    shape = ((1 + len(extra)) * depth, cols)
    return call(
        functools.partial(split_kernel, resid is not None),
        2,
        grid=(count,),
        in_specs=[SMEM, pl.BlockSpec(block, lambda i: (0, 0, first + i)), pl.BlockSpec(block, lambda i: (0, 0, i))]
        + [pl.BlockSpec((G * depth, width), lambda i: (0, i))] * len(extra)
        + [ANY] * len(tokens),
        out_specs=[across(shape, width)] * G,
        results=[value(shape, BF16)] * G,
        scratch_shapes=[wide_tile(depth * rows)],
    )(here, far(own), got, *extra, *tokens)


def patch_kernel(slabs, here_ref, cover_ref, offset_ref, *refs):
    w_ref, *refs = refs
    end_refs, (vol_ref, sino_ref), (r_ref, tv_ref) = refs[:4], refs[4:6], refs[-10:-8]
    vol, s, r, wide, tv, slices, fixed, sem = refs[-8:]
    depth, rows, cols = sino_ref.shape
    place = lax.rem(here_ref[0], G)
    near, next_level, far_end, last_level = (ref[...] for ref in end_refs)
    low = jnp.where(place == 0, last_level, jnp.where(place == 2, far_end, near))[rows:].astype(F32)
    high = jnp.where(place == G - 1, next_level, jnp.where(place == 1, far_end, near))[:rows].astype(F32)

    for n, z in enumerate((0, depth - 2)):
        pltpu.make_async_copy(vol_ref.at[z : z + 2], slices.at[2 * n : 2 * n + 2], sem.at[n]).start()
    for n, z in enumerate((0, depth - 2)):
        pltpu.make_async_copy(vol_ref.at[z : z + 2], slices.at[2 * n : 2 * n + 2], sem.at[n]).wait()
    fixed[0] = tv_slice(slices[0], slices[1], tv_below(low, slices[0]))[0]
    fixed[1] = tv_slice(slices[3], high, tv_below(slices[2], slices[3]))[0]
    for n, z in enumerate((0, depth - 1)):
        pltpu.make_async_copy(fixed.at[n], tv_ref.at[z], sem.at[n]).start()
    for n, z in enumerate((0, depth - 1)):
        pltpu.make_async_copy(fixed.at[n], tv_ref.at[z], sem.at[n]).wait()

    @pl.when(here_ref[0] == slabs - 1)
    def _():
        pltpu.make_async_copy(vol_ref, vol, sem.at[2]).start()
        pltpu.make_async_copy(sino_ref, s, sem.at[3]).start()
        pltpu.make_async_copy(tv_ref, tv, sem.at[4]).start()
        pltpu.make_async_copy(vol_ref, vol, sem.at[2]).wait()
        pltpu.make_async_copy(sino_ref, s, sem.at[3]).wait()
        pltpu.make_async_copy(tv_ref, tv, sem.at[4]).wait()
        block = w_ref[offset_ref[slabs - 1, 0]]
        block = jnp.where(cover_ref[slabs - 1, 0] == 1, block, jnp.zeros_like(block))
        turned = block.astype(F32).T.astype(BF16)

        def column(j, _):
            at = pl.ds(pl.multiple_of(j * LANES, LANES), LANES)
            for n, ref in enumerate((s, tv, vol)):
                wide[n] = ref[:, :, at].astype(F32).reshape(wide.shape[1:])
            for row in range(rows):
                spot = pl.ds(row, depth, stride=rows)
                seen = jnp.dot(block, wide.at[2][spot, :].astype(BF16), preferred_element_type=F32)
                resid = (seen - wide.at[0][spot, :]).astype(BF16)
                wide.at[0][spot, :] = resid.astype(F32)
                wide.at[1][spot, :] += jnp.dot(turned, resid, preferred_element_type=F32)
            r[:, :, at] = wide[0].reshape(depth, rows, LANES).astype(BF16)
            tv[:, :, at] = wide[1].reshape(depth, rows, LANES)
            return 0

        lax.fori_loop(0, cols // LANES, column, 0)
        pltpu.make_async_copy(r, r_ref, sem.at[3]).start()
        pltpu.make_async_copy(tv, tv_ref, sem.at[4]).start()
        pltpu.make_async_copy(r, r_ref, sem.at[3]).wait()
        pltpu.make_async_copy(tv, tv_ref, sem.at[4]).wait()


def patch(here, coverage, offsets, weights, ends, volume, sinogram, tv, *tokens):
    slabs = coverage.shape[0]
    depth, rows, cols = sinogram.shape
    edges = [pl.BlockSpec((2 * rows, cols), lambda i, last=end.shape[0] // (2 * rows) - 1: (last, 0)) for end in ends]
    return call(
        functools.partial(patch_kernel, slabs),
        3,
        vmem=32,
        grid=(1,),
        in_specs=[SMEM, SMEM, SMEM, pl.BlockSpec(weights.shape, lambda i: (0, 0, 0))]
        + edges
        + [ANY] * (3 + len(tokens)),
        out_specs=[ANY, ANY],
        results=[pltpu.HBM(sinogram.shape, BF16), pltpu.HBM(volume.shape, F32)],
        input_output_aliases={10: 1},
        scratch_shapes=[
            pltpu.VMEM(volume.shape, F32),
            pltpu.VMEM(sinogram.shape, BF16),
            pltpu.VMEM(sinogram.shape, BF16),
            pltpu.VMEM((3, depth * rows, LANES), F32),
            pltpu.VMEM(volume.shape, F32),
            pltpu.VMEM((4, rows, cols), F32),
            pltpu.VMEM((2, rows, cols), F32),
            pltpu.SemaphoreType.DMA((5,)),
        ],
    )(here, coverage, offsets, weights, *ends, far(volume), far(sinogram), far(tv), *tokens)


def natural(place, in_refs, wide, j):
    depth = in_refs[0].shape[0]
    rows = ROWS * len(in_refs)
    for m, ref in enumerate(in_refs):
        for start, row in rows_of(place, m):
            value = ref[:, start + j * LANES : start + (j + 1) * LANES].astype(F32)
            wide.at[j][pl.ds(row, depth, stride=rows), :] = value
    return wide[j].reshape(depth, rows, LANES)


def join_kernel(here_ref, *refs):
    in_refs, (out_ref, wide) = refs[:G], refs[-2:]
    for j in range(out_ref.shape[2] // LANES):
        out_ref[:, :, j * LANES : (j + 1) * LANES] = natural(lax.rem(here_ref[0], G), in_refs, wide, j).astype(BF16)


def join_rows(here, pieces, shape, *tokens):
    depth, rows, cols = shape
    _, count = chunk_tiles(0, cols)
    return call(
        join_kernel,
        1.5,
        grid=(count,),
        in_specs=[SMEM] + piece_specs(pieces, depth, ROWS * TILE) + [ANY] * len(tokens),
        out_specs=pl.BlockSpec((depth, rows, TILE), lambda i: (0, 0, i)),
        results=value((depth, rows, cols // CHUNKS), BF16),
        scratch_shapes=[wide_tile(depth * rows)],
    )(here, *arrays_of(pieces), *tokens)


def settle_kernel(slabs, count, here_ref, own_ref, above_ref, *refs):
    in_refs, (base_ref, out_ref, wide) = refs[:G], refs[-3:]
    step = pl.program_id(0)
    cols = out_ref.shape[2]
    place = lax.rem(here_ref[0], G)
    last = here_ref[0] == slabs - 1

    @pl.when(last)
    def _():
        pltpu.sync_copy(base_ref.at[:, :, pl.ds(pl.multiple_of(step * cols, cols), cols)], out_ref)

    @pl.when(jnp.logical_not(last) & (step < count) & (place == G - 1))
    def _():
        out_ref[...] = above_ref[...]

    @pl.when(jnp.logical_not(last) & (step < count) & (place != G - 1))
    def _():
        out_ref[...] = own_ref[...]

    @pl.when(jnp.logical_not(last) & (step >= count))
    def _():
        for j in range(cols // LANES):
            out_ref[:, :, j * LANES : (j + 1) * LANES] = natural(place, in_refs, wide, j).astype(BF16)


def settle(here, slabs, own, above, pieces, base, *tokens):
    depth, rows, cols = base.shape
    _, count = chunk_tiles(0, cols)
    block = (depth, rows, TILE)
    early = pl.BlockSpec(block, lambda i: (0, 0, jnp.minimum(i, count - 1)))
    late = [
        pl.BlockSpec((depth, ROWS * TILE), lambda i, at=at: (at, jnp.maximum(i - count, 0))) for _, at in pieces
    ]
    return call(
        functools.partial(settle_kernel, slabs, count),
        2.6,
        grid=(CHUNKS * count,),
        in_specs=[SMEM, early, early] + late + [ANY] * (len(tokens) + 1),
        out_specs=pl.BlockSpec(block, lambda i: (0, 0, i)),
        results=value(base.shape, BF16),
        scratch_shapes=[wide_tile(depth * rows)],
    )(here, own, above, *arrays_of(pieces), *tokens, far(base))


def finish_kernel(here_ref, tv_ref, *refs):
    in_refs, (out_ref, wide) = refs[:G], refs[-2:]
    for j in range(out_ref.shape[2] // LANES):
        at = pl.ds(j * LANES, LANES)
        out_ref[:, :, at] = tv_ref[:, :, at] + natural(lax.rem(here_ref[0], G), in_refs, wide, j)


def finish(here, chunk, tv, pieces, *tokens):
    depth, rows, cols = tv.shape
    first, count = chunk_tiles(chunk, cols)
    part = pl.BlockSpec((depth, rows, TILE), lambda i: (0, 0, first + i))
    return call(
        finish_kernel,
        2.6,
        grid=(count,),
        in_specs=[SMEM, part] + piece_specs(pieces, depth, ROWS * TILE) + [ANY] * len(tokens),
        out_specs=part,
        results=pltpu.HBM(tv.shape, F32),
        input_output_aliases={1: 0},
        scratch_shapes=[wide_tile(depth * rows)],
    )(here, far(tv), *arrays_of(pieces), *tokens)


def band_kernel(slabs, span, here_ref, cover_ref, offset_ref, w_ref, *refs):
    proj_ref, back_ref, turned = refs[-3:]
    side = w_ref.shape[1]
    place = lax.rem(here_ref[0], G)
    first = here_ref[0] - place
    zero = jnp.zeros((side, side), BF16)
    for i in range(w_ref.shape[0]):
        turned[i] = w_ref[i].astype(F32).T.astype(BF16)

    def block(ref, i, j):
        k = j - i
        known, step = jnp.clip(i, 0, slabs - 1), jnp.clip(k, 0, span - 1)
        inside = (i >= 0) & (i < slabs) & (j >= 0) & (j < slabs) & (k >= 0) & (k < span)
        live = inside & (cover_ref[known, step] == 1)
        return jnp.where(live, ref[offset_ref[known, step]], zero)

    def slab(m):
        return first + jnp.bitwise_xor(place, m)

    def group(m):
        to = jnp.bitwise_xor(place, m)
        return first + jnp.where(to == G - 1, -1, to)

    seen = [slab(m) for m in range(G)] + [slab(m) + G for m in range(G)] + [first - 1]
    seeing = [group(m) for m in range(G)] + [group(m) - G for m in range(G)] + [first + G - 1]
    for r in range(G):
        for s in range(2 * G + 1):
            at = (pl.ds(r * side, side), pl.ds(s * side, side))
            proj_ref[at] = block(w_ref, group(r), seen[s])
            back_ref[at] = block(turned, seeing[s], slab(r))


def bands(here, coverage, offsets, weights, *tokens):
    slabs, span = coverage.shape
    side = weights.shape[1]
    shape = (G * side, (2 * G + 1) * side)
    return call(
        functools.partial(band_kernel, slabs, span),
        1.6,
        in_specs=[SMEM, SMEM, SMEM, pl.BlockSpec(weights.shape, lambda i: (0, 0, 0))] + [ANY] * len(tokens),
        grid=(1,),
        out_specs=[pl.BlockSpec(shape, lambda i: (0, 0))] * 2,
        results=[pltpu.HBM(shape, BF16)] * 2,
        scratch_shapes=[pltpu.VMEM(weights.shape, BF16)],
    )(here, coverage, offsets, weights, *tokens)


def residual_blocks(band, seen, sino_refs):
    side = sino_refs[0].shape[0]
    total = jnp.dot(band, jnp.concatenate(seen, axis=0), preferred_element_type=F32)
    return [(total[m * side : (m + 1) * side] - ref[...].astype(F32)).astype(BF16) for m, ref in enumerate(sino_refs)]


def first_kernel(here_ref, band_ref, own_ref, high_ref, low_ref, *refs):
    sino_refs, next_refs, (up_ref, down_ref) = refs[:G], refs[G : 2 * G], refs[-2:]
    side = sino_refs[0].shape[0]
    resid = residual_blocks(band_ref[...], [own_ref[...], high_ref[...], low_ref[...]], sino_refs)
    following = [ref[...] for ref in next_refs]
    for m in range(G):
        at = slice(m * side, (m + 1) * side)
        up_ref[at, :] = resid[m]
        down_ref[at, :] = following[m]
    up_ref[G * side :] = last_block(here_ref, following)
    down_ref[G * side :] = last_block(here_ref, resid)


def project_first(here, band, own, high, low, sinos, following, *tokens):
    n, side = band.shape[0], band.shape[0] // G
    cols = own.shape[1]
    tile = 512
    many, one = pl.BlockSpec((n, tile), lambda i: (0, i)), pl.BlockSpec((side, tile), lambda i: (0, i))
    out = (n + side, cols)
    return call(
        first_kernel,
        4,
        grid=(cols // tile,),
        in_specs=[SMEM, pl.BlockSpec(band.shape, lambda i: (0, 0)), many, many, one]
        + piece_specs(sinos + following, side, tile)
        + [ANY] * len(tokens),
        out_specs=[across(out, tile)] * 2,
        results=[value(out, BF16)] * 2,
    )(here, band, own, high, low, *arrays_of(sinos + following), *tokens)


def second_kernel(here_ref, band_ref, own_ref, high_ref, low_ref, *refs):
    sino_refs, (up_ref, down_ref) = refs[:G], refs[-2:]
    side = sino_refs[0].shape[0]
    resid = residual_blocks(band_ref[...], [own_ref[...], high_ref[...], low_ref[...]], sino_refs)
    for m in range(G):
        up_ref[m * side : (m + 1) * side] = resid[m]
    down_ref[...] = last_block(here_ref, resid)


def project_second(here, band, own, high, low, sinos, *tokens):
    n, side = band.shape[0], band.shape[0] // G
    cols = own.shape[1]
    tile = 512
    many = pl.BlockSpec((n, tile), lambda i: (0, i))
    return call(
        second_kernel,
        3,
        grid=(cols // tile,),
        in_specs=[SMEM, pl.BlockSpec(band.shape, lambda i: (0, 0)), many, many]
        + piece_specs([(low, G)] + sinos, side, tile)
        + [ANY] * len(tokens),
        out_specs=[across((n, cols), tile), across((side, cols), tile)],
        results=[value((n, cols), BF16), value((side, cols), BF16)],
    )(here, band, own, high, low, *arrays_of(sinos), *tokens)


def back_kernel(dealing, here_ref, band_ref, own_ref, low_ref, high_ref, *refs):
    out_refs = refs[-G:]
    side = high_ref.shape[0]
    seeing = jnp.concatenate([own_ref[...], low_ref[...], high_ref[...]], axis=0)
    total = jnp.dot(band_ref[...], seeing, preferred_element_type=F32)
    place = lax.rem(here_ref[0], G)
    for m, out_ref in enumerate(out_refs):
        out_ref[:side] = total[m * side : (m + 1) * side].astype(BF16)
        if dealing:
            last = jnp.bitwise_xor(place, m) == G - 1
            out_ref[side:] = jnp.where(last, refs[1][...], refs[0][m * side : (m + 1) * side])


def back(here, band, own, low, high, dealt, *tokens):
    n, side = band.shape[0], band.shape[0] // G
    cols = own.shape[1]
    tile = 512
    many = pl.BlockSpec((n, tile), lambda i: (0, i))
    one = pl.BlockSpec((side, tile), lambda i: (0, i))
    out = ((2 if dealt else 1) * side, cols)
    return call(
        functools.partial(back_kernel, bool(dealt)),
        3,
        grid=(cols // tile,),
        in_specs=[SMEM, pl.BlockSpec(band.shape, lambda i: (0, 0)), many, many]
        + piece_specs([high], side, tile)
        + ([many, one] if dealt else [])
        + [ANY] * len(tokens),
        out_specs=[across(out, tile)] * G,
        results=[value(out, BF16)] * G,
    )(here, band, own, low, high[0], *dealt, *tokens)


def tv_flux(cur, above):
    rows, cols = cur.shape
    row = lax.broadcasted_iota(jnp.int32, (rows, cols), 0)
    col = lax.broadcasted_iota(jnp.int32, (rows, cols), 1)
    dz = above - cur
    dy = jnp.where(row == rows - 1, 0.0, pltpu.roll(cur, rows - 1, 0)) - cur
    dx = jnp.where(col == cols - 1, 0.0, pltpu.roll(cur, cols - 1, 1)) - cur
    scale = 0.5 * lax.rsqrt(dz * dz + dy * dy + dx * dx + 0.25)
    return dz * scale, dy * scale, dx * scale


def tv_below(cur, above):
    return tv_flux(cur, above)[0]


def tv_slice(cur, above, below_flux):
    rows, cols = cur.shape
    row = lax.broadcasted_iota(jnp.int32, (rows, cols), 0)
    col = lax.broadcasted_iota(jnp.int32, (rows, cols), 1)
    fz, fy, fx = tv_flux(cur, above)
    sides = 0.5 * cur * lax.rsqrt(cur * cur + 0.25)
    fy_low = jnp.where(row == 0, sides, pltpu.roll(fy, 1, 0))
    fx_low = jnp.where(col == 0, sides, pltpu.roll(fx, 1, 1))
    return (below_flux - fz) + (fy_low - fy) + (fx_low - fx), fz


def tv_kernel(last_ref, next_ref, vol_ref, *refs):
    out_ref, done_ref, flux_ref = refs[-3:]
    deep = vol_ref.shape[0]

    @pl.when(pl.program_id(0) == 0)
    def _():
        flux_ref[...] = tv_below(last_ref[0], vol_ref[0])

    def body(z, flux):
        out_ref[z], flux = tv_slice(vol_ref[z], vol_ref[z + 1], flux)
        return flux

    flux = lax.fori_loop(0, deep - 1, body, flux_ref[...], unroll=5)
    out_ref[deep - 1], flux_ref[...] = tv_slice(vol_ref[deep - 1], next_ref[0], flux)
    done_ref[...] = flux_ref[:, : done_ref.shape[1]]


def half_tv(volume, half, base, *tokens):
    depth, rows, cols = volume.shape
    deep = 16
    steps = depth // deep // 2
    first = half * steps
    body = pl.BlockSpec((deep, rows, cols), lambda i: (first + i, 0, 0))
    before = pl.BlockSpec((1, rows, cols), lambda i: (max(first * deep - 1, 0), 0, 0))
    after = pl.BlockSpec((1, rows, cols), lambda i: (jnp.minimum((first + i + 1) * deep, depth - 1), 0, 0))
    bases = [] if base is None else [far(base)]
    return call(
        tv_kernel,
        5,
        grid=(steps,),
        in_specs=[before, after, body] + [ANY] * (len(bases) + len(tokens)),
        out_specs=[body, pl.BlockSpec((rows, LANES), lambda i: (0, 0))],
        results=[pltpu.HBM(volume.shape, F32), value((rows, LANES), F32)],
        input_output_aliases={3: 0} if bases else {},
        scratch_shapes=[pltpu.VMEM((rows, cols), F32)],
    )(*[far(volume)] * 3, *bases, *tokens)


def local(volume, sinogram, weights, coverage, offsets):
    slabs = lax.axis_size("slab")
    here = lax.axis_index("slab").astype(jnp.int32).reshape(1)
    depth = volume.shape[0]

    *blocks, sent0, sent1 = cast_rows(here, volume, sinogram)
    vols0, (v0, v1, v23) = blocks[:G], blocks[G:]
    got0 = moved(sent0, G, only=G - 1)
    got_vols0 = direct(vols0)
    near, over = swapped(v1, 1), swapped(v23, 2)
    tv, tv_done = half_tv(volume, 0, None, vols0[0])
    own0, edge0 = pack(here, got_vols0, tv_done, near)
    high0 = moved(own0, -G)
    sino0 = split_rows(here, sinogram, got0, 0, None, own0)
    sinos0 = [(array, 0) for array in direct(sino0)]
    edge0, sent1, over = lax.optimization_barrier((edge0, sent1, over, sinos0[1][0]))[:3]
    low0 = moved(edge0, G)
    got1 = moved(sent1, G, only=G - 1)
    vols1 = [(v0, 0), (near, 0), (over, 0), (swapped(over[depth:], 1), 0)]
    band_p, band_b = bands(here, coverage, offsets, weights, own0)

    up0, down0 = project_first(here, band_p, own0, high0, low0, sinos0, vols1)
    from_high, from_low = moved(down0, -G), moved(up0, G)
    mixed = split_rows(here, sinogram, got1, 1, up0)
    got_mixed = direct(mixed)
    tv, tv_done = half_tv(volume, 1, tv, mixed[0])
    ends = [got_vols0[1], high0, got_vols0[3], low0]
    r_last, tv = patch(here, coverage, offsets, weights, ends, volume, sinogram, tv, tv_done)
    sinos1 = [(array, 0) for array in got_mixed]
    up1, down1 = project_second(here, band_p, down0, from_high, from_low, sinos1, r_last)
    from_low1, from_high1 = moved(up1, G), moved(down1, -G)

    backs0 = back(here, band_b, up0, from_low, (from_high, G), [up1, from_high1])
    got_backs0 = direct(backs0)
    resid0 = join_rows(here, [(array, 1) for array in got_mixed], sinogram.shape, backs0[0])
    resid0_above = moved(resid0, -G, only=G - 1)
    backs1 = back(here, band_b, up1, from_low1, (from_high1, 0), [], resid0)
    got_backs1 = direct(backs1)
    residual = settle(here, slabs, resid0, resid0_above, [(array, 1) for array in got_backs0], r_last, backs1[0])
    gradient = finish(here, 0, tv, [(array, 0) for array in got_backs0], backs1[0])
    gradient = finish(here, 1, gradient, [(array, 0) for array in got_backs1])
    return (gradient, residual)


def solution(mesh):
    placed = (P("slab", "grp", None), P("slab", "grp", None), P(), P(), P())
    return jax.shard_map(
        local,
        mesh=mesh,
        in_specs=placed,
        out_specs=(P("slab", "grp", None), P("slab", "grp", None)),
        check_vma=False,
    )
```

```python
import functools

import jax
import jax.numpy as jnp
from jax import lax
from jax.experimental import pallas as pl
from jax.experimental.pallas import tpu as pltpu
from jax.sharding import PartitionSpec as P

G = 4
CHUNKS = 2
ROWS = 2
TILE = 256
F32 = jnp.float32
BF16 = jnp.bfloat16
MIB = 1024 * 1024
LANES = 128
SMEM = pl.BlockSpec(memory_space=pltpu.SMEM)
VMEM = pl.BlockSpec(memory_space=pltpu.VMEM)
ANY = pl.BlockSpec(memory_space=pl.ANY)


def moved(value, steps, only=None):
    count = lax.axis_size("slab")
    first, last = max(0, -steps), min(count, count - steps)
    pairs = [(i, i + steps) for i in range(first, last) if only is None or i % G == only]
    return lax.ppermute(value, "slab", pairs)


def swapped(value, bits):
    count = lax.axis_size("slab")
    return lax.ppermute(value, "slab", [(i, i ^ bits) for i in range(count)])


def direct(arrays):
    return [array if m == 0 else swapped(array, m) for m, array in enumerate(arrays)]


def call(kernel, us, *, results, vmem=16, **how):
    return pl.pallas_call(
        kernel,
        out_shape=results,
        compiler_params=pltpu.CompilerParams(vmem_limit_bytes=vmem * MIB),
        cost_estimate=pl.CostEstimate(flops=int(us * 1.15e9), bytes_accessed=1000, transcendentals=0),
        **how,
    )


def value(shape, dtype):
    return jax.ShapeDtypeStruct(shape, dtype)


def far(array):
    return pltpu.with_memory_space_constraint(array, pltpu.HBM)


def across(shape, tile):
    block = shape[:-1] + (tile,)
    return pl.BlockSpec(block, lambda i: (0,) * (len(shape) - 1) + (i,))


def piece_specs(pieces, side, tile):
    return [pl.BlockSpec((side, tile), lambda i, at=at: (at, i)) for _, at in pieces]


def arrays_of(pieces):
    return [array for array, _ in pieces]


def rows_of(place, m):
    first = ROWS * jnp.bitwise_xor(place, m)
    return [(h * TILE, first + h) for h in range(ROWS)]


def wide_tile(rows_deep):
    return pltpu.VMEM((TILE // LANES, rows_deep, LANES), F32)


def chunk_tiles(chunk, cols):
    count = cols // CHUNKS // TILE
    return chunk * count, count


CAST_GROUPS = ((0, (0,)), (0, (1,)), (0, (2,)), (0, (3,)), (1, (0,)), (1, (1,)), (1, (2, 3)))


def cast_kernel(count, here_ref, *refs):
    parts = TILE // LANES
    vol_refs, (top_ref, end_ref), block_refs = refs[:parts], refs[parts : parts + 2], refs[parts + 2 :]
    step = pl.program_id(0)
    rows = ROWS * G
    depth = vol_refs[0].shape[0] // rows
    place = lax.rem(here_ref[0], G)

    for c in range(CHUNKS):

        @pl.when(step // count == c)
        def _():
            for j, vol_ref in enumerate(vol_refs):
                for (chunk, group), out_ref in zip(CAST_GROUPS, block_refs):
                    if chunk != c:
                        continue
                    for n, m in enumerate(group):
                        for start, row in rows_of(place, m):
                            at = pl.ds(start + j * LANES, LANES)
                            block = vol_ref[pl.ds(row, depth, stride=rows), :].astype(BF16)
                            out_ref[n * depth : (n + 1) * depth, at] = block
            if c == 0:
                both = jnp.concatenate([top_ref[...], end_ref[...]], axis=0).astype(BF16)
                for (chunk, group), out_ref in zip(CAST_GROUPS, block_refs):
                    if chunk == 0 and group[0] % 2:
                        out_ref[depth:, :] = both


def cast_rows(here, volume):
    depth, rows, cols = volume.shape
    flat = far(volume.reshape(depth * rows, cols))
    _, count = chunk_tiles(0, cols)
    parts, width = TILE // LANES, ROWS * TILE

    def step_of(chunk):
        return lambda i: jnp.clip(i - chunk * count, 0, count - 1)

    shapes = [(len(g) * depth + (2 * rows if c == 0 and g[0] % 2 else 0), cols) for c, g in CAST_GROUPS]
    out_specs = [
        pl.BlockSpec((shape[0], width), lambda i, at=step_of(c): (0, at(i))) for (c, _), shape in zip(CAST_GROUPS, shapes)
    ]
    in_specs = [SMEM]
    in_specs += [pl.BlockSpec((depth * rows, LANES), lambda i, j=j: (0, i * parts + j)) for j in range(parts)]
    in_specs += [pl.BlockSpec((rows, width), lambda i, z=z, at=step_of(0): (z, at(i))) for z in (0, depth - 1)]
    return call(
        functools.partial(cast_kernel, count),
        4,
        grid=(CHUNKS * count,),
        in_specs=in_specs,
        out_specs=out_specs,
        results=[value(shape, BF16) for shape in shapes],
    )(here, *[flat] * parts, flat, flat)


def last_block(here_ref, blocks):
    spot = jnp.bitwise_xor(lax.rem(here_ref[0], G), G - 1)
    last = blocks[0]
    for m in range(1, G):
        last = jnp.where(spot == m, blocks[m], last)
    return last


def pack_kernel(here_ref, *refs):
    in_refs, (all_ref, last_ref) = refs[:G], refs[-2:]
    side = in_refs[0].shape[0]
    for m in range(G):
        all_ref[m * side : (m + 1) * side] = in_refs[m][:side]
    last_ref[:side] = last_block(here_ref, [ref[:side] for ref in in_refs])
    if last_ref.shape[0] > side:
        all_ref[G * side :] = in_refs[G - 1][side:]
        last_ref[side:] = in_refs[G - 1][side:]


def pack(here, pieces, more, *tokens):
    side, cols = pieces[0][0].shape
    tile = 512
    shapes = [(G * side + more, cols), (side + more, cols)]
    specs = [across(array.shape, tile) for array in arrays_of(pieces)] if more else piece_specs(pieces, side, tile)
    return call(
        pack_kernel,
        1,
        grid=(cols // tile,),
        in_specs=[SMEM] + specs + [ANY] * len(tokens),
        out_specs=[across(shape, tile) for shape in shapes],
        results=[value(shape, BF16) for shape in shapes],
    )(here, *arrays_of(pieces), *tokens)


def split_kernel(groups, passing, here_ref, own_ref, got_ref, *refs):
    out_refs, wide = refs[-len(groups) - passing - 1 : -1], refs[-1]
    if passing:
        out_refs[-1][...] = refs[0][...]
    depth, rows, cols = own_ref.shape
    place = lax.rem(here_ref[0], G)

    def fill(ref):
        for j in range(cols // LANES):
            wide[j] = ref[:, :, j * LANES : (j + 1) * LANES].astype(F32).reshape(wide.shape[1:])

    @pl.when(place == G - 1)
    def _():
        fill(got_ref)

    @pl.when(place != G - 1)
    def _():
        fill(own_ref)

    for group, out_ref in zip(groups, out_refs):
        for n, m in enumerate(group):
            for j in range(cols // LANES):
                for start, row in rows_of(place, m):
                    block = wide.at[j][pl.ds(row, depth, stride=rows), :].astype(BF16)
                    out_ref[n * depth : (n + 1) * depth, start + j * LANES : start + (j + 1) * LANES] = block


def split_rows(here, own, got, chunk, groups, passing, *tokens):
    depth, rows, cols = own.shape
    first, count = chunk_tiles(chunk, cols)
    block = pl.BlockSpec((depth, rows, TILE), lambda i: (0, 0, first + i))
    shapes = [(len(group) * depth, cols) for group in groups] + [(depth, cols)] * len(passing)
    return call(
        functools.partial(split_kernel, groups, len(passing)),
        2,
        grid=(count,),
        in_specs=[SMEM, block, block] + piece_specs(passing, depth, ROWS * TILE) + [ANY] * len(tokens),
        out_specs=[across(shape, ROWS * TILE) for shape in shapes],
        results=[value(shape, BF16) for shape in shapes],
        scratch_shapes=[wide_tile(depth * rows)],
    )(here, far(own), got, *arrays_of(passing), *tokens)


def patch_kernel(slabs, here_ref, cover_ref, offset_ref, *refs):
    w_ref, *refs = refs
    end_refs, (vol_ref, sino_ref), (r_ref, tv_ref) = refs[:4], refs[4:6], refs[-10:-8]
    vol, s, r, wide, tv, slices, fixed, sem = refs[-8:]
    depth, rows, cols = sino_ref.shape
    place = lax.rem(here_ref[0], G)
    near, next_level, far_end, last_level = (ref[...] for ref in end_refs)
    low = jnp.where(place == 0, last_level, jnp.where(place == 2, far_end, near))[rows:].astype(F32)
    high = jnp.where(place == G - 1, next_level, jnp.where(place == 1, far_end, near))[:rows].astype(F32)

    for n, z in enumerate((0, depth - 2)):
        pltpu.make_async_copy(vol_ref.at[z : z + 2], slices.at[2 * n : 2 * n + 2], sem.at[n]).start()
    for n, z in enumerate((0, depth - 2)):
        pltpu.make_async_copy(vol_ref.at[z : z + 2], slices.at[2 * n : 2 * n + 2], sem.at[n]).wait()
    fixed[0] = tv_slice(slices[0], slices[1], tv_below(low, slices[0]))[0]
    fixed[1] = tv_slice(slices[3], high, tv_below(slices[2], slices[3]))[0]
    for n, z in enumerate((0, depth - 1)):
        pltpu.make_async_copy(fixed.at[n], tv_ref.at[z], sem.at[n]).start()
    for n, z in enumerate((0, depth - 1)):
        pltpu.make_async_copy(fixed.at[n], tv_ref.at[z], sem.at[n]).wait()

    @pl.when(here_ref[0] == slabs - 1)
    def _():
        pltpu.make_async_copy(vol_ref, vol, sem.at[2]).start()
        pltpu.make_async_copy(sino_ref, s, sem.at[3]).start()
        pltpu.make_async_copy(tv_ref, tv, sem.at[4]).start()
        pltpu.make_async_copy(vol_ref, vol, sem.at[2]).wait()
        pltpu.make_async_copy(sino_ref, s, sem.at[3]).wait()
        pltpu.make_async_copy(tv_ref, tv, sem.at[4]).wait()
        block = w_ref[offset_ref[slabs - 1, 0]]
        block = jnp.where(cover_ref[slabs - 1, 0] == 1, block, jnp.zeros_like(block))
        turned = block.astype(F32).T.astype(BF16)

        def column(j, _):
            at = pl.ds(pl.multiple_of(j * LANES, LANES), LANES)
            for n, ref in enumerate((s, tv, vol)):
                wide[n] = ref[:, :, at].astype(F32).reshape(wide.shape[1:])
            for row in range(rows):
                spot = pl.ds(row, depth, stride=rows)
                seen = jnp.dot(block, wide.at[2][spot, :].astype(BF16), preferred_element_type=F32)
                resid = (seen - wide.at[0][spot, :]).astype(BF16)
                wide.at[0][spot, :] = resid.astype(F32)
                wide.at[1][spot, :] += jnp.dot(turned, resid, preferred_element_type=F32)
            r[:, :, at] = wide[0].reshape(depth, rows, LANES).astype(BF16)
            tv[:, :, at] = wide[1].reshape(depth, rows, LANES)
            return 0

        lax.fori_loop(0, cols // LANES, column, 0)
        pltpu.make_async_copy(r, r_ref, sem.at[3]).start()
        pltpu.make_async_copy(tv, tv_ref, sem.at[4]).start()
        pltpu.make_async_copy(r, r_ref, sem.at[3]).wait()
        pltpu.make_async_copy(tv, tv_ref, sem.at[4]).wait()


def patch(here, coverage, offsets, weights, ends, volume, sinogram, tv, *tokens):
    slabs = coverage.shape[0]
    depth, rows, cols = sinogram.shape
    edges = [pl.BlockSpec((2 * rows, cols), lambda i, last=end.shape[0] // (2 * rows) - 1: (last, 0)) for end in ends]
    return call(
        functools.partial(patch_kernel, slabs),
        3,
        vmem=32,
        grid=(1,),
        in_specs=[SMEM, SMEM, SMEM, pl.BlockSpec(weights.shape, lambda i: (0, 0, 0))]
        + edges
        + [ANY] * (3 + len(tokens)),
        out_specs=[ANY, ANY],
        results=[pltpu.HBM(sinogram.shape, BF16), pltpu.HBM(volume.shape, F32)],
        input_output_aliases={10: 1},
        scratch_shapes=[
            pltpu.VMEM(volume.shape, F32),
            pltpu.VMEM(sinogram.shape, BF16),
            pltpu.VMEM(sinogram.shape, BF16),
            pltpu.VMEM((3, depth * rows, LANES), F32),
            pltpu.VMEM(volume.shape, F32),
            pltpu.VMEM((4, rows, cols), F32),
            pltpu.VMEM((2, rows, cols), F32),
            pltpu.SemaphoreType.DMA((5,)),
        ],
    )(here, coverage, offsets, weights, *ends, far(volume), far(sinogram), far(tv), *tokens)


def natural(place, in_refs, wide, j):
    depth = in_refs[0].shape[0]
    rows = ROWS * len(in_refs)
    for m, ref in enumerate(in_refs):
        for start, row in rows_of(place, m):
            value = ref[:, start + j * LANES : start + (j + 1) * LANES].astype(F32)
            wide.at[j][pl.ds(row, depth, stride=rows), :] = value
    return wide[j].reshape(depth, rows, LANES)


def join_kernel(here_ref, *refs):
    in_refs, (out_ref, wide) = refs[:G], refs[-2:]
    for j in range(out_ref.shape[2] // LANES):
        out_ref[:, :, j * LANES : (j + 1) * LANES] = natural(lax.rem(here_ref[0], G), in_refs, wide, j).astype(BF16)


def join_rows(here, pieces, shape, *tokens):
    depth, rows, cols = shape
    _, count = chunk_tiles(0, cols)
    return call(
        join_kernel,
        1.5,
        grid=(count,),
        in_specs=[SMEM] + piece_specs(pieces, depth, ROWS * TILE) + [ANY] * len(tokens),
        out_specs=pl.BlockSpec((depth, rows, TILE), lambda i: (0, 0, i)),
        results=value((depth, rows, cols // CHUNKS), BF16),
        scratch_shapes=[wide_tile(depth * rows)],
    )(here, *arrays_of(pieces), *tokens)


def settle_kernel(slabs, count, here_ref, own_ref, above_ref, *refs):
    in_refs, (base_ref, out_ref, wide) = refs[:G], refs[-3:]
    step = pl.program_id(0)
    cols = out_ref.shape[2]
    place = lax.rem(here_ref[0], G)
    last = here_ref[0] == slabs - 1

    @pl.when(last)
    def _():
        pltpu.sync_copy(base_ref.at[:, :, pl.ds(pl.multiple_of(step * cols, cols), cols)], out_ref)

    @pl.when(jnp.logical_not(last) & (step < count) & (place == G - 1))
    def _():
        out_ref[...] = above_ref[...]

    @pl.when(jnp.logical_not(last) & (step < count) & (place != G - 1))
    def _():
        out_ref[...] = own_ref[...]

    @pl.when(jnp.logical_not(last) & (step >= count))
    def _():
        for j in range(cols // LANES):
            out_ref[:, :, j * LANES : (j + 1) * LANES] = natural(place, in_refs, wide, j).astype(BF16)


def settle(here, slabs, own, above, pieces, base, *tokens):
    depth, rows, cols = base.shape
    _, count = chunk_tiles(0, cols)
    block = (depth, rows, TILE)
    early = pl.BlockSpec(block, lambda i: (0, 0, jnp.minimum(i, count - 1)))
    late = [
        pl.BlockSpec((depth, ROWS * TILE), lambda i, at=at: (at, jnp.maximum(i - count, 0))) for _, at in pieces
    ]
    return call(
        functools.partial(settle_kernel, slabs, count),
        2.6,
        grid=(CHUNKS * count,),
        in_specs=[SMEM, early, early] + late + [ANY] * (len(tokens) + 1),
        out_specs=pl.BlockSpec(block, lambda i: (0, 0, i)),
        results=value(base.shape, BF16),
        scratch_shapes=[wide_tile(depth * rows)],
    )(here, own, above, *arrays_of(pieces), *tokens, far(base))


def finish_kernel(here_ref, tv_ref, *refs):
    in_refs, (out_ref, wide) = refs[:G], refs[-2:]
    for j in range(out_ref.shape[2] // LANES):
        at = pl.ds(j * LANES, LANES)
        out_ref[:, :, at] = tv_ref[:, :, at] + natural(lax.rem(here_ref[0], G), in_refs, wide, j)


def finish(here, chunk, tv, pieces, *tokens):
    depth, rows, cols = tv.shape
    first, count = chunk_tiles(chunk, cols)
    part = pl.BlockSpec((depth, rows, TILE), lambda i: (0, 0, first + i))
    return call(
        finish_kernel,
        2.6,
        grid=(count,),
        in_specs=[SMEM, part] + piece_specs(pieces, depth, ROWS * TILE) + [ANY] * len(tokens),
        out_specs=part,
        results=pltpu.HBM(tv.shape, F32),
        input_output_aliases={1: 0},
        scratch_shapes=[wide_tile(depth * rows)],
    )(here, far(tv), *arrays_of(pieces), *tokens)


def band_kernel(slabs, span, here_ref, cover_ref, offset_ref, w_ref, *refs):
    proj_ref, back_ref, turned = refs[-3:]
    side = w_ref.shape[1]
    place = lax.rem(here_ref[0], G)
    first = here_ref[0] - place
    zero = jnp.zeros((side, side), BF16)
    for i in range(w_ref.shape[0]):
        turned[i] = w_ref[i].astype(F32).T.astype(BF16)

    def block(ref, i, j):
        k = j - i
        known, step = jnp.clip(i, 0, slabs - 1), jnp.clip(k, 0, span - 1)
        inside = (i >= 0) & (i < slabs) & (j >= 0) & (j < slabs) & (k >= 0) & (k < span)
        live = inside & (cover_ref[known, step] == 1)
        return jnp.where(live, ref[offset_ref[known, step]], zero)

    def slab(m):
        return first + jnp.bitwise_xor(place, m)

    def group(m):
        to = jnp.bitwise_xor(place, m)
        return first + jnp.where(to == G - 1, -1, to)

    seen = [slab(m) for m in range(G)] + [slab(m) + G for m in range(G)] + [first - 1]
    seeing = [group(m) for m in range(G)] + [group(m) - G for m in range(G)] + [first + G - 1]
    for r in range(G):
        for s in range(2 * G + 1):
            at = (pl.ds(r * side, side), pl.ds(s * side, side))
            proj_ref[at] = block(w_ref, group(r), seen[s])
            back_ref[at] = block(turned, seeing[s], slab(r))


def bands(here, coverage, offsets, weights, *tokens):
    slabs, span = coverage.shape
    side = weights.shape[1]
    shape = (G * side, (2 * G + 1) * side)
    return call(
        functools.partial(band_kernel, slabs, span),
        1.6,
        in_specs=[SMEM, SMEM, SMEM, pl.BlockSpec(weights.shape, lambda i: (0, 0, 0))] + [ANY] * len(tokens),
        grid=(1,),
        out_specs=[pl.BlockSpec(shape, lambda i: (0, 0))] * 2,
        results=[pltpu.HBM(shape, BF16)] * 2,
        scratch_shapes=[pltpu.VMEM(weights.shape, BF16)],
    )(here, coverage, offsets, weights, *tokens)


def project_kernel(groups, here_ref, band_ref, own_ref, high_ref, low_ref, *refs):
    sino_refs, (r_ref, down_ref, *group_refs) = refs[:G], refs[-len(groups) - 2 :]
    side = sino_refs[0].shape[0]
    seen = jnp.concatenate([own_ref[...], high_ref[...], low_ref[...]], axis=0)
    total = jnp.dot(band_ref[...], seen, preferred_element_type=F32)
    resid = [(total[m * side : (m + 1) * side] - ref[...].astype(F32)).astype(BF16) for m, ref in enumerate(sino_refs)]
    for m in range(G):
        r_ref[m * side : (m + 1) * side] = resid[m]
    for group, group_ref in zip(groups, group_refs):
        for n, m in enumerate(group):
            group_ref[n * side : (n + 1) * side] = resid[m]
    down_ref[...] = last_block(here_ref, resid)


def project(here, band, own, high, low, sinos, groups, *tokens):
    n, side = band.shape[0], band.shape[0] // G
    cols = own.shape[1]
    tile = 512
    many, one = pl.BlockSpec((n, tile), lambda i: (0, i)), pl.BlockSpec((side, tile), lambda i: (0, i))
    shapes = [(n, cols), (side, cols)] + [(len(group) * side, cols) for group in groups]
    return call(
        functools.partial(project_kernel, groups),
        3,
        grid=(cols // tile,),
        in_specs=[SMEM, pl.BlockSpec(band.shape, lambda i: (0, 0)), many, many, one]
        + piece_specs(sinos, side, tile)
        + [ANY] * len(tokens),
        out_specs=[across(shape, tile) for shape in shapes],
        results=[value(shape, BF16) for shape in shapes],
    )(here, band, own, high, low, *arrays_of(sinos), *tokens)


def back_kernel(dealing, here_ref, band_ref, own_ref, low_ref, high_ref, *refs):
    out_refs = refs[-G:]
    side = high_ref.shape[0]
    seeing = jnp.concatenate([own_ref[...], low_ref[...], high_ref[...]], axis=0)
    total = jnp.dot(band_ref[...], seeing, preferred_element_type=F32)
    place = lax.rem(here_ref[0], G)
    for m, out_ref in enumerate(out_refs):
        out_ref[:side] = total[m * side : (m + 1) * side].astype(BF16)
        if dealing:
            last = jnp.bitwise_xor(place, m) == G - 1
            out_ref[side:] = jnp.where(last, refs[1][...], refs[0][m * side : (m + 1) * side])


def back(here, band, own, low, high, dealt, *tokens):
    n, side = band.shape[0], band.shape[0] // G
    cols = own.shape[1]
    tile = 512
    many = pl.BlockSpec((n, tile), lambda i: (0, i))
    one = pl.BlockSpec((side, tile), lambda i: (0, i))
    out = ((2 if dealt else 1) * side, cols)
    return call(
        functools.partial(back_kernel, bool(dealt)),
        3,
        grid=(cols // tile,),
        in_specs=[SMEM, pl.BlockSpec(band.shape, lambda i: (0, 0)), many, many]
        + piece_specs([high], side, tile)
        + ([many, one] if dealt else [])
        + [ANY] * len(tokens),
        out_specs=[across(out, tile)] * G,
        results=[value(out, BF16)] * G,
    )(here, band, own, low, high[0], *dealt, *tokens)


def tv_flux(cur, above):
    rows, cols = cur.shape
    row = lax.broadcasted_iota(jnp.int32, (rows, cols), 0)
    col = lax.broadcasted_iota(jnp.int32, (rows, cols), 1)
    dz = above - cur
    dy = jnp.where(row == rows - 1, 0.0, pltpu.roll(cur, rows - 1, 0)) - cur
    dx = jnp.where(col == cols - 1, 0.0, pltpu.roll(cur, cols - 1, 1)) - cur
    scale = 0.5 * lax.rsqrt(dz * dz + dy * dy + dx * dx + 0.25)
    return dz * scale, dy * scale, dx * scale


def tv_below(cur, above):
    return tv_flux(cur, above)[0]


def tv_slice(cur, above, below_flux):
    rows, cols = cur.shape
    row = lax.broadcasted_iota(jnp.int32, (rows, cols), 0)
    col = lax.broadcasted_iota(jnp.int32, (rows, cols), 1)
    fz, fy, fx = tv_flux(cur, above)
    sides = 0.5 * cur * lax.rsqrt(cur * cur + 0.25)
    fy_low = jnp.where(row == 0, sides, pltpu.roll(fy, 1, 0))
    fx_low = jnp.where(col == 0, sides, pltpu.roll(fx, 1, 1))
    return (below_flux - fz) + (fy_low - fy) + (fx_low - fx), fz


def tv_kernel(next_ref, vol_ref, *refs):
    out_ref, done_ref, flux_ref = refs[-3:]
    deep = vol_ref.shape[0]

    @pl.when(pl.program_id(0) == 0)
    def _():
        flux_ref[...] = jnp.zeros_like(flux_ref)

    def body(z, flux):
        out_ref[z], flux = tv_slice(vol_ref[z], vol_ref[z + 1], flux)
        return flux

    flux = lax.fori_loop(0, deep - 1, body, flux_ref[...], unroll=5)
    out_ref[deep - 1], flux_ref[...] = tv_slice(vol_ref[deep - 1], next_ref[0], flux)
    done_ref[...] = flux_ref[:, : done_ref.shape[1]]


def half_tv(volume, *tokens):
    depth, rows, cols = volume.shape
    deep = 16
    body = pl.BlockSpec((deep, rows, cols), lambda i: (i, 0, 0))
    after = pl.BlockSpec((1, rows, cols), lambda i: (jnp.minimum((i + 1) * deep, depth - 1), 0, 0))
    return call(
        tv_kernel,
        9,
        grid=(depth // deep,),
        in_specs=[after, body] + [ANY] * len(tokens),
        out_specs=[body, pl.BlockSpec((rows, LANES), lambda i: (0, 0))],
        results=[pltpu.HBM(volume.shape, F32), value((rows, LANES), F32)],
        scratch_shapes=[pltpu.VMEM((rows, cols), F32)],
    )(far(volume), far(volume), *tokens)


def local(volume, sinogram, weights, coverage, offsets):
    slabs = lax.axis_size("slab")
    here = lax.axis_index("slab").astype(jnp.int32).reshape(1)
    depth, rows, _ = volume.shape
    single = ((0,), (1,), (2,), (3,))
    paired = ((0,), (1,), (2, 3))

    def tied(array, *others):
        return lax.optimization_barrier((array, *others))[0]

    def beyond(over, *others):
        return swapped(tied(over, *others)[depth:], 1)

    *vols0, v0, v1, v23 = cast_rows(here, volume)
    got = moved(tied(sinogram, vols0[0]), G, only=G - 1)
    got_vols0 = direct(vols0)
    near, over = swapped(v1, 1), swapped(v23, 2)
    tv, tv_done = half_tv(volume, vols0[0])
    own0, edge0 = pack(here, [(array, 0) for array in got_vols0], 2 * rows, tv_done)
    high0, low0 = moved(own0, -G), moved(edge0, G)
    band_p, band_b = bands(here, coverage, offsets, weights, own0)
    *sino0, over_beyond = split_rows(here, sinogram, got, 0, single, [(over, 1)], band_p, near)
    sinos0 = [(array, 0) for array in direct(sino0)]
    own1, edge1 = pack(here, [(v0, 0), (near, 0), (over, 0), (swapped(over_beyond, 1), 0)], 0)
    low1, high1 = moved(edge1, G), moved(own1, -G)
    s0, s1, s23 = split_rows(here, sinogram, got, 1, paired, [], own1)

    resid0, down0, r1, r23 = project(here, band_p, own0, high0, low0, sinos0, paired[1:], low1, s0)
    from_low0, from_high0 = moved(resid0, G), moved(down0, -G)
    s_near, s_over = swapped(s1, 1), swapped(s23, 2)
    ends = [got_vols0[1], high0, got_vols0[3], low0]
    r_last, tv = patch(here, coverage, offsets, weights, ends, volume, sinogram, tv, resid0)
    sinos1 = [(s0, 0), (s_near, 0), (s_over, 0), (beyond(s_over, r_last), 0)]
    r_near, r_over = swapped(tied(r1, s_over), 1), swapped(tied(r23, s_over), 2)
    resid1, down1 = project(here, band_p, own1, high1, low1, sinos1, (), r_last)
    from_low1, from_high1 = moved(resid1, G), moved(down1, -G)

    backs0 = back(here, band_b, resid0, from_low0, (from_high0, 0), [resid1, from_high1])
    got_backs0 = direct(backs0)
    r_pieces = [(resid0, 0), (r_near, 0), (r_over, 0), (beyond(r_over, backs0[0]), 0)]
    natural0 = join_rows(here, r_pieces, sinogram.shape, backs0[0])
    above0 = moved(natural0, -G, only=G - 1)
    backs1 = back(here, band_b, resid1, from_low1, (from_high1, 0), [], natural0)
    got_backs1 = direct(backs1)
    residual = settle(here, slabs, natural0, above0, [(array, 1) for array in got_backs0], r_last, backs1[0])
    gradient = finish(here, 0, tv, [(array, 0) for array in got_backs0], backs1[0])
    gradient = finish(here, 1, gradient, [(array, 0) for array in got_backs1], residual)
    return (gradient, residual)


def solution(mesh):
    placed = (P("slab", "grp", None), P("slab", "grp", None), P(), P(), P())
    return jax.shard_map(
        local,
        mesh=mesh,
        in_specs=placed,
        out_specs=(P("slab", "grp", None), P("slab", "grp", None)),
        check_vma=False,
    )
```

```python
import functools

import jax
import jax.numpy as jnp
from jax import lax
from jax.experimental import pallas as pl
from jax.experimental.pallas import tpu as pltpu
from jax.sharding import PartitionSpec as P

G = 4
CHUNKS = 2
ROWS = 2
TILE = 256
F32 = jnp.float32
BF16 = jnp.bfloat16
MIB = 1024 * 1024
LANES = 128
SMEM = pl.BlockSpec(memory_space=pltpu.SMEM)
VMEM = pl.BlockSpec(memory_space=pltpu.VMEM)
ANY = pl.BlockSpec(memory_space=pl.ANY)


def moved(value, steps, only=None):
    count = lax.axis_size("slab")
    first, last = max(0, -steps), min(count, count - steps)
    pairs = [(i, i + steps) for i in range(first, last) if only is None or i % G == only]
    return lax.ppermute(value, "slab", pairs)


def swapped(value, bits):
    count = lax.axis_size("slab")
    return lax.ppermute(value, "slab", [(i, i ^ bits) for i in range(count)])


def direct(arrays):
    return [array if m == 0 else swapped(array, m) for m, array in enumerate(arrays)]


def call(kernel, us, *, results, vmem=16, **how):
    return pl.pallas_call(
        kernel,
        out_shape=results,
        compiler_params=pltpu.CompilerParams(vmem_limit_bytes=vmem * MIB),
        cost_estimate=pl.CostEstimate(flops=int(us * 1.15e9), bytes_accessed=1000, transcendentals=0),
        **how,
    )


def value(shape, dtype):
    return jax.ShapeDtypeStruct(shape, dtype)


def far(array):
    return pltpu.with_memory_space_constraint(array, pltpu.HBM)


def across(shape, tile):
    block = shape[:-1] + (tile,)
    return pl.BlockSpec(block, lambda i: (0,) * (len(shape) - 1) + (i,))


def piece_specs(pieces, side, tile):
    return [pl.BlockSpec((side, tile), lambda i, at=at: (at, i)) for _, at in pieces]


def arrays_of(pieces):
    return [array for array, _ in pieces]


def rows_of(place, m):
    first = ROWS * jnp.bitwise_xor(place, m)
    return [(h * TILE, first + h) for h in range(ROWS)]


def wide_tile(rows_deep):
    return pltpu.VMEM((TILE // LANES, rows_deep, LANES), F32)


def chunk_tiles(chunk, cols):
    count = cols // CHUNKS // TILE
    return chunk * count, count


def cast_kernel(groups, ends, here_ref, *refs):
    parts = TILE // LANES
    vol_refs, end_refs, out_refs = refs[:parts], refs[parts : parts + ends], refs[-len(groups) :]
    rows = ROWS * G
    depth = vol_refs[0].shape[0] // rows
    place = lax.rem(here_ref[0], G)
    for j, vol_ref in enumerate(vol_refs):
        for group, out_ref in zip(groups, out_refs):
            for n, m in enumerate(group):
                for start, row in rows_of(place, m):
                    at = pl.ds(start + j * LANES, LANES)
                    out_ref[n * depth : (n + 1) * depth, at] = vol_ref[pl.ds(row, depth, stride=rows), :].astype(BF16)
    if ends:
        both = jnp.concatenate([ref[...] for ref in end_refs], axis=0).astype(BF16)
        for group, out_ref in zip(groups, out_refs):
            if group[0] % 2:
                out_ref[depth:, :] = both


def cast_rows(here, volume, chunk, groups, ends, *tokens):
    depth, rows, cols = volume.shape
    flat = far(volume.reshape(depth * rows, cols))
    first, count = chunk_tiles(chunk, cols)
    parts, width = TILE // LANES, ROWS * TILE
    shapes = [(len(group) * depth + (2 * rows if ends and group[0] % 2 else 0), cols) for group in groups]
    edges = [pl.BlockSpec((rows, width), lambda i, z=z: (z, i)) for z in (0, depth - 1)] if ends else []
    return call(
        functools.partial(cast_kernel, groups, len(edges)),
        2,
        grid=(count,),
        in_specs=[SMEM]
        + [pl.BlockSpec((depth * rows, LANES), lambda i, j=j: (0, (first + i) * parts + j)) for j in range(parts)]
        + edges
        + [ANY] * len(tokens),
        out_specs=[across(shape, width) for shape in shapes],
        results=[(pltpu.HBM if group[0] == 0 else value)(shape, BF16) for group, shape in zip(groups, shapes)],
    )(here, *[flat] * (parts + len(edges)), *tokens)


def last_block(here_ref, blocks):
    spot = jnp.bitwise_xor(lax.rem(here_ref[0], G), G - 1)
    last = blocks[0]
    for m in range(1, G):
        last = jnp.where(spot == m, blocks[m], last)
    return last


def pack_kernel(here_ref, *refs):
    in_refs, (all_ref, last_ref) = refs[:G], refs[-2:]
    side = in_refs[0].shape[0]
    for m in range(G):
        all_ref[m * side : (m + 1) * side] = in_refs[m][:side]
    last_ref[:side] = last_block(here_ref, [ref[:side] for ref in in_refs])
    if last_ref.shape[0] > side:
        all_ref[G * side :] = in_refs[G - 1][side:]
        last_ref[side:] = in_refs[G - 1][side:]


def pack(here, pieces, more, *tokens):
    side, cols = pieces[0][0].shape
    tile = 512
    shapes = [(G * side + more, cols), (side + more, cols)]
    specs = [across(array.shape, tile) for array in arrays_of(pieces)] if more else piece_specs(pieces, side, tile)
    return call(
        pack_kernel,
        1,
        grid=(cols // tile,),
        in_specs=[SMEM] + specs + [ANY] * len(tokens),
        out_specs=[across(shape, tile) for shape in shapes],
        results=[pltpu.HBM(shape, BF16) for shape in shapes],
    )(here, *arrays_of(pieces), *tokens)


def split_kernel(groups, passing, here_ref, own_ref, got_ref, *refs):
    out_refs, wide = refs[-len(groups) - passing - 1 : -1], refs[-1]
    if passing:
        out_refs[-1][...] = refs[0][...]
    depth, rows, cols = own_ref.shape
    place = lax.rem(here_ref[0], G)

    def fill(ref):
        for j in range(cols // LANES):
            wide[j] = ref[:, :, j * LANES : (j + 1) * LANES].astype(F32).reshape(wide.shape[1:])

    @pl.when(place == G - 1)
    def _():
        fill(got_ref)

    @pl.when(place != G - 1)
    def _():
        fill(own_ref)

    for group, out_ref in zip(groups, out_refs):
        for n, m in enumerate(group):
            for j in range(cols // LANES):
                for start, row in rows_of(place, m):
                    block = wide.at[j][pl.ds(row, depth, stride=rows), :].astype(BF16)
                    out_ref[n * depth : (n + 1) * depth, start + j * LANES : start + (j + 1) * LANES] = block


def split_rows(here, own, got, chunk, groups, passing, *tokens):
    depth, rows, cols = own.shape
    first, count = chunk_tiles(chunk, cols)
    block = pl.BlockSpec((depth, rows, TILE), lambda i: (0, 0, first + i))
    shapes = [(len(group) * depth, cols) for group in groups] + [(depth, cols)] * len(passing)
    return call(
        functools.partial(split_kernel, groups, len(passing)),
        2,
        grid=(count,),
        in_specs=[SMEM, block, block] + piece_specs(passing, depth, ROWS * TILE) + [ANY] * len(tokens),
        out_specs=[across(shape, ROWS * TILE) for shape in shapes],
        results=[value(shape, BF16) for shape in shapes],
        scratch_shapes=[wide_tile(depth * rows)],
    )(here, far(own), got, *arrays_of(passing), *tokens)


def patch_kernel(slabs, here_ref, cover_ref, offset_ref, *refs):
    w_ref, *refs = refs
    end_refs, (vol_ref, sino_ref), (r_ref, tv_ref) = refs[:4], refs[4:6], refs[-10:-8]
    vol, s, r, wide, tv, slices, fixed, sem = refs[-8:]
    depth, rows, cols = sino_ref.shape
    place = lax.rem(here_ref[0], G)
    near, next_level, far_end, last_level = (ref[...] for ref in end_refs)
    low = jnp.where(place == 0, last_level, jnp.where(place == 2, far_end, near))[rows:].astype(F32)
    high = jnp.where(place == G - 1, next_level, jnp.where(place == 1, far_end, near))[:rows].astype(F32)

    for n, z in enumerate((0, depth - 2)):
        pltpu.make_async_copy(vol_ref.at[z : z + 2], slices.at[2 * n : 2 * n + 2], sem.at[n]).start()
    for n, z in enumerate((0, depth - 2)):
        pltpu.make_async_copy(vol_ref.at[z : z + 2], slices.at[2 * n : 2 * n + 2], sem.at[n]).wait()
    fixed[0] = tv_slice(slices[0], slices[1], tv_below(low, slices[0]))[0]
    fixed[1] = tv_slice(slices[3], high, tv_below(slices[2], slices[3]))[0]
    for n, z in enumerate((0, depth - 1)):
        pltpu.make_async_copy(fixed.at[n], tv_ref.at[z], sem.at[n]).start()
    for n, z in enumerate((0, depth - 1)):
        pltpu.make_async_copy(fixed.at[n], tv_ref.at[z], sem.at[n]).wait()

    @pl.when(here_ref[0] == slabs - 1)
    def _():
        pltpu.make_async_copy(vol_ref, vol, sem.at[2]).start()
        pltpu.make_async_copy(sino_ref, s, sem.at[3]).start()
        pltpu.make_async_copy(tv_ref, tv, sem.at[4]).start()
        pltpu.make_async_copy(vol_ref, vol, sem.at[2]).wait()
        pltpu.make_async_copy(sino_ref, s, sem.at[3]).wait()
        pltpu.make_async_copy(tv_ref, tv, sem.at[4]).wait()
        block = w_ref[offset_ref[slabs - 1, 0]]
        block = jnp.where(cover_ref[slabs - 1, 0] == 1, block, jnp.zeros_like(block))
        turned = block.astype(F32).T.astype(BF16)

        def column(j, _):
            at = pl.ds(pl.multiple_of(j * LANES, LANES), LANES)
            for n, ref in enumerate((s, tv, vol)):
                wide[n] = ref[:, :, at].astype(F32).reshape(wide.shape[1:])
            for row in range(rows):
                spot = pl.ds(row, depth, stride=rows)
                seen = jnp.dot(block, wide.at[2][spot, :].astype(BF16), preferred_element_type=F32)
                resid = (seen - wide.at[0][spot, :]).astype(BF16)
                wide.at[0][spot, :] = resid.astype(F32)
                wide.at[1][spot, :] += jnp.dot(turned, resid, preferred_element_type=F32)
            r[:, :, at] = wide[0].reshape(depth, rows, LANES).astype(BF16)
            tv[:, :, at] = wide[1].reshape(depth, rows, LANES)
            return 0

        lax.fori_loop(0, cols // LANES, column, 0)
        pltpu.make_async_copy(r, r_ref, sem.at[3]).start()
        pltpu.make_async_copy(tv, tv_ref, sem.at[4]).start()
        pltpu.make_async_copy(r, r_ref, sem.at[3]).wait()
        pltpu.make_async_copy(tv, tv_ref, sem.at[4]).wait()


def patch(here, coverage, offsets, weights, ends, volume, sinogram, tv, *tokens):
    slabs = coverage.shape[0]
    depth, rows, cols = sinogram.shape
    edges = [pl.BlockSpec((2 * rows, cols), lambda i, last=end.shape[0] // (2 * rows) - 1: (last, 0)) for end in ends]
    return call(
        functools.partial(patch_kernel, slabs),
        3,
        vmem=32,
        grid=(1,),
        in_specs=[SMEM, SMEM, SMEM, pl.BlockSpec(weights.shape, lambda i: (0, 0, 0))]
        + edges
        + [ANY] * (3 + len(tokens)),
        out_specs=[ANY, ANY],
        results=[pltpu.HBM(sinogram.shape, BF16), pltpu.HBM(volume.shape, F32)],
        input_output_aliases={10: 1},
        scratch_shapes=[
            pltpu.VMEM(volume.shape, F32),
            pltpu.VMEM(sinogram.shape, BF16),
            pltpu.VMEM(sinogram.shape, BF16),
            pltpu.VMEM((3, depth * rows, LANES), F32),
            pltpu.VMEM(volume.shape, F32),
            pltpu.VMEM((4, rows, cols), F32),
            pltpu.VMEM((2, rows, cols), F32),
            pltpu.SemaphoreType.DMA((5,)),
        ],
    )(here, coverage, offsets, weights, *ends, far(volume), far(sinogram), far(tv), *tokens)


def natural(place, in_refs, wide, j):
    depth = in_refs[0].shape[0]
    rows = ROWS * len(in_refs)
    for m, ref in enumerate(in_refs):
        for start, row in rows_of(place, m):
            value = ref[:, start + j * LANES : start + (j + 1) * LANES].astype(F32)
            wide.at[j][pl.ds(row, depth, stride=rows), :] = value
    return wide[j].reshape(depth, rows, LANES)


def join_kernel(here_ref, *refs):
    in_refs, (out_ref, wide) = refs[:G], refs[-2:]
    for j in range(out_ref.shape[2] // LANES):
        out_ref[:, :, j * LANES : (j + 1) * LANES] = natural(lax.rem(here_ref[0], G), in_refs, wide, j).astype(BF16)


def join_rows(here, pieces, shape, *tokens):
    depth, rows, cols = shape
    _, count = chunk_tiles(0, cols)
    return call(
        join_kernel,
        0,
        grid=(count,),
        in_specs=[SMEM] + piece_specs(pieces, depth, ROWS * TILE) + [ANY] * len(tokens),
        out_specs=pl.BlockSpec((depth, rows, TILE), lambda i: (0, 0, i)),
        results=value((depth, rows, cols // CHUNKS), BF16),
        scratch_shapes=[wide_tile(depth * rows)],
    )(here, *arrays_of(pieces), *tokens)


def settle_kernel(slabs, count, here_ref, *refs):
    in_refs, (base_ref, out_ref) = refs[: 2 * CHUNKS], refs[-2:]
    step = pl.program_id(0)
    cols = out_ref.shape[2]
    last = here_ref[0] == slabs - 1
    above = lax.rem(here_ref[0], G) == G - 1

    @pl.when(last)
    def _():
        pltpu.sync_copy(base_ref.at[:, :, pl.ds(pl.multiple_of(step * cols, cols), cols)], out_ref)

    for c in range(CHUNKS):
        for n in range(2):

            @pl.when(jnp.logical_not(last) & (step // count == c) & (above == (n == 1)))
            def _():
                out_ref[...] = in_refs[c * 2 + n][...]


def settle(here, slabs, own_above, base, *tokens):
    depth, rows, cols = base.shape
    _, count = chunk_tiles(0, cols)
    block = (depth, rows, TILE)
    specs = [
        pl.BlockSpec(block, lambda i, c=c: (0, 0, jnp.clip(i - c * count, 0, count - 1)))
        for c in range(CHUNKS)
        for _ in range(2)
    ]
    return call(
        functools.partial(settle_kernel, slabs, count),
        0,
        grid=(CHUNKS * count,),
        in_specs=[SMEM] + specs + [ANY] * (len(tokens) + 1),
        out_specs=pl.BlockSpec(block, lambda i: (0, 0, i)),
        results=pltpu.HBM(base.shape, BF16),
    )(here, *[array for pair in own_above for array in pair], *tokens, far(base))


def finish_kernel(here_ref, tv_ref, *refs):
    in_refs, (out_ref, wide) = refs[:G], refs[-2:]
    for j in range(out_ref.shape[2] // LANES):
        at = pl.ds(j * LANES, LANES)
        out_ref[:, :, at] = tv_ref[:, :, at] + natural(lax.rem(here_ref[0], G), in_refs, wide, j)


def finish(here, chunk, tv, pieces, *tokens):
    depth, rows, cols = tv.shape
    first, count = chunk_tiles(chunk, cols)
    part = pl.BlockSpec((depth, rows, TILE), lambda i: (0, 0, first + i))
    return call(
        finish_kernel,
        0,
        grid=(count,),
        in_specs=[SMEM, part] + piece_specs(pieces, depth, ROWS * TILE) + [ANY] * len(tokens),
        out_specs=part,
        results=pltpu.HBM(tv.shape, F32),
        input_output_aliases={1: 0},
        scratch_shapes=[wide_tile(depth * rows)],
    )(here, far(tv), *arrays_of(pieces), *tokens)


def band_kernel(slabs, span, here_ref, cover_ref, offset_ref, w_ref, *refs):
    proj_ref, back_ref, turned = refs[-3:]
    side = w_ref.shape[1]
    place = lax.rem(here_ref[0], G)
    first = here_ref[0] - place
    zero = jnp.zeros((side, side), BF16)
    for i in range(w_ref.shape[0]):
        turned[i] = w_ref[i].astype(F32).T.astype(BF16)

    def block(ref, i, j):
        k = j - i
        known, step = jnp.clip(i, 0, slabs - 1), jnp.clip(k, 0, span - 1)
        inside = (i >= 0) & (i < slabs) & (j >= 0) & (j < slabs) & (k >= 0) & (k < span)
        live = inside & (cover_ref[known, step] == 1)
        return jnp.where(live, ref[offset_ref[known, step]], zero)

    def slab(m):
        return first + jnp.bitwise_xor(place, m)

    def group(m):
        to = jnp.bitwise_xor(place, m)
        return first + jnp.where(to == G - 1, -1, to)

    seen = [slab(m) for m in range(G)] + [slab(m) + G for m in range(G)] + [first - 1]
    seeing = [group(m) for m in range(G)] + [group(m) - G for m in range(G)] + [first + G - 1]
    for r in range(G):
        for s in range(2 * G + 1):
            at = (pl.ds(r * side, side), pl.ds(s * side, side))
            proj_ref[at] = block(w_ref, group(r), seen[s])
            back_ref[at] = block(turned, seeing[s], slab(r))


def bands(here, coverage, offsets, weights, *tokens):
    slabs, span = coverage.shape
    side = weights.shape[1]
    shape = (G * side, (2 * G + 1) * side)
    return call(
        functools.partial(band_kernel, slabs, span),
        1.6,
        in_specs=[SMEM, SMEM, SMEM, pl.BlockSpec(weights.shape, lambda i: (0, 0, 0))] + [ANY] * len(tokens),
        grid=(1,),
        out_specs=[pl.BlockSpec(shape, lambda i: (0, 0))] * 2,
        results=[pltpu.HBM(shape, BF16)] * 2,
        scratch_shapes=[pltpu.VMEM(weights.shape, BF16)],
    )(here, coverage, offsets, weights, *tokens)


def project_kernel(groups, here_ref, band_ref, own_ref, high_ref, low_ref, *refs):
    sino_refs, (r_ref, down_ref, *group_refs) = refs[:G], refs[-len(groups) - 2 :]
    side = sino_refs[0].shape[0]
    seen = jnp.concatenate([own_ref[...], high_ref[...], low_ref[...]], axis=0)
    total = jnp.dot(band_ref[...], seen, preferred_element_type=F32)
    resid = [(total[m * side : (m + 1) * side] - ref[...].astype(F32)).astype(BF16) for m, ref in enumerate(sino_refs)]
    for m in range(G):
        r_ref[m * side : (m + 1) * side] = resid[m]
    for group, group_ref in zip(groups, group_refs):
        for n, m in enumerate(group):
            group_ref[n * side : (n + 1) * side] = resid[m]
    down_ref[...] = last_block(here_ref, resid)


def project(here, band, own, high, low, sinos, groups, *tokens):
    n, side = band.shape[0], band.shape[0] // G
    cols = own.shape[1]
    tile = 512
    many, one = pl.BlockSpec((n, tile), lambda i: (0, i)), pl.BlockSpec((side, tile), lambda i: (0, i))
    shapes = [(n, cols), (side, cols)] + [(len(group) * side, cols) for group in groups]
    return call(
        functools.partial(project_kernel, groups),
        3,
        grid=(cols // tile,),
        in_specs=[SMEM, pl.BlockSpec(band.shape, lambda i: (0, 0)), many, many, one]
        + piece_specs(sinos, side, tile)
        + [ANY] * len(tokens),
        out_specs=[across(shape, tile) for shape in shapes],
        results=[value(shape, BF16) for shape in shapes],
    )(here, far(band), own, high, low, *arrays_of(sinos), *tokens)


def back_kernel(dealing, band_ref, own_ref, low_ref, high_ref, *refs):
    out_refs = refs[-G:]
    side = high_ref.shape[0]
    seeing = jnp.concatenate([own_ref[...], low_ref[...], high_ref[...]], axis=0)
    total = jnp.dot(band_ref[...], seeing, preferred_element_type=F32)
    for m, out_ref in enumerate(out_refs):
        out_ref[:side] = total[m * side : (m + 1) * side].astype(BF16)
        if dealing:
            out_ref[side:] = refs[0][m * side : (m + 1) * side]


def back(band, own, low, high, dealt, *tokens):
    n, side = band.shape[0], band.shape[0] // G
    cols = own.shape[1]
    tile = 512
    many = pl.BlockSpec((n, tile), lambda i: (0, i))
    one = pl.BlockSpec((side, tile), lambda i: (0, i))
    out = ((2 if dealt else 1) * side, cols)
    return call(
        functools.partial(back_kernel, bool(dealt)),
        0,
        grid=(cols // tile,),
        in_specs=[pl.BlockSpec(band.shape, lambda i: (0, 0)), many, many, one]
        + [many] * len(dealt)
        + [ANY] * len(tokens),
        out_specs=[across(out, tile)] * G,
        results=[value(out, BF16)] * G,
    )(far(band), own, low, high, *dealt, *tokens)


def tv_flux(cur, above):
    rows, cols = cur.shape
    row = lax.broadcasted_iota(jnp.int32, (rows, cols), 0)
    col = lax.broadcasted_iota(jnp.int32, (rows, cols), 1)
    dz = above - cur
    dy = jnp.where(row == rows - 1, 0.0, pltpu.roll(cur, rows - 1, 0)) - cur
    dx = jnp.where(col == cols - 1, 0.0, pltpu.roll(cur, cols - 1, 1)) - cur
    scale = 0.5 * lax.rsqrt(dz * dz + dy * dy + dx * dx + 0.25)
    return dz * scale, dy * scale, dx * scale


def tv_below(cur, above):
    return tv_flux(cur, above)[0]


def tv_slice(cur, above, below_flux):
    rows, cols = cur.shape
    row = lax.broadcasted_iota(jnp.int32, (rows, cols), 0)
    col = lax.broadcasted_iota(jnp.int32, (rows, cols), 1)
    fz, fy, fx = tv_flux(cur, above)
    sides = 0.5 * cur * lax.rsqrt(cur * cur + 0.25)
    fy_low = jnp.where(row == 0, sides, pltpu.roll(fy, 1, 0))
    fx_low = jnp.where(col == 0, sides, pltpu.roll(fx, 1, 1))
    return (below_flux - fz) + (fy_low - fy) + (fx_low - fx), fz


def tv_kernel(next_ref, vol_ref, *refs):
    out_ref, done_ref, flux_ref = refs[-3:]
    deep = vol_ref.shape[0]

    @pl.when(pl.program_id(0) == 0)
    def _():
        flux_ref[...] = jnp.zeros_like(flux_ref)

    def body(z, flux):
        out_ref[z], flux = tv_slice(vol_ref[z], vol_ref[z + 1], flux)
        return flux

    flux = lax.fori_loop(0, deep - 1, body, flux_ref[...], unroll=5)
    out_ref[deep - 1], flux_ref[...] = tv_slice(vol_ref[deep - 1], next_ref[0], flux)
    done_ref[...] = flux_ref[:, : done_ref.shape[1]]


def half_tv(volume, *tokens):
    depth, rows, cols = volume.shape
    deep = 16
    body = pl.BlockSpec((deep, rows, cols), lambda i: (i, 0, 0))
    after = pl.BlockSpec((1, rows, cols), lambda i: (jnp.minimum((i + 1) * deep, depth - 1), 0, 0))
    return call(
        tv_kernel,
        9,
        grid=(depth // deep,),
        in_specs=[after, body] + [ANY] * len(tokens),
        out_specs=[body, pl.BlockSpec((rows, LANES), lambda i: (0, 0))],
        results=[pltpu.HBM(volume.shape, F32), value((rows, LANES), F32)],
        scratch_shapes=[pltpu.VMEM((rows, cols), F32)],
    )(far(volume), far(volume), *tokens)


def local(volume, sinogram, weights, coverage, offsets):
    slabs = lax.axis_size("slab")
    here = lax.axis_index("slab").astype(jnp.int32).reshape(1)
    depth, rows, _ = volume.shape
    single = ((0,), (1,), (2,), (3,))
    paired = ((0,), (1,), (2, 3))

    def tied(array, *others):
        return lax.optimization_barrier((array, *others))[0]

    def beyond(over, *others):
        return swapped(tied(over, *others)[depth:], 1)

    vols0 = cast_rows(here, volume, 0, single, True)
    v0, v1, v23 = cast_rows(here, volume, 1, paired, False, vols0[1])
    got = moved(tied(sinogram, vols0[0]), G, only=G - 1)
    got_vols0 = direct(vols0)
    over = swapped(v23, 2)
    tv, tv_done = half_tv(volume, v1)
    own0, edge0 = pack(here, [(array, 0) for array in got_vols0], 2 * rows, tv_done)
    high0, near = moved(own0, -G), swapped(tied(v1, own0), 1)
    band_p, band_b = bands(here, coverage, offsets, weights, own0)
    sino0 = split_rows(here, sinogram, got, 0, single, [], band_p, near)
    sinos0 = [(array, 0) for array in direct(sino0)]
    low0 = moved(tied(edge0, sinos0[1][0]), G)
    own1, edge1 = pack(here, [(v0, 0), (near, 0), (over, 0), (beyond(over, sinos0[1][0]), 0)], 0)
    low1, high1 = moved(edge1, G), moved(own1, -G)
    s0, s1, s23 = split_rows(here, sinogram, got, 1, paired, [], own1)

    resid0, down0, r1, r23 = project(here, band_p, own0, high0, low0, sinos0, paired[1:], low1, s0)
    from_low0, from_high0 = moved(resid0, G), moved(down0, -G)
    s_near, s_over = swapped(s1, 1), swapped(s23, 2)
    ends = [got_vols0[1], high0, got_vols0[3], low0]
    r_last, tv = patch(here, coverage, offsets, weights, ends, volume, sinogram, tv, resid0)
    sinos1 = [(s0, 0), (s_near, 0), (s_over, 0), (beyond(s_over, r_last), 0)]
    r_near, r_over = swapped(tied(r1, s_near), 1), swapped(tied(r23, s_near), 2)
    resid1, down1 = project(here, band_p, own1, high1, low1, sinos1, (), r_last, r_near, r_over)
    from_low1, from_high1 = moved(resid1, G), moved(down1, -G)

    backs0 = back(band_b, resid0, from_low0, from_high0, [resid1])
    got_backs0 = direct(backs0)
    r_pieces = [(resid0, 0), (r_near, 0), (r_over, 0), (beyond(r_over, got_backs0[1]), 0)]
    natural0 = join_rows(here, r_pieces, sinogram.shape, backs0[0])
    above0 = moved(natural0, -G, only=G - 1)
    backs1 = back(band_b, resid1, from_low1, from_high1, [], natural0)
    got_backs1 = direct(backs1)
    natural1 = join_rows(here, [(array, 1) for array in got_backs0], sinogram.shape, backs1[0])
    above1 = moved(natural1, -G, only=G - 1)
    gradient = finish(here, 0, tv, [(array, 0) for array in got_backs0], natural1)
    residual = settle(here, slabs, [(natural0, above0), (natural1, above1)], r_last)
    gradient = finish(here, 1, gradient, [(array, 0) for array in got_backs1], residual)
    return (gradient, residual)


def solution(mesh):
    placed = (P("slab", "grp", None), P("slab", "grp", None), P(), P(), P())
    return jax.shard_map(
        local,
        mesh=mesh,
        in_specs=placed,
        out_specs=(P("slab", "grp", None), P("slab", "grp", None)),
        check_vma=False,
    )
```

```python
import functools

import jax
import jax.numpy as jnp
from jax import lax
from jax.experimental import pallas as pl
from jax.experimental.pallas import tpu as pltpu
from jax.sharding import PartitionSpec as P

G = 4
CHUNKS = 2
ROWS = 2
TILE = 256
F32 = jnp.float32
BF16 = jnp.bfloat16
MIB = 1024 * 1024
LANES = 128
SMEM = pl.BlockSpec(memory_space=pltpu.SMEM)
VMEM = pl.BlockSpec(memory_space=pltpu.VMEM)
ANY = pl.BlockSpec(memory_space=pl.ANY)


def moved(value, steps, only=None):
    count = lax.axis_size("slab")
    first, last = max(0, -steps), min(count, count - steps)
    pairs = [(i, i + steps) for i in range(first, last) if only is None or i % G == only]
    return lax.ppermute(value, "slab", pairs)


def swapped(value, bits):
    count = lax.axis_size("slab")
    return lax.ppermute(value, "slab", [(i, i ^ bits) for i in range(count)])


def direct(arrays):
    return [array if m == 0 else swapped(array, m) for m, array in enumerate(arrays)]


def call(kernel, us, *, results, vmem=16, **how):
    return pl.pallas_call(
        kernel,
        out_shape=results,
        compiler_params=pltpu.CompilerParams(vmem_limit_bytes=vmem * MIB),
        cost_estimate=pl.CostEstimate(flops=int(us * 1.15e9), bytes_accessed=1000, transcendentals=0),
        **how,
    )


def value(shape, dtype):
    return jax.ShapeDtypeStruct(shape, dtype)


def far(array):
    return pltpu.with_memory_space_constraint(array, pltpu.HBM)


def across(shape, tile):
    block = shape[:-1] + (tile,)
    return pl.BlockSpec(block, lambda i: (0,) * (len(shape) - 1) + (i,))


def piece_specs(pieces, side, tile):
    return [pl.BlockSpec((side, tile), lambda i, at=at: (at, i)) for _, at in pieces]


def arrays_of(pieces):
    return [array for array, _ in pieces]


def rows_of(place, m):
    first = ROWS * jnp.bitwise_xor(place, m)
    return [(h * TILE, first + h) for h in range(ROWS)]


def wide_tile(rows_deep):
    return pltpu.VMEM((TILE // LANES, rows_deep, LANES), F32)


def chunk_tiles(chunk, cols):
    count = cols // CHUNKS // TILE
    return chunk * count, count


def cast_kernel(groups, ends, here_ref, *refs):
    parts = TILE // LANES
    vol_refs, end_refs, out_refs = refs[:parts], refs[parts : parts + ends], refs[-len(groups) :]
    rows = ROWS * G
    depth = vol_refs[0].shape[0] // rows
    place = lax.rem(here_ref[0], G)
    for j, vol_ref in enumerate(vol_refs):
        for group, out_ref in zip(groups, out_refs):
            for n, m in enumerate(group):
                for start, row in rows_of(place, m):
                    at = pl.ds(start + j * LANES, LANES)
                    out_ref[n * depth : (n + 1) * depth, at] = vol_ref[pl.ds(row, depth, stride=rows), :].astype(BF16)
    if ends:
        both = jnp.concatenate([ref[...] for ref in end_refs], axis=0).astype(BF16)
        for group, out_ref in zip(groups, out_refs):
            if group[0] % 2:
                out_ref[depth:, :] = both


def cast_rows(here, volume, chunk, groups, ends, *tokens):
    depth, rows, cols = volume.shape
    flat = far(volume.reshape(depth * rows, cols))
    first, count = chunk_tiles(chunk, cols)
    parts, width = TILE // LANES, ROWS * TILE
    shapes = [(len(group) * depth + (2 * rows if ends and group[0] % 2 else 0), cols) for group in groups]
    edges = [pl.BlockSpec((rows, width), lambda i, z=z: (z, i)) for z in (0, depth - 1)] if ends else []
    return call(
        functools.partial(cast_kernel, groups, len(edges)),
        2,
        grid=(count,),
        in_specs=[SMEM]
        + [pl.BlockSpec((depth * rows, LANES), lambda i, j=j: (0, (first + i) * parts + j)) for j in range(parts)]
        + edges
        + [ANY] * len(tokens),
        out_specs=[across(shape, width) for shape in shapes],
        results=[(pltpu.HBM if group[0] == 0 else value)(shape, BF16) for group, shape in zip(groups, shapes)],
    )(here, *[flat] * (parts + len(edges)), *tokens)


def last_block(here_ref, blocks):
    spot = jnp.bitwise_xor(lax.rem(here_ref[0], G), G - 1)
    last = blocks[0]
    for m in range(1, G):
        last = jnp.where(spot == m, blocks[m], last)
    return last


def pack_kernel(here_ref, *refs):
    in_refs, (all_ref, last_ref) = refs[:G], refs[-2:]
    side = in_refs[0].shape[0]
    for m in range(G):
        all_ref[m * side : (m + 1) * side] = in_refs[m][:side]
    last_ref[:side] = last_block(here_ref, [ref[:side] for ref in in_refs])
    if last_ref.shape[0] > side:
        all_ref[G * side :] = in_refs[G - 1][side:]
        last_ref[side:] = in_refs[G - 1][side:]


def pack(here, pieces, more, *tokens):
    side, cols = pieces[0][0].shape
    tile = 512
    shapes = [(G * side + more, cols), (side + more, cols)]
    specs = [across(array.shape, tile) for array in arrays_of(pieces)] if more else piece_specs(pieces, side, tile)
    return call(
        pack_kernel,
        1,
        grid=(cols // tile,),
        in_specs=[SMEM] + specs + [ANY] * len(tokens),
        out_specs=[across(shape, tile) for shape in shapes],
        results=[pltpu.HBM(shape, BF16) for shape in shapes],
    )(here, *arrays_of(pieces), *tokens)


def split_kernel(groups, passing, here_ref, own_ref, got_ref, *refs):
    out_refs, wide = refs[-len(groups) - passing - 1 : -1], refs[-1]
    if passing:
        out_refs[-1][...] = refs[0][...]
    depth, rows, cols = own_ref.shape
    place = lax.rem(here_ref[0], G)

    def fill(ref):
        for j in range(cols // LANES):
            wide[j] = ref[:, :, j * LANES : (j + 1) * LANES].astype(F32).reshape(wide.shape[1:])

    @pl.when(place == G - 1)
    def _():
        fill(got_ref)

    @pl.when(place != G - 1)
    def _():
        fill(own_ref)

    for group, out_ref in zip(groups, out_refs):
        for n, m in enumerate(group):
            for j in range(cols // LANES):
                for start, row in rows_of(place, m):
                    block = wide.at[j][pl.ds(row, depth, stride=rows), :].astype(BF16)
                    out_ref[n * depth : (n + 1) * depth, start + j * LANES : start + (j + 1) * LANES] = block


def split_rows(here, own, got, chunk, groups, passing, *tokens):
    depth, rows, cols = own.shape
    first, count = chunk_tiles(chunk, cols)
    block = pl.BlockSpec((depth, rows, TILE), lambda i: (0, 0, first + i))
    shapes = [(len(group) * depth, cols) for group in groups] + [(depth, cols)] * len(passing)
    return call(
        functools.partial(split_kernel, groups, len(passing)),
        2,
        grid=(count,),
        in_specs=[SMEM, block, block] + piece_specs(passing, depth, ROWS * TILE) + [ANY] * len(tokens),
        out_specs=[across(shape, ROWS * TILE) for shape in shapes],
        results=[value(shape, BF16) for shape in shapes],
        scratch_shapes=[wide_tile(depth * rows)],
    )(here, far(own), got, *arrays_of(passing), *tokens)


def last_kernel(slabs, here_ref, cover_ref, offset_ref, *refs):
    w_ref, vol_ref, sino_ref, *refs = refs
    r_ref, tv_ref, vol, s, r, wide, tv, sem = refs[-8:]
    depth, rows, cols = sino_ref.shape

    @pl.when(here_ref[0] == slabs - 1)
    def _():
        arrivals = [(vol_ref, vol), (sino_ref, s), (tv_ref, tv)]
        for n, (src, dst) in enumerate(arrivals):
            pltpu.make_async_copy(src, dst, sem.at[n]).start()
        for n, (src, dst) in enumerate(arrivals):
            pltpu.make_async_copy(src, dst, sem.at[n]).wait()
        block = w_ref[offset_ref[slabs - 1, 0]]
        block = jnp.where(cover_ref[slabs - 1, 0] == 1, block, jnp.zeros_like(block))
        turned = block.astype(F32).T.astype(BF16)

        def column(j, _):
            at = pl.ds(pl.multiple_of(j * LANES, LANES), LANES)
            for n, ref in enumerate((s, tv, vol)):
                wide[n] = ref[:, :, at].astype(F32).reshape(wide.shape[1:])
            for row in range(rows):
                spot = pl.ds(row, depth, stride=rows)
                seen = jnp.dot(block, wide.at[2][spot, :].astype(BF16), preferred_element_type=F32)
                resid = (seen - wide.at[0][spot, :]).astype(BF16)
                wide.at[0][spot, :] = resid.astype(F32)
                wide.at[1][spot, :] += jnp.dot(turned, resid, preferred_element_type=F32)
            r[:, :, at] = wide[0].reshape(depth, rows, LANES).astype(BF16)
            tv[:, :, at] = wide[1].reshape(depth, rows, LANES)
            return 0

        lax.fori_loop(0, cols // LANES, column, 0)
        departures = [(r, r_ref), (tv, tv_ref)]
        for n, (src, dst) in enumerate(departures):
            pltpu.make_async_copy(src, dst, sem.at[n]).start()
        for n, (src, dst) in enumerate(departures):
            pltpu.make_async_copy(src, dst, sem.at[n]).wait()


def last_group(here, coverage, offsets, weights, volume, sinogram, tv, *tokens):
    slabs = coverage.shape[0]
    depth, rows, cols = sinogram.shape
    return call(
        functools.partial(last_kernel, slabs),
        0,
        vmem=32,
        grid=(1,),
        in_specs=[SMEM, SMEM, SMEM, pl.BlockSpec(weights.shape, lambda i: (0, 0, 0))] + [ANY] * (3 + len(tokens)),
        out_specs=[ANY, ANY],
        results=[pltpu.HBM(sinogram.shape, BF16), pltpu.HBM(volume.shape, F32)],
        input_output_aliases={6: 1},
        scratch_shapes=[
            pltpu.VMEM(volume.shape, F32),
            pltpu.VMEM(sinogram.shape, BF16),
            pltpu.VMEM(sinogram.shape, BF16),
            pltpu.VMEM((3, depth * rows, LANES), F32),
            pltpu.VMEM(volume.shape, F32),
            pltpu.SemaphoreType.DMA((3,)),
        ],
    )(here, coverage, offsets, weights, far(volume), far(sinogram), far(tv), *tokens)


def natural(place, in_refs, wide, j):
    depth = in_refs[0].shape[0]
    rows = ROWS * len(in_refs)
    for m, ref in enumerate(in_refs):
        for start, row in rows_of(place, m):
            value = ref[:, start + j * LANES : start + (j + 1) * LANES].astype(F32)
            wide.at[j][pl.ds(row, depth, stride=rows), :] = value
    return wide[j].reshape(depth, rows, LANES)


def join_kernel(here_ref, *refs):
    in_refs, (out_ref, wide) = refs[:G], refs[-2:]
    for j in range(out_ref.shape[2] // LANES):
        out_ref[:, :, j * LANES : (j + 1) * LANES] = natural(lax.rem(here_ref[0], G), in_refs, wide, j).astype(BF16)


def join_rows(here, pieces, shape, *tokens):
    depth, rows, cols = shape
    _, count = chunk_tiles(0, cols)
    return call(
        join_kernel,
        0,
        grid=(count,),
        in_specs=[SMEM] + piece_specs(pieces, depth, ROWS * TILE) + [ANY] * len(tokens),
        out_specs=pl.BlockSpec((depth, rows, TILE), lambda i: (0, 0, i)),
        results=value((depth, rows, cols // CHUNKS), BF16),
        scratch_shapes=[wide_tile(depth * rows)],
    )(here, *arrays_of(pieces), *tokens)


def settle_kernel(slabs, count, here_ref, *refs):
    in_refs, (base_ref, out_ref) = refs[: 2 * CHUNKS], refs[-2:]
    step = pl.program_id(0)
    cols = out_ref.shape[2]
    last = here_ref[0] == slabs - 1
    above = lax.rem(here_ref[0], G) == G - 1

    @pl.when(last)
    def _():
        pltpu.sync_copy(base_ref.at[:, :, pl.ds(pl.multiple_of(step * cols, cols), cols)], out_ref)

    for c in range(CHUNKS):
        for n in range(2):

            @pl.when(jnp.logical_not(last) & (step // count == c) & (above == (n == 1)))
            def _():
                out_ref[...] = in_refs[c * 2 + n][...]


def settle(here, slabs, own_above, base, *tokens):
    depth, rows, cols = base.shape
    _, count = chunk_tiles(0, cols)
    block = (depth, rows, TILE)
    specs = [
        pl.BlockSpec(block, lambda i, c=c: (0, 0, jnp.clip(i - c * count, 0, count - 1)))
        for c in range(CHUNKS)
        for _ in range(2)
    ]
    return call(
        functools.partial(settle_kernel, slabs, count),
        0,
        grid=(CHUNKS * count,),
        in_specs=[SMEM] + specs + [ANY] * (len(tokens) + 1),
        out_specs=pl.BlockSpec(block, lambda i: (0, 0, i)),
        results=pltpu.HBM(base.shape, BF16),
    )(here, *[array for pair in own_above for array in pair], *tokens, far(base))


def finish_kernel(here_ref, tv_ref, *refs):
    in_refs, (out_ref, wide) = refs[:G], refs[-2:]
    for j in range(out_ref.shape[2] // LANES):
        at = pl.ds(j * LANES, LANES)
        out_ref[:, :, at] = tv_ref[:, :, at] + natural(lax.rem(here_ref[0], G), in_refs, wide, j)


def finish(here, chunk, tv, pieces, *tokens):
    depth, rows, cols = tv.shape
    first, count = chunk_tiles(chunk, cols)
    part = pl.BlockSpec((depth, rows, TILE), lambda i: (0, 0, first + i))
    return call(
        finish_kernel,
        0,
        grid=(count,),
        in_specs=[SMEM, part] + piece_specs(pieces, depth, ROWS * TILE) + [ANY] * len(tokens),
        out_specs=part,
        results=pltpu.HBM(tv.shape, F32),
        input_output_aliases={1: 0},
        scratch_shapes=[wide_tile(depth * rows)],
    )(here, far(tv), *arrays_of(pieces), *tokens)


def band_kernel(slabs, span, here_ref, cover_ref, offset_ref, w_ref, *refs):
    proj_ref, back_ref, turned = refs[-3:]
    side = w_ref.shape[1]
    place = lax.rem(here_ref[0], G)
    first = here_ref[0] - place
    zero = jnp.zeros((side, side), BF16)
    for i in range(w_ref.shape[0]):
        turned[i] = w_ref[i].astype(F32).T.astype(BF16)

    def block(ref, i, j):
        k = j - i
        known, step = jnp.clip(i, 0, slabs - 1), jnp.clip(k, 0, span - 1)
        inside = (i >= 0) & (i < slabs) & (j >= 0) & (j < slabs) & (k >= 0) & (k < span)
        live = inside & (cover_ref[known, step] == 1)
        return jnp.where(live, ref[offset_ref[known, step]], zero)

    def slab(m):
        return first + jnp.bitwise_xor(place, m)

    def group(m):
        to = jnp.bitwise_xor(place, m)
        return first + jnp.where(to == G - 1, -1, to)

    seen = [slab(m) for m in range(G)] + [slab(m) + G for m in range(G)] + [first - 1]
    seeing = [group(m) for m in range(G)] + [group(m) - G for m in range(G)] + [first + G - 1]
    for r in range(G):
        for s in range(2 * G + 1):
            at = (pl.ds(r * side, side), pl.ds(s * side, side))
            proj_ref[at] = block(w_ref, group(r), seen[s])
            back_ref[at] = block(turned, seeing[s], slab(r))


def bands(here, coverage, offsets, weights, *tokens):
    slabs, span = coverage.shape
    side = weights.shape[1]
    shape = (G * side, (2 * G + 1) * side)
    return call(
        functools.partial(band_kernel, slabs, span),
        9,
        in_specs=[SMEM, SMEM, SMEM, pl.BlockSpec(weights.shape, lambda i: (0, 0, 0))] + [ANY] * len(tokens),
        grid=(1,),
        out_specs=[pl.BlockSpec(shape, lambda i: (0, 0))] * 2,
        results=[pltpu.HBM(shape, BF16)] * 2,
        scratch_shapes=[pltpu.VMEM(weights.shape, BF16)],
    )(here, coverage, offsets, weights, *tokens)


def project_kernel(groups, here_ref, band_ref, own_ref, high_ref, low_ref, *refs):
    sino_refs, (r_ref, down_ref, *group_refs) = refs[:G], refs[-len(groups) - 2 :]
    side = sino_refs[0].shape[0]
    seen = jnp.concatenate([own_ref[...], high_ref[...], low_ref[...]], axis=0)
    total = jnp.dot(band_ref[...], seen, preferred_element_type=F32)
    resid = [(total[m * side : (m + 1) * side] - ref[...].astype(F32)).astype(BF16) for m, ref in enumerate(sino_refs)]
    for m in range(G):
        r_ref[m * side : (m + 1) * side] = resid[m]
    for group, group_ref in zip(groups, group_refs):
        for n, m in enumerate(group):
            group_ref[n * side : (n + 1) * side] = resid[m]
    down_ref[...] = last_block(here_ref, resid)


def project(here, band, own, high, low, sinos, groups, *tokens):
    n, side = band.shape[0], band.shape[0] // G
    cols = own.shape[1]
    tile = 512
    many, one = pl.BlockSpec((n, tile), lambda i: (0, i)), pl.BlockSpec((side, tile), lambda i: (0, i))
    shapes = [(n, cols), (side, cols)] + [(len(group) * side, cols) for group in groups]
    return call(
        functools.partial(project_kernel, groups),
        3,
        grid=(cols // tile,),
        in_specs=[SMEM, pl.BlockSpec(band.shape, lambda i: (0, 0)), many, many, one]
        + piece_specs(sinos, side, tile)
        + [ANY] * len(tokens),
        out_specs=[across(shape, tile) for shape in shapes],
        results=[value(shape, BF16) for shape in shapes],
    )(here, far(band), far(own), high, low, *arrays_of(sinos), *tokens)


def back_kernel(dealing, band_ref, own_ref, low_ref, high_ref, *refs):
    out_refs = refs[-G:]
    side = high_ref.shape[0]
    seeing = jnp.concatenate([own_ref[...], low_ref[...], high_ref[...]], axis=0)
    total = jnp.dot(band_ref[...], seeing, preferred_element_type=F32)
    for m, out_ref in enumerate(out_refs):
        out_ref[:side] = total[m * side : (m + 1) * side].astype(BF16)
        if dealing:
            out_ref[side:] = refs[0][m * side : (m + 1) * side]


def back(band, own, low, high, dealt, *tokens):
    n, side = band.shape[0], band.shape[0] // G
    cols = own.shape[1]
    tile = 512
    many = pl.BlockSpec((n, tile), lambda i: (0, i))
    one = pl.BlockSpec((side, tile), lambda i: (0, i))
    out = ((2 if dealt else 1) * side, cols)
    return call(
        functools.partial(back_kernel, bool(dealt)),
        0,
        grid=(cols // tile,),
        in_specs=[pl.BlockSpec(band.shape, lambda i: (0, 0)), many, many, one]
        + [many] * len(dealt)
        + [ANY] * len(tokens),
        out_specs=[across(out, tile)] * G,
        results=[value(out, BF16)] * G,
    )(far(band), own, low, high, *dealt, *tokens)


def tv_flux(cur, above):
    rows, cols = cur.shape
    row = lax.broadcasted_iota(jnp.int32, (rows, cols), 0)
    col = lax.broadcasted_iota(jnp.int32, (rows, cols), 1)
    dz = above - cur
    dy = jnp.where(row == rows - 1, 0.0, pltpu.roll(cur, rows - 1, 0)) - cur
    dx = jnp.where(col == cols - 1, 0.0, pltpu.roll(cur, cols - 1, 1)) - cur
    scale = 0.5 * lax.rsqrt(dz * dz + dy * dy + dx * dx + 0.25)
    return dz * scale, dy * scale, dx * scale


def tv_below(cur, above):
    return tv_flux(cur, above)[0]


def tv_slice(cur, above, below_flux):
    rows, cols = cur.shape
    row = lax.broadcasted_iota(jnp.int32, (rows, cols), 0)
    col = lax.broadcasted_iota(jnp.int32, (rows, cols), 1)
    fz, fy, fx = tv_flux(cur, above)
    sides = 0.5 * cur * lax.rsqrt(cur * cur + 0.25)
    fy_low = jnp.where(row == 0, sides, pltpu.roll(fy, 1, 0))
    fx_low = jnp.where(col == 0, sides, pltpu.roll(fx, 1, 1))
    return (below_flux - fz) + (fy_low - fy) + (fx_low - fx), fz


def tv_kernel(here_ref, near_ref, next_level_ref, far_ref, last_level_ref, next_ref, vol_ref, *refs):
    out_ref, done_ref, flux_ref = refs[-3:]
    step = pl.program_id(0)
    deep, rows, _ = vol_ref.shape
    place = lax.rem(here_ref[0], G)

    @pl.when(step == 0)
    def _():
        inside = jnp.where(place == 2, far_ref[...], near_ref[...])
        low = jnp.where(place == 0, last_level_ref[...], inside)[rows:].astype(F32)
        flux_ref[...] = tv_below(low, vol_ref[0])

    def body(z, flux):
        out_ref[z], flux = tv_slice(vol_ref[z], vol_ref[z + 1], flux)
        return flux

    flux = lax.fori_loop(0, deep - 1, body, flux_ref[...], unroll=5)
    inside = jnp.where(place == 1, far_ref[...], near_ref[...])
    high = jnp.where(place == G - 1, next_level_ref[...], inside)[:rows].astype(F32)
    above = jnp.where(step == pl.num_programs(0) - 1, high, next_ref[0])
    out_ref[deep - 1], flux_ref[...] = tv_slice(vol_ref[deep - 1], above, flux)
    done_ref[...] = flux_ref[:, : done_ref.shape[1]]


def half_tv(here, volume, ends, *tokens):
    depth, rows, cols = volume.shape
    deep = 16
    edges = [pl.BlockSpec((2 * rows, cols), lambda i, last=end.shape[0] // (2 * rows) - 1: (last, 0)) for end in ends]
    body = pl.BlockSpec((deep, rows, cols), lambda i: (i, 0, 0))
    after = pl.BlockSpec((1, rows, cols), lambda i: (jnp.minimum((i + 1) * deep, depth - 1), 0, 0))
    return call(
        tv_kernel,
        0,
        grid=(depth // deep,),
        in_specs=[SMEM] + edges + [after, body] + [ANY] * len(tokens),
        out_specs=[body, pl.BlockSpec((rows, LANES), lambda i: (0, 0))],
        results=[pltpu.HBM(volume.shape, F32), value((rows, LANES), F32)],
        scratch_shapes=[pltpu.VMEM((rows, cols), F32)],
    )(here, *ends, far(volume), far(volume), *tokens)


def local(volume, sinogram, weights, coverage, offsets):
    slabs = lax.axis_size("slab")
    here = lax.axis_index("slab").astype(jnp.int32).reshape(1)
    depth, rows, _ = volume.shape
    single = ((0,), (1,), (2,), (3,))
    paired = ((0,), (1,), (2, 3))

    def tied(array, *others):
        return lax.optimization_barrier((array, *others))[0]

    def beyond(over, *others):
        return swapped(tied(over, *others)[depth:], 1)

    vols0 = cast_rows(here, volume, 0, single, True)
    got = moved(tied(sinogram, vols0[0]), G, only=G - 1)
    got_vols0 = direct(vols0)
    v0, v1, v23 = cast_rows(here, volume, 1, paired, False, vols0[1])
    over = swapped(v23, 2)
    band_p, band_b = bands(here, coverage, offsets, weights, v1)
    own0, edge0 = pack(here, [(array, 0) for array in got_vols0], 2 * rows, far(band_p))
    high0, near = moved(own0, -G), swapped(tied(v1, own0), 1)
    *sino0, over_beyond = split_rows(here, sinogram, got, 0, single, [(over, 1)], near)
    sinos0 = [(array, 0) for array in direct(sino0)]
    low0 = moved(tied(edge0, sinos0[1][0]), G)
    own1, edge1 = pack(here, [(v0, 0), (near, 0), (over, 0), (swapped(over_beyond, 1), 0)], 0)
    low1, high1 = moved(edge1, G), moved(own1, -G)

    s0, s1, s23 = split_rows(here, sinogram, got, 1, paired, [], far(own1))

    resid0, down0, r1, r23 = project(here, band_p, own0, high0, low0, sinos0, paired[1:], low1, s0)
    from_low0, from_high0 = moved(resid0, G), moved(down0, -G)
    s_near, s_over = swapped(s1, 1), swapped(s23, 2)
    r_near, r_over = swapped(tied(r1, s_near), 1), swapped(tied(r23, s_near), 2)
    tv, tv_done = half_tv(here, volume, [got_vols0[1], high0, got_vols0[3], low0], resid0)
    sinos1 = [(s0, 0), (s_near, 0), (s_over, 0), (beyond(s_over, tv_done), 0)]
    resid1, down1 = project(here, band_p, own1, high1, low1, sinos1, (), tv_done, r_near, r_over)
    from_low1, from_high1 = moved(resid1, G), moved(down1, -G)

    backs0 = back(band_b, resid0, from_low0, from_high0, [resid1])
    got_backs0 = direct(backs0)
    r_pieces = [(resid0, 0), (r_near, 0), (r_over, 0), (beyond(r_over, got_backs0[1]), 0)]
    natural0 = join_rows(here, r_pieces, sinogram.shape, backs0[0])
    above0 = moved(natural0, -G, only=G - 1)
    r_last, tv = last_group(here, coverage, offsets, weights, volume, sinogram, tv, natural0)
    backs1 = back(band_b, resid1, from_low1, from_high1, [], far(r_last))
    got_backs1 = direct(backs1)
    natural1 = join_rows(here, [(array, 1) for array in got_backs0], sinogram.shape, backs1[0])
    above1 = moved(natural1, -G, only=G - 1)
    gradient = finish(here, 0, tv, [(array, 0) for array in got_backs0], natural1)
    residual = settle(here, slabs, [(natural0, above0), (natural1, above1)], r_last)
    gradient = finish(here, 1, gradient, [(array, 0) for array in got_backs1], far(residual))
    return (gradient, residual)


def solution(mesh):
    placed = (P("slab", "grp", None), P("slab", "grp", None), P(), P(), P())
    return jax.shard_map(
        local,
        mesh=mesh,
        in_specs=placed,
        out_specs=(P("slab", "grp", None), P("slab", "grp", None)),
        check_vma=False,
    )
```

```python
import functools

import jax
import jax.numpy as jnp
from jax import lax
from jax.experimental import pallas as pl
from jax.experimental.pallas import tpu as pltpu
from jax.sharding import PartitionSpec as P

G = 4
CHUNKS = 2
ROWS = 2
TILE = 256
F32 = jnp.float32
BF16 = jnp.bfloat16
MIB = 1024 * 1024
LANES = 128
SMEM = pl.BlockSpec(memory_space=pltpu.SMEM)
VMEM = pl.BlockSpec(memory_space=pltpu.VMEM)
ANY = pl.BlockSpec(memory_space=pl.ANY)


def moved(value, steps, only=None):
    count = lax.axis_size("slab")
    first, last = max(0, -steps), min(count, count - steps)
    pairs = [(i, i + steps) for i in range(first, last) if only is None or i % G == only]
    return lax.ppermute(value, "slab", pairs)


def swapped(value, bits):
    count = lax.axis_size("slab")
    return lax.ppermute(value, "slab", [(i, i ^ bits) for i in range(count)])


def direct(arrays):
    return [array if m == 0 else swapped(array, m) for m, array in enumerate(arrays)]


def call(kernel, us, *, results, vmem=16, **how):
    return pl.pallas_call(
        kernel,
        out_shape=results,
        compiler_params=pltpu.CompilerParams(vmem_limit_bytes=vmem * MIB),
        cost_estimate=pl.CostEstimate(flops=int(us * 1.15e9), bytes_accessed=1000, transcendentals=0),
        **how,
    )


def value(shape, dtype):
    return jax.ShapeDtypeStruct(shape, dtype)


def far(array):
    return pltpu.with_memory_space_constraint(array, pltpu.HBM)


def across(shape, tile):
    block = shape[:-1] + (tile,)
    return pl.BlockSpec(block, lambda i: (0,) * (len(shape) - 1) + (i,))


def piece_specs(pieces, side, tile):
    return [pl.BlockSpec((side, tile), lambda i, at=at: (at, i)) for _, at in pieces]


def arrays_of(pieces):
    return [array for array, _ in pieces]


def rows_of(place, m):
    first = ROWS * jnp.bitwise_xor(place, m)
    return [(h * TILE, first + h) for h in range(ROWS)]


def wide_tile(rows_deep):
    return pltpu.VMEM((TILE // LANES, rows_deep, LANES), F32)


def chunk_tiles(chunk, cols):
    count = cols // CHUNKS // TILE
    return chunk * count, count


def cast_kernel(groups, ends, here_ref, *refs):
    parts = TILE // LANES
    vol_refs, end_refs, out_refs = refs[:parts], refs[parts : parts + ends], refs[-len(groups) :]
    rows = ROWS * G
    depth = vol_refs[0].shape[0] // rows
    place = lax.rem(here_ref[0], G)
    for j, vol_ref in enumerate(vol_refs):
        for group, out_ref in zip(groups, out_refs):
            for n, m in enumerate(group):
                for start, row in rows_of(place, m):
                    at = pl.ds(start + j * LANES, LANES)
                    out_ref[n * depth : (n + 1) * depth, at] = vol_ref[pl.ds(row, depth, stride=rows), :].astype(BF16)
    if ends:
        both = jnp.concatenate([ref[...] for ref in end_refs], axis=0).astype(BF16)
        for group, out_ref in zip(groups, out_refs):
            if group[0] % 2:
                out_ref[depth:, :] = both


def cast_rows(here, volume, chunk, groups, ends, *tokens):
    depth, rows, cols = volume.shape
    flat = far(volume.reshape(depth * rows, cols))
    first, count = chunk_tiles(chunk, cols)
    parts, width = TILE // LANES, ROWS * TILE
    shapes = [(len(group) * depth + (2 * rows if ends and group[0] % 2 else 0), cols) for group in groups]
    edges = [pl.BlockSpec((rows, width), lambda i, z=z: (z, i)) for z in (0, depth - 1)] if ends else []
    return call(
        functools.partial(cast_kernel, groups, len(edges)),
        2,
        grid=(count,),
        in_specs=[SMEM]
        + [pl.BlockSpec((depth * rows, LANES), lambda i, j=j: (0, (first + i) * parts + j)) for j in range(parts)]
        + edges
        + [ANY] * len(tokens),
        out_specs=[across(shape, width) for shape in shapes],
        results=[(pltpu.HBM if group[0] == 0 else value)(shape, BF16) for group, shape in zip(groups, shapes)],
    )(here, *[flat] * (parts + len(edges)), *tokens)


def last_block(here_ref, blocks):
    spot = jnp.bitwise_xor(lax.rem(here_ref[0], G), G - 1)
    last = blocks[0]
    for m in range(1, G):
        last = jnp.where(spot == m, blocks[m], last)
    return last


def pack_kernel(here_ref, *refs):
    in_refs, (all_ref, last_ref) = refs[:G], refs[-2:]
    side = in_refs[0].shape[0]
    for m in range(G):
        all_ref[m * side : (m + 1) * side] = in_refs[m][:side]
    last_ref[:side] = last_block(here_ref, [ref[:side] for ref in in_refs])
    if last_ref.shape[0] > side:
        all_ref[G * side :] = in_refs[G - 1][side:]
        last_ref[side:] = in_refs[G - 1][side:]


def pack(here, pieces, more, *tokens):
    side, cols = pieces[0][0].shape
    tile = 512
    shapes = [(G * side + more, cols), (side + more, cols)]
    specs = [across(array.shape, tile) for array in arrays_of(pieces)] if more else piece_specs(pieces, side, tile)
    return call(
        pack_kernel,
        1,
        grid=(cols // tile,),
        in_specs=[SMEM] + specs + [ANY] * len(tokens),
        out_specs=[across(shape, tile) for shape in shapes],
        results=[pltpu.HBM(shape, BF16) for shape in shapes],
    )(here, *arrays_of(pieces), *tokens)


def split_kernel(groups, passing, here_ref, own_ref, got_ref, *refs):
    out_refs, wide = refs[-len(groups) - passing - 1 : -1], refs[-1]
    if passing:
        out_refs[-1][...] = refs[0][...]
    depth, rows, cols = own_ref.shape
    place = lax.rem(here_ref[0], G)

    def fill(ref):
        for j in range(cols // LANES):
            wide[j] = ref[:, :, j * LANES : (j + 1) * LANES].astype(F32).reshape(wide.shape[1:])

    @pl.when(place == G - 1)
    def _():
        fill(got_ref)

    @pl.when(place != G - 1)
    def _():
        fill(own_ref)

    for group, out_ref in zip(groups, out_refs):
        for n, m in enumerate(group):
            for j in range(cols // LANES):
                for start, row in rows_of(place, m):
                    block = wide.at[j][pl.ds(row, depth, stride=rows), :].astype(BF16)
                    out_ref[n * depth : (n + 1) * depth, start + j * LANES : start + (j + 1) * LANES] = block


def split_rows(here, own, got, chunk, groups, passing, *tokens):
    depth, rows, cols = own.shape
    first, count = chunk_tiles(chunk, cols)
    block = pl.BlockSpec((depth, rows, TILE), lambda i: (0, 0, first + i))
    shapes = [(len(group) * depth, cols) for group in groups] + [(depth, cols)] * len(passing)
    return call(
        functools.partial(split_kernel, groups, len(passing)),
        2,
        grid=(count,),
        in_specs=[SMEM, block, block] + piece_specs(passing, depth, ROWS * TILE) + [ANY] * len(tokens),
        out_specs=[across(shape, ROWS * TILE) for shape in shapes],
        results=[value(shape, BF16) for shape in shapes],
        scratch_shapes=[wide_tile(depth * rows)],
    )(here, far(own), got, *arrays_of(passing), *tokens)


def last_kernel(slabs, here_ref, cover_ref, offset_ref, *refs):
    w_ref, vol_ref, sino_ref, *refs = refs
    r_ref, tv_ref, vol, s, r, wide, tv, sem = refs[-8:]
    depth, rows, cols = sino_ref.shape

    @pl.when(here_ref[0] == slabs - 1)
    def _():
        arrivals = [(vol_ref, vol), (sino_ref, s), (tv_ref, tv)]
        for n, (src, dst) in enumerate(arrivals):
            pltpu.make_async_copy(src, dst, sem.at[n]).start()
        for n, (src, dst) in enumerate(arrivals):
            pltpu.make_async_copy(src, dst, sem.at[n]).wait()
        block = w_ref[offset_ref[slabs - 1, 0]]
        block = jnp.where(cover_ref[slabs - 1, 0] == 1, block, jnp.zeros_like(block))
        turned = block.astype(F32).T.astype(BF16)

        def column(j, _):
            at = pl.ds(pl.multiple_of(j * LANES, LANES), LANES)
            for n, ref in enumerate((s, tv, vol)):
                wide[n] = ref[:, :, at].astype(F32).reshape(wide.shape[1:])
            for row in range(rows):
                spot = pl.ds(row, depth, stride=rows)
                seen = jnp.dot(block, wide.at[2][spot, :].astype(BF16), preferred_element_type=F32)
                resid = (seen - wide.at[0][spot, :]).astype(BF16)
                wide.at[0][spot, :] = resid.astype(F32)
                wide.at[1][spot, :] += jnp.dot(turned, resid, preferred_element_type=F32)
            r[:, :, at] = wide[0].reshape(depth, rows, LANES).astype(BF16)
            tv[:, :, at] = wide[1].reshape(depth, rows, LANES)
            return 0

        lax.fori_loop(0, cols // LANES, column, 0)
        departures = [(r, r_ref), (tv, tv_ref)]
        for n, (src, dst) in enumerate(departures):
            pltpu.make_async_copy(src, dst, sem.at[n]).start()
        for n, (src, dst) in enumerate(departures):
            pltpu.make_async_copy(src, dst, sem.at[n]).wait()


def last_group(here, coverage, offsets, weights, volume, sinogram, tv, *tokens):
    slabs = coverage.shape[0]
    depth, rows, cols = sinogram.shape
    return call(
        functools.partial(last_kernel, slabs),
        0,
        vmem=32,
        grid=(1,),
        in_specs=[SMEM, SMEM, SMEM, pl.BlockSpec(weights.shape, lambda i: (0, 0, 0))] + [ANY] * (3 + len(tokens)),
        out_specs=[ANY, ANY],
        results=[pltpu.HBM(sinogram.shape, BF16), pltpu.HBM(volume.shape, F32)],
        input_output_aliases={6: 1},
        scratch_shapes=[
            pltpu.VMEM(volume.shape, F32),
            pltpu.VMEM(sinogram.shape, BF16),
            pltpu.VMEM(sinogram.shape, BF16),
            pltpu.VMEM((3, depth * rows, LANES), F32),
            pltpu.VMEM(volume.shape, F32),
            pltpu.SemaphoreType.DMA((3,)),
        ],
    )(here, coverage, offsets, weights, far(volume), far(sinogram), far(tv), *tokens)


def natural(place, in_refs, wide, j):
    depth = in_refs[0].shape[0]
    rows = ROWS * len(in_refs)
    for m, ref in enumerate(in_refs):
        for start, row in rows_of(place, m):
            value = ref[:, start + j * LANES : start + (j + 1) * LANES].astype(F32)
            wide.at[j][pl.ds(row, depth, stride=rows), :] = value
    return wide[j].reshape(depth, rows, LANES)


def join_kernel(here_ref, *refs):
    in_refs, (out_ref, wide) = refs[:G], refs[-2:]
    for j in range(out_ref.shape[2] // LANES):
        out_ref[:, :, j * LANES : (j + 1) * LANES] = natural(lax.rem(here_ref[0], G), in_refs, wide, j).astype(BF16)


def join_rows(here, pieces, shape, *tokens):
    depth, rows, cols = shape
    _, count = chunk_tiles(0, cols)
    return call(
        join_kernel,
        0,
        grid=(count,),
        in_specs=[SMEM] + piece_specs(pieces, depth, ROWS * TILE) + [ANY] * len(tokens),
        out_specs=pl.BlockSpec((depth, rows, TILE), lambda i: (0, 0, i)),
        results=value((depth, rows, cols // CHUNKS), BF16),
        scratch_shapes=[wide_tile(depth * rows)],
    )(here, *arrays_of(pieces), *tokens)


def settle_kernel(slabs, count, here_ref, own_ref, above_ref, *refs):
    in_refs, (base_ref, out_ref, wide) = refs[:G], refs[-3:]
    step = pl.program_id(0)
    cols = out_ref.shape[2]
    place = lax.rem(here_ref[0], G)
    last = here_ref[0] == slabs - 1

    @pl.when(last)
    def _():
        pltpu.sync_copy(base_ref.at[:, :, pl.ds(pl.multiple_of(step * cols, cols), cols)], out_ref)

    @pl.when(jnp.logical_not(last) & (step < count) & (place == G - 1))
    def _():
        out_ref[...] = above_ref[...]

    @pl.when(jnp.logical_not(last) & (step < count) & (place != G - 1))
    def _():
        out_ref[...] = own_ref[...]

    @pl.when(jnp.logical_not(last) & (step >= count))
    def _():
        for j in range(cols // LANES):
            out_ref[:, :, j * LANES : (j + 1) * LANES] = natural(place, in_refs, wide, j).astype(BF16)


def settle(here, slabs, own, above, pieces, base, *tokens):
    depth, rows, cols = base.shape
    _, count = chunk_tiles(0, cols)
    block = (depth, rows, TILE)
    early = pl.BlockSpec(block, lambda i: (0, 0, jnp.minimum(i, count - 1)))
    late = [
        pl.BlockSpec((depth, ROWS * TILE), lambda i, at=at: (at, jnp.maximum(i - count, 0))) for _, at in pieces
    ]
    return call(
        functools.partial(settle_kernel, slabs, count),
        0,
        grid=(CHUNKS * count,),
        in_specs=[SMEM, early, early] + late + [ANY] * (len(tokens) + 1),
        out_specs=pl.BlockSpec(block, lambda i: (0, 0, i)),
        results=pltpu.HBM(base.shape, BF16),
        scratch_shapes=[wide_tile(depth * rows)],
    )(here, own, above, *arrays_of(pieces), *tokens, far(base))


def finish_kernel(here_ref, tv_ref, *refs):
    in_refs, (out_ref, wide) = refs[:G], refs[-2:]
    for j in range(out_ref.shape[2] // LANES):
        at = pl.ds(j * LANES, LANES)
        out_ref[:, :, at] = tv_ref[:, :, at] + natural(lax.rem(here_ref[0], G), in_refs, wide, j)


def finish(here, chunk, tv, pieces, *tokens):
    depth, rows, cols = tv.shape
    first, count = chunk_tiles(chunk, cols)
    part = pl.BlockSpec((depth, rows, TILE), lambda i: (0, 0, first + i))
    return call(
        finish_kernel,
        0,
        grid=(count,),
        in_specs=[SMEM, part] + piece_specs(pieces, depth, ROWS * TILE) + [ANY] * len(tokens),
        out_specs=part,
        results=pltpu.HBM(tv.shape, F32),
        input_output_aliases={1: 0},
        scratch_shapes=[wide_tile(depth * rows)],
    )(here, far(tv), *arrays_of(pieces), *tokens)


def band_kernel(slabs, span, here_ref, cover_ref, offset_ref, w_ref, *refs):
    proj_ref, back_ref, turned = refs[-3:]
    side = w_ref.shape[1]
    place = lax.rem(here_ref[0], G)
    first = here_ref[0] - place
    zero = jnp.zeros((side, side), BF16)
    for i in range(w_ref.shape[0]):
        turned[i] = w_ref[i].astype(F32).T.astype(BF16)

    def block(ref, i, j):
        k = j - i
        known, step = jnp.clip(i, 0, slabs - 1), jnp.clip(k, 0, span - 1)
        inside = (i >= 0) & (i < slabs) & (j >= 0) & (j < slabs) & (k >= 0) & (k < span)
        live = inside & (cover_ref[known, step] == 1)
        return jnp.where(live, ref[offset_ref[known, step]], zero)

    def slab(m):
        return first + jnp.bitwise_xor(place, m)

    def group(m):
        to = jnp.bitwise_xor(place, m)
        return first + jnp.where(to == G - 1, -1, to)

    seen = [slab(m) for m in range(G)] + [slab(m) + G for m in range(G)] + [first - 1]
    seeing = [group(m) for m in range(G)] + [group(m) - G for m in range(G)] + [first + G - 1]
    for r in range(G):
        for s in range(2 * G + 1):
            at = (pl.ds(r * side, side), pl.ds(s * side, side))
            proj_ref[at] = block(w_ref, group(r), seen[s])
            back_ref[at] = block(turned, seeing[s], slab(r))


def bands(here, coverage, offsets, weights, *tokens):
    slabs, span = coverage.shape
    side = weights.shape[1]
    shape = (G * side, (2 * G + 1) * side)
    return call(
        functools.partial(band_kernel, slabs, span),
        9,
        in_specs=[SMEM, SMEM, SMEM, pl.BlockSpec(weights.shape, lambda i: (0, 0, 0))] + [ANY] * len(tokens),
        grid=(1,),
        out_specs=[pl.BlockSpec(shape, lambda i: (0, 0))] * 2,
        results=[pltpu.HBM(shape, BF16)] * 2,
        scratch_shapes=[pltpu.VMEM(weights.shape, BF16)],
    )(here, coverage, offsets, weights, *tokens)


def project_kernel(groups, here_ref, band_ref, own_ref, high_ref, low_ref, *refs):
    sino_refs, (r_ref, down_ref, *group_refs) = refs[:G], refs[-len(groups) - 2 :]
    side = sino_refs[0].shape[0]
    seen = jnp.concatenate([own_ref[...], high_ref[...], low_ref[...]], axis=0)
    total = jnp.dot(band_ref[...], seen, preferred_element_type=F32)
    resid = [(total[m * side : (m + 1) * side] - ref[...].astype(F32)).astype(BF16) for m, ref in enumerate(sino_refs)]
    for m in range(G):
        r_ref[m * side : (m + 1) * side] = resid[m]
    for group, group_ref in zip(groups, group_refs):
        for n, m in enumerate(group):
            group_ref[n * side : (n + 1) * side] = resid[m]
    down_ref[...] = last_block(here_ref, resid)


def project(here, band, own, high, low, sinos, groups, *tokens):
    n, side = band.shape[0], band.shape[0] // G
    cols = own.shape[1]
    tile = 512
    many, one = pl.BlockSpec((n, tile), lambda i: (0, i)), pl.BlockSpec((side, tile), lambda i: (0, i))
    shapes = [(n, cols), (side, cols)] + [(len(group) * side, cols) for group in groups]
    return call(
        functools.partial(project_kernel, groups),
        3,
        grid=(cols // tile,),
        in_specs=[SMEM, pl.BlockSpec(band.shape, lambda i: (0, 0)), many, many, one]
        + piece_specs(sinos, side, tile)
        + [ANY] * len(tokens),
        out_specs=[across(shape, tile) for shape in shapes],
        results=[value(shape, BF16) for shape in shapes],
    )(here, far(band), far(own), high, low, *arrays_of(sinos), *tokens)


def back_kernel(dealing, here_ref, band_ref, own_ref, low_ref, high_ref, *refs):
    out_refs = refs[-G:]
    side = high_ref.shape[0]
    seeing = jnp.concatenate([own_ref[...], low_ref[...], high_ref[...]], axis=0)
    total = jnp.dot(band_ref[...], seeing, preferred_element_type=F32)
    place = lax.rem(here_ref[0], G)
    for m, out_ref in enumerate(out_refs):
        out_ref[:side] = total[m * side : (m + 1) * side].astype(BF16)
        if dealing:
            last = jnp.bitwise_xor(place, m) == G - 1
            out_ref[side:] = jnp.where(last, refs[1][...], refs[0][m * side : (m + 1) * side])


def back(here, band, own, low, high, dealt, *tokens):
    n, side = band.shape[0], band.shape[0] // G
    cols = own.shape[1]
    tile = 512
    many = pl.BlockSpec((n, tile), lambda i: (0, i))
    one = pl.BlockSpec((side, tile), lambda i: (0, i))
    out = ((2 if dealt else 1) * side, cols)
    return call(
        functools.partial(back_kernel, bool(dealt)),
        0,
        grid=(cols // tile,),
        in_specs=[SMEM, pl.BlockSpec(band.shape, lambda i: (0, 0)), many, many, one]
        + ([many, one] if dealt else [])
        + [ANY] * len(tokens),
        out_specs=[across(out, tile)] * G,
        results=[value(out, BF16)] * G,
    )(here, far(band), own, low, high, *dealt, *tokens)


def tv_flux(cur, above):
    rows, cols = cur.shape
    row = lax.broadcasted_iota(jnp.int32, (rows, cols), 0)
    col = lax.broadcasted_iota(jnp.int32, (rows, cols), 1)
    dz = above - cur
    dy = jnp.where(row == rows - 1, 0.0, pltpu.roll(cur, rows - 1, 0)) - cur
    dx = jnp.where(col == cols - 1, 0.0, pltpu.roll(cur, cols - 1, 1)) - cur
    scale = 0.5 * lax.rsqrt(dz * dz + dy * dy + dx * dx + 0.25)
    return dz * scale, dy * scale, dx * scale


def tv_below(cur, above):
    return tv_flux(cur, above)[0]


def tv_slice(cur, above, below_flux):
    rows, cols = cur.shape
    row = lax.broadcasted_iota(jnp.int32, (rows, cols), 0)
    col = lax.broadcasted_iota(jnp.int32, (rows, cols), 1)
    fz, fy, fx = tv_flux(cur, above)
    sides = 0.5 * cur * lax.rsqrt(cur * cur + 0.25)
    fy_low = jnp.where(row == 0, sides, pltpu.roll(fy, 1, 0))
    fx_low = jnp.where(col == 0, sides, pltpu.roll(fx, 1, 1))
    return (below_flux - fz) + (fy_low - fy) + (fx_low - fx), fz


def tv_kernel(here_ref, near_ref, next_level_ref, far_ref, last_level_ref, next_ref, vol_ref, *refs):
    out_ref, done_ref, flux_ref = refs[-3:]
    step = pl.program_id(0)
    deep, rows, _ = vol_ref.shape
    place = lax.rem(here_ref[0], G)

    @pl.when(step == 0)
    def _():
        inside = jnp.where(place == 2, far_ref[...], near_ref[...])
        low = jnp.where(place == 0, last_level_ref[...], inside)[rows:].astype(F32)
        flux_ref[...] = tv_below(low, vol_ref[0])

    def body(z, flux):
        out_ref[z], flux = tv_slice(vol_ref[z], vol_ref[z + 1], flux)
        return flux

    flux = lax.fori_loop(0, deep - 1, body, flux_ref[...], unroll=5)
    inside = jnp.where(place == 1, far_ref[...], near_ref[...])
    high = jnp.where(place == G - 1, next_level_ref[...], inside)[:rows].astype(F32)
    above = jnp.where(step == pl.num_programs(0) - 1, high, next_ref[0])
    out_ref[deep - 1], flux_ref[...] = tv_slice(vol_ref[deep - 1], above, flux)
    done_ref[...] = flux_ref[:, : done_ref.shape[1]]


def half_tv(here, volume, ends, *tokens):
    depth, rows, cols = volume.shape
    deep = 16
    edges = [pl.BlockSpec((2 * rows, cols), lambda i, last=end.shape[0] // (2 * rows) - 1: (last, 0)) for end in ends]
    body = pl.BlockSpec((deep, rows, cols), lambda i: (i, 0, 0))
    after = pl.BlockSpec((1, rows, cols), lambda i: (jnp.minimum((i + 1) * deep, depth - 1), 0, 0))
    return call(
        tv_kernel,
        0,
        grid=(depth // deep,),
        in_specs=[SMEM] + edges + [after, body] + [ANY] * len(tokens),
        out_specs=[body, pl.BlockSpec((rows, LANES), lambda i: (0, 0))],
        results=[pltpu.HBM(volume.shape, F32), value((rows, LANES), F32)],
        scratch_shapes=[pltpu.VMEM((rows, cols), F32)],
    )(here, *ends, far(volume), far(volume), *tokens)


def local(volume, sinogram, weights, coverage, offsets):
    slabs = lax.axis_size("slab")
    here = lax.axis_index("slab").astype(jnp.int32).reshape(1)
    depth, rows, _ = volume.shape
    single = ((0,), (1,), (2,), (3,))
    paired = ((0,), (1,), (2, 3))

    def tied(array, *others):
        return lax.optimization_barrier((array, *others))[0]

    def beyond(over, *others):
        return swapped(tied(over, *others)[depth:], 1)

    vols0 = cast_rows(here, volume, 0, single, True)
    got = moved(tied(sinogram, vols0[0]), G, only=G - 1)
    got_vols0 = direct(vols0)
    v0, v1, v23 = cast_rows(here, volume, 1, paired, False, vols0[1])
    over = swapped(v23, 2)
    band_p, band_b = bands(here, coverage, offsets, weights, v1)
    own0, edge0 = pack(here, [(array, 0) for array in got_vols0], 2 * rows, far(band_p))
    high0, near = moved(own0, -G), swapped(tied(v1, own0), 1)
    s0, s1, s23, over_beyond = split_rows(here, sinogram, got, 0, paired, [(over, 1)], near)
    s_near, s_over = swapped(s1, 1), swapped(s23, 2)
    low0 = moved(tied(edge0, s_near), G)
    own1, edge1 = pack(here, [(v0, 0), (near, 0), (over, 0), (swapped(over_beyond, 1), 0)], 0)
    low1, high1 = moved(edge1, G), moved(own1, -G)
    sinos0 = [(s0, 0), (s_near, 0), (s_over, 0), (beyond(s_over, own1), 0)]

    s0, s1, s23 = split_rows(here, sinogram, got, 1, paired, [], far(own1))

    resid0, down0, r1, r23 = project(here, band_p, own0, high0, low0, sinos0, paired[1:], low1, s0)
    from_low0, from_high0 = moved(resid0, G), moved(down0, -G)
    s_near, s_over = swapped(s1, 1), swapped(s23, 2)
    r_near, r_over = swapped(tied(r1, s_near), 1), swapped(tied(r23, s_near), 2)
    tv, tv_done = half_tv(here, volume, [got_vols0[1], high0, got_vols0[3], low0], resid0)
    sinos1 = [(s0, 0), (s_near, 0), (s_over, 0), (beyond(s_over, tv_done), 0)]
    resid1, down1 = project(here, band_p, own1, high1, low1, sinos1, (), tv_done, r_near, r_over)
    from_low1, from_high1 = moved(resid1, G), moved(down1, -G)

    backs0 = back(here, band_b, resid0, from_low0, from_high0, [resid1, from_high1])
    got_backs0 = direct(backs0)
    r_pieces = [(resid0, 0), (r_near, 0), (r_over, 0), (beyond(r_over, resid1), 0)]
    natural0 = join_rows(here, r_pieces, sinogram.shape, backs0[0])
    above0 = moved(natural0, -G, only=G - 1)
    r_last, tv = last_group(here, coverage, offsets, weights, volume, sinogram, tv, backs0[0])
    backs1 = back(here, band_b, resid1, from_low1, from_high1, [], far(r_last), natural0)
    got_backs1 = direct(backs1)
    gradient = finish(here, 0, tv, [(array, 0) for array in got_backs0], backs1[0])
    residual = settle(here, slabs, natural0, above0, [(array, 1) for array in got_backs0], r_last, backs1[0])
    gradient = finish(here, 1, gradient, [(array, 0) for array in got_backs1], far(residual))
    return (gradient, residual)


def solution(mesh):
    placed = (P("slab", "grp", None), P("slab", "grp", None), P(), P(), P())
    return jax.shard_map(
        local,
        mesh=mesh,
        in_specs=placed,
        out_specs=(P("slab", "grp", None), P("slab", "grp", None)),
        check_vma=False,
    )
```

```python
import functools

import jax
import jax.numpy as jnp
from jax import lax
from jax.experimental import pallas as pl
from jax.experimental.pallas import tpu as pltpu
from jax.sharding import PartitionSpec as P

G = 4
CHUNKS = 2
ROWS = 2
TILE = 256
F32 = jnp.float32
BF16 = jnp.bfloat16
MIB = 1024 * 1024
LANES = 128
SMEM = pl.BlockSpec(memory_space=pltpu.SMEM)
VMEM = pl.BlockSpec(memory_space=pltpu.VMEM)
ANY = pl.BlockSpec(memory_space=pl.ANY)


def moved(value, steps, only=None):
    count = lax.axis_size("slab")
    first, last = max(0, -steps), min(count, count - steps)
    pairs = [(i, i + steps) for i in range(first, last) if only is None or i % G == only]
    return lax.ppermute(value, "slab", pairs)


def swapped(value, bits):
    count = lax.axis_size("slab")
    return lax.ppermute(value, "slab", [(i, i ^ bits) for i in range(count)])


def direct(arrays):
    return [array if m == 0 else swapped(array, m) for m, array in enumerate(arrays)]


def call(kernel, us, *, results, vmem=16, **how):
    return pl.pallas_call(
        kernel,
        out_shape=results,
        compiler_params=pltpu.CompilerParams(vmem_limit_bytes=vmem * MIB),
        cost_estimate=pl.CostEstimate(flops=int(us * 1.15e9), bytes_accessed=1000, transcendentals=0),
        **how,
    )


def value(shape, dtype):
    return jax.ShapeDtypeStruct(shape, dtype)


def far(array):
    return pltpu.with_memory_space_constraint(array, pltpu.HBM)


def across(shape, tile):
    block = shape[:-1] + (tile,)
    return pl.BlockSpec(block, lambda i: (0,) * (len(shape) - 1) + (i,))


def piece_specs(pieces, side, tile):
    return [pl.BlockSpec((side, tile), lambda i, at=at: (at, i)) for _, at in pieces]


def arrays_of(pieces):
    return [array for array, _ in pieces]


def rows_of(place, m):
    first = ROWS * jnp.bitwise_xor(place, m)
    return [(h * TILE, first + h) for h in range(ROWS)]


def wide_tile(rows_deep):
    return pltpu.VMEM((TILE // LANES, rows_deep, LANES), F32)


def chunk_tiles(chunk, cols):
    count = cols // CHUNKS // TILE
    return chunk * count, count


def cast_kernel(groups, ends, here_ref, *refs):
    parts = TILE // LANES
    vol_refs, end_refs, out_refs = refs[:parts], refs[parts : parts + ends], refs[-len(groups) :]
    rows = ROWS * G
    depth = vol_refs[0].shape[0] // rows
    place = lax.rem(here_ref[0], G)
    for j, vol_ref in enumerate(vol_refs):
        for group, out_ref in zip(groups, out_refs):
            for n, m in enumerate(group):
                for start, row in rows_of(place, m):
                    at = pl.ds(start + j * LANES, LANES)
                    out_ref[n * depth : (n + 1) * depth, at] = vol_ref[pl.ds(row, depth, stride=rows), :].astype(BF16)
    if ends:
        both = jnp.concatenate([ref[...] for ref in end_refs], axis=0).astype(BF16)
        for group, out_ref in zip(groups, out_refs):
            if group[0] % 2:
                out_ref[depth:, :] = both


def cast_rows(here, volume, chunk, groups, ends, *tokens):
    depth, rows, cols = volume.shape
    flat = far(volume.reshape(depth * rows, cols))
    first, count = chunk_tiles(chunk, cols)
    parts, width = TILE // LANES, ROWS * TILE
    shapes = [(len(group) * depth + (2 * rows if ends and group[0] % 2 else 0), cols) for group in groups]
    edges = [pl.BlockSpec((rows, width), lambda i, z=z: (z, i)) for z in (0, depth - 1)] if ends else []
    return call(
        functools.partial(cast_kernel, groups, len(edges)),
        2,
        grid=(count,),
        in_specs=[SMEM]
        + [pl.BlockSpec((depth * rows, LANES), lambda i, j=j: (0, (first + i) * parts + j)) for j in range(parts)]
        + edges
        + [ANY] * len(tokens),
        out_specs=[across(shape, width) for shape in shapes],
        results=[(pltpu.HBM if group[0] == 0 else value)(shape, BF16) for group, shape in zip(groups, shapes)],
    )(here, *[flat] * (parts + len(edges)), *tokens)


def last_block(here_ref, blocks):
    spot = jnp.bitwise_xor(lax.rem(here_ref[0], G), G - 1)
    last = blocks[0]
    for m in range(1, G):
        last = jnp.where(spot == m, blocks[m], last)
    return last


def pack_kernel(here_ref, *refs):
    in_refs, (all_ref, last_ref) = refs[:G], refs[-2:]
    side = in_refs[0].shape[0]
    for m in range(G):
        all_ref[m * side : (m + 1) * side] = in_refs[m][:side]
    last_ref[:side] = last_block(here_ref, [ref[:side] for ref in in_refs])
    if last_ref.shape[0] > side:
        all_ref[G * side :] = in_refs[G - 1][side:]
        last_ref[side:] = in_refs[G - 1][side:]


def pack(here, pieces, more, *tokens):
    side, cols = pieces[0][0].shape
    tile = 512
    shapes = [(G * side + more, cols), (side + more, cols)]
    specs = [across(array.shape, tile) for array in arrays_of(pieces)] if more else piece_specs(pieces, side, tile)
    return call(
        pack_kernel,
        1,
        grid=(cols // tile,),
        in_specs=[SMEM] + specs + [ANY] * len(tokens),
        out_specs=[across(shape, tile) for shape in shapes],
        results=[value(shape, BF16) for shape in shapes],
    )(here, *arrays_of(pieces), *tokens)


def split_kernel(groups, passing, here_ref, own_ref, got_ref, *refs):
    out_refs, wide = refs[-len(groups) - passing - 1 : -1], refs[-1]
    if passing:
        out_refs[-1][...] = refs[0][...]
    depth, rows, cols = own_ref.shape
    place = lax.rem(here_ref[0], G)

    def fill(ref):
        for j in range(cols // LANES):
            wide[j] = ref[:, :, j * LANES : (j + 1) * LANES].astype(F32).reshape(wide.shape[1:])

    @pl.when(place == G - 1)
    def _():
        fill(got_ref)

    @pl.when(place != G - 1)
    def _():
        fill(own_ref)

    for group, out_ref in zip(groups, out_refs):
        for n, m in enumerate(group):
            for j in range(cols // LANES):
                for start, row in rows_of(place, m):
                    block = wide.at[j][pl.ds(row, depth, stride=rows), :].astype(BF16)
                    out_ref[n * depth : (n + 1) * depth, start + j * LANES : start + (j + 1) * LANES] = block


def split_rows(here, own, got, chunk, groups, passing, *tokens):
    depth, rows, cols = own.shape
    first, count = chunk_tiles(chunk, cols)
    block = pl.BlockSpec((depth, rows, TILE), lambda i: (0, 0, first + i))
    shapes = [(len(group) * depth, cols) for group in groups] + [(depth, cols)] * len(passing)
    return call(
        functools.partial(split_kernel, groups, len(passing)),
        2,
        grid=(count,),
        in_specs=[SMEM, block, block] + piece_specs(passing, depth, ROWS * TILE) + [ANY] * len(tokens),
        out_specs=[across(shape, ROWS * TILE) for shape in shapes],
        results=[value(shape, BF16) for shape in shapes],
        scratch_shapes=[wide_tile(depth * rows)],
    )(here, far(own), got, *arrays_of(passing), *tokens)


def last_kernel(slabs, here_ref, cover_ref, offset_ref, *refs):
    w_ref, vol_ref, sino_ref, *refs = refs
    r_ref, tv_ref, vol, s, r, wide, tv, sem = refs[-8:]
    depth, rows, cols = sino_ref.shape

    count = cols // LANES

    def columns(j):
        return pl.ds(pl.multiple_of(j * LANES, LANES), LANES)

    def arrival(n, j):
        src, dst = ((vol_ref, vol), (sino_ref, s), (tv_ref, tv))[n]
        return pltpu.make_async_copy(src.at[:, :, columns(j)], dst.at[:, :, columns(j)], sem.at[n, j])

    def departure(n, j):
        src, dst = ((r, r_ref), (tv, tv_ref))[n]
        return pltpu.make_async_copy(src.at[:, :, columns(j)], dst.at[:, :, columns(j)], sem.at[3 + n, j])

    @pl.when(here_ref[0] == slabs - 1)
    def _():
        for j in range(count):
            for n in range(3):
                arrival(n, j).start()
        block = w_ref[offset_ref[slabs - 1, 0]]
        block = jnp.where(cover_ref[slabs - 1, 0] == 1, block, jnp.zeros_like(block))
        turned = block.astype(F32).T.astype(BF16)

        def column(j, _):
            at = columns(j)
            for n in range(3):
                arrival(n, j).wait()
            for n, ref in enumerate((s, tv, vol)):
                wide[n] = ref[:, :, at].astype(F32).reshape(wide.shape[1:])
            for row in range(rows):
                spot = pl.ds(row, depth, stride=rows)
                seen = jnp.dot(block, wide.at[2][spot, :].astype(BF16), preferred_element_type=F32)
                resid = (seen - wide.at[0][spot, :]).astype(BF16)
                wide.at[0][spot, :] = resid.astype(F32)
                wide.at[1][spot, :] += jnp.dot(turned, resid, preferred_element_type=F32)
            r[:, :, at] = wide[0].reshape(depth, rows, LANES).astype(BF16)
            tv[:, :, at] = wide[1].reshape(depth, rows, LANES)
            for n in range(2):
                departure(n, j).start()
            return 0

        lax.fori_loop(0, count, column, 0)
        for j in range(count):
            for n in range(2):
                departure(n, j).wait()


def last_group(here, coverage, offsets, weights, volume, sinogram, tv, *tokens):
    slabs = coverage.shape[0]
    depth, rows, cols = sinogram.shape
    return call(
        functools.partial(last_kernel, slabs),
        0,
        vmem=32,
        grid=(1,),
        in_specs=[SMEM, SMEM, SMEM, pl.BlockSpec(weights.shape, lambda i: (0, 0, 0))] + [ANY] * (3 + len(tokens)),
        out_specs=[ANY, ANY],
        results=[pltpu.HBM(sinogram.shape, BF16), pltpu.HBM(volume.shape, F32)],
        input_output_aliases={6: 1},
        scratch_shapes=[
            pltpu.VMEM(volume.shape, F32),
            pltpu.VMEM(sinogram.shape, BF16),
            pltpu.VMEM(sinogram.shape, BF16),
            pltpu.VMEM((3, depth * rows, LANES), F32),
            pltpu.VMEM(volume.shape, F32),
            pltpu.SemaphoreType.DMA((5, cols // LANES)),
        ],
    )(here, coverage, offsets, weights, far(volume), far(sinogram), far(tv), *tokens)


def natural(place, in_refs, wide, j):
    depth = in_refs[0].shape[0]
    rows = ROWS * len(in_refs)
    for m, ref in enumerate(in_refs):
        for start, row in rows_of(place, m):
            value = ref[:, start + j * LANES : start + (j + 1) * LANES].astype(F32)
            wide.at[j][pl.ds(row, depth, stride=rows), :] = value
    return wide[j].reshape(depth, rows, LANES)


def join_kernel(here_ref, *refs):
    in_refs, (out_ref, wide) = refs[:G], refs[-2:]
    for j in range(out_ref.shape[2] // LANES):
        out_ref[:, :, j * LANES : (j + 1) * LANES] = natural(lax.rem(here_ref[0], G), in_refs, wide, j).astype(BF16)


def join_rows(here, pieces, shape, *tokens):
    depth, rows, cols = shape
    _, count = chunk_tiles(0, cols)
    return call(
        join_kernel,
        0,
        grid=(count,),
        in_specs=[SMEM] + piece_specs(pieces, depth, ROWS * TILE) + [ANY] * len(tokens),
        out_specs=pl.BlockSpec((depth, rows, TILE), lambda i: (0, 0, i)),
        results=value((depth, rows, cols // CHUNKS), BF16),
        scratch_shapes=[wide_tile(depth * rows)],
    )(here, *arrays_of(pieces), *tokens)


def settle_kernel(slabs, count, here_ref, own_ref, above_ref, *refs):
    in_refs, (base_ref, out_ref, wide) = refs[:G], refs[-3:]
    step = pl.program_id(0)
    cols = out_ref.shape[2]
    place = lax.rem(here_ref[0], G)
    last = here_ref[0] == slabs - 1

    @pl.when(last)
    def _():
        pltpu.sync_copy(base_ref.at[:, :, pl.ds(pl.multiple_of(step * cols, cols), cols)], out_ref)

    @pl.when(jnp.logical_not(last) & (step < count) & (place == G - 1))
    def _():
        out_ref[...] = above_ref[...]

    @pl.when(jnp.logical_not(last) & (step < count) & (place != G - 1))
    def _():
        out_ref[...] = own_ref[...]

    @pl.when(jnp.logical_not(last) & (step >= count))
    def _():
        for j in range(cols // LANES):
            out_ref[:, :, j * LANES : (j + 1) * LANES] = natural(place, in_refs, wide, j).astype(BF16)


def settle(here, slabs, own, above, pieces, base, *tokens):
    depth, rows, cols = base.shape
    _, count = chunk_tiles(0, cols)
    block = (depth, rows, TILE)
    early = pl.BlockSpec(block, lambda i: (0, 0, jnp.minimum(i, count - 1)))
    late = [
        pl.BlockSpec((depth, ROWS * TILE), lambda i, at=at: (at, jnp.maximum(i - count, 0))) for _, at in pieces
    ]
    return call(
        functools.partial(settle_kernel, slabs, count),
        0,
        grid=(CHUNKS * count,),
        in_specs=[SMEM, early, early] + late + [ANY] * (len(tokens) + 1),
        out_specs=pl.BlockSpec(block, lambda i: (0, 0, i)),
        results=pltpu.HBM(base.shape, BF16),
        scratch_shapes=[wide_tile(depth * rows)],
    )(here, own, above, *arrays_of(pieces), *tokens, far(base))


def finish_kernel(here_ref, tv_ref, *refs):
    in_refs, (out_ref, wide) = refs[:G], refs[-2:]
    for j in range(out_ref.shape[2] // LANES):
        at = pl.ds(j * LANES, LANES)
        out_ref[:, :, at] = tv_ref[:, :, at] + natural(lax.rem(here_ref[0], G), in_refs, wide, j)


def finish(here, chunk, tv, pieces, *tokens):
    depth, rows, cols = tv.shape
    first, count = chunk_tiles(chunk, cols)
    part = pl.BlockSpec((depth, rows, TILE), lambda i: (0, 0, first + i))
    return call(
        finish_kernel,
        0,
        grid=(count,),
        in_specs=[SMEM, part] + piece_specs(pieces, depth, ROWS * TILE) + [ANY] * len(tokens),
        out_specs=part,
        results=pltpu.HBM(tv.shape, F32),
        input_output_aliases={1: 0},
        scratch_shapes=[wide_tile(depth * rows)],
    )(here, far(tv), *arrays_of(pieces), *tokens)


def band_kernel(slabs, span, here_ref, cover_ref, offset_ref, w_ref, *refs):
    proj_ref, back_ref, turned = refs[-3:]
    side = w_ref.shape[1]
    place = lax.rem(here_ref[0], G)
    first = here_ref[0] - place
    zero = jnp.zeros((side, side), BF16)
    for i in range(w_ref.shape[0]):
        turned[i] = w_ref[i].astype(F32).T.astype(BF16)

    def block(ref, i, j):
        k = j - i
        known, step = jnp.clip(i, 0, slabs - 1), jnp.clip(k, 0, span - 1)
        inside = (i >= 0) & (i < slabs) & (j >= 0) & (j < slabs) & (k >= 0) & (k < span)
        live = inside & (cover_ref[known, step] == 1)
        return jnp.where(live, ref[offset_ref[known, step]], zero)

    def slab(m):
        return first + jnp.bitwise_xor(place, m)

    def group(m):
        to = jnp.bitwise_xor(place, m)
        return first + jnp.where(to == G - 1, -1, to)

    seen = [slab(m) for m in range(G)] + [slab(m) + G for m in range(G)] + [first - 1]
    seeing = [group(m) for m in range(G)] + [group(m) - G for m in range(G)] + [first + G - 1]
    for r in range(G):
        for s in range(2 * G + 1):
            at = (pl.ds(r * side, side), pl.ds(s * side, side))
            proj_ref[at] = block(w_ref, group(r), seen[s])
            back_ref[at] = block(turned, seeing[s], slab(r))


def bands(here, coverage, offsets, weights, *tokens):
    slabs, span = coverage.shape
    side = weights.shape[1]
    shape = (G * side, (2 * G + 1) * side)
    return call(
        functools.partial(band_kernel, slabs, span),
        9,
        in_specs=[SMEM, SMEM, SMEM, pl.BlockSpec(weights.shape, lambda i: (0, 0, 0))] + [ANY] * len(tokens),
        grid=(1,),
        out_specs=[pl.BlockSpec(shape, lambda i: (0, 0))] * 2,
        results=[value(shape, BF16)] * 2,
        scratch_shapes=[pltpu.VMEM(weights.shape, BF16)],
    )(here, coverage, offsets, weights, *tokens)


def project_kernel(groups, here_ref, band_ref, own_ref, high_ref, low_ref, *refs):
    sino_refs, (r_ref, down_ref, *group_refs) = refs[:G], refs[-len(groups) - 2 :]
    side = sino_refs[0].shape[0]
    seen = jnp.concatenate([own_ref[...], high_ref[...], low_ref[...]], axis=0)
    total = jnp.dot(band_ref[...], seen, preferred_element_type=F32)
    resid = [(total[m * side : (m + 1) * side] - ref[...].astype(F32)).astype(BF16) for m, ref in enumerate(sino_refs)]
    for m in range(G):
        r_ref[m * side : (m + 1) * side] = resid[m]
    for group, group_ref in zip(groups, group_refs):
        for n, m in enumerate(group):
            group_ref[n * side : (n + 1) * side] = resid[m]
    down_ref[...] = last_block(here_ref, resid)


def project(here, band, own, high, low, sinos, groups, *tokens):
    n, side = band.shape[0], band.shape[0] // G
    cols = own.shape[1]
    tile = 512
    many, one = pl.BlockSpec((n, tile), lambda i: (0, i)), pl.BlockSpec((side, tile), lambda i: (0, i))
    shapes = [(n, cols), (side, cols)] + [(len(group) * side, cols) for group in groups]
    return call(
        functools.partial(project_kernel, groups),
        3,
        grid=(cols // tile,),
        in_specs=[SMEM, pl.BlockSpec(band.shape, lambda i: (0, 0)), many, many, one]
        + piece_specs(sinos, side, tile)
        + [ANY] * len(tokens),
        out_specs=[across(shape, tile) for shape in shapes],
        results=[value(shape, BF16) for shape in shapes],
    )(here, band, own, high, low, *arrays_of(sinos), *tokens)


def back_kernel(dealing, here_ref, band_ref, own_ref, low_ref, high_ref, *refs):
    out_refs = refs[-G:]
    side = high_ref.shape[0]
    seeing = jnp.concatenate([own_ref[...], low_ref[...], high_ref[...]], axis=0)
    total = jnp.dot(band_ref[...], seeing, preferred_element_type=F32)
    place = lax.rem(here_ref[0], G)
    for m, out_ref in enumerate(out_refs):
        out_ref[:side] = total[m * side : (m + 1) * side].astype(BF16)
        if dealing:
            last = jnp.bitwise_xor(place, m) == G - 1
            out_ref[side:] = jnp.where(last, refs[1][...], refs[0][m * side : (m + 1) * side])


def back(here, band, own, low, high, dealt, *tokens):
    n, side = band.shape[0], band.shape[0] // G
    cols = own.shape[1]
    tile = 512
    many = pl.BlockSpec((n, tile), lambda i: (0, i))
    one = pl.BlockSpec((side, tile), lambda i: (0, i))
    out = ((2 if dealt else 1) * side, cols)
    return call(
        functools.partial(back_kernel, bool(dealt)),
        0,
        grid=(cols // tile,),
        in_specs=[SMEM, pl.BlockSpec(band.shape, lambda i: (0, 0)), many, many, one]
        + ([many, one] if dealt else [])
        + [ANY] * len(tokens),
        out_specs=[across(out, tile)] * G,
        results=[value(out, BF16)] * G,
    )(here, band, own, low, high, *dealt, *tokens)


def tv_flux(cur, above):
    rows, cols = cur.shape
    row = lax.broadcasted_iota(jnp.int32, (rows, cols), 0)
    col = lax.broadcasted_iota(jnp.int32, (rows, cols), 1)
    dz = above - cur
    dy = jnp.where(row == rows - 1, 0.0, pltpu.roll(cur, rows - 1, 0)) - cur
    dx = jnp.where(col == cols - 1, 0.0, pltpu.roll(cur, cols - 1, 1)) - cur
    scale = 0.5 * lax.rsqrt(dz * dz + dy * dy + dx * dx + 0.25)
    return dz * scale, dy * scale, dx * scale


def tv_below(cur, above):
    return tv_flux(cur, above)[0]


def tv_slice(cur, above, below_flux):
    rows, cols = cur.shape
    row = lax.broadcasted_iota(jnp.int32, (rows, cols), 0)
    col = lax.broadcasted_iota(jnp.int32, (rows, cols), 1)
    fz, fy, fx = tv_flux(cur, above)
    sides = 0.5 * cur * lax.rsqrt(cur * cur + 0.25)
    fy_low = jnp.where(row == 0, sides, pltpu.roll(fy, 1, 0))
    fx_low = jnp.where(col == 0, sides, pltpu.roll(fx, 1, 1))
    return (below_flux - fz) + (fy_low - fy) + (fx_low - fx), fz


def tv_kernel(here_ref, near_ref, next_level_ref, far_ref, last_level_ref, next_ref, vol_ref, *refs):
    out_ref, done_ref, flux_ref = refs[-3:]
    step = pl.program_id(0)
    deep, rows, _ = vol_ref.shape
    place = lax.rem(here_ref[0], G)

    @pl.when(step == 0)
    def _():
        inside = jnp.where(place == 2, far_ref[...], near_ref[...])
        low = jnp.where(place == 0, last_level_ref[...], inside)[rows:].astype(F32)
        flux_ref[...] = tv_below(low, vol_ref[0])

    def body(z, flux):
        out_ref[z], flux = tv_slice(vol_ref[z], vol_ref[z + 1], flux)
        return flux

    flux = lax.fori_loop(0, deep - 1, body, flux_ref[...], unroll=5)
    inside = jnp.where(place == 1, far_ref[...], near_ref[...])
    high = jnp.where(place == G - 1, next_level_ref[...], inside)[:rows].astype(F32)
    above = jnp.where(step == pl.num_programs(0) - 1, high, next_ref[0])
    out_ref[deep - 1], flux_ref[...] = tv_slice(vol_ref[deep - 1], above, flux)
    done_ref[...] = flux_ref[:, : done_ref.shape[1]]


def half_tv(here, volume, ends, *tokens):
    depth, rows, cols = volume.shape
    deep = 16
    edges = [pl.BlockSpec((2 * rows, cols), lambda i, last=end.shape[0] // (2 * rows) - 1: (last, 0)) for end in ends]
    body = pl.BlockSpec((deep, rows, cols), lambda i: (i, 0, 0))
    after = pl.BlockSpec((1, rows, cols), lambda i: (jnp.minimum((i + 1) * deep, depth - 1), 0, 0))
    return call(
        tv_kernel,
        0,
        grid=(depth // deep,),
        in_specs=[SMEM] + edges + [after, body] + [ANY] * len(tokens),
        out_specs=[body, pl.BlockSpec((rows, LANES), lambda i: (0, 0))],
        results=[pltpu.HBM(volume.shape, F32), value((rows, LANES), F32)],
        scratch_shapes=[pltpu.VMEM((rows, cols), F32)],
    )(here, *ends, far(volume), far(volume), *tokens)


def local(volume, sinogram, weights, coverage, offsets):
    slabs = lax.axis_size("slab")
    here = lax.axis_index("slab").astype(jnp.int32).reshape(1)
    depth, rows, _ = volume.shape
    single = ((0,), (1,), (2,), (3,))
    paired = ((0,), (1,), (2, 3))

    def tied(array, *others):
        return lax.optimization_barrier((array, *others))[0]

    def beyond(over, *others):
        return swapped(tied(over, *others)[depth:], 1)

    vols0 = cast_rows(here, volume, 0, single, True)
    got = moved(tied(sinogram, vols0[0]), G, only=G - 1)
    got_vols0 = direct(vols0)
    v0, v1, v23 = cast_rows(here, volume, 1, paired, False, vols0[1])
    over = swapped(v23, 2)
    band_p, band_b = bands(here, coverage, offsets, weights, v1)
    own0, edge0 = pack(here, [(array, 0) for array in got_vols0], 2 * rows, band_p)
    high0, near = moved(own0, -G), swapped(tied(v1, own0), 1)
    s0, s1, s23, over_beyond = split_rows(here, sinogram, got, 0, paired, [(over, 1)], near)
    s_near, s_over = swapped(s1, 1), swapped(s23, 2)
    low0 = moved(tied(edge0, s_near), G)
    own1, edge1 = pack(here, [(v0, 0), (near, 0), (over, 0), (swapped(over_beyond, 1), 0)], 0)
    low1, high1 = moved(edge1, G), moved(own1, -G)
    sinos0 = [(s0, 0), (s_near, 0), (s_over, 0), (beyond(s_over, own1), 0)]

    s0, s1, s23 = split_rows(here, sinogram, got, 1, paired, [], own1)

    resid0, down0, r1, r23 = project(here, band_p, own0, high0, low0, sinos0, paired[1:], low1, s0)
    from_low0, from_high0 = moved(resid0, G), moved(down0, -G)
    s_near, s_over = swapped(s1, 1), swapped(s23, 2)
    r_near, r_over = swapped(tied(r1, s_near), 1), swapped(tied(r23, s_near), 2)
    tv, tv_done = half_tv(here, volume, [got_vols0[1], high0, got_vols0[3], low0], resid0)
    sinos1 = [(s0, 0), (s_near, 0), (s_over, 0), (beyond(s_over, tv_done), 0)]
    resid1, down1 = project(here, band_p, own1, high1, low1, sinos1, (), tv_done, r_near, r_over)
    from_low1, from_high1 = moved(resid1, G), moved(down1, -G)

    backs0 = back(here, band_b, resid0, from_low0, from_high0, [resid1, from_high1])
    got_backs0 = direct(backs0)
    r_pieces = [(resid0, 0), (r_near, 0), (r_over, 0), (beyond(r_over, resid1), 0)]
    natural0 = join_rows(here, r_pieces, sinogram.shape, backs0[0])
    above0 = moved(natural0, -G, only=G - 1)
    r_last, tv = last_group(here, coverage, offsets, weights, volume, sinogram, tv, backs0[0])
    backs1 = back(here, band_b, resid1, from_low1, from_high1, [], far(r_last), natural0)
    got_backs1 = direct(backs1)
    gradient = finish(here, 0, tv, [(array, 0) for array in got_backs0], backs1[0])
    residual = settle(here, slabs, natural0, above0, [(array, 1) for array in got_backs0], r_last, backs1[0])
    gradient = finish(here, 1, gradient, [(array, 0) for array in got_backs1], far(residual))
    return (gradient, residual)


def solution(mesh):
    placed = (P("slab", "grp", None), P("slab", "grp", None), P(), P(), P())
    return jax.shard_map(
        local,
        mesh=mesh,
        in_specs=placed,
        out_specs=(P("slab", "grp", None), P("slab", "grp", None)),
        check_vma=False,
    )
```

```python
import functools

import jax
import jax.numpy as jnp
from jax import lax
from jax.experimental import pallas as pl
from jax.experimental.pallas import tpu as pltpu
from jax.sharding import PartitionSpec as P

G = 4
CHUNKS = 2
ROWS = 2
TILE = 256
F32 = jnp.float32
BF16 = jnp.bfloat16
MIB = 1024 * 1024
LANES = 128
SMEM = pl.BlockSpec(memory_space=pltpu.SMEM)
VMEM = pl.BlockSpec(memory_space=pltpu.VMEM)
ANY = pl.BlockSpec(memory_space=pl.ANY)


def moved(value, steps, only=None):
    count = lax.axis_size("slab")
    first, last = max(0, -steps), min(count, count - steps)
    pairs = [(i, i + steps) for i in range(first, last) if only is None or i % G == only]
    return lax.ppermute(value, "slab", pairs)


def swapped(value, bits):
    count = lax.axis_size("slab")
    return lax.ppermute(value, "slab", [(i, i ^ bits) for i in range(count)])


def direct(arrays):
    return [array if m == 0 else swapped(array, m) for m, array in enumerate(arrays)]


def call(kernel, us, *, results, vmem=16, **how):
    return pl.pallas_call(
        kernel,
        out_shape=results,
        compiler_params=pltpu.CompilerParams(vmem_limit_bytes=vmem * MIB),
        cost_estimate=pl.CostEstimate(flops=int(us * 1.15e9), bytes_accessed=1000, transcendentals=0),
        **how,
    )


def value(shape, dtype):
    return jax.ShapeDtypeStruct(shape, dtype)


def far(array):
    return pltpu.with_memory_space_constraint(array, pltpu.HBM)


def across(shape, tile):
    block = shape[:-1] + (tile,)
    return pl.BlockSpec(block, lambda i: (0,) * (len(shape) - 1) + (i,))


def piece_specs(pieces, side, tile):
    return [pl.BlockSpec((side, tile), lambda i, at=at: (at, i)) for _, at in pieces]


def arrays_of(pieces):
    return [array for array, _ in pieces]


def rows_of(place, m):
    first = ROWS * jnp.bitwise_xor(place, m)
    return [(h * TILE, first + h) for h in range(ROWS)]


def wide_tile(rows_deep):
    return pltpu.VMEM((TILE // LANES, rows_deep, LANES), F32)


def chunk_tiles(chunk, cols):
    count = cols // CHUNKS // TILE
    return chunk * count, count


def cast_kernel(groups, ends, here_ref, *refs):
    parts = TILE // LANES
    vol_refs, end_refs, out_refs = refs[:parts], refs[parts : parts + ends], refs[-len(groups) :]
    rows = ROWS * G
    depth = vol_refs[0].shape[0] // rows
    place = lax.rem(here_ref[0], G)
    for j, vol_ref in enumerate(vol_refs):
        for group, out_ref in zip(groups, out_refs):
            for n, m in enumerate(group):
                for start, row in rows_of(place, m):
                    at = pl.ds(start + j * LANES, LANES)
                    out_ref[n * depth : (n + 1) * depth, at] = vol_ref[pl.ds(row, depth, stride=rows), :].astype(BF16)
    if ends:
        both = jnp.concatenate([ref[...] for ref in end_refs], axis=0).astype(BF16)
        for group, out_ref in zip(groups, out_refs):
            if group[0] % 2:
                out_ref[depth:, :] = both


def cast_rows(here, volume, chunk, groups, ends, *tokens):
    depth, rows, cols = volume.shape
    flat = far(volume.reshape(depth * rows, cols))
    first, count = chunk_tiles(chunk, cols)
    parts, width = TILE // LANES, ROWS * TILE
    shapes = [(len(group) * depth + (2 * rows if ends and group[0] % 2 else 0), cols) for group in groups]
    edges = [pl.BlockSpec((rows, width), lambda i, z=z: (z, i)) for z in (0, depth - 1)] if ends else []
    return call(
        functools.partial(cast_kernel, groups, len(edges)),
        2,
        grid=(count,),
        in_specs=[SMEM]
        + [pl.BlockSpec((depth * rows, LANES), lambda i, j=j: (0, (first + i) * parts + j)) for j in range(parts)]
        + edges
        + [ANY] * len(tokens),
        out_specs=[across(shape, width) for shape in shapes],
        results=[(pltpu.HBM if group[0] == 0 else value)(shape, BF16) for group, shape in zip(groups, shapes)],
    )(here, *[flat] * (parts + len(edges)), *tokens)


def last_block(here_ref, blocks):
    spot = jnp.bitwise_xor(lax.rem(here_ref[0], G), G - 1)
    last = blocks[0]
    for m in range(1, G):
        last = jnp.where(spot == m, blocks[m], last)
    return last


def pack_kernel(here_ref, *refs):
    in_refs, (all_ref, last_ref) = refs[:G], refs[-2:]
    side = in_refs[0].shape[0]
    for m in range(G):
        all_ref[m * side : (m + 1) * side] = in_refs[m][:side]
    last_ref[:side] = last_block(here_ref, [ref[:side] for ref in in_refs])
    if last_ref.shape[0] > side:
        all_ref[G * side :] = in_refs[G - 1][side:]
        last_ref[side:] = in_refs[G - 1][side:]


def pack(here, pieces, more, *tokens):
    side, cols = pieces[0][0].shape
    tile = 512
    shapes = [(G * side + more, cols), (side + more, cols)]
    specs = [across(array.shape, tile) for array in arrays_of(pieces)] if more else piece_specs(pieces, side, tile)
    return call(
        pack_kernel,
        1,
        grid=(cols // tile,),
        in_specs=[SMEM] + specs + [ANY] * len(tokens),
        out_specs=[across(shape, tile) for shape in shapes],
        results=[value(shape, BF16) for shape in shapes],
    )(here, *arrays_of(pieces), *tokens)


def split_kernel(groups, passing, here_ref, own_ref, got_ref, *refs):
    out_refs, wide = refs[-len(groups) - passing - 1 : -1], refs[-1]
    if passing:
        out_refs[-1][...] = refs[0][...]
    depth, rows, cols = own_ref.shape
    place = lax.rem(here_ref[0], G)

    def fill(ref):
        for j in range(cols // LANES):
            wide[j] = ref[:, :, j * LANES : (j + 1) * LANES].astype(F32).reshape(wide.shape[1:])

    @pl.when(place == G - 1)
    def _():
        fill(got_ref)

    @pl.when(place != G - 1)
    def _():
        fill(own_ref)

    for group, out_ref in zip(groups, out_refs):
        for n, m in enumerate(group):
            for j in range(cols // LANES):
                for start, row in rows_of(place, m):
                    block = wide.at[j][pl.ds(row, depth, stride=rows), :].astype(BF16)
                    out_ref[n * depth : (n + 1) * depth, start + j * LANES : start + (j + 1) * LANES] = block


def split_rows(here, own, got, chunk, groups, passing, *tokens):
    depth, rows, cols = own.shape
    first, count = chunk_tiles(chunk, cols)
    block = pl.BlockSpec((depth, rows, TILE), lambda i: (0, 0, first + i))
    shapes = [(len(group) * depth, cols) for group in groups] + [(depth, cols)] * len(passing)
    return call(
        functools.partial(split_kernel, groups, len(passing)),
        2,
        grid=(count,),
        in_specs=[SMEM, block, block] + piece_specs(passing, depth, ROWS * TILE) + [ANY] * len(tokens),
        out_specs=[across(shape, ROWS * TILE) for shape in shapes],
        results=[value(shape, BF16) for shape in shapes],
        scratch_shapes=[wide_tile(depth * rows)],
    )(here, far(own), got, *arrays_of(passing), *tokens)


def last_kernel(slabs, here_ref, cover_ref, offset_ref, *refs):
    w_ref, vol_ref, sino_ref, *refs = refs
    r_ref, tv_ref, vol, s, r, wide, tv, sem = refs[-8:]
    depth, rows, cols = sino_ref.shape

    count = cols // LANES

    def columns(j):
        return pl.ds(pl.multiple_of(j * LANES, LANES), LANES)

    def arrival(n, j):
        src, dst = ((vol_ref, vol), (sino_ref, s), (tv_ref, tv))[n]
        return pltpu.make_async_copy(src.at[:, :, columns(j)], dst.at[:, :, columns(j)], sem.at[n, j])

    def departure(n, j):
        src, dst = ((r, r_ref), (tv, tv_ref))[n]
        return pltpu.make_async_copy(src.at[:, :, columns(j)], dst.at[:, :, columns(j)], sem.at[3 + n, j])

    @pl.when(here_ref[0] == slabs - 1)
    def _():
        for j in range(count):
            for n in range(3):
                arrival(n, j).start()
        block = w_ref[offset_ref[slabs - 1, 0]]
        block = jnp.where(cover_ref[slabs - 1, 0] == 1, block, jnp.zeros_like(block))
        turned = block.astype(F32).T.astype(BF16)

        def column(j, _):
            at = columns(j)
            for n in range(3):
                arrival(n, j).wait()
            for n, ref in enumerate((s, tv, vol)):
                wide[n] = ref[:, :, at].astype(F32).reshape(wide.shape[1:])
            for row in range(rows):
                spot = pl.ds(row, depth, stride=rows)
                seen = jnp.dot(block, wide.at[2][spot, :].astype(BF16), preferred_element_type=F32)
                resid = (seen - wide.at[0][spot, :]).astype(BF16)
                wide.at[0][spot, :] = resid.astype(F32)
                wide.at[1][spot, :] += jnp.dot(turned, resid, preferred_element_type=F32)
            r[:, :, at] = wide[0].reshape(depth, rows, LANES).astype(BF16)
            tv[:, :, at] = wide[1].reshape(depth, rows, LANES)
            for n in range(2):
                departure(n, j).start()
            return 0

        lax.fori_loop(0, count, column, 0)
        for j in range(count):
            for n in range(2):
                departure(n, j).wait()


def last_group(here, coverage, offsets, weights, volume, sinogram, tv, *tokens):
    slabs = coverage.shape[0]
    depth, rows, cols = sinogram.shape
    return call(
        functools.partial(last_kernel, slabs),
        0,
        vmem=32,
        grid=(1,),
        in_specs=[SMEM, SMEM, SMEM, pl.BlockSpec(weights.shape, lambda i: (0, 0, 0))] + [ANY] * (3 + len(tokens)),
        out_specs=[ANY, ANY],
        results=[pltpu.HBM(sinogram.shape, BF16), pltpu.HBM(volume.shape, F32)],
        input_output_aliases={6: 1},
        scratch_shapes=[
            pltpu.VMEM(volume.shape, F32),
            pltpu.VMEM(sinogram.shape, BF16),
            pltpu.VMEM(sinogram.shape, BF16),
            pltpu.VMEM((3, depth * rows, LANES), F32),
            pltpu.VMEM(volume.shape, F32),
            pltpu.SemaphoreType.DMA((5, cols // LANES)),
        ],
    )(here, coverage, offsets, weights, far(volume), far(sinogram), far(tv), *tokens)


def natural(place, in_refs, wide, j):
    depth = in_refs[0].shape[0]
    rows = ROWS * len(in_refs)
    for m, ref in enumerate(in_refs):
        for start, row in rows_of(place, m):
            value = ref[:, start + j * LANES : start + (j + 1) * LANES].astype(F32)
            wide.at[j][pl.ds(row, depth, stride=rows), :] = value
    return wide[j].reshape(depth, rows, LANES)


def join_kernel(here_ref, *refs):
    in_refs, (out_ref, wide) = refs[:G], refs[-2:]
    for j in range(out_ref.shape[2] // LANES):
        out_ref[:, :, j * LANES : (j + 1) * LANES] = natural(lax.rem(here_ref[0], G), in_refs, wide, j).astype(BF16)


def join_rows(here, pieces, shape, *tokens):
    depth, rows, cols = shape
    _, count = chunk_tiles(0, cols)
    return call(
        join_kernel,
        0,
        grid=(count,),
        in_specs=[SMEM] + piece_specs(pieces, depth, ROWS * TILE) + [ANY] * len(tokens),
        out_specs=pl.BlockSpec((depth, rows, TILE), lambda i: (0, 0, i)),
        results=value((depth, rows, cols // CHUNKS), BF16),
        scratch_shapes=[wide_tile(depth * rows)],
    )(here, *arrays_of(pieces), *tokens)


def settle_kernel(slabs, count, here_ref, own_ref, above_ref, *refs):
    in_refs, (base_ref, out_ref, wide) = refs[:G], refs[-3:]
    step = pl.program_id(0)
    cols = out_ref.shape[2]
    place = lax.rem(here_ref[0], G)
    last = here_ref[0] == slabs - 1

    @pl.when(last)
    def _():
        pltpu.sync_copy(base_ref.at[:, :, pl.ds(pl.multiple_of(step * cols, cols), cols)], out_ref)

    @pl.when(jnp.logical_not(last) & (step < count) & (place == G - 1))
    def _():
        out_ref[...] = above_ref[...]

    @pl.when(jnp.logical_not(last) & (step < count) & (place != G - 1))
    def _():
        out_ref[...] = own_ref[...]

    @pl.when(jnp.logical_not(last) & (step >= count))
    def _():
        for j in range(cols // LANES):
            out_ref[:, :, j * LANES : (j + 1) * LANES] = natural(place, in_refs, wide, j).astype(BF16)


def settle(here, slabs, own, above, pieces, base, *tokens):
    depth, rows, cols = base.shape
    _, count = chunk_tiles(0, cols)
    block = (depth, rows, TILE)
    early = pl.BlockSpec(block, lambda i: (0, 0, jnp.minimum(i, count - 1)))
    late = [
        pl.BlockSpec((depth, ROWS * TILE), lambda i, at=at: (at, jnp.maximum(i - count, 0))) for _, at in pieces
    ]
    return call(
        functools.partial(settle_kernel, slabs, count),
        0,
        grid=(CHUNKS * count,),
        in_specs=[SMEM, early, early] + late + [ANY] * (len(tokens) + 1),
        out_specs=pl.BlockSpec(block, lambda i: (0, 0, i)),
        results=pltpu.HBM(base.shape, BF16),
        scratch_shapes=[wide_tile(depth * rows)],
    )(here, own, above, *arrays_of(pieces), *tokens, far(base))


def finish_kernel(here_ref, tv_ref, *refs):
    in_refs, (out_ref, wide) = refs[:G], refs[-2:]
    for j in range(out_ref.shape[2] // LANES):
        at = pl.ds(j * LANES, LANES)
        out_ref[:, :, at] = tv_ref[:, :, at] + natural(lax.rem(here_ref[0], G), in_refs, wide, j)


def finish(here, chunk, tv, pieces, *tokens):
    depth, rows, cols = tv.shape
    first, count = chunk_tiles(chunk, cols)
    part = pl.BlockSpec((depth, rows, TILE), lambda i: (0, 0, first + i))
    return call(
        finish_kernel,
        0,
        grid=(count,),
        in_specs=[SMEM, part] + piece_specs(pieces, depth, ROWS * TILE) + [ANY] * len(tokens),
        out_specs=part,
        results=pltpu.HBM(tv.shape, F32),
        input_output_aliases={1: 0},
        scratch_shapes=[wide_tile(depth * rows)],
    )(here, far(tv), *arrays_of(pieces), *tokens)


def band_kernel(slabs, span, here_ref, cover_ref, offset_ref, w_ref, *refs):
    proj_ref, back_ref, turned = refs[-3:]
    side = w_ref.shape[1]
    place = lax.rem(here_ref[0], G)
    first = here_ref[0] - place
    zero = jnp.zeros((side, side), BF16)
    for i in range(w_ref.shape[0]):
        turned[i] = w_ref[i].astype(F32).T.astype(BF16)

    def block(ref, i, j):
        k = j - i
        known, step = jnp.clip(i, 0, slabs - 1), jnp.clip(k, 0, span - 1)
        inside = (i >= 0) & (i < slabs) & (j >= 0) & (j < slabs) & (k >= 0) & (k < span)
        live = inside & (cover_ref[known, step] == 1)
        return jnp.where(live, ref[offset_ref[known, step]], zero)

    def slab(m):
        return first + jnp.bitwise_xor(place, m)

    def group(m):
        to = jnp.bitwise_xor(place, m)
        return first + jnp.where(to == G - 1, -1, to)

    seen = [slab(m) for m in range(G)] + [slab(m) + G for m in range(G)] + [first - 1]
    seeing = [group(m) for m in range(G)] + [group(m) - G for m in range(G)] + [first + G - 1]
    for r in range(G):
        for s in range(2 * G + 1):
            at = (pl.ds(r * side, side), pl.ds(s * side, side))
            proj_ref[at] = block(w_ref, group(r), seen[s])
            back_ref[at] = block(turned, seeing[s], slab(r))


def bands(here, coverage, offsets, weights, *tokens):
    slabs, span = coverage.shape
    side = weights.shape[1]
    shape = (G * side, (2 * G + 1) * side)
    return call(
        functools.partial(band_kernel, slabs, span),
        9,
        in_specs=[SMEM, SMEM, SMEM, pl.BlockSpec(weights.shape, lambda i: (0, 0, 0))] + [ANY] * len(tokens),
        grid=(1,),
        out_specs=[pl.BlockSpec(shape, lambda i: (0, 0))] * 2,
        results=[value(shape, BF16)] * 2,
        scratch_shapes=[pltpu.VMEM(weights.shape, BF16)],
    )(here, coverage, offsets, weights, *tokens)


def project_kernel(groups, here_ref, band_ref, own_ref, high_ref, low_ref, *refs):
    sino_refs, (r_ref, down_ref, *group_refs) = refs[:G], refs[-len(groups) - 2 :]
    side = sino_refs[0].shape[0]
    seen = jnp.concatenate([own_ref[...], high_ref[...], low_ref[...]], axis=0)
    total = jnp.dot(band_ref[...], seen, preferred_element_type=F32)
    resid = [(total[m * side : (m + 1) * side] - ref[...].astype(F32)).astype(BF16) for m, ref in enumerate(sino_refs)]
    for m in range(G):
        r_ref[m * side : (m + 1) * side] = resid[m]
    for group, group_ref in zip(groups, group_refs):
        for n, m in enumerate(group):
            group_ref[n * side : (n + 1) * side] = resid[m]
    down_ref[...] = last_block(here_ref, resid)


def project(here, band, own, high, low, sinos, groups, *tokens):
    n, side = band.shape[0], band.shape[0] // G
    cols = own.shape[1]
    tile = 512
    many, one = pl.BlockSpec((n, tile), lambda i: (0, i)), pl.BlockSpec((side, tile), lambda i: (0, i))
    shapes = [(n, cols), (side, cols)] + [(len(group) * side, cols) for group in groups]
    return call(
        functools.partial(project_kernel, groups),
        3,
        grid=(cols // tile,),
        in_specs=[SMEM, pl.BlockSpec(band.shape, lambda i: (0, 0)), many, many, one]
        + piece_specs(sinos, side, tile)
        + [ANY] * len(tokens),
        out_specs=[across(shape, tile) for shape in shapes],
        results=[value(shape, BF16) for shape in shapes],
    )(here, band, own, high, low, *arrays_of(sinos), *tokens)


def back_kernel(dealing, here_ref, band_ref, own_ref, low_ref, high_ref, *refs):
    out_refs = refs[-G:]
    side = high_ref.shape[0]
    seeing = jnp.concatenate([own_ref[...], low_ref[...], high_ref[...]], axis=0)
    total = jnp.dot(band_ref[...], seeing, preferred_element_type=F32)
    place = lax.rem(here_ref[0], G)
    for m, out_ref in enumerate(out_refs):
        out_ref[:side] = total[m * side : (m + 1) * side].astype(BF16)
        if dealing:
            last = jnp.bitwise_xor(place, m) == G - 1
            out_ref[side:] = jnp.where(last, refs[1][...], refs[0][m * side : (m + 1) * side])


def back(here, band, own, low, high, dealt, *tokens):
    n, side = band.shape[0], band.shape[0] // G
    cols = own.shape[1]
    tile = 512
    many = pl.BlockSpec((n, tile), lambda i: (0, i))
    one = pl.BlockSpec((side, tile), lambda i: (0, i))
    out = ((2 if dealt else 1) * side, cols)
    return call(
        functools.partial(back_kernel, bool(dealt)),
        0,
        grid=(cols // tile,),
        in_specs=[SMEM, pl.BlockSpec(band.shape, lambda i: (0, 0)), many, many, one]
        + ([many, one] if dealt else [])
        + [ANY] * len(tokens),
        out_specs=[across(out, tile)] * G,
        results=[value(out, BF16)] * G,
    )(here, band, own, low, high, *dealt, *tokens)


def tv_flux(cur, above):
    rows, cols = cur.shape
    row = lax.broadcasted_iota(jnp.int32, (rows, cols), 0)
    col = lax.broadcasted_iota(jnp.int32, (rows, cols), 1)
    dz = above - cur
    dy = jnp.where(row == rows - 1, 0.0, pltpu.roll(cur, rows - 1, 0)) - cur
    dx = jnp.where(col == cols - 1, 0.0, pltpu.roll(cur, cols - 1, 1)) - cur
    scale = 0.5 * lax.rsqrt(dz * dz + dy * dy + dx * dx + 0.25)
    return dz * scale, dy * scale, dx * scale


def tv_below(cur, above):
    return tv_flux(cur, above)[0]


def tv_slice(cur, above, below_flux):
    rows, cols = cur.shape
    row = lax.broadcasted_iota(jnp.int32, (rows, cols), 0)
    col = lax.broadcasted_iota(jnp.int32, (rows, cols), 1)
    fz, fy, fx = tv_flux(cur, above)
    sides = 0.5 * cur * lax.rsqrt(cur * cur + 0.25)
    fy_low = jnp.where(row == 0, sides, pltpu.roll(fy, 1, 0))
    fx_low = jnp.where(col == 0, sides, pltpu.roll(fx, 1, 1))
    return (below_flux - fz) + (fy_low - fy) + (fx_low - fx), fz


def tv_kernel(here_ref, near_ref, next_level_ref, far_ref, last_level_ref, next_ref, vol_ref, *refs):
    out_ref, done_ref, flux_ref = refs[-3:]
    step = pl.program_id(0)
    deep, rows, _ = vol_ref.shape
    place = lax.rem(here_ref[0], G)

    @pl.when(step == 0)
    def _():
        inside = jnp.where(place == 2, far_ref[...], near_ref[...])
        low = jnp.where(place == 0, last_level_ref[...], inside)[rows:].astype(F32)
        flux_ref[...] = tv_below(low, vol_ref[0])

    def body(z, flux):
        out_ref[z], flux = tv_slice(vol_ref[z], vol_ref[z + 1], flux)
        return flux

    flux = lax.fori_loop(0, deep - 1, body, flux_ref[...], unroll=5)
    inside = jnp.where(place == 1, far_ref[...], near_ref[...])
    high = jnp.where(place == G - 1, next_level_ref[...], inside)[:rows].astype(F32)
    above = jnp.where(step == pl.num_programs(0) - 1, high, next_ref[0])
    out_ref[deep - 1], flux_ref[...] = tv_slice(vol_ref[deep - 1], above, flux)
    done_ref[...] = flux_ref[:, : done_ref.shape[1]]


def half_tv(here, volume, ends, *tokens):
    depth, rows, cols = volume.shape
    deep = 16
    edges = [pl.BlockSpec((2 * rows, cols), lambda i, last=end.shape[0] // (2 * rows) - 1: (last, 0)) for end in ends]
    body = pl.BlockSpec((deep, rows, cols), lambda i: (i, 0, 0))
    after = pl.BlockSpec((1, rows, cols), lambda i: (jnp.minimum((i + 1) * deep, depth - 1), 0, 0))
    return call(
        tv_kernel,
        0,
        grid=(depth // deep,),
        in_specs=[SMEM] + edges + [after, body] + [ANY] * len(tokens),
        out_specs=[body, pl.BlockSpec((rows, LANES), lambda i: (0, 0))],
        results=[pltpu.HBM(volume.shape, F32), value((rows, LANES), F32)],
        scratch_shapes=[pltpu.VMEM((rows, cols), F32)],
    )(here, *ends, far(volume), far(volume), *tokens)


def local(volume, sinogram, weights, coverage, offsets):
    slabs = lax.axis_size("slab")
    here = lax.axis_index("slab").astype(jnp.int32).reshape(1)
    depth, rows, _ = volume.shape
    single = ((0,), (1,), (2,), (3,))
    paired = ((0,), (1,), (2, 3))

    def tied(array, *others):
        return lax.optimization_barrier((array, *others))[0]

    def beyond(over, *others):
        return swapped(tied(over, *others)[depth:], 1)

    vols0 = cast_rows(here, volume, 0, single, True)
    got = moved(sinogram, G, only=G - 1)
    got_vols0 = direct(vols0)
    v0, v1, v23 = cast_rows(here, volume, 1, paired, False, vols0[1])
    over = swapped(v23, 2)
    band_p, band_b = bands(here, coverage, offsets, weights, v1)
    own0, edge0 = pack(here, [(array, 0) for array in got_vols0], 2 * rows, band_p)
    high0, near = moved(own0, -G), swapped(tied(v1, own0), 1)
    s0, s1, s23, over_beyond = split_rows(here, sinogram, got, 0, paired, [(over, 1)], near)
    s_near, s_over = swapped(s1, 1), swapped(s23, 2)
    low0 = moved(tied(edge0, s_near), G)
    own1, edge1 = pack(here, [(v0, 0), (near, 0), (over, 0), (swapped(over_beyond, 1), 0)], 0)
    low1, high1 = moved(edge1, G), moved(own1, -G)
    sinos0 = [(s0, 0), (s_near, 0), (s_over, 0), (beyond(s_over, own1), 0)]

    s0, s1, s23 = split_rows(here, sinogram, got, 1, paired, [], own1)

    resid0, down0, *r = project(here, band_p, own0, high0, low0, sinos0, single[1:], low1, s0)
    from_low0, from_high0 = moved(resid0, G), moved(down0, -G)
    s_near, s_over = swapped(s1, 1), swapped(s23, 2)
    got_r = [swapped(tied(array, s_near), m + 1) for m, array in enumerate(r)]
    tv, tv_done = half_tv(here, volume, [got_vols0[1], high0, got_vols0[3], low0], resid0)
    sinos1 = [(s0, 0), (s_near, 0), (s_over, 0), (beyond(s_over, tv_done), 0)]
    resid1, down1 = project(here, band_p, own1, high1, low1, sinos1, (), tv_done, *got_r)
    from_low1, from_high1 = moved(resid1, G), moved(down1, -G)

    backs0 = back(here, band_b, resid0, from_low0, from_high0, [resid1, from_high1])
    got_backs0 = direct(backs0)
    r_pieces = [(array, 0) for array in [resid0] + got_r]
    natural0 = join_rows(here, r_pieces, sinogram.shape, backs0[0])
    above0 = moved(natural0, -G, only=G - 1)
    r_last, tv = last_group(here, coverage, offsets, weights, volume, sinogram, tv, backs0[0])
    backs1 = back(here, band_b, resid1, from_low1, from_high1, [], far(r_last), natural0)
    got_backs1 = direct(backs1)
    gradient = finish(here, 0, tv, [(array, 0) for array in got_backs0], backs1[0])
    residual = settle(here, slabs, natural0, above0, [(array, 1) for array in got_backs0], r_last, backs1[0])
    gradient = finish(here, 1, gradient, [(array, 0) for array in got_backs1], far(residual))
    return (gradient, residual)


def solution(mesh):
    placed = (P("slab", "grp", None), P("slab", "grp", None), P(), P(), P())
    return jax.shard_map(
        local,
        mesh=mesh,
        in_specs=placed,
        out_specs=(P("slab", "grp", None), P("slab", "grp", None)),
        check_vma=False,
    )
```

```python
import functools

import jax
import jax.numpy as jnp
from jax import lax
from jax.experimental import pallas as pl
from jax.experimental.pallas import tpu as pltpu
from jax.sharding import PartitionSpec as P

G = 4
CHUNKS = 2
ROWS = 2
TILE = 256
F32 = jnp.float32
BF16 = jnp.bfloat16
MIB = 1024 * 1024
LANES = 128
SMEM = pl.BlockSpec(memory_space=pltpu.SMEM)
VMEM = pl.BlockSpec(memory_space=pltpu.VMEM)
ANY = pl.BlockSpec(memory_space=pl.ANY)


def moved(value, steps, only=None):
    count = lax.axis_size("slab")
    first, last = max(0, -steps), min(count, count - steps)
    pairs = [(i, i + steps) for i in range(first, last) if only is None or i % G == only]
    return lax.ppermute(value, "slab", pairs)


def swapped(value, bits):
    count = lax.axis_size("slab")
    return lax.ppermute(value, "slab", [(i, i ^ bits) for i in range(count)])


def direct(arrays):
    return [array if m == 0 else swapped(array, m) for m, array in enumerate(arrays)]


def call(kernel, us, *, results, vmem=16, **how):
    return pl.pallas_call(
        kernel,
        out_shape=results,
        compiler_params=pltpu.CompilerParams(vmem_limit_bytes=vmem * MIB),
        cost_estimate=pl.CostEstimate(flops=int(us * 1.15e9), bytes_accessed=1000, transcendentals=0),
        **how,
    )


def value(shape, dtype):
    return jax.ShapeDtypeStruct(shape, dtype)


def far(array):
    return pltpu.with_memory_space_constraint(array, pltpu.HBM)


def across(shape, tile):
    block = shape[:-1] + (tile,)
    return pl.BlockSpec(block, lambda i: (0,) * (len(shape) - 1) + (i,))


def piece_specs(pieces, side, tile):
    return [pl.BlockSpec((side, tile), lambda i, at=at: (at, i)) for _, at in pieces]


def arrays_of(pieces):
    return [array for array, _ in pieces]


def rows_of(place, m):
    first = ROWS * jnp.bitwise_xor(place, m)
    return [(h * TILE, first + h) for h in range(ROWS)]


def wide_tile(rows_deep):
    return pltpu.VMEM((TILE // LANES, rows_deep, LANES), F32)


def chunk_tiles(chunk, cols):
    count = cols // CHUNKS // TILE
    return chunk * count, count


def cast_kernel(groups, ends, halves, here_ref, *refs):
    parts = TILE // LANES
    vol_refs, end_refs = refs[:parts], refs[parts : parts + ends]
    for half_ref, sent_ref in zip(refs[parts + ends : parts + ends + halves], refs[len(refs) - halves :]):
        sent_ref[...] = half_ref[...]
    out_refs = refs[len(refs) - halves - len(groups) : len(refs) - halves]
    rows = ROWS * G
    depth = vol_refs[0].shape[0] // rows
    place = lax.rem(here_ref[0], G)
    for j, vol_ref in enumerate(vol_refs):
        for group, out_ref in zip(groups, out_refs):
            for n, m in enumerate(group):
                for start, row in rows_of(place, m):
                    at = pl.ds(start + j * LANES, LANES)
                    out_ref[n * depth : (n + 1) * depth, at] = vol_ref[pl.ds(row, depth, stride=rows), :].astype(BF16)
    if ends:
        both = jnp.concatenate([ref[...] for ref in end_refs], axis=0).astype(BF16)
        for group, out_ref in zip(groups, out_refs):
            if group[0] % 2:
                out_ref[depth:, :] = both


def cast_rows(here, volume, chunk, groups, ends, sinogram, *tokens):
    depth, rows, cols = volume.shape
    flat = far(volume.reshape(depth * rows, cols))
    first, count = chunk_tiles(chunk, cols)
    parts, width = TILE // LANES, ROWS * TILE
    shapes = [(len(group) * depth + (2 * rows if ends and group[0] % 2 else 0), cols) for group in groups]
    edges = [pl.BlockSpec((rows, width), lambda i, z=z: (z, i)) for z in (0, depth - 1)] if ends else []
    halves = 0 if sinogram is None else CHUNKS
    block = (depth, rows, TILE)
    return call(
        functools.partial(cast_kernel, groups, len(edges), halves),
        2,
        grid=(count,),
        in_specs=[SMEM]
        + [pl.BlockSpec((depth * rows, LANES), lambda i, j=j: (0, (first + i) * parts + j)) for j in range(parts)]
        + edges
        + [pl.BlockSpec(block, lambda i, c=c: (0, 0, c * count + i)) for c in range(halves)]
        + [ANY] * len(tokens),
        out_specs=[across(shape, width) for shape in shapes] + [pl.BlockSpec(block, lambda i: (0, 0, i))] * halves,
        results=[(pltpu.HBM if group[0] == 0 else value)(shape, BF16) for group, shape in zip(groups, shapes)]
        + [value((depth, rows, cols // CHUNKS), BF16)] * halves,
    )(here, *[flat] * (parts + len(edges)), *[sinogram if halves == 0 else far(sinogram)] * halves, *tokens)


def last_block(here_ref, blocks):
    spot = jnp.bitwise_xor(lax.rem(here_ref[0], G), G - 1)
    last = blocks[0]
    for m in range(1, G):
        last = jnp.where(spot == m, blocks[m], last)
    return last


def pack_kernel(here_ref, *refs):
    in_refs, (all_ref, last_ref) = refs[:G], refs[-2:]
    side = in_refs[0].shape[0]
    for m in range(G):
        all_ref[m * side : (m + 1) * side] = in_refs[m][:side]
    last_ref[:side] = last_block(here_ref, [ref[:side] for ref in in_refs])
    if last_ref.shape[0] > side:
        all_ref[G * side :] = in_refs[G - 1][side:]
        last_ref[side:] = in_refs[G - 1][side:]


def pack(here, pieces, more, *tokens):
    side, cols = pieces[0][0].shape
    tile = 512
    shapes = [(G * side + more, cols), (side + more, cols)]
    specs = [across(array.shape, tile) for array in arrays_of(pieces)] if more else piece_specs(pieces, side, tile)
    return call(
        pack_kernel,
        1,
        grid=(cols // tile,),
        in_specs=[SMEM] + specs + [ANY] * len(tokens),
        out_specs=[across(shape, tile) for shape in shapes],
        results=[value(shape, BF16) for shape in shapes],
    )(here, *arrays_of(pieces), *tokens)


def split_kernel(groups, passing, here_ref, own_ref, got_ref, *refs):
    out_refs, wide = refs[-len(groups) - passing - 1 : -1], refs[-1]
    if passing:
        out_refs[-1][...] = refs[0][...]
    depth, rows, cols = own_ref.shape
    place = lax.rem(here_ref[0], G)

    def fill(ref):
        for j in range(cols // LANES):
            wide[j] = ref[:, :, j * LANES : (j + 1) * LANES].astype(F32).reshape(wide.shape[1:])

    @pl.when(place == G - 1)
    def _():
        fill(got_ref)

    @pl.when(place != G - 1)
    def _():
        fill(own_ref)

    for group, out_ref in zip(groups, out_refs):
        for n, m in enumerate(group):
            for j in range(cols // LANES):
                for start, row in rows_of(place, m):
                    block = wide.at[j][pl.ds(row, depth, stride=rows), :].astype(BF16)
                    out_ref[n * depth : (n + 1) * depth, start + j * LANES : start + (j + 1) * LANES] = block


def split_rows(here, own, got, chunk, groups, passing, *tokens):
    depth, rows, cols = own.shape
    first, count = chunk_tiles(chunk, cols)
    block = pl.BlockSpec((depth, rows, TILE), lambda i: (0, 0, first + i))
    shapes = [(len(group) * depth, cols) for group in groups] + [(depth, cols)] * len(passing)
    return call(
        functools.partial(split_kernel, groups, len(passing)),
        2,
        grid=(count,),
        in_specs=[SMEM, block, pl.BlockSpec((depth, rows, TILE), lambda i: (0, 0, i))]
        + piece_specs(passing, depth, ROWS * TILE) + [ANY] * len(tokens),
        out_specs=[across(shape, ROWS * TILE) for shape in shapes],
        results=[value(shape, BF16) for shape in shapes],
        scratch_shapes=[wide_tile(depth * rows)],
    )(here, far(own), got, *arrays_of(passing), *tokens)


def last_kernel(slabs, here_ref, cover_ref, offset_ref, *refs):
    w_ref, vol_ref, sino_ref, *refs = refs
    r_ref, tv_ref, vol, s, r, wide, tv, sem = refs[-8:]
    depth, rows, cols = sino_ref.shape

    count = cols // LANES

    def columns(j):
        return pl.ds(pl.multiple_of(j * LANES, LANES), LANES)

    def arrival(n, j):
        src, dst = ((vol_ref, vol), (sino_ref, s), (tv_ref, tv))[n]
        return pltpu.make_async_copy(src.at[:, :, columns(j)], dst.at[:, :, columns(j)], sem.at[n, j])

    def departure(n, j):
        src, dst = ((r, r_ref), (tv, tv_ref))[n]
        return pltpu.make_async_copy(src.at[:, :, columns(j)], dst.at[:, :, columns(j)], sem.at[3 + n, j])

    @pl.when(here_ref[0] == slabs - 1)
    def _():
        for j in range(count):
            for n in range(3):
                arrival(n, j).start()
        block = w_ref[offset_ref[slabs - 1, 0]]
        block = jnp.where(cover_ref[slabs - 1, 0] == 1, block, jnp.zeros_like(block))
        turned = block.astype(F32).T.astype(BF16)

        def column(j, _):
            at = columns(j)
            for n in range(3):
                arrival(n, j).wait()
            for n, ref in enumerate((s, tv, vol)):
                wide[n] = ref[:, :, at].astype(F32).reshape(wide.shape[1:])
            for row in range(rows):
                spot = pl.ds(row, depth, stride=rows)
                seen = jnp.dot(block, wide.at[2][spot, :].astype(BF16), preferred_element_type=F32)
                resid = (seen - wide.at[0][spot, :]).astype(BF16)
                wide.at[0][spot, :] = resid.astype(F32)
                wide.at[1][spot, :] += jnp.dot(turned, resid, preferred_element_type=F32)
            r[:, :, at] = wide[0].reshape(depth, rows, LANES).astype(BF16)
            tv[:, :, at] = wide[1].reshape(depth, rows, LANES)
            for n in range(2):
                departure(n, j).start()
            return 0

        lax.fori_loop(0, count, column, 0)
        for j in range(count):
            for n in range(2):
                departure(n, j).wait()


def last_group(here, coverage, offsets, weights, volume, sinogram, tv, *tokens):
    slabs = coverage.shape[0]
    depth, rows, cols = sinogram.shape
    return call(
        functools.partial(last_kernel, slabs),
        0,
        vmem=32,
        grid=(1,),
        in_specs=[SMEM, SMEM, SMEM, pl.BlockSpec(weights.shape, lambda i: (0, 0, 0))] + [ANY] * (3 + len(tokens)),
        out_specs=[ANY, ANY],
        results=[pltpu.HBM(sinogram.shape, BF16), pltpu.HBM(volume.shape, F32)],
        input_output_aliases={6: 1},
        scratch_shapes=[
            pltpu.VMEM(volume.shape, F32),
            pltpu.VMEM(sinogram.shape, BF16),
            pltpu.VMEM(sinogram.shape, BF16),
            pltpu.VMEM((3, depth * rows, LANES), F32),
            pltpu.VMEM(volume.shape, F32),
            pltpu.SemaphoreType.DMA((5, cols // LANES)),
        ],
    )(here, coverage, offsets, weights, far(volume), far(sinogram), far(tv), *tokens)


def natural(place, in_refs, wide, j):
    depth = in_refs[0].shape[0]
    rows = ROWS * len(in_refs)
    for m, ref in enumerate(in_refs):
        for start, row in rows_of(place, m):
            value = ref[:, start + j * LANES : start + (j + 1) * LANES].astype(F32)
            wide.at[j][pl.ds(row, depth, stride=rows), :] = value
    return wide[j].reshape(depth, rows, LANES)


def join_kernel(here_ref, *refs):
    in_refs, (out_ref, wide) = refs[:G], refs[-2:]
    for j in range(out_ref.shape[2] // LANES):
        out_ref[:, :, j * LANES : (j + 1) * LANES] = natural(lax.rem(here_ref[0], G), in_refs, wide, j).astype(BF16)


def join_rows(here, pieces, shape, *tokens):
    depth, rows, cols = shape
    _, count = chunk_tiles(0, cols)
    return call(
        join_kernel,
        0,
        grid=(count,),
        in_specs=[SMEM] + piece_specs(pieces, depth, ROWS * TILE) + [ANY] * len(tokens),
        out_specs=pl.BlockSpec((depth, rows, TILE), lambda i: (0, 0, i)),
        results=value((depth, rows, cols // CHUNKS), BF16),
        scratch_shapes=[wide_tile(depth * rows)],
    )(here, *arrays_of(pieces), *tokens)


def settle_kernel(slabs, count, here_ref, own_ref, above_ref, *refs):
    in_refs, (base_ref, out_ref, wide) = refs[:G], refs[-3:]
    step = pl.program_id(0)
    cols = out_ref.shape[2]
    place = lax.rem(here_ref[0], G)
    last = here_ref[0] == slabs - 1

    @pl.when(last)
    def _():
        pltpu.sync_copy(base_ref.at[:, :, pl.ds(pl.multiple_of(step * cols, cols), cols)], out_ref)

    @pl.when(jnp.logical_not(last) & (step < count) & (place == G - 1))
    def _():
        out_ref[...] = above_ref[...]

    @pl.when(jnp.logical_not(last) & (step < count) & (place != G - 1))
    def _():
        out_ref[...] = own_ref[...]

    @pl.when(jnp.logical_not(last) & (step >= count))
    def _():
        for j in range(cols // LANES):
            out_ref[:, :, j * LANES : (j + 1) * LANES] = natural(place, in_refs, wide, j).astype(BF16)


def settle(here, slabs, own, above, pieces, base, *tokens):
    depth, rows, cols = base.shape
    _, count = chunk_tiles(0, cols)
    block = (depth, rows, TILE)
    early = pl.BlockSpec(block, lambda i: (0, 0, jnp.minimum(i, count - 1)))
    late = [
        pl.BlockSpec((depth, ROWS * TILE), lambda i, at=at: (at, jnp.maximum(i - count, 0))) for _, at in pieces
    ]
    return call(
        functools.partial(settle_kernel, slabs, count),
        0,
        grid=(CHUNKS * count,),
        in_specs=[SMEM, early, early] + late + [ANY] * (len(tokens) + 1),
        out_specs=pl.BlockSpec(block, lambda i: (0, 0, i)),
        results=pltpu.HBM(base.shape, BF16),
        scratch_shapes=[wide_tile(depth * rows)],
    )(here, own, above, *arrays_of(pieces), *tokens, far(base))


def finish_kernel(here_ref, tv_ref, *refs):
    in_refs, (out_ref, wide) = refs[:G], refs[-2:]
    for j in range(out_ref.shape[2] // LANES):
        at = pl.ds(j * LANES, LANES)
        out_ref[:, :, at] = tv_ref[:, :, at] + natural(lax.rem(here_ref[0], G), in_refs, wide, j)


def finish(here, chunk, tv, pieces, *tokens):
    depth, rows, cols = tv.shape
    first, count = chunk_tiles(chunk, cols)
    part = pl.BlockSpec((depth, rows, TILE), lambda i: (0, 0, first + i))
    return call(
        finish_kernel,
        0,
        grid=(count,),
        in_specs=[SMEM, part] + piece_specs(pieces, depth, ROWS * TILE) + [ANY] * len(tokens),
        out_specs=part,
        results=pltpu.HBM(tv.shape, F32),
        input_output_aliases={1: 0},
        scratch_shapes=[wide_tile(depth * rows)],
    )(here, far(tv), *arrays_of(pieces), *tokens)


def band_kernel(slabs, span, here_ref, cover_ref, offset_ref, w_ref, *refs):
    proj_ref, back_ref, turned = refs[-3:]
    side = w_ref.shape[1]
    place = lax.rem(here_ref[0], G)
    first = here_ref[0] - place
    zero = jnp.zeros((side, side), BF16)
    for i in range(w_ref.shape[0]):
        turned[i] = w_ref[i].astype(F32).T.astype(BF16)

    def block(ref, i, j):
        k = j - i
        known, step = jnp.clip(i, 0, slabs - 1), jnp.clip(k, 0, span - 1)
        inside = (i >= 0) & (i < slabs) & (j >= 0) & (j < slabs) & (k >= 0) & (k < span)
        live = inside & (cover_ref[known, step] == 1)
        return jnp.where(live, ref[offset_ref[known, step]], zero)

    def slab(m):
        return first + jnp.bitwise_xor(place, m)

    def group(m):
        to = jnp.bitwise_xor(place, m)
        return first + jnp.where(to == G - 1, -1, to)

    seen = [slab(m) for m in range(G)] + [slab(m) + G for m in range(G)] + [first - 1]
    seeing = [group(m) for m in range(G)] + [group(m) - G for m in range(G)] + [first + G - 1]
    for r in range(G):
        for s in range(2 * G + 1):
            at = (pl.ds(r * side, side), pl.ds(s * side, side))
            proj_ref[at] = block(w_ref, group(r), seen[s])
            back_ref[at] = block(turned, seeing[s], slab(r))


def bands(here, coverage, offsets, weights, *tokens):
    slabs, span = coverage.shape
    side = weights.shape[1]
    shape = (G * side, (2 * G + 1) * side)
    return call(
        functools.partial(band_kernel, slabs, span),
        9,
        in_specs=[SMEM, SMEM, SMEM, pl.BlockSpec(weights.shape, lambda i: (0, 0, 0))] + [ANY] * len(tokens),
        grid=(1,),
        out_specs=[pl.BlockSpec(shape, lambda i: (0, 0))] * 2,
        results=[value(shape, BF16)] * 2,
        scratch_shapes=[pltpu.VMEM(weights.shape, BF16)],
    )(here, coverage, offsets, weights, *tokens)


def project_kernel(groups, here_ref, band_ref, own_ref, high_ref, low_ref, *refs):
    sino_refs, (r_ref, down_ref, *group_refs) = refs[:G], refs[-len(groups) - 2 :]
    side = sino_refs[0].shape[0]
    seen = jnp.concatenate([own_ref[...], high_ref[...], low_ref[...]], axis=0)
    total = jnp.dot(band_ref[...], seen, preferred_element_type=F32)
    resid = [(total[m * side : (m + 1) * side] - ref[...].astype(F32)).astype(BF16) for m, ref in enumerate(sino_refs)]
    for m in range(G):
        r_ref[m * side : (m + 1) * side] = resid[m]
    for group, group_ref in zip(groups, group_refs):
        for n, m in enumerate(group):
            group_ref[n * side : (n + 1) * side] = resid[m]
    down_ref[...] = last_block(here_ref, resid)


def project(here, band, own, high, low, sinos, groups, *tokens):
    n, side = band.shape[0], band.shape[0] // G
    cols = own.shape[1]
    tile = 512
    many, one = pl.BlockSpec((n, tile), lambda i: (0, i)), pl.BlockSpec((side, tile), lambda i: (0, i))
    shapes = [(n, cols), (side, cols)] + [(len(group) * side, cols) for group in groups]
    return call(
        functools.partial(project_kernel, groups),
        3,
        grid=(cols // tile,),
        in_specs=[SMEM, pl.BlockSpec(band.shape, lambda i: (0, 0)), many, many, one]
        + piece_specs(sinos, side, tile)
        + [ANY] * len(tokens),
        out_specs=[across(shape, tile) for shape in shapes],
        results=[value(shape, BF16) for shape in shapes],
    )(here, band, own, high, low, *arrays_of(sinos), *tokens)


def back_kernel(dealing, here_ref, band_ref, own_ref, low_ref, high_ref, *refs):
    out_refs = refs[-G:]
    side = high_ref.shape[0]
    seeing = jnp.concatenate([own_ref[...], low_ref[...], high_ref[...]], axis=0)
    total = jnp.dot(band_ref[...], seeing, preferred_element_type=F32)
    place = lax.rem(here_ref[0], G)
    for m, out_ref in enumerate(out_refs):
        out_ref[:side] = total[m * side : (m + 1) * side].astype(BF16)
        if dealing:
            last = jnp.bitwise_xor(place, m) == G - 1
            out_ref[side:] = jnp.where(last, refs[1][...], refs[0][m * side : (m + 1) * side])


def back(here, band, own, low, high, dealt, *tokens):
    n, side = band.shape[0], band.shape[0] // G
    cols = own.shape[1]
    tile = 512
    many = pl.BlockSpec((n, tile), lambda i: (0, i))
    one = pl.BlockSpec((side, tile), lambda i: (0, i))
    out = ((2 if dealt else 1) * side, cols)
    return call(
        functools.partial(back_kernel, bool(dealt)),
        0,
        grid=(cols // tile,),
        in_specs=[SMEM, pl.BlockSpec(band.shape, lambda i: (0, 0)), many, many, one]
        + ([many, one] if dealt else [])
        + [ANY] * len(tokens),
        out_specs=[across(out, tile)] * G,
        results=[value(out, BF16)] * G,
    )(here, band, own, low, high, *dealt, *tokens)


def tv_flux(cur, above):
    rows, cols = cur.shape
    row = lax.broadcasted_iota(jnp.int32, (rows, cols), 0)
    col = lax.broadcasted_iota(jnp.int32, (rows, cols), 1)
    dz = above - cur
    dy = jnp.where(row == rows - 1, 0.0, pltpu.roll(cur, rows - 1, 0)) - cur
    dx = jnp.where(col == cols - 1, 0.0, pltpu.roll(cur, cols - 1, 1)) - cur
    scale = 0.5 * lax.rsqrt(dz * dz + dy * dy + dx * dx + 0.25)
    return dz * scale, dy * scale, dx * scale


def tv_below(cur, above):
    return tv_flux(cur, above)[0]


def tv_slice(cur, above, below_flux):
    rows, cols = cur.shape
    row = lax.broadcasted_iota(jnp.int32, (rows, cols), 0)
    col = lax.broadcasted_iota(jnp.int32, (rows, cols), 1)
    fz, fy, fx = tv_flux(cur, above)
    sides = 0.5 * cur * lax.rsqrt(cur * cur + 0.25)
    fy_low = jnp.where(row == 0, sides, pltpu.roll(fy, 1, 0))
    fx_low = jnp.where(col == 0, sides, pltpu.roll(fx, 1, 1))
    return (below_flux - fz) + (fy_low - fy) + (fx_low - fx), fz


def tv_kernel(here_ref, near_ref, next_level_ref, far_ref, last_level_ref, next_ref, vol_ref, *refs):
    out_ref, done_ref, flux_ref = refs[-3:]
    step = pl.program_id(0)
    deep, rows, _ = vol_ref.shape
    place = lax.rem(here_ref[0], G)

    @pl.when(step == 0)
    def _():
        inside = jnp.where(place == 2, far_ref[...], near_ref[...])
        low = jnp.where(place == 0, last_level_ref[...], inside)[rows:].astype(F32)
        flux_ref[...] = tv_below(low, vol_ref[0])

    def body(z, flux):
        out_ref[z], flux = tv_slice(vol_ref[z], vol_ref[z + 1], flux)
        return flux

    flux = lax.fori_loop(0, deep - 1, body, flux_ref[...], unroll=5)
    inside = jnp.where(place == 1, far_ref[...], near_ref[...])
    high = jnp.where(place == G - 1, next_level_ref[...], inside)[:rows].astype(F32)
    above = jnp.where(step == pl.num_programs(0) - 1, high, next_ref[0])
    out_ref[deep - 1], flux_ref[...] = tv_slice(vol_ref[deep - 1], above, flux)
    done_ref[...] = flux_ref[:, : done_ref.shape[1]]


def half_tv(here, volume, ends, *tokens):
    depth, rows, cols = volume.shape
    deep = 16
    edges = [pl.BlockSpec((2 * rows, cols), lambda i, last=end.shape[0] // (2 * rows) - 1: (last, 0)) for end in ends]
    body = pl.BlockSpec((deep, rows, cols), lambda i: (i, 0, 0))
    after = pl.BlockSpec((1, rows, cols), lambda i: (jnp.minimum((i + 1) * deep, depth - 1), 0, 0))
    return call(
        tv_kernel,
        0,
        grid=(depth // deep,),
        in_specs=[SMEM] + edges + [after, body] + [ANY] * len(tokens),
        out_specs=[body, pl.BlockSpec((rows, LANES), lambda i: (0, 0))],
        results=[pltpu.HBM(volume.shape, F32), value((rows, LANES), F32)],
        scratch_shapes=[pltpu.VMEM((rows, cols), F32)],
    )(here, *ends, far(volume), far(volume), *tokens)


def local(volume, sinogram, weights, coverage, offsets):
    slabs = lax.axis_size("slab")
    here = lax.axis_index("slab").astype(jnp.int32).reshape(1)
    depth, rows, _ = volume.shape
    single = ((0,), (1,), (2,), (3,))
    paired = ((0,), (1,), (2, 3))

    def tied(array, *others):
        return lax.optimization_barrier((array, *others))[0]

    def beyond(over, *others):
        return swapped(tied(over, *others)[depth:], 1)

    vols0 = cast_rows(here, volume, 0, single, True, None)
    got_vols0 = direct(vols0)
    v0, v1, v23, sent0, sent1 = cast_rows(here, volume, 1, paired, False, sinogram, vols0[1])
    got0 = moved(sent0, G, only=G - 1)
    over = swapped(v23, 2)
    band_p, band_b = bands(here, coverage, offsets, weights, v1)
    own0, edge0 = pack(here, [(array, 0) for array in got_vols0], 2 * rows, band_p)
    high0, near = moved(own0, -G), swapped(tied(v1, own0), 1)
    got1 = moved(tied(sent1, own0), G, only=G - 1)
    s0, s1, s23, over_beyond = split_rows(here, sinogram, got0, 0, paired, [(over, 1)], near)
    s_near, s_over = swapped(s1, 1), swapped(s23, 2)
    low0 = moved(tied(edge0, s_near), G)
    own1, edge1 = pack(here, [(v0, 0), (near, 0), (over, 0), (swapped(over_beyond, 1), 0)], 0)
    low1, high1 = moved(edge1, G), moved(own1, -G)
    sinos0 = [(s0, 0), (s_near, 0), (s_over, 0), (beyond(s_over, own1), 0)]

    s0, s1, s23 = split_rows(here, sinogram, got1, 1, paired, [], own1)

    resid0, down0, r1, r23 = project(here, band_p, own0, high0, low0, sinos0, paired[1:], low1, s0)
    from_low0, from_high0 = moved(resid0, G), moved(down0, -G)
    s_near, s_over = swapped(s1, 1), swapped(s23, 2)
    r_near, r_over = swapped(tied(r1, s_near), 1), swapped(tied(r23, s_near), 2)
    tv, tv_done = half_tv(here, volume, [got_vols0[1], high0, got_vols0[3], low0], resid0)
    sinos1 = [(s0, 0), (s_near, 0), (s_over, 0), (beyond(s_over, tv_done), 0)]
    resid1, down1 = project(here, band_p, own1, high1, low1, sinos1, (), tv_done, r_near, r_over)
    from_low1, from_high1 = moved(resid1, G), moved(down1, -G)

    backs0 = back(here, band_b, resid0, from_low0, from_high0, [resid1, from_high1])
    got_backs0 = direct(backs0)
    r_pieces = [(resid0, 0), (r_near, 0), (r_over, 0), (beyond(r_over, resid1), 0)]
    natural0 = join_rows(here, r_pieces, sinogram.shape, backs0[0])
    above0 = moved(natural0, -G, only=G - 1)
    r_last, tv = last_group(here, coverage, offsets, weights, volume, sinogram, tv, backs0[0])
    backs1 = back(here, band_b, resid1, from_low1, from_high1, [], far(r_last), natural0)
    got_backs1 = direct(backs1)
    gradient = finish(here, 0, tv, [(array, 0) for array in got_backs0], backs1[0])
    residual = settle(here, slabs, natural0, above0, [(array, 1) for array in got_backs0], r_last, backs1[0])
    gradient = finish(here, 1, gradient, [(array, 0) for array in got_backs1], far(residual))
    return (gradient, residual)


def solution(mesh):
    placed = (P("slab", "grp", None), P("slab", "grp", None), P(), P(), P())
    return jax.shard_map(
        local,
        mesh=mesh,
        in_specs=placed,
        out_specs=(P("slab", "grp", None), P("slab", "grp", None)),
        check_vma=False,
    )
```

```python
import functools

import jax
import jax.numpy as jnp
from jax import lax
from jax.experimental import pallas as pl
from jax.experimental.pallas import tpu as pltpu
from jax.sharding import PartitionSpec as P

G = 4
CHUNKS = 2
ROWS = 2
TILE = 256
F32 = jnp.float32
BF16 = jnp.bfloat16
MIB = 1024 * 1024
LANES = 128
SMEM = pl.BlockSpec(memory_space=pltpu.SMEM)
VMEM = pl.BlockSpec(memory_space=pltpu.VMEM)
ANY = pl.BlockSpec(memory_space=pl.ANY)


def moved(value, steps, only=None):
    count = lax.axis_size("slab")
    first, last = max(0, -steps), min(count, count - steps)
    pairs = [(i, i + steps) for i in range(first, last) if only is None or i % G == only]
    return lax.ppermute(value, "slab", pairs)


def swapped(value, bits):
    count = lax.axis_size("slab")
    return lax.ppermute(value, "slab", [(i, i ^ bits) for i in range(count)])


def direct(arrays):
    return [array if m == 0 else swapped(array, m) for m, array in enumerate(arrays)]


def call(kernel, us, *, results, vmem=16, **how):
    return pl.pallas_call(
        kernel,
        out_shape=results,
        compiler_params=pltpu.CompilerParams(vmem_limit_bytes=vmem * MIB),
        cost_estimate=pl.CostEstimate(flops=int(us * 1.15e9), bytes_accessed=1000, transcendentals=0),
        **how,
    )


def value(shape, dtype):
    return jax.ShapeDtypeStruct(shape, dtype)


def far(array):
    return pltpu.with_memory_space_constraint(array, pltpu.HBM)


def across(shape, tile):
    block = shape[:-1] + (tile,)
    return pl.BlockSpec(block, lambda i: (0,) * (len(shape) - 1) + (i,))


def piece_specs(pieces, side, tile):
    return [pl.BlockSpec((side, tile), lambda i, at=at: (at, i)) for _, at in pieces]


def arrays_of(pieces):
    return [array for array, _ in pieces]


def rows_of(place, m):
    first = ROWS * jnp.bitwise_xor(place, m)
    return [(h * TILE, first + h) for h in range(ROWS)]


def wide_tile(rows_deep):
    return pltpu.VMEM((TILE // LANES, rows_deep, LANES), F32)


def chunk_tiles(chunk, cols):
    count = cols // CHUNKS // TILE
    return chunk * count, count


def cast_kernel(groups, ends, halves, here_ref, *refs):
    parts = TILE // LANES
    vol_refs, end_refs = refs[:parts], refs[parts : parts + ends]
    for half_ref, sent_ref in zip(refs[parts + ends : parts + ends + halves], refs[len(refs) - halves :]):
        sent_ref[...] = half_ref[...]
    out_refs = refs[len(refs) - halves - len(groups) : len(refs) - halves]
    rows = ROWS * G
    depth = vol_refs[0].shape[0] // rows
    place = lax.rem(here_ref[0], G)
    for j, vol_ref in enumerate(vol_refs):
        for group, out_ref in zip(groups, out_refs):
            for n, m in enumerate(group):
                for start, row in rows_of(place, m):
                    at = pl.ds(start + j * LANES, LANES)
                    out_ref[n * depth : (n + 1) * depth, at] = vol_ref[pl.ds(row, depth, stride=rows), :].astype(BF16)
    if ends:
        both = jnp.concatenate([ref[...] for ref in end_refs], axis=0).astype(BF16)
        for group, out_ref in zip(groups, out_refs):
            if group[0] % 2:
                out_ref[depth:, :] = both


def cast_rows(here, volume, chunk, groups, ends, sinogram, *tokens):
    depth, rows, cols = volume.shape
    flat = far(volume.reshape(depth * rows, cols))
    first, count = chunk_tiles(chunk, cols)
    parts, width = TILE // LANES, ROWS * TILE
    shapes = [(len(group) * depth + (2 * rows if ends and group[0] % 2 else 0), cols) for group in groups]
    edges = [pl.BlockSpec((rows, width), lambda i, z=z: (z, i)) for z in (0, depth - 1)] if ends else []
    halves = 0 if sinogram is None else CHUNKS
    block = (depth, rows, TILE)
    return call(
        functools.partial(cast_kernel, groups, len(edges), halves),
        2,
        grid=(count,),
        in_specs=[SMEM]
        + [pl.BlockSpec((depth * rows, LANES), lambda i, j=j: (0, (first + i) * parts + j)) for j in range(parts)]
        + edges
        + [pl.BlockSpec(block, lambda i, c=c: (0, 0, c * count + i)) for c in range(halves)]
        + [ANY] * len(tokens),
        out_specs=[across(shape, width) for shape in shapes] + [pl.BlockSpec(block, lambda i: (0, 0, i))] * halves,
        results=[(pltpu.HBM if group[0] == 0 else value)(shape, BF16) for group, shape in zip(groups, shapes)]
        + [value((depth, rows, cols // CHUNKS), BF16)] * halves,
    )(here, *[flat] * (parts + len(edges)), *[sinogram if halves == 0 else far(sinogram)] * halves, *tokens)


def last_block(here_ref, blocks):
    spot = jnp.bitwise_xor(lax.rem(here_ref[0], G), G - 1)
    last = blocks[0]
    for m in range(1, G):
        last = jnp.where(spot == m, blocks[m], last)
    return last


def pack_kernel(here_ref, *refs):
    in_refs, (all_ref, last_ref) = refs[:G], refs[-2:]
    side = in_refs[0].shape[0]
    for m in range(G):
        all_ref[m * side : (m + 1) * side] = in_refs[m][:side]
    last_ref[:side] = last_block(here_ref, [ref[:side] for ref in in_refs])
    if last_ref.shape[0] > side:
        all_ref[G * side :] = in_refs[G - 1][side:]
        last_ref[side:] = in_refs[G - 1][side:]


def pack(here, pieces, more, *tokens):
    side, cols = pieces[0][0].shape
    tile = 512
    shapes = [(G * side + more, cols), (side + more, cols)]
    specs = [across(array.shape, tile) for array in arrays_of(pieces)] if more else piece_specs(pieces, side, tile)
    return call(
        pack_kernel,
        1,
        grid=(cols // tile,),
        in_specs=[SMEM] + specs + [ANY] * len(tokens),
        out_specs=[across(shape, tile) for shape in shapes],
        results=[value(shape, BF16) for shape in shapes],
    )(here, *arrays_of(pieces), *tokens)


def split_kernel(groups, passing, here_ref, own_ref, got_ref, *refs):
    out_refs, wide = refs[-len(groups) - passing - 1 : -1], refs[-1]
    if passing:
        out_refs[-1][...] = refs[0][...]
    depth, rows, cols = own_ref.shape
    place = lax.rem(here_ref[0], G)

    def fill(ref):
        for j in range(cols // LANES):
            wide[j] = ref[:, :, j * LANES : (j + 1) * LANES].astype(F32).reshape(wide.shape[1:])

    @pl.when(place == G - 1)
    def _():
        fill(got_ref)

    @pl.when(place != G - 1)
    def _():
        fill(own_ref)

    for group, out_ref in zip(groups, out_refs):
        for n, m in enumerate(group):
            for j in range(cols // LANES):
                for start, row in rows_of(place, m):
                    block = wide.at[j][pl.ds(row, depth, stride=rows), :].astype(BF16)
                    out_ref[n * depth : (n + 1) * depth, start + j * LANES : start + (j + 1) * LANES] = block


def split_rows(here, own, got, chunk, groups, passing, *tokens):
    depth, rows, cols = own.shape
    first, count = chunk_tiles(chunk, cols)
    block = pl.BlockSpec((depth, rows, TILE), lambda i: (0, 0, first + i))
    shapes = [(len(group) * depth, cols) for group in groups] + [(depth, cols)] * len(passing)
    return call(
        functools.partial(split_kernel, groups, len(passing)),
        2,
        grid=(count,),
        in_specs=[SMEM, block, pl.BlockSpec((depth, rows, TILE), lambda i: (0, 0, i))]
        + piece_specs(passing, depth, ROWS * TILE) + [ANY] * len(tokens),
        out_specs=[across(shape, ROWS * TILE) for shape in shapes],
        results=[value(shape, BF16) for shape in shapes],
        scratch_shapes=[wide_tile(depth * rows)],
    )(here, far(own), got, *arrays_of(passing), *tokens)


def last_kernel(slabs, here_ref, cover_ref, offset_ref, *refs):
    w_ref, vol_ref, sino_ref, *refs = refs
    r_ref, tv_ref, vol, s, r, wide, tv, sem = refs[-8:]
    depth, rows, cols = sino_ref.shape

    count = cols // LANES

    def columns(j):
        return pl.ds(pl.multiple_of(j * LANES, LANES), LANES)

    def arrival(n, j):
        src, dst = ((vol_ref, vol), (sino_ref, s), (tv_ref, tv))[n]
        return pltpu.make_async_copy(src.at[:, :, columns(j)], dst.at[:, :, columns(j)], sem.at[n, j])

    def departure(n, j):
        src, dst = ((r, r_ref), (tv, tv_ref))[n]
        return pltpu.make_async_copy(src.at[:, :, columns(j)], dst.at[:, :, columns(j)], sem.at[3 + n, j])

    @pl.when(here_ref[0] == slabs - 1)
    def _():
        for j in range(count):
            for n in range(3):
                arrival(n, j).start()
        block = w_ref[offset_ref[slabs - 1, 0]]
        block = jnp.where(cover_ref[slabs - 1, 0] == 1, block, jnp.zeros_like(block))
        turned = block.astype(F32).T.astype(BF16)

        def column(j, _):
            at = columns(j)
            for n in range(3):
                arrival(n, j).wait()
            for n, ref in enumerate((s, tv, vol)):
                wide[n] = ref[:, :, at].astype(F32).reshape(wide.shape[1:])
            for row in range(rows):
                spot = pl.ds(row, depth, stride=rows)
                seen = jnp.dot(block, wide.at[2][spot, :].astype(BF16), preferred_element_type=F32)
                resid = (seen - wide.at[0][spot, :]).astype(BF16)
                wide.at[0][spot, :] = resid.astype(F32)
                wide.at[1][spot, :] += jnp.dot(turned, resid, preferred_element_type=F32)
            r[:, :, at] = wide[0].reshape(depth, rows, LANES).astype(BF16)
            tv[:, :, at] = wide[1].reshape(depth, rows, LANES)
            for n in range(2):
                departure(n, j).start()
            return 0

        lax.fori_loop(0, count, column, 0)
        for j in range(count):
            for n in range(2):
                departure(n, j).wait()


def last_group(here, coverage, offsets, weights, volume, sinogram, tv, *tokens):
    slabs = coverage.shape[0]
    depth, rows, cols = sinogram.shape
    return call(
        functools.partial(last_kernel, slabs),
        0,
        vmem=32,
        grid=(1,),
        in_specs=[SMEM, SMEM, SMEM, pl.BlockSpec(weights.shape, lambda i: (0, 0, 0))] + [ANY] * (3 + len(tokens)),
        out_specs=[ANY, ANY],
        results=[pltpu.HBM(sinogram.shape, BF16), pltpu.HBM(volume.shape, F32)],
        input_output_aliases={6: 1},
        scratch_shapes=[
            pltpu.VMEM(volume.shape, F32),
            pltpu.VMEM(sinogram.shape, BF16),
            pltpu.VMEM(sinogram.shape, BF16),
            pltpu.VMEM((3, depth * rows, LANES), F32),
            pltpu.VMEM(volume.shape, F32),
            pltpu.SemaphoreType.DMA((5, cols // LANES)),
        ],
    )(here, coverage, offsets, weights, far(volume), far(sinogram), far(tv), *tokens)


def natural(place, in_refs, wide, j):
    depth = in_refs[0].shape[0]
    rows = ROWS * len(in_refs)
    for m, ref in enumerate(in_refs):
        for start, row in rows_of(place, m):
            value = ref[:, start + j * LANES : start + (j + 1) * LANES].astype(F32)
            wide.at[j][pl.ds(row, depth, stride=rows), :] = value
    return wide[j].reshape(depth, rows, LANES)


def join_kernel(here_ref, *refs):
    in_refs, (out_ref, wide) = refs[:G], refs[-2:]
    for j in range(out_ref.shape[2] // LANES):
        out_ref[:, :, j * LANES : (j + 1) * LANES] = natural(lax.rem(here_ref[0], G), in_refs, wide, j).astype(BF16)


def join_rows(here, pieces, shape, *tokens):
    depth, rows, cols = shape
    _, count = chunk_tiles(0, cols)
    return call(
        join_kernel,
        0,
        grid=(count,),
        in_specs=[SMEM] + piece_specs(pieces, depth, ROWS * TILE) + [ANY] * len(tokens),
        out_specs=pl.BlockSpec((depth, rows, TILE), lambda i: (0, 0, i)),
        results=value((depth, rows, cols // CHUNKS), BF16),
        scratch_shapes=[wide_tile(depth * rows)],
    )(here, *arrays_of(pieces), *tokens)


def settle_kernel(slabs, count, here_ref, own_ref, above_ref, *refs):
    in_refs, (base_ref, out_ref, wide) = refs[:G], refs[-3:]
    step = pl.program_id(0)
    cols = out_ref.shape[2]
    place = lax.rem(here_ref[0], G)
    last = here_ref[0] == slabs - 1

    @pl.when(last)
    def _():
        pltpu.sync_copy(base_ref.at[:, :, pl.ds(pl.multiple_of(step * cols, cols), cols)], out_ref)

    @pl.when(jnp.logical_not(last) & (step < count) & (place == G - 1))
    def _():
        out_ref[...] = above_ref[...]

    @pl.when(jnp.logical_not(last) & (step < count) & (place != G - 1))
    def _():
        out_ref[...] = own_ref[...]

    @pl.when(jnp.logical_not(last) & (step >= count))
    def _():
        for j in range(cols // LANES):
            out_ref[:, :, j * LANES : (j + 1) * LANES] = natural(place, in_refs, wide, j).astype(BF16)


def settle(here, slabs, own, above, pieces, base, *tokens):
    depth, rows, cols = base.shape
    _, count = chunk_tiles(0, cols)
    block = (depth, rows, TILE)
    early = pl.BlockSpec(block, lambda i: (0, 0, jnp.minimum(i, count - 1)))
    late = [
        pl.BlockSpec((depth, ROWS * TILE), lambda i, at=at: (at, jnp.maximum(i - count, 0))) for _, at in pieces
    ]
    return call(
        functools.partial(settle_kernel, slabs, count),
        0,
        grid=(CHUNKS * count,),
        in_specs=[SMEM, early, early] + late + [ANY] * (len(tokens) + 1),
        out_specs=pl.BlockSpec(block, lambda i: (0, 0, i)),
        results=pltpu.HBM(base.shape, BF16),
        scratch_shapes=[wide_tile(depth * rows)],
    )(here, own, above, *arrays_of(pieces), *tokens, far(base))


def finish_kernel(here_ref, tv_ref, *refs):
    in_refs, (out_ref, wide) = refs[:G], refs[-2:]
    for j in range(out_ref.shape[2] // LANES):
        at = pl.ds(j * LANES, LANES)
        out_ref[:, :, at] = tv_ref[:, :, at] + natural(lax.rem(here_ref[0], G), in_refs, wide, j)


def finish(here, chunk, tv, pieces, *tokens):
    depth, rows, cols = tv.shape
    first, count = chunk_tiles(chunk, cols)
    part = pl.BlockSpec((depth, rows, TILE), lambda i: (0, 0, first + i))
    return call(
        finish_kernel,
        0,
        grid=(count,),
        in_specs=[SMEM, part] + piece_specs(pieces, depth, ROWS * TILE) + [ANY] * len(tokens),
        out_specs=part,
        results=pltpu.HBM(tv.shape, F32),
        input_output_aliases={1: 0},
        scratch_shapes=[wide_tile(depth * rows)],
    )(here, far(tv), *arrays_of(pieces), *tokens)


def band_kernel(slabs, span, here_ref, cover_ref, offset_ref, w_ref, *refs):
    proj_ref, back_ref, turned = refs[-3:]
    side = w_ref.shape[1]
    place = lax.rem(here_ref[0], G)
    first = here_ref[0] - place
    zero = jnp.zeros((side, side), BF16)
    for i in range(w_ref.shape[0]):
        turned[i] = w_ref[i].astype(F32).T.astype(BF16)

    def block(ref, i, j):
        k = j - i
        known, step = jnp.clip(i, 0, slabs - 1), jnp.clip(k, 0, span - 1)
        inside = (i >= 0) & (i < slabs) & (j >= 0) & (j < slabs) & (k >= 0) & (k < span)
        live = inside & (cover_ref[known, step] == 1)
        return jnp.where(live, ref[offset_ref[known, step]], zero)

    def slab(m):
        return first + jnp.bitwise_xor(place, m)

    def group(m):
        to = jnp.bitwise_xor(place, m)
        return first + jnp.where(to == G - 1, -1, to)

    seen = [slab(m) for m in range(G)] + [slab(m) + G for m in range(G)] + [first - 1]
    seeing = [group(m) for m in range(G)] + [group(m) - G for m in range(G)] + [first + G - 1]
    for r in range(G):
        for s in range(2 * G + 1):
            at = (pl.ds(r * side, side), pl.ds(s * side, side))
            proj_ref[at] = block(w_ref, group(r), seen[s])
            back_ref[at] = block(turned, seeing[s], slab(r))


def bands(here, coverage, offsets, weights, *tokens):
    slabs, span = coverage.shape
    side = weights.shape[1]
    shape = (G * side, (2 * G + 1) * side)
    return call(
        functools.partial(band_kernel, slabs, span),
        9,
        in_specs=[SMEM, SMEM, SMEM, pl.BlockSpec(weights.shape, lambda i: (0, 0, 0))] + [ANY] * len(tokens),
        grid=(1,),
        out_specs=[pl.BlockSpec(shape, lambda i: (0, 0))] * 2,
        results=[value(shape, BF16)] * 2,
        scratch_shapes=[pltpu.VMEM(weights.shape, BF16)],
    )(here, coverage, offsets, weights, *tokens)


def project_kernel(groups, here_ref, band_ref, own_ref, high_ref, low_ref, *refs):
    sino_refs, (r_ref, down_ref, *group_refs) = refs[:G], refs[-len(groups) - 2 :]
    side = sino_refs[0].shape[0]
    seen = jnp.concatenate([own_ref[...], high_ref[...], low_ref[...]], axis=0)
    total = jnp.dot(band_ref[...], seen, preferred_element_type=F32)
    resid = [(total[m * side : (m + 1) * side] - ref[...].astype(F32)).astype(BF16) for m, ref in enumerate(sino_refs)]
    for m in range(G):
        r_ref[m * side : (m + 1) * side] = resid[m]
    for group, group_ref in zip(groups, group_refs):
        for n, m in enumerate(group):
            group_ref[n * side : (n + 1) * side] = resid[m]
    down_ref[...] = last_block(here_ref, resid)


def project(here, band, own, high, low, sinos, groups, *tokens):
    n, side = band.shape[0], band.shape[0] // G
    cols = own.shape[1]
    tile = 512
    many, one = pl.BlockSpec((n, tile), lambda i: (0, i)), pl.BlockSpec((side, tile), lambda i: (0, i))
    shapes = [(n, cols), (side, cols)] + [(len(group) * side, cols) for group in groups]
    return call(
        functools.partial(project_kernel, groups),
        3,
        grid=(cols // tile,),
        in_specs=[SMEM, pl.BlockSpec(band.shape, lambda i: (0, 0)), many, many, one]
        + piece_specs(sinos, side, tile)
        + [ANY] * len(tokens),
        out_specs=[across(shape, tile) for shape in shapes],
        results=[value(shape, BF16) for shape in shapes],
    )(here, band, own, high, low, *arrays_of(sinos), *tokens)


def back_kernel(dealing, here_ref, band_ref, own_ref, low_ref, high_ref, *refs):
    out_refs = refs[-G:]
    side = high_ref.shape[0]
    seeing = jnp.concatenate([own_ref[...], low_ref[...], high_ref[...]], axis=0)
    total = jnp.dot(band_ref[...], seeing, preferred_element_type=F32)
    place = lax.rem(here_ref[0], G)
    for m, out_ref in enumerate(out_refs):
        out_ref[:side] = total[m * side : (m + 1) * side].astype(BF16)
        if dealing:
            last = jnp.bitwise_xor(place, m) == G - 1
            out_ref[side:] = jnp.where(last, refs[1][...], refs[0][m * side : (m + 1) * side])


def back(here, band, own, low, high, dealt, *tokens):
    n, side = band.shape[0], band.shape[0] // G
    cols = own.shape[1]
    tile = 512
    many = pl.BlockSpec((n, tile), lambda i: (0, i))
    one = pl.BlockSpec((side, tile), lambda i: (0, i))
    out = ((2 if dealt else 1) * side, cols)
    return call(
        functools.partial(back_kernel, bool(dealt)),
        0,
        grid=(cols // tile,),
        in_specs=[SMEM, pl.BlockSpec(band.shape, lambda i: (0, 0)), many, many, one]
        + ([many, one] if dealt else [])
        + [ANY] * len(tokens),
        out_specs=[across(out, tile)] * G,
        results=[value(out, BF16)] * G,
    )(here, band, own, low, high, *dealt, *tokens)


def tv_flux(cur, above):
    rows, cols = cur.shape
    row = lax.broadcasted_iota(jnp.int32, (rows, cols), 0)
    col = lax.broadcasted_iota(jnp.int32, (rows, cols), 1)
    dz = above - cur
    dy = jnp.where(row == rows - 1, 0.0, pltpu.roll(cur, rows - 1, 0)) - cur
    dx = jnp.where(col == cols - 1, 0.0, pltpu.roll(cur, cols - 1, 1)) - cur
    scale = 0.5 * lax.rsqrt(dz * dz + dy * dy + dx * dx + 0.25)
    return dz * scale, dy * scale, dx * scale


def tv_below(cur, above):
    return tv_flux(cur, above)[0]


def tv_slice(cur, above, below_flux):
    rows, cols = cur.shape
    row = lax.broadcasted_iota(jnp.int32, (rows, cols), 0)
    col = lax.broadcasted_iota(jnp.int32, (rows, cols), 1)
    fz, fy, fx = tv_flux(cur, above)
    sides = 0.5 * cur * lax.rsqrt(cur * cur + 0.25)
    fy_low = jnp.where(row == 0, sides, pltpu.roll(fy, 1, 0))
    fx_low = jnp.where(col == 0, sides, pltpu.roll(fx, 1, 1))
    return (below_flux - fz) + (fy_low - fy) + (fx_low - fx), fz


def tv_kernel(here_ref, near_ref, next_level_ref, far_ref, last_level_ref, next_ref, vol_ref, *refs):
    out_ref, done_ref, flux_ref = refs[-3:]
    step = pl.program_id(0)
    deep, rows, _ = vol_ref.shape
    place = lax.rem(here_ref[0], G)

    @pl.when(step == 0)
    def _():
        inside = jnp.where(place == 2, far_ref[...], near_ref[...])
        low = jnp.where(place == 0, last_level_ref[...], inside)[rows:].astype(F32)
        flux_ref[...] = tv_below(low, vol_ref[0])

    def body(z, flux):
        out_ref[z], flux = tv_slice(vol_ref[z], vol_ref[z + 1], flux)
        return flux

    flux = lax.fori_loop(0, deep - 1, body, flux_ref[...], unroll=5)
    inside = jnp.where(place == 1, far_ref[...], near_ref[...])
    high = jnp.where(place == G - 1, next_level_ref[...], inside)[:rows].astype(F32)
    above = jnp.where(step == pl.num_programs(0) - 1, high, next_ref[0])
    out_ref[deep - 1], flux_ref[...] = tv_slice(vol_ref[deep - 1], above, flux)
    done_ref[...] = flux_ref[:, : done_ref.shape[1]]


def half_tv(here, volume, ends, *tokens):
    depth, rows, cols = volume.shape
    deep = 16
    edges = [pl.BlockSpec((2 * rows, cols), lambda i, last=end.shape[0] // (2 * rows) - 1: (last, 0)) for end in ends]
    body = pl.BlockSpec((deep, rows, cols), lambda i: (i, 0, 0))
    after = pl.BlockSpec((1, rows, cols), lambda i: (jnp.minimum((i + 1) * deep, depth - 1), 0, 0))
    return call(
        tv_kernel,
        0,
        grid=(depth // deep,),
        in_specs=[SMEM] + edges + [after, body] + [ANY] * len(tokens),
        out_specs=[body, pl.BlockSpec((rows, LANES), lambda i: (0, 0))],
        results=[pltpu.HBM(volume.shape, F32), value((rows, LANES), F32)],
        scratch_shapes=[pltpu.VMEM((rows, cols), F32)],
    )(here, *ends, far(volume), far(volume), *tokens)


def local(volume, sinogram, weights, coverage, offsets):
    slabs = lax.axis_size("slab")
    here = lax.axis_index("slab").astype(jnp.int32).reshape(1)
    depth, rows, _ = volume.shape
    single = ((0,), (1,), (2,), (3,))
    paired = ((0,), (1,), (2, 3))

    def tied(array, *others):
        return lax.optimization_barrier((array, *others))[0]

    def beyond(over, *others):
        return swapped(tied(over, *others)[depth:], 1)

    vols0 = cast_rows(here, volume, 0, single, True, None)
    got_vols0 = direct(vols0)
    v0, v1, v23, sent0, sent1 = cast_rows(here, volume, 1, paired, False, sinogram, vols0[1])
    got0 = moved(sent0, G, only=G - 1)
    over = swapped(v23, 2)
    band_p, band_b = bands(here, coverage, offsets, weights, v1)
    own0, edge0 = pack(here, [(array, 0) for array in got_vols0], 2 * rows, band_p)
    high0, near = moved(own0, -G), swapped(tied(v1, own0), 1)
    got1 = moved(tied(sent1, own0), G, only=G - 1)
    s0, s1, s23, over_beyond = split_rows(here, sinogram, got0, 0, paired, [(over, 1)], near)
    s_near, s_over = swapped(s1, 1), swapped(s23, 2)
    low0 = moved(tied(edge0, s_near), G)
    own1, edge1 = pack(here, [(v0, 0), (near, 0), (over, 0), (swapped(over_beyond, 1), 0)], 0)
    low1, high1 = moved(edge1, G), moved(own1, -G)
    sinos0 = [(s0, 0), (s_near, 0), (s_over, 0), (beyond(s_over, own1), 0)]

    s0, s1, s23 = split_rows(here, sinogram, got1, 1, paired, [], own1)

    resid0, down0, *r = project(here, band_p, own0, high0, low0, sinos0, single[1:], low1, s0)
    from_low0, from_high0 = moved(resid0, G), moved(down0, -G)
    s_near, s_over = swapped(s1, 1), swapped(s23, 2)
    got_r = [swapped(tied(array, s_near), m + 1) for m, array in enumerate(r)]
    tv, tv_done = half_tv(here, volume, [got_vols0[1], high0, got_vols0[3], low0], resid0)
    sinos1 = [(s0, 0), (s_near, 0), (s_over, 0), (beyond(s_over, tv_done), 0)]
    resid1, down1 = project(here, band_p, own1, high1, low1, sinos1, (), tv_done, *got_r)
    from_low1, from_high1 = moved(resid1, G), moved(down1, -G)

    backs0 = back(here, band_b, resid0, from_low0, from_high0, [resid1, from_high1])
    got_backs0 = direct(backs0)
    r_pieces = [(array, 0) for array in [resid0] + got_r]
    natural0 = join_rows(here, r_pieces, sinogram.shape, backs0[0])
    above0 = moved(natural0, -G, only=G - 1)
    r_last, tv = last_group(here, coverage, offsets, weights, volume, sinogram, tv, backs0[0])
    backs1 = back(here, band_b, resid1, from_low1, from_high1, [], far(r_last), natural0)
    got_backs1 = direct(backs1)
    gradient = finish(here, 0, tv, [(array, 0) for array in got_backs0], backs1[0])
    residual = settle(here, slabs, natural0, above0, [(array, 1) for array in got_backs0], r_last, backs1[0])
    gradient = finish(here, 1, gradient, [(array, 0) for array in got_backs1], far(residual))
    return (gradient, residual)


def solution(mesh):
    placed = (P("slab", "grp", None), P("slab", "grp", None), P(), P(), P())
    return jax.shard_map(
        local,
        mesh=mesh,
        in_specs=placed,
        out_specs=(P("slab", "grp", None), P("slab", "grp", None)),
        check_vma=False,
    )
```

```python
import functools

import jax
import jax.numpy as jnp
from jax import lax
from jax.experimental import pallas as pl
from jax.experimental.pallas import tpu as pltpu
from jax.sharding import PartitionSpec as P

G = 4
CHUNKS = 2
ROWS = 2
TILE = 256
F32 = jnp.float32
BF16 = jnp.bfloat16
MIB = 1024 * 1024
LANES = 128
SMEM = pl.BlockSpec(memory_space=pltpu.SMEM)
VMEM = pl.BlockSpec(memory_space=pltpu.VMEM)
ANY = pl.BlockSpec(memory_space=pl.ANY)


def moved(value, steps, only=None):
    count = lax.axis_size("slab")
    first, last = max(0, -steps), min(count, count - steps)
    pairs = [(i, i + steps) for i in range(first, last) if only is None or i % G == only]
    return lax.ppermute(value, "slab", pairs)


def swapped(value, bits):
    count = lax.axis_size("slab")
    return lax.ppermute(value, "slab", [(i, i ^ bits) for i in range(count)])


def direct(arrays):
    return [array if m == 0 else swapped(array, m) for m, array in enumerate(arrays)]


def call(kernel, us, *, results, vmem=16, **how):
    return pl.pallas_call(
        kernel,
        out_shape=results,
        compiler_params=pltpu.CompilerParams(vmem_limit_bytes=vmem * MIB),
        cost_estimate=pl.CostEstimate(flops=int(us * 1.15e9), bytes_accessed=1000, transcendentals=0),
        **how,
    )


def value(shape, dtype):
    return jax.ShapeDtypeStruct(shape, dtype)


def far(array):
    return pltpu.with_memory_space_constraint(array, pltpu.HBM)


def across(shape, tile):
    block = shape[:-1] + (tile,)
    return pl.BlockSpec(block, lambda i: (0,) * (len(shape) - 1) + (i,))


def piece_specs(pieces, side, tile):
    return [pl.BlockSpec((side, tile), lambda i, at=at: (at, i)) for _, at in pieces]


def arrays_of(pieces):
    return [array for array, _ in pieces]


def rows_of(place, m):
    first = ROWS * jnp.bitwise_xor(place, m)
    return [(h * TILE, first + h) for h in range(ROWS)]


def wide_tile(rows_deep):
    return pltpu.VMEM((TILE // LANES, rows_deep, LANES), F32)


def chunk_tiles(chunk, cols):
    count = cols // CHUNKS // TILE
    return chunk * count, count


def cast_kernel(groups, ends, halves, here_ref, *refs):
    parts = TILE // LANES
    vol_refs, end_refs = refs[:parts], refs[parts : parts + ends]
    for half_ref, sent_ref in zip(refs[parts + ends : parts + ends + halves], refs[len(refs) - halves :]):
        sent_ref[...] = half_ref[...]
    out_refs = refs[len(refs) - halves - len(groups) : len(refs) - halves]
    rows = ROWS * G
    depth = vol_refs[0].shape[0] // rows
    place = lax.rem(here_ref[0], G)
    for j, vol_ref in enumerate(vol_refs):
        for group, out_ref in zip(groups, out_refs):
            for n, m in enumerate(group):
                for start, row in rows_of(place, m):
                    at = pl.ds(start + j * LANES, LANES)
                    out_ref[n * depth : (n + 1) * depth, at] = vol_ref[pl.ds(row, depth, stride=rows), :].astype(BF16)
    if ends:
        both = jnp.concatenate([ref[...] for ref in end_refs], axis=0).astype(BF16)
        for group, out_ref in zip(groups, out_refs):
            if group[0] % 2:
                out_ref[depth:, :] = both


def cast_rows(here, volume, chunk, groups, ends, sinogram, *tokens):
    depth, rows, cols = volume.shape
    flat = far(volume.reshape(depth * rows, cols))
    first, count = chunk_tiles(chunk, cols)
    parts, width = TILE // LANES, ROWS * TILE
    shapes = [(len(group) * depth + (2 * rows if ends and group[0] % 2 else 0), cols) for group in groups]
    edges = [pl.BlockSpec((rows, width), lambda i, z=z: (z, i)) for z in (0, depth - 1)] if ends else []
    halves = 0 if sinogram is None else CHUNKS
    block = (depth, rows, TILE)
    return call(
        functools.partial(cast_kernel, groups, len(edges), halves),
        2,
        grid=(count,),
        in_specs=[SMEM]
        + [pl.BlockSpec((depth * rows, LANES), lambda i, j=j: (0, (first + i) * parts + j)) for j in range(parts)]
        + edges
        + [pl.BlockSpec(block, lambda i, c=c: (0, 0, c * count + i)) for c in range(halves)]
        + [ANY] * len(tokens),
        out_specs=[across(shape, width) for shape in shapes] + [pl.BlockSpec(block, lambda i: (0, 0, i))] * halves,
        results=[(pltpu.HBM if group[0] == 0 else value)(shape, BF16) for group, shape in zip(groups, shapes)]
        + [value((depth, rows, cols // CHUNKS), BF16)] * halves,
    )(here, *[flat] * (parts + len(edges)), *[sinogram if halves == 0 else far(sinogram)] * halves, *tokens)


def last_block(here_ref, blocks):
    spot = jnp.bitwise_xor(lax.rem(here_ref[0], G), G - 1)
    last = blocks[0]
    for m in range(1, G):
        last = jnp.where(spot == m, blocks[m], last)
    return last


def pack_kernel(here_ref, *refs):
    in_refs, (all_ref, last_ref) = refs[:G], refs[-2:]
    side = in_refs[0].shape[0]
    for m in range(G):
        all_ref[m * side : (m + 1) * side] = in_refs[m][:side]
    last_ref[:side] = last_block(here_ref, [ref[:side] for ref in in_refs])
    if last_ref.shape[0] > side:
        all_ref[G * side :] = in_refs[G - 1][side:]
        last_ref[side:] = in_refs[G - 1][side:]


def pack(here, pieces, more, *tokens):
    side, cols = pieces[0][0].shape
    tile = 512
    shapes = [(G * side + more, cols), (side + more, cols)]
    specs = [across(array.shape, tile) for array in arrays_of(pieces)] if more else piece_specs(pieces, side, tile)
    return call(
        pack_kernel,
        1,
        grid=(cols // tile,),
        in_specs=[SMEM] + specs + [ANY] * len(tokens),
        out_specs=[across(shape, tile) for shape in shapes],
        results=[value(shape, BF16) for shape in shapes],
    )(here, *arrays_of(pieces), *tokens)


def split_kernel(groups, passing, here_ref, own_ref, got_ref, *refs):
    out_refs, wide = refs[-len(groups) - passing - 1 : -1], refs[-1]
    if passing:
        out_refs[-1][...] = refs[0][...]
    depth, rows, cols = own_ref.shape
    place = lax.rem(here_ref[0], G)

    def fill(ref):
        for j in range(cols // LANES):
            wide[j] = ref[:, :, j * LANES : (j + 1) * LANES].astype(F32).reshape(wide.shape[1:])

    @pl.when(place == G - 1)
    def _():
        fill(got_ref)

    @pl.when(place != G - 1)
    def _():
        fill(own_ref)

    for group, out_ref in zip(groups, out_refs):
        for n, m in enumerate(group):
            for j in range(cols // LANES):
                for start, row in rows_of(place, m):
                    block = wide.at[j][pl.ds(row, depth, stride=rows), :].astype(BF16)
                    out_ref[n * depth : (n + 1) * depth, start + j * LANES : start + (j + 1) * LANES] = block


def split_rows(here, own, got, chunk, groups, passing, *tokens):
    depth, rows, cols = own.shape
    first, count = chunk_tiles(chunk, cols)
    block = pl.BlockSpec((depth, rows, TILE), lambda i: (0, 0, first + i))
    shapes = [(len(group) * depth, cols) for group in groups] + [(depth, cols)] * len(passing)
    return call(
        functools.partial(split_kernel, groups, len(passing)),
        2,
        grid=(count,),
        in_specs=[SMEM, block, pl.BlockSpec((depth, rows, TILE), lambda i: (0, 0, i))]
        + piece_specs(passing, depth, ROWS * TILE) + [ANY] * len(tokens),
        out_specs=[across(shape, ROWS * TILE) for shape in shapes],
        results=[value(shape, BF16) for shape in shapes],
        scratch_shapes=[wide_tile(depth * rows)],
    )(here, far(own), got, *arrays_of(passing), *tokens)


def last_kernel(slabs, here_ref, cover_ref, offset_ref, *refs):
    w_ref, vol_ref, sino_ref, *refs = refs
    r_ref, tv_ref, vol, s, r, wide, tv, sem = refs[-8:]
    depth, rows, cols = sino_ref.shape

    count = cols // LANES

    def columns(j):
        return pl.ds(pl.multiple_of(j * LANES, LANES), LANES)

    def arrival(n, j):
        src, dst = ((vol_ref, vol), (sino_ref, s), (tv_ref, tv))[n]
        return pltpu.make_async_copy(src.at[:, :, columns(j)], dst.at[:, :, columns(j)], sem.at[n, j])

    def departure(n, j):
        src, dst = ((r, r_ref), (tv, tv_ref))[n]
        return pltpu.make_async_copy(src.at[:, :, columns(j)], dst.at[:, :, columns(j)], sem.at[3 + n, j])

    @pl.when(here_ref[0] == slabs - 1)
    def _():
        for j in range(count):
            for n in range(3):
                arrival(n, j).start()
        block = w_ref[offset_ref[slabs - 1, 0]]
        block = jnp.where(cover_ref[slabs - 1, 0] == 1, block, jnp.zeros_like(block))
        turned = block.astype(F32).T.astype(BF16)

        def column(j, _):
            at = columns(j)
            for n in range(3):
                arrival(n, j).wait()
            for n, ref in enumerate((s, tv, vol)):
                wide[n] = ref[:, :, at].astype(F32).reshape(wide.shape[1:])
            for row in range(rows):
                spot = pl.ds(row, depth, stride=rows)
                seen = jnp.dot(block, wide.at[2][spot, :].astype(BF16), preferred_element_type=F32)
                resid = (seen - wide.at[0][spot, :]).astype(BF16)
                wide.at[0][spot, :] = resid.astype(F32)
                wide.at[1][spot, :] += jnp.dot(turned, resid, preferred_element_type=F32)
            r[:, :, at] = wide[0].reshape(depth, rows, LANES).astype(BF16)
            tv[:, :, at] = wide[1].reshape(depth, rows, LANES)
            for n in range(2):
                departure(n, j).start()
            return 0

        lax.fori_loop(0, count, column, 0)
        for j in range(count):
            for n in range(2):
                departure(n, j).wait()


def last_group(here, coverage, offsets, weights, volume, sinogram, tv, *tokens):
    slabs = coverage.shape[0]
    depth, rows, cols = sinogram.shape
    return call(
        functools.partial(last_kernel, slabs),
        0,
        vmem=32,
        grid=(1,),
        in_specs=[SMEM, SMEM, SMEM, pl.BlockSpec(weights.shape, lambda i: (0, 0, 0))] + [ANY] * (3 + len(tokens)),
        out_specs=[ANY, ANY],
        results=[pltpu.HBM(sinogram.shape, BF16), pltpu.HBM(volume.shape, F32)],
        input_output_aliases={6: 1},
        scratch_shapes=[
            pltpu.VMEM(volume.shape, F32),
            pltpu.VMEM(sinogram.shape, BF16),
            pltpu.VMEM(sinogram.shape, BF16),
            pltpu.VMEM((3, depth * rows, LANES), F32),
            pltpu.VMEM(volume.shape, F32),
            pltpu.SemaphoreType.DMA((5, cols // LANES)),
        ],
    )(here, coverage, offsets, weights, far(volume), far(sinogram), far(tv), *tokens)


def natural(place, in_refs, wide, j):
    depth = in_refs[0].shape[0]
    rows = ROWS * len(in_refs)
    for m, ref in enumerate(in_refs):
        for start, row in rows_of(place, m):
            value = ref[:, start + j * LANES : start + (j + 1) * LANES].astype(F32)
            wide.at[j][pl.ds(row, depth, stride=rows), :] = value
    return wide[j].reshape(depth, rows, LANES)


def join_kernel(here_ref, *refs):
    in_refs, (out_ref, wide) = refs[:G], refs[-2:]
    for j in range(out_ref.shape[2] // LANES):
        out_ref[:, :, j * LANES : (j + 1) * LANES] = natural(lax.rem(here_ref[0], G), in_refs, wide, j).astype(BF16)


def join_rows(here, pieces, shape, *tokens):
    depth, rows, cols = shape
    _, count = chunk_tiles(0, cols)
    return call(
        join_kernel,
        0,
        grid=(count,),
        in_specs=[SMEM] + piece_specs(pieces, depth, ROWS * TILE) + [ANY] * len(tokens),
        out_specs=pl.BlockSpec((depth, rows, TILE), lambda i: (0, 0, i)),
        results=value((depth, rows, cols // CHUNKS), BF16),
        scratch_shapes=[wide_tile(depth * rows)],
    )(here, *arrays_of(pieces), *tokens)


def settle_kernel(slabs, count, here_ref, own_ref, above_ref, *refs):
    in_refs, (base_ref, out_ref, wide) = refs[:G], refs[-3:]
    step = pl.program_id(0)
    cols = out_ref.shape[2]
    place = lax.rem(here_ref[0], G)
    last = here_ref[0] == slabs - 1

    @pl.when(last)
    def _():
        pltpu.sync_copy(base_ref.at[:, :, pl.ds(pl.multiple_of(step * cols, cols), cols)], out_ref)

    @pl.when(jnp.logical_not(last) & (step < count) & (place == G - 1))
    def _():
        out_ref[...] = above_ref[...]

    @pl.when(jnp.logical_not(last) & (step < count) & (place != G - 1))
    def _():
        out_ref[...] = own_ref[...]

    @pl.when(jnp.logical_not(last) & (step >= count))
    def _():
        for j in range(cols // LANES):
            out_ref[:, :, j * LANES : (j + 1) * LANES] = natural(place, in_refs, wide, j).astype(BF16)


def settle(here, slabs, own, above, pieces, base, *tokens):
    depth, rows, cols = base.shape
    _, count = chunk_tiles(0, cols)
    block = (depth, rows, TILE)
    early = pl.BlockSpec(block, lambda i: (0, 0, jnp.minimum(i, count - 1)))
    late = [
        pl.BlockSpec((depth, ROWS * TILE), lambda i, at=at: (at, jnp.maximum(i - count, 0))) for _, at in pieces
    ]
    return call(
        functools.partial(settle_kernel, slabs, count),
        0,
        grid=(CHUNKS * count,),
        in_specs=[SMEM, early, early] + late + [ANY] * (len(tokens) + 1),
        out_specs=pl.BlockSpec(block, lambda i: (0, 0, i)),
        results=pltpu.HBM(base.shape, BF16),
        scratch_shapes=[wide_tile(depth * rows)],
    )(here, own, above, *arrays_of(pieces), *tokens, far(base))


def finish_kernel(here_ref, tv_ref, *refs):
    in_refs, (out_ref, wide) = refs[:G], refs[-2:]
    for j in range(out_ref.shape[2] // LANES):
        at = pl.ds(j * LANES, LANES)
        out_ref[:, :, at] = tv_ref[:, :, at] + natural(lax.rem(here_ref[0], G), in_refs, wide, j)


def finish(here, chunk, tv, pieces, *tokens):
    depth, rows, cols = tv.shape
    first, count = chunk_tiles(chunk, cols)
    cuts = 2
    deep = depth // cuts
    part = pl.BlockSpec((deep, rows, TILE), lambda i, z: (z, 0, first + i))
    blocks = [pl.BlockSpec((deep, ROWS * TILE), lambda i, z, at=at: (at * cuts + z, i)) for _, at in pieces]
    return call(
        finish_kernel,
        0,
        grid=(count, cuts),
        in_specs=[SMEM, part] + blocks + [ANY] * len(tokens),
        out_specs=part,
        results=pltpu.HBM(tv.shape, F32),
        input_output_aliases={1: 0},
        scratch_shapes=[wide_tile(deep * rows)],
    )(here, far(tv), *arrays_of(pieces), *tokens)


def band_kernel(slabs, span, here_ref, cover_ref, offset_ref, w_ref, *refs):
    proj_ref, back_ref, turned = refs[-3:]
    side = w_ref.shape[1]
    place = lax.rem(here_ref[0], G)
    first = here_ref[0] - place
    zero = jnp.zeros((side, side), BF16)
    for i in range(w_ref.shape[0]):
        turned[i] = w_ref[i].astype(F32).T.astype(BF16)

    def block(ref, i, j):
        k = j - i
        known, step = jnp.clip(i, 0, slabs - 1), jnp.clip(k, 0, span - 1)
        inside = (i >= 0) & (i < slabs) & (j >= 0) & (j < slabs) & (k >= 0) & (k < span)
        live = inside & (cover_ref[known, step] == 1)
        return jnp.where(live, ref[offset_ref[known, step]], zero)

    def slab(m):
        return first + jnp.bitwise_xor(place, m)

    def group(m):
        to = jnp.bitwise_xor(place, m)
        return first + jnp.where(to == G - 1, -1, to)

    seen = [slab(m) for m in range(G)] + [slab(m) + G for m in range(G)] + [first - 1]
    seeing = [group(m) for m in range(G)] + [group(m) - G for m in range(G)] + [first + G - 1]
    for r in range(G):
        for s in range(2 * G + 1):
            at = (pl.ds(r * side, side), pl.ds(s * side, side))
            proj_ref[at] = block(w_ref, group(r), seen[s])
            back_ref[at] = block(turned, seeing[s], slab(r))


def bands(here, coverage, offsets, weights, *tokens):
    slabs, span = coverage.shape
    side = weights.shape[1]
    shape = (G * side, (2 * G + 1) * side)
    return call(
        functools.partial(band_kernel, slabs, span),
        9,
        in_specs=[SMEM, SMEM, SMEM, pl.BlockSpec(weights.shape, lambda i: (0, 0, 0))] + [ANY] * len(tokens),
        grid=(1,),
        out_specs=[pl.BlockSpec(shape, lambda i: (0, 0))] * 2,
        results=[value(shape, BF16)] * 2,
        scratch_shapes=[pltpu.VMEM(weights.shape, BF16)],
    )(here, coverage, offsets, weights, *tokens)


def project_kernel(groups, here_ref, band_ref, own_ref, high_ref, low_ref, *refs):
    sino_refs, (r_ref, down_ref, *group_refs) = refs[:G], refs[-len(groups) - 2 :]
    side = sino_refs[0].shape[0]
    seen = jnp.concatenate([own_ref[...], high_ref[...], low_ref[...]], axis=0)
    total = jnp.dot(band_ref[...], seen, preferred_element_type=F32)
    resid = [(total[m * side : (m + 1) * side] - ref[...].astype(F32)).astype(BF16) for m, ref in enumerate(sino_refs)]
    for m in range(G):
        r_ref[m * side : (m + 1) * side] = resid[m]
    for group, group_ref in zip(groups, group_refs):
        for n, m in enumerate(group):
            group_ref[n * side : (n + 1) * side] = resid[m]
    down_ref[...] = last_block(here_ref, resid)


def project(here, band, own, high, low, sinos, groups, *tokens):
    n, side = band.shape[0], band.shape[0] // G
    cols = own.shape[1]
    tile = 512
    many, one = pl.BlockSpec((n, tile), lambda i: (0, i)), pl.BlockSpec((side, tile), lambda i: (0, i))
    shapes = [(n, cols), (side, cols)] + [(len(group) * side, cols) for group in groups]
    return call(
        functools.partial(project_kernel, groups),
        3,
        grid=(cols // tile,),
        in_specs=[SMEM, pl.BlockSpec(band.shape, lambda i: (0, 0)), many, many, one]
        + piece_specs(sinos, side, tile)
        + [ANY] * len(tokens),
        out_specs=[across(shape, tile) for shape in shapes],
        results=[value(shape, BF16) for shape in shapes],
    )(here, band, own, high, low, *arrays_of(sinos), *tokens)


def back_kernel(dealing, here_ref, band_ref, own_ref, low_ref, high_ref, *refs):
    out_refs = refs[-G:]
    side = high_ref.shape[0]
    seeing = jnp.concatenate([own_ref[...], low_ref[...], high_ref[...]], axis=0)
    total = jnp.dot(band_ref[...], seeing, preferred_element_type=F32)
    place = lax.rem(here_ref[0], G)
    for m, out_ref in enumerate(out_refs):
        out_ref[:side] = total[m * side : (m + 1) * side].astype(BF16)
        if dealing:
            last = jnp.bitwise_xor(place, m) == G - 1
            out_ref[side:] = jnp.where(last, refs[1][...], refs[0][m * side : (m + 1) * side])


def back(here, band, own, low, high, dealt, *tokens):
    n, side = band.shape[0], band.shape[0] // G
    cols = own.shape[1]
    tile = 512
    many = pl.BlockSpec((n, tile), lambda i: (0, i))
    one = pl.BlockSpec((side, tile), lambda i: (0, i))
    out = ((2 if dealt else 1) * side, cols)
    return call(
        functools.partial(back_kernel, bool(dealt)),
        0,
        grid=(cols // tile,),
        in_specs=[SMEM, pl.BlockSpec(band.shape, lambda i: (0, 0)), many, many, one]
        + ([many, one] if dealt else [])
        + [ANY] * len(tokens),
        out_specs=[across(out, tile)] * G,
        results=[value(out, BF16)] * G,
    )(here, band, own, low, high, *dealt, *tokens)


def tv_flux(cur, above):
    rows, cols = cur.shape
    row = lax.broadcasted_iota(jnp.int32, (rows, cols), 0)
    col = lax.broadcasted_iota(jnp.int32, (rows, cols), 1)
    dz = above - cur
    dy = jnp.where(row == rows - 1, 0.0, pltpu.roll(cur, rows - 1, 0)) - cur
    dx = jnp.where(col == cols - 1, 0.0, pltpu.roll(cur, cols - 1, 1)) - cur
    scale = 0.5 * lax.rsqrt(dz * dz + dy * dy + dx * dx + 0.25)
    return dz * scale, dy * scale, dx * scale


def tv_below(cur, above):
    return tv_flux(cur, above)[0]


def tv_slice(cur, above, below_flux):
    rows, cols = cur.shape
    row = lax.broadcasted_iota(jnp.int32, (rows, cols), 0)
    col = lax.broadcasted_iota(jnp.int32, (rows, cols), 1)
    fz, fy, fx = tv_flux(cur, above)
    sides = 0.5 * cur * lax.rsqrt(cur * cur + 0.25)
    fy_low = jnp.where(row == 0, sides, pltpu.roll(fy, 1, 0))
    fx_low = jnp.where(col == 0, sides, pltpu.roll(fx, 1, 1))
    return (below_flux - fz) + (fy_low - fy) + (fx_low - fx), fz


def tv_kernel(here_ref, near_ref, next_level_ref, far_ref, last_level_ref, next_ref, vol_ref, *refs):
    out_ref, done_ref, flux_ref = refs[-3:]
    step = pl.program_id(0)
    deep, rows, _ = vol_ref.shape
    place = lax.rem(here_ref[0], G)

    @pl.when(step == 0)
    def _():
        inside = jnp.where(place == 2, far_ref[...], near_ref[...])
        low = jnp.where(place == 0, last_level_ref[...], inside)[rows:].astype(F32)
        flux_ref[...] = tv_below(low, vol_ref[0])

    def body(z, flux):
        out_ref[z], flux = tv_slice(vol_ref[z], vol_ref[z + 1], flux)
        return flux

    flux = lax.fori_loop(0, deep - 1, body, flux_ref[...], unroll=5)
    inside = jnp.where(place == 1, far_ref[...], near_ref[...])
    high = jnp.where(place == G - 1, next_level_ref[...], inside)[:rows].astype(F32)
    above = jnp.where(step == pl.num_programs(0) - 1, high, next_ref[0])
    out_ref[deep - 1], flux_ref[...] = tv_slice(vol_ref[deep - 1], above, flux)
    done_ref[...] = flux_ref[:, : done_ref.shape[1]]


def half_tv(here, volume, ends, *tokens):
    depth, rows, cols = volume.shape
    deep = 16
    edges = [pl.BlockSpec((2 * rows, cols), lambda i, last=end.shape[0] // (2 * rows) - 1: (last, 0)) for end in ends]
    body = pl.BlockSpec((deep, rows, cols), lambda i: (i, 0, 0))
    after = pl.BlockSpec((1, rows, cols), lambda i: (jnp.minimum((i + 1) * deep, depth - 1), 0, 0))
    return call(
        tv_kernel,
        0,
        grid=(depth // deep,),
        in_specs=[SMEM] + edges + [after, body] + [ANY] * len(tokens),
        out_specs=[body, pl.BlockSpec((rows, LANES), lambda i: (0, 0))],
        results=[pltpu.HBM(volume.shape, F32), value((rows, LANES), F32)],
        scratch_shapes=[pltpu.VMEM((rows, cols), F32)],
    )(here, *ends, far(volume), far(volume), *tokens)


def local(volume, sinogram, weights, coverage, offsets):
    slabs = lax.axis_size("slab")
    here = lax.axis_index("slab").astype(jnp.int32).reshape(1)
    depth, rows, _ = volume.shape
    single = ((0,), (1,), (2,), (3,))
    paired = ((0,), (1,), (2, 3))

    def tied(array, *others):
        return lax.optimization_barrier((array, *others))[0]

    def beyond(over, *others):
        return swapped(tied(over, *others)[depth:], 1)

    vols0 = cast_rows(here, volume, 0, single, True, None)
    got_vols0 = direct(vols0)
    v0, v1, v23, sent0, sent1 = cast_rows(here, volume, 1, paired, False, sinogram, vols0[1])
    got0 = moved(sent0, G, only=G - 1)
    over = swapped(v23, 2)
    band_p, band_b = bands(here, coverage, offsets, weights, v1)
    own0, edge0 = pack(here, [(array, 0) for array in got_vols0], 2 * rows, band_p)
    high0, near = moved(own0, -G), swapped(tied(v1, own0), 1)
    got1 = moved(tied(sent1, own0), G, only=G - 1)
    s0, s1, s23, over_beyond = split_rows(here, sinogram, got0, 0, paired, [(over, 1)], near)
    s_near, s_over = swapped(s1, 1), swapped(s23, 2)
    low0 = moved(tied(edge0, s_near), G)
    own1, edge1 = pack(here, [(v0, 0), (near, 0), (over, 0), (swapped(over_beyond, 1), 0)], 0)
    low1, high1 = moved(edge1, G), moved(own1, -G)
    t0, t1, t23 = split_rows(here, sinogram, got1, 1, paired, [], own1)
    sinos0 = [(s0, 0), (s_near, 0), (s_over, 0), (beyond(s_over, t0), 0)]


    resid0, down0, r1, r23 = project(here, band_p, own0, high0, low0, sinos0, paired[1:], low1)
    from_low0, from_high0 = moved(resid0, G), moved(down0, -G)
    t_near, t_over = swapped(t1, 1), swapped(t23, 2)
    r_near, r_over = swapped(tied(r1, t_near), 1), swapped(tied(r23, t_near), 2)
    tv, tv_done = half_tv(here, volume, [got_vols0[1], high0, got_vols0[3], low0], resid0)
    sinos1 = [(t0, 0), (t_near, 0), (t_over, 0), (beyond(t_over, tv_done), 0)]
    resid1, down1 = project(here, band_p, own1, high1, low1, sinos1, (), tv_done, r_near, r_over)
    from_low1, from_high1 = moved(resid1, G), moved(down1, -G)

    backs0 = back(here, band_b, resid0, from_low0, from_high0, [resid1, from_high1])
    got_backs0 = direct(backs0)
    r_pieces = [(resid0, 0), (r_near, 0), (r_over, 0), (beyond(r_over, resid1), 0)]
    natural0 = join_rows(here, r_pieces, sinogram.shape, backs0[0])
    above0 = moved(natural0, -G, only=G - 1)
    r_last, tv = last_group(here, coverage, offsets, weights, volume, sinogram, tv, backs0[0])
    backs1 = back(here, band_b, resid1, from_low1, from_high1, [], far(r_last), natural0)
    got_backs1 = direct(backs1)
    gradient = finish(here, 0, tv, [(array, 0) for array in got_backs0], backs1[0])
    residual = settle(here, slabs, natural0, above0, [(array, 1) for array in got_backs0], r_last, backs1[0])
    gradient = finish(here, 1, gradient, [(array, 0) for array in got_backs1], far(residual))
    return (gradient, residual)


def solution(mesh):
    placed = (P("slab", "grp", None), P("slab", "grp", None), P(), P(), P())
    return jax.shard_map(
        local,
        mesh=mesh,
        in_specs=placed,
        out_specs=(P("slab", "grp", None), P("slab", "grp", None)),
        check_vma=False,
    )
```

```python
import functools

import jax
import jax.numpy as jnp
from jax import lax
from jax.experimental import pallas as pl
from jax.experimental.pallas import tpu as pltpu
from jax.sharding import PartitionSpec as P

G = 4
CHUNKS = 2
ROWS = 2
TILE = 256
F32 = jnp.float32
BF16 = jnp.bfloat16
MIB = 1024 * 1024
LANES = 128
SMEM = pl.BlockSpec(memory_space=pltpu.SMEM)
VMEM = pl.BlockSpec(memory_space=pltpu.VMEM)
ANY = pl.BlockSpec(memory_space=pl.ANY)


def moved(value, steps, only=None):
    count = lax.axis_size("slab")
    first, last = max(0, -steps), min(count, count - steps)
    pairs = [(i, i + steps) for i in range(first, last) if only is None or i % G == only]
    return lax.ppermute(value, "slab", pairs)


def swapped(value, bits):
    count = lax.axis_size("slab")
    return lax.ppermute(value, "slab", [(i, i ^ bits) for i in range(count)])


def direct(arrays):
    return [array if m == 0 else swapped(array, m) for m, array in enumerate(arrays)]


def call(kernel, us, *, results, vmem=16, **how):
    return pl.pallas_call(
        kernel,
        out_shape=results,
        compiler_params=pltpu.CompilerParams(vmem_limit_bytes=vmem * MIB),
        cost_estimate=pl.CostEstimate(flops=int(us * 1.15e9), bytes_accessed=1000, transcendentals=0),
        **how,
    )


def value(shape, dtype):
    return jax.ShapeDtypeStruct(shape, dtype)


def far(array):
    return pltpu.with_memory_space_constraint(array, pltpu.HBM)


def across(shape, tile):
    block = shape[:-1] + (tile,)
    return pl.BlockSpec(block, lambda i: (0,) * (len(shape) - 1) + (i,))


def piece_specs(pieces, side, tile):
    return [pl.BlockSpec((side, tile), lambda i, at=at: (at, i)) for _, at in pieces]


def arrays_of(pieces):
    return [array for array, _ in pieces]


def rows_of(place, m):
    first = ROWS * jnp.bitwise_xor(place, m)
    return [(h * TILE, first + h) for h in range(ROWS)]


def wide_tile(rows_deep):
    return pltpu.VMEM((TILE // LANES, rows_deep, LANES), F32)


def chunk_tiles(chunk, cols):
    count = cols // CHUNKS // TILE
    return chunk * count, count


def cast_kernel(groups, ends, halves, here_ref, *refs):
    parts = TILE // LANES
    vol_refs, end_refs = refs[:parts], refs[parts : parts + ends]
    for half_ref, sent_ref in zip(refs[parts + ends : parts + ends + halves], refs[len(refs) - halves :]):
        sent_ref[...] = half_ref[...]
    out_refs = refs[len(refs) - halves - len(groups) : len(refs) - halves]
    rows = ROWS * G
    depth = vol_refs[0].shape[0] // rows
    place = lax.rem(here_ref[0], G)
    for j, vol_ref in enumerate(vol_refs):
        for group, out_ref in zip(groups, out_refs):
            for n, m in enumerate(group):
                for start, row in rows_of(place, m):
                    at = pl.ds(start + j * LANES, LANES)
                    out_ref[n * depth : (n + 1) * depth, at] = vol_ref[pl.ds(row, depth, stride=rows), :].astype(BF16)
    if ends:
        both = jnp.concatenate([ref[...] for ref in end_refs], axis=0).astype(BF16)
        for group, out_ref in zip(groups, out_refs):
            if group[0] % 2:
                out_ref[depth:, :] = both


def cast_rows(here, volume, chunk, groups, ends, sinogram, *tokens):
    depth, rows, cols = volume.shape
    flat = far(volume.reshape(depth * rows, cols))
    first, count = chunk_tiles(chunk, cols)
    parts, width = TILE // LANES, ROWS * TILE
    shapes = [(len(group) * depth + (2 * rows if ends and group[0] % 2 else 0), cols) for group in groups]
    edges = [pl.BlockSpec((rows, width), lambda i, z=z: (z, i)) for z in (0, depth - 1)] if ends else []
    halves = 0 if sinogram is None else CHUNKS
    block = (depth, rows, TILE)
    return call(
        functools.partial(cast_kernel, groups, len(edges), halves),
        2,
        grid=(count,),
        in_specs=[SMEM]
        + [pl.BlockSpec((depth * rows, LANES), lambda i, j=j: (0, (first + i) * parts + j)) for j in range(parts)]
        + edges
        + [pl.BlockSpec(block, lambda i, c=c: (0, 0, c * count + i)) for c in range(halves)]
        + [ANY] * len(tokens),
        out_specs=[across(shape, width) for shape in shapes] + [pl.BlockSpec(block, lambda i: (0, 0, i))] * halves,
        results=[(pltpu.HBM if group[0] == 0 else value)(shape, BF16) for group, shape in zip(groups, shapes)]
        + [value((depth, rows, cols // CHUNKS), BF16)] * halves,
    )(here, *[flat] * (parts + len(edges)), *[sinogram if halves == 0 else far(sinogram)] * halves, *tokens)


def last_block(here_ref, blocks):
    spot = jnp.bitwise_xor(lax.rem(here_ref[0], G), G - 1)
    last = blocks[0]
    for m in range(1, G):
        last = jnp.where(spot == m, blocks[m], last)
    return last


def pack_kernel(here_ref, *refs):
    in_refs, (all_ref, last_ref) = refs[:G], refs[-2:]
    side = in_refs[0].shape[0]
    for m in range(G):
        all_ref[m * side : (m + 1) * side] = in_refs[m][:side]
    last_ref[:side] = last_block(here_ref, [ref[:side] for ref in in_refs])
    if last_ref.shape[0] > side:
        all_ref[G * side :] = in_refs[G - 1][side:]
        last_ref[side:] = in_refs[G - 1][side:]


def pack(here, pieces, more, *tokens):
    side, cols = pieces[0][0].shape
    tile = 512
    shapes = [(G * side + more, cols), (side + more, cols)]
    specs = [across(array.shape, tile) for array in arrays_of(pieces)] if more else piece_specs(pieces, side, tile)
    return call(
        pack_kernel,
        1,
        grid=(cols // tile,),
        in_specs=[SMEM] + specs + [ANY] * len(tokens),
        out_specs=[across(shape, tile) for shape in shapes],
        results=[value(shape, BF16) for shape in shapes],
    )(here, *arrays_of(pieces), *tokens)


def split_kernel(groups, passing, here_ref, own_ref, got_ref, *refs):
    out_refs, wide = refs[-len(groups) - passing - 1 : -1], refs[-1]
    if passing:
        out_refs[-1][...] = refs[0][...]
    depth, rows, cols = own_ref.shape
    place = lax.rem(here_ref[0], G)

    def fill(ref):
        for j in range(cols // LANES):
            wide[j] = ref[:, :, j * LANES : (j + 1) * LANES].astype(F32).reshape(wide.shape[1:])

    @pl.when(place == G - 1)
    def _():
        fill(got_ref)

    @pl.when(place != G - 1)
    def _():
        fill(own_ref)

    for group, out_ref in zip(groups, out_refs):
        for n, m in enumerate(group):
            for j in range(cols // LANES):
                for start, row in rows_of(place, m):
                    block = wide.at[j][pl.ds(row, depth, stride=rows), :].astype(BF16)
                    out_ref[n * depth : (n + 1) * depth, start + j * LANES : start + (j + 1) * LANES] = block


def split_rows(here, own, got, chunk, groups, passing, *tokens):
    depth, rows, cols = own.shape
    first, count = chunk_tiles(chunk, cols)
    block = pl.BlockSpec((depth, rows, TILE), lambda i: (0, 0, first + i))
    shapes = [(len(group) * depth, cols) for group in groups] + [(depth, cols)] * len(passing)
    return call(
        functools.partial(split_kernel, groups, len(passing)),
        2,
        grid=(count,),
        in_specs=[SMEM, block, pl.BlockSpec((depth, rows, TILE), lambda i: (0, 0, i))]
        + piece_specs(passing, depth, ROWS * TILE) + [ANY] * len(tokens),
        out_specs=[across(shape, ROWS * TILE) for shape in shapes],
        results=[value(shape, BF16) for shape in shapes],
        scratch_shapes=[wide_tile(depth * rows)],
    )(here, far(own), got, *arrays_of(passing), *tokens)


def last_kernel(slabs, here_ref, cover_ref, offset_ref, *refs):
    w_ref, vol_ref, sino_ref, *refs = refs
    r_ref, tv_ref, vol, s, r, wide, tv, sem = refs[-8:]
    depth, rows, cols = sino_ref.shape

    count = cols // LANES

    def columns(j):
        return pl.ds(pl.multiple_of(j * LANES, LANES), LANES)

    def arrival(n, j):
        src, dst = ((vol_ref, vol), (sino_ref, s), (tv_ref, tv))[n]
        return pltpu.make_async_copy(src.at[:, :, columns(j)], dst.at[:, :, columns(j)], sem.at[n, j])

    def departure(n, j):
        src, dst = ((r, r_ref), (tv, tv_ref))[n]
        return pltpu.make_async_copy(src.at[:, :, columns(j)], dst.at[:, :, columns(j)], sem.at[3 + n, j])

    @pl.when(here_ref[0] == slabs - 1)
    def _():
        for j in range(count):
            for n in range(3):
                arrival(n, j).start()
        block = w_ref[offset_ref[slabs - 1, 0]]
        block = jnp.where(cover_ref[slabs - 1, 0] == 1, block, jnp.zeros_like(block))
        turned = block.astype(F32).T.astype(BF16)

        def column(j, _):
            at = columns(j)
            for n in range(3):
                arrival(n, j).wait()
            for n, ref in enumerate((s, tv, vol)):
                wide[n] = ref[:, :, at].astype(F32).reshape(wide.shape[1:])
            for row in range(rows):
                spot = pl.ds(row, depth, stride=rows)
                seen = jnp.dot(block, wide.at[2][spot, :].astype(BF16), preferred_element_type=F32)
                resid = (seen - wide.at[0][spot, :]).astype(BF16)
                wide.at[0][spot, :] = resid.astype(F32)
                wide.at[1][spot, :] += jnp.dot(turned, resid, preferred_element_type=F32)
            r[:, :, at] = wide[0].reshape(depth, rows, LANES).astype(BF16)
            tv[:, :, at] = wide[1].reshape(depth, rows, LANES)
            for n in range(2):
                departure(n, j).start()
            return 0

        lax.fori_loop(0, count, column, 0)
        for j in range(count):
            for n in range(2):
                departure(n, j).wait()


def last_group(here, coverage, offsets, weights, volume, sinogram, tv, *tokens):
    slabs = coverage.shape[0]
    depth, rows, cols = sinogram.shape
    return call(
        functools.partial(last_kernel, slabs),
        0,
        vmem=32,
        grid=(1,),
        in_specs=[SMEM, SMEM, SMEM, pl.BlockSpec(weights.shape, lambda i: (0, 0, 0))] + [ANY] * (3 + len(tokens)),
        out_specs=[ANY, ANY],
        results=[pltpu.HBM(sinogram.shape, BF16), pltpu.HBM(volume.shape, F32)],
        input_output_aliases={6: 1},
        scratch_shapes=[
            pltpu.VMEM(volume.shape, F32),
            pltpu.VMEM(sinogram.shape, BF16),
            pltpu.VMEM(sinogram.shape, BF16),
            pltpu.VMEM((3, depth * rows, LANES), F32),
            pltpu.VMEM(volume.shape, F32),
            pltpu.SemaphoreType.DMA((5, cols // LANES)),
        ],
    )(here, coverage, offsets, weights, far(volume), far(sinogram), far(tv), *tokens)


def natural(place, in_refs, wide, j):
    depth = in_refs[0].shape[0]
    rows = ROWS * len(in_refs)
    for m, ref in enumerate(in_refs):
        for start, row in rows_of(place, m):
            value = ref[:, start + j * LANES : start + (j + 1) * LANES].astype(F32)
            wide.at[j][pl.ds(row, depth, stride=rows), :] = value
    return wide[j].reshape(depth, rows, LANES)


def join_kernel(here_ref, *refs):
    in_refs, (out_ref, wide) = refs[:G], refs[-2:]
    for j in range(out_ref.shape[2] // LANES):
        out_ref[:, :, j * LANES : (j + 1) * LANES] = natural(lax.rem(here_ref[0], G), in_refs, wide, j).astype(BF16)


def join_rows(here, pieces, shape, *tokens):
    depth, rows, cols = shape
    _, count = chunk_tiles(0, cols)
    return call(
        join_kernel,
        0,
        grid=(count,),
        in_specs=[SMEM] + piece_specs(pieces, depth, ROWS * TILE) + [ANY] * len(tokens),
        out_specs=pl.BlockSpec((depth, rows, TILE), lambda i: (0, 0, i)),
        results=value((depth, rows, cols // CHUNKS), BF16),
        scratch_shapes=[wide_tile(depth * rows)],
    )(here, *arrays_of(pieces), *tokens)


def settle_kernel(slabs, count, here_ref, own_ref, above_ref, *refs):
    in_refs, (base_ref, out_ref, wide) = refs[:G], refs[-3:]
    step = pl.program_id(0)
    cols = out_ref.shape[2]
    place = lax.rem(here_ref[0], G)
    last = here_ref[0] == slabs - 1

    @pl.when(last)
    def _():
        pltpu.sync_copy(base_ref.at[:, :, pl.ds(pl.multiple_of(step * cols, cols), cols)], out_ref)

    @pl.when(jnp.logical_not(last) & (step < count) & (place == G - 1))
    def _():
        out_ref[...] = above_ref[...]

    @pl.when(jnp.logical_not(last) & (step < count) & (place != G - 1))
    def _():
        out_ref[...] = own_ref[...]

    @pl.when(jnp.logical_not(last) & (step >= count))
    def _():
        for j in range(cols // LANES):
            out_ref[:, :, j * LANES : (j + 1) * LANES] = natural(place, in_refs, wide, j).astype(BF16)


def settle(here, slabs, own, above, pieces, base, *tokens):
    depth, rows, cols = base.shape
    _, count = chunk_tiles(0, cols)
    block = (depth, rows, TILE)
    early = pl.BlockSpec(block, lambda i: (0, 0, jnp.minimum(i, count - 1)))
    late = [
        pl.BlockSpec((depth, ROWS * TILE), lambda i, at=at: (at, jnp.maximum(i - count, 0))) for _, at in pieces
    ]
    return call(
        functools.partial(settle_kernel, slabs, count),
        0,
        grid=(CHUNKS * count,),
        in_specs=[SMEM, early, early] + late + [ANY] * (len(tokens) + 1),
        out_specs=pl.BlockSpec(block, lambda i: (0, 0, i)),
        results=pltpu.HBM(base.shape, BF16),
        scratch_shapes=[wide_tile(depth * rows)],
    )(here, own, above, *arrays_of(pieces), *tokens, far(base))


def finish_kernel(here_ref, tv_ref, *refs):
    in_refs, (out_ref, wide) = refs[:G], refs[-2:]
    for j in range(out_ref.shape[2] // LANES):
        at = pl.ds(j * LANES, LANES)
        out_ref[:, :, at] = tv_ref[:, :, at] + natural(lax.rem(here_ref[0], G), in_refs, wide, j)


def finish(here, chunk, tv, pieces, *tokens):
    depth, rows, cols = tv.shape
    first, count = chunk_tiles(chunk, cols)
    part = pl.BlockSpec((depth, rows, TILE), lambda i: (0, 0, first + i))
    return call(
        finish_kernel,
        0,
        grid=(count,),
        in_specs=[SMEM, part] + piece_specs(pieces, depth, ROWS * TILE) + [ANY] * len(tokens),
        out_specs=part,
        results=pltpu.HBM(tv.shape, F32),
        input_output_aliases={1: 0},
        scratch_shapes=[wide_tile(depth * rows)],
    )(here, far(tv), *arrays_of(pieces), *tokens)


def band_kernel(slabs, span, here_ref, cover_ref, offset_ref, w_ref, *refs):
    proj_ref, back_ref, turned = refs[-3:]
    side = w_ref.shape[1]
    place = lax.rem(here_ref[0], G)
    first = here_ref[0] - place
    zero = jnp.zeros((side, side), BF16)
    for i in range(w_ref.shape[0]):
        turned[i] = w_ref[i].astype(F32).T.astype(BF16)

    def block(ref, i, j):
        k = j - i
        known, step = jnp.clip(i, 0, slabs - 1), jnp.clip(k, 0, span - 1)
        inside = (i >= 0) & (i < slabs) & (j >= 0) & (j < slabs) & (k >= 0) & (k < span)
        live = inside & (cover_ref[known, step] == 1)
        return jnp.where(live, ref[offset_ref[known, step]], zero)

    def slab(m):
        return first + jnp.bitwise_xor(place, m)

    def group(m):
        to = jnp.bitwise_xor(place, m)
        return first + jnp.where(to == G - 1, -1, to)

    seen = [slab(m) for m in range(G)] + [slab(m) + G for m in range(G)] + [first - 1]
    seeing = [group(m) for m in range(G)] + [group(m) - G for m in range(G)] + [first + G - 1]
    for r in range(G):
        for s in range(2 * G + 1):
            at = (pl.ds(r * side, side), pl.ds(s * side, side))
            proj_ref[at] = block(w_ref, group(r), seen[s])
            back_ref[at] = block(turned, seeing[s], slab(r))


def bands(here, coverage, offsets, weights, *tokens):
    slabs, span = coverage.shape
    side = weights.shape[1]
    shape = (G * side, (2 * G + 1) * side)
    return call(
        functools.partial(band_kernel, slabs, span),
        9,
        in_specs=[SMEM, SMEM, SMEM, pl.BlockSpec(weights.shape, lambda i: (0, 0, 0))] + [ANY] * len(tokens),
        grid=(1,),
        out_specs=[pl.BlockSpec(shape, lambda i: (0, 0))] * 2,
        results=[value(shape, BF16)] * 2,
        scratch_shapes=[pltpu.VMEM(weights.shape, BF16)],
    )(here, coverage, offsets, weights, *tokens)


def project_kernel(groups, here_ref, band_ref, own_ref, high_ref, low_ref, *refs):
    sino_refs, (r_ref, down_ref, *group_refs) = refs[:G], refs[-len(groups) - 2 :]
    side = sino_refs[0].shape[0]
    seen = jnp.concatenate([own_ref[...], high_ref[...], low_ref[...]], axis=0)
    total = jnp.dot(band_ref[...], seen, preferred_element_type=F32)
    resid = [(total[m * side : (m + 1) * side] - ref[...].astype(F32)).astype(BF16) for m, ref in enumerate(sino_refs)]
    for m in range(G):
        r_ref[m * side : (m + 1) * side] = resid[m]
    for group, group_ref in zip(groups, group_refs):
        for n, m in enumerate(group):
            group_ref[n * side : (n + 1) * side] = resid[m]
    down_ref[...] = last_block(here_ref, resid)


def project(here, band, own, high, low, sinos, groups, *tokens):
    n, side = band.shape[0], band.shape[0] // G
    cols = own.shape[1]
    tile = 512
    many, one = pl.BlockSpec((n, tile), lambda i: (0, i)), pl.BlockSpec((side, tile), lambda i: (0, i))
    shapes = [(n, cols), (side, cols)] + [(len(group) * side, cols) for group in groups]
    return call(
        functools.partial(project_kernel, groups),
        3,
        grid=(cols // tile,),
        in_specs=[SMEM, pl.BlockSpec(band.shape, lambda i: (0, 0)), many, many, one]
        + piece_specs(sinos, side, tile)
        + [ANY] * len(tokens),
        out_specs=[across(shape, tile) for shape in shapes],
        results=[value(shape, BF16) for shape in shapes],
    )(here, band, own, high, low, *arrays_of(sinos), *tokens)


def back_kernel(dealing, here_ref, band_ref, own_ref, low_ref, high_ref, *refs):
    out_refs = refs[-G:]
    side = high_ref.shape[0]
    seeing = jnp.concatenate([own_ref[...], low_ref[...], high_ref[...]], axis=0)
    total = jnp.dot(band_ref[...], seeing, preferred_element_type=F32)
    place = lax.rem(here_ref[0], G)
    for m, out_ref in enumerate(out_refs):
        out_ref[:side] = total[m * side : (m + 1) * side].astype(BF16)
        if dealing:
            last = jnp.bitwise_xor(place, m) == G - 1
            out_ref[side:] = jnp.where(last, refs[1][...], refs[0][m * side : (m + 1) * side])


def back(here, band, own, low, high, dealt, *tokens):
    n, side = band.shape[0], band.shape[0] // G
    cols = own.shape[1]
    tile = 512
    many = pl.BlockSpec((n, tile), lambda i: (0, i))
    one = pl.BlockSpec((side, tile), lambda i: (0, i))
    out = ((2 if dealt else 1) * side, cols)
    return call(
        functools.partial(back_kernel, bool(dealt)),
        0,
        grid=(cols // tile,),
        in_specs=[SMEM, pl.BlockSpec(band.shape, lambda i: (0, 0)), many, many, one]
        + ([many, one] if dealt else [])
        + [ANY] * len(tokens),
        out_specs=[across(out, tile)] * G,
        results=[value(out, BF16)] * G,
    )(here, band, own, low, high, *dealt, *tokens)


def tv_flux(cur, above):
    rows, cols = cur.shape
    row = lax.broadcasted_iota(jnp.int32, (rows, cols), 0)
    col = lax.broadcasted_iota(jnp.int32, (rows, cols), 1)
    dz = above - cur
    dy = jnp.where(row == rows - 1, 0.0, pltpu.roll(cur, rows - 1, 0)) - cur
    dx = jnp.where(col == cols - 1, 0.0, pltpu.roll(cur, cols - 1, 1)) - cur
    scale = 0.5 * lax.rsqrt(dz * dz + dy * dy + dx * dx + 0.25)
    return dz * scale, dy * scale, dx * scale


def tv_below(cur, above):
    return tv_flux(cur, above)[0]


def tv_slice(cur, above, below_flux):
    rows, cols = cur.shape
    row = lax.broadcasted_iota(jnp.int32, (rows, cols), 0)
    col = lax.broadcasted_iota(jnp.int32, (rows, cols), 1)
    fz, fy, fx = tv_flux(cur, above)
    sides = 0.5 * cur * lax.rsqrt(cur * cur + 0.25)
    fy_low = jnp.where(row == 0, sides, pltpu.roll(fy, 1, 0))
    fx_low = jnp.where(col == 0, sides, pltpu.roll(fx, 1, 1))
    return (below_flux - fz) + (fy_low - fy) + (fx_low - fx), fz


def tv_kernel(here_ref, near_ref, next_level_ref, far_ref, last_level_ref, next_ref, vol_ref, *refs):
    out_ref, done_ref, flux_ref = refs[-3:]
    step = pl.program_id(0)
    deep, rows, _ = vol_ref.shape
    place = lax.rem(here_ref[0], G)

    @pl.when(step == 0)
    def _():
        inside = jnp.where(place == 2, far_ref[...], near_ref[...])
        low = jnp.where(place == 0, last_level_ref[...], inside)[rows:].astype(F32)
        flux_ref[...] = tv_below(low, vol_ref[0])

    def body(z, flux):
        out_ref[z], flux = tv_slice(vol_ref[z], vol_ref[z + 1], flux)
        return flux

    flux = lax.fori_loop(0, deep - 1, body, flux_ref[...], unroll=5)
    inside = jnp.where(place == 1, far_ref[...], near_ref[...])
    high = jnp.where(place == G - 1, next_level_ref[...], inside)[:rows].astype(F32)
    above = jnp.where(step == pl.num_programs(0) - 1, high, next_ref[0])
    out_ref[deep - 1], flux_ref[...] = tv_slice(vol_ref[deep - 1], above, flux)
    done_ref[...] = flux_ref[:, : done_ref.shape[1]]


def half_tv(here, volume, ends, *tokens):
    depth, rows, cols = volume.shape
    deep = 16
    edges = [pl.BlockSpec((2 * rows, cols), lambda i, last=end.shape[0] // (2 * rows) - 1: (last, 0)) for end in ends]
    body = pl.BlockSpec((deep, rows, cols), lambda i: (i, 0, 0))
    after = pl.BlockSpec((1, rows, cols), lambda i: (jnp.minimum((i + 1) * deep, depth - 1), 0, 0))
    return call(
        tv_kernel,
        0,
        grid=(depth // deep,),
        in_specs=[SMEM] + edges + [after, body] + [ANY] * len(tokens),
        out_specs=[body, pl.BlockSpec((rows, LANES), lambda i: (0, 0))],
        results=[pltpu.HBM(volume.shape, F32), value((rows, LANES), F32)],
        scratch_shapes=[pltpu.VMEM((rows, cols), F32)],
    )(here, *ends, far(volume), far(volume), *tokens)


def local(volume, sinogram, weights, coverage, offsets):
    slabs = lax.axis_size("slab")
    here = lax.axis_index("slab").astype(jnp.int32).reshape(1)
    depth, rows, _ = volume.shape
    single = ((0,), (1,), (2,), (3,))
    paired = ((0,), (1,), (2, 3))

    def tied(array, *others):
        return lax.optimization_barrier((array, *others))[0]

    def beyond(over, *others):
        return swapped(tied(over, *others)[depth:], 1)

    vols0 = cast_rows(here, volume, 0, single, True, None)
    got_vols0 = direct(vols0)
    v0, v1, v23, sent0, sent1 = cast_rows(here, volume, 1, paired, False, sinogram, vols0[1])
    got0 = moved(sent0, G, only=G - 1)
    over = swapped(v23, 2)
    band_p, band_b = bands(here, coverage, offsets, weights, v1)
    got1 = moved(tied(sent1, band_p), G, only=G - 1)
    own0, edge0 = pack(here, [(array, 0) for array in got_vols0], 2 * rows, band_p)
    high0, near = moved(own0, -G), swapped(tied(v1, own0), 1)
    s0, s1, s23, over_beyond = split_rows(here, sinogram, got0, 0, paired, [(over, 1)], near)
    s_near, s_over = swapped(s1, 1), swapped(s23, 2)
    low0 = moved(tied(edge0, s_near), G)
    own1, edge1 = pack(here, [(v0, 0), (near, 0), (over, 0), (swapped(over_beyond, 1), 0)], 0)
    low1, high1 = moved(edge1, G), moved(own1, -G)
    sinos0 = [(s0, 0), (s_near, 0), (s_over, 0), (beyond(s_over, own1), 0)]

    s0, s1, s23 = split_rows(here, sinogram, got1, 1, paired, [], own1)

    resid0, down0, r1, r23 = project(here, band_p, own0, high0, low0, sinos0, paired[1:], low1, s0)
    from_low0, from_high0 = moved(resid0, G), moved(down0, -G)
    s_near, s_over = swapped(s1, 1), swapped(s23, 2)
    r_near, r_over = swapped(tied(r1, s_near), 1), swapped(tied(r23, s_near), 2)
    tv, tv_done = half_tv(here, volume, [got_vols0[1], high0, got_vols0[3], low0], resid0)
    sinos1 = [(s0, 0), (s_near, 0), (s_over, 0), (beyond(s_over, tv_done), 0)]
    resid1, down1 = project(here, band_p, own1, high1, low1, sinos1, (), tv_done, r_near, r_over)
    from_low1, from_high1 = moved(resid1, G), moved(down1, -G)

    backs0 = back(here, band_b, resid0, from_low0, from_high0, [resid1, from_high1])
    got_backs0 = direct(backs0)
    r_pieces = [(resid0, 0), (r_near, 0), (r_over, 0), (beyond(r_over, resid1), 0)]
    natural0 = join_rows(here, r_pieces, sinogram.shape, backs0[0])
    above0 = moved(natural0, -G, only=G - 1)
    r_last, tv = last_group(here, coverage, offsets, weights, volume, sinogram, tv, backs0[0])
    backs1 = back(here, band_b, resid1, from_low1, from_high1, [], far(r_last), natural0)
    got_backs1 = direct(backs1)
    gradient = finish(here, 0, tv, [(array, 0) for array in got_backs0], backs1[0])
    residual = settle(here, slabs, natural0, above0, [(array, 1) for array in got_backs0], r_last, backs1[0])
    gradient = finish(here, 1, gradient, [(array, 0) for array in got_backs1], far(residual))
    return (gradient, residual)


def solution(mesh):
    placed = (P("slab", "grp", None), P("slab", "grp", None), P(), P(), P())
    return jax.shard_map(
        local,
        mesh=mesh,
        in_specs=placed,
        out_specs=(P("slab", "grp", None), P("slab", "grp", None)),
        check_vma=False,
    )
```

```python
import functools

import jax
import jax.numpy as jnp
from jax import lax
from jax.experimental import pallas as pl
from jax.experimental.pallas import tpu as pltpu
from jax.sharding import PartitionSpec as P

G = 4
CHUNKS = 2
ROWS = 2
TILE = 256
F32 = jnp.float32
BF16 = jnp.bfloat16
MIB = 1024 * 1024
LANES = 128
SMEM = pl.BlockSpec(memory_space=pltpu.SMEM)
VMEM = pl.BlockSpec(memory_space=pltpu.VMEM)
ANY = pl.BlockSpec(memory_space=pl.ANY)


def moved(value, steps, only=None):
    count = lax.axis_size("slab")
    first, last = max(0, -steps), min(count, count - steps)
    pairs = [(i, i + steps) for i in range(first, last) if only is None or i % G == only]
    return lax.ppermute(value, "slab", pairs)


def swapped(value, bits):
    count = lax.axis_size("slab")
    return lax.ppermute(value, "slab", [(i, i ^ bits) for i in range(count)])


def direct(arrays):
    return [array if m == 0 else swapped(array, m) for m, array in enumerate(arrays)]


def call(kernel, us, *, results, vmem=16, **how):
    return pl.pallas_call(
        kernel,
        out_shape=results,
        compiler_params=pltpu.CompilerParams(vmem_limit_bytes=vmem * MIB),
        cost_estimate=pl.CostEstimate(flops=int(us * 1.15e9), bytes_accessed=1000, transcendentals=0),
        **how,
    )


def value(shape, dtype):
    return jax.ShapeDtypeStruct(shape, dtype)


def far(array):
    return pltpu.with_memory_space_constraint(array, pltpu.HBM)


def across(shape, tile):
    block = shape[:-1] + (tile,)
    return pl.BlockSpec(block, lambda i: (0,) * (len(shape) - 1) + (i,))


def piece_specs(pieces, side, tile):
    return [pl.BlockSpec((side, tile), lambda i, at=at: (at, i)) for _, at in pieces]


def arrays_of(pieces):
    return [array for array, _ in pieces]


def rows_of(place, m):
    first = ROWS * jnp.bitwise_xor(place, m)
    return [(h * TILE, first + h) for h in range(ROWS)]


def wide_tile(rows_deep):
    return pltpu.VMEM((TILE // LANES, rows_deep, LANES), F32)


def chunk_tiles(chunk, cols):
    count = cols // CHUNKS // TILE
    return chunk * count, count


def cast_kernel(groups, ends, halves, here_ref, *refs):
    parts = TILE // LANES
    vol_refs, end_refs = refs[:parts], refs[parts : parts + ends]
    for half_ref, sent_ref in zip(refs[parts + ends : parts + ends + halves], refs[len(refs) - halves :]):
        sent_ref[...] = half_ref[...]
    out_refs = refs[len(refs) - halves - len(groups) : len(refs) - halves]
    rows = ROWS * G
    depth = vol_refs[0].shape[0] // rows
    place = lax.rem(here_ref[0], G)
    for j, vol_ref in enumerate(vol_refs):
        for group, out_ref in zip(groups, out_refs):
            for n, m in enumerate(group):
                for start, row in rows_of(place, m):
                    at = pl.ds(start + j * LANES, LANES)
                    out_ref[n * depth : (n + 1) * depth, at] = vol_ref[pl.ds(row, depth, stride=rows), :].astype(BF16)
    if ends:
        both = jnp.concatenate([ref[...] for ref in end_refs], axis=0).astype(BF16)
        for group, out_ref in zip(groups, out_refs):
            if group[0] % 2:
                out_ref[depth:, :] = both


def cast_rows(here, volume, chunk, groups, ends, sinogram, *tokens):
    depth, rows, cols = volume.shape
    flat = far(volume.reshape(depth * rows, cols))
    first, count = chunk_tiles(chunk, cols)
    parts, width = TILE // LANES, ROWS * TILE
    shapes = [(len(group) * depth + (2 * rows if ends and group[0] % 2 else 0), cols) for group in groups]
    edges = [pl.BlockSpec((rows, width), lambda i, z=z: (z, i)) for z in (0, depth - 1)] if ends else []
    halves = 0 if sinogram is None else CHUNKS
    block = (depth, rows, TILE)
    return call(
        functools.partial(cast_kernel, groups, len(edges), halves),
        2,
        grid=(count,),
        in_specs=[SMEM]
        + [pl.BlockSpec((depth * rows, LANES), lambda i, j=j: (0, (first + i) * parts + j)) for j in range(parts)]
        + edges
        + [pl.BlockSpec(block, lambda i, c=c: (0, 0, c * count + i)) for c in range(halves)]
        + [ANY] * len(tokens),
        out_specs=[across(shape, width) for shape in shapes] + [pl.BlockSpec(block, lambda i: (0, 0, i))] * halves,
        results=[(pltpu.HBM if group[0] == 0 else value)(shape, BF16) for group, shape in zip(groups, shapes)]
        + [value((depth, rows, cols // CHUNKS), BF16)] * halves,
    )(here, *[flat] * (parts + len(edges)), *[sinogram if halves == 0 else far(sinogram)] * halves, *tokens)


def last_block(here_ref, blocks):
    spot = jnp.bitwise_xor(lax.rem(here_ref[0], G), G - 1)
    last = blocks[0]
    for m in range(1, G):
        last = jnp.where(spot == m, blocks[m], last)
    return last


def pack_kernel(here_ref, *refs):
    in_refs, (all_ref, last_ref) = refs[:G], refs[-2:]
    side = in_refs[0].shape[0]
    for m in range(G):
        all_ref[m * side : (m + 1) * side] = in_refs[m][:side]
    last_ref[:side] = last_block(here_ref, [ref[:side] for ref in in_refs])
    if last_ref.shape[0] > side:
        all_ref[G * side :] = in_refs[G - 1][side:]
        last_ref[side:] = in_refs[G - 1][side:]


def pack(here, pieces, more, *tokens):
    side, cols = pieces[0][0].shape
    tile = 512
    shapes = [(G * side + more, cols), (side + more, cols)]
    specs = [across(array.shape, tile) for array in arrays_of(pieces)] if more else piece_specs(pieces, side, tile)
    return call(
        pack_kernel,
        1,
        grid=(cols // tile,),
        in_specs=[SMEM] + specs + [ANY] * len(tokens),
        out_specs=[across(shape, tile) for shape in shapes],
        results=[value(shape, BF16) for shape in shapes],
    )(here, *arrays_of(pieces), *tokens)


def split_kernel(groups, passing, here_ref, own_ref, got_ref, *refs):
    out_refs, wide = refs[-len(groups) - passing - 1 : -1], refs[-1]
    if passing:
        out_refs[-1][...] = refs[0][...]
    depth, rows, cols = own_ref.shape
    place = lax.rem(here_ref[0], G)

    def fill(ref):
        for j in range(cols // LANES):
            wide[j] = ref[:, :, j * LANES : (j + 1) * LANES].astype(F32).reshape(wide.shape[1:])

    @pl.when(place == G - 1)
    def _():
        fill(got_ref)

    @pl.when(place != G - 1)
    def _():
        fill(own_ref)

    for group, out_ref in zip(groups, out_refs):
        for n, m in enumerate(group):
            for j in range(cols // LANES):
                for start, row in rows_of(place, m):
                    block = wide.at[j][pl.ds(row, depth, stride=rows), :].astype(BF16)
                    out_ref[n * depth : (n + 1) * depth, start + j * LANES : start + (j + 1) * LANES] = block


def split_rows(here, own, got, chunk, groups, passing, *tokens):
    depth, rows, cols = own.shape
    first, count = chunk_tiles(chunk, cols)
    block = pl.BlockSpec((depth, rows, TILE), lambda i: (0, 0, first + i))
    shapes = [(len(group) * depth, cols) for group in groups] + [(depth, cols)] * len(passing)
    return call(
        functools.partial(split_kernel, groups, len(passing)),
        2,
        grid=(count,),
        in_specs=[SMEM, block, pl.BlockSpec((depth, rows, TILE), lambda i: (0, 0, i))]
        + piece_specs(passing, depth, ROWS * TILE) + [ANY] * len(tokens),
        out_specs=[across(shape, ROWS * TILE) for shape in shapes],
        results=[value(shape, BF16) for shape in shapes],
        scratch_shapes=[wide_tile(depth * rows)],
    )(here, far(own), got, *arrays_of(passing), *tokens)


def last_kernel(slabs, here_ref, cover_ref, offset_ref, *refs):
    w_ref, vol_ref, sino_ref, *refs = refs
    r_ref, tv_ref, vol, s, r, wide, tv, sem = refs[-8:]
    depth, rows, cols = sino_ref.shape

    count = cols // LANES

    def columns(j):
        return pl.ds(pl.multiple_of(j * LANES, LANES), LANES)

    def arrival(n, j):
        src, dst = ((vol_ref, vol), (sino_ref, s), (tv_ref, tv))[n]
        return pltpu.make_async_copy(src.at[:, :, columns(j)], dst.at[:, :, columns(j)], sem.at[n, j])

    def departure(n, j):
        src, dst = ((r, r_ref), (tv, tv_ref))[n]
        return pltpu.make_async_copy(src.at[:, :, columns(j)], dst.at[:, :, columns(j)], sem.at[3 + n, j])

    @pl.when(here_ref[0] == slabs - 1)
    def _():
        for j in range(count):
            for n in range(3):
                arrival(n, j).start()
        block = w_ref[offset_ref[slabs - 1, 0]]
        block = jnp.where(cover_ref[slabs - 1, 0] == 1, block, jnp.zeros_like(block))
        turned = block.astype(F32).T.astype(BF16)

        def column(j, _):
            at = columns(j)
            for n in range(3):
                arrival(n, j).wait()
            for n, ref in enumerate((s, tv, vol)):
                wide[n] = ref[:, :, at].astype(F32).reshape(wide.shape[1:])
            for row in range(rows):
                spot = pl.ds(row, depth, stride=rows)
                seen = jnp.dot(block, wide.at[2][spot, :].astype(BF16), preferred_element_type=F32)
                resid = (seen - wide.at[0][spot, :]).astype(BF16)
                wide.at[0][spot, :] = resid.astype(F32)
                wide.at[1][spot, :] += jnp.dot(turned, resid, preferred_element_type=F32)
            r[:, :, at] = wide[0].reshape(depth, rows, LANES).astype(BF16)
            tv[:, :, at] = wide[1].reshape(depth, rows, LANES)
            for n in range(2):
                departure(n, j).start()
            return 0

        lax.fori_loop(0, count, column, 0)
        for j in range(count):
            for n in range(2):
                departure(n, j).wait()


def last_group(here, coverage, offsets, weights, volume, sinogram, tv, *tokens):
    slabs = coverage.shape[0]
    depth, rows, cols = sinogram.shape
    return call(
        functools.partial(last_kernel, slabs),
        0,
        vmem=32,
        grid=(1,),
        in_specs=[SMEM, SMEM, SMEM, pl.BlockSpec(weights.shape, lambda i: (0, 0, 0))] + [ANY] * (3 + len(tokens)),
        out_specs=[ANY, ANY],
        results=[pltpu.HBM(sinogram.shape, BF16), pltpu.HBM(volume.shape, F32)],
        input_output_aliases={6: 1},
        scratch_shapes=[
            pltpu.VMEM(volume.shape, F32),
            pltpu.VMEM(sinogram.shape, BF16),
            pltpu.VMEM(sinogram.shape, BF16),
            pltpu.VMEM((3, depth * rows, LANES), F32),
            pltpu.VMEM(volume.shape, F32),
            pltpu.SemaphoreType.DMA((5, cols // LANES)),
        ],
    )(here, coverage, offsets, weights, far(volume), far(sinogram), far(tv), *tokens)


def natural(place, in_refs, wide, j):
    depth = in_refs[0].shape[0]
    rows = ROWS * len(in_refs)
    for m, ref in enumerate(in_refs):
        for start, row in rows_of(place, m):
            value = ref[:, start + j * LANES : start + (j + 1) * LANES].astype(F32)
            wide.at[j][pl.ds(row, depth, stride=rows), :] = value
    return wide[j].reshape(depth, rows, LANES)


def join_kernel(here_ref, *refs):
    in_refs, (out_ref, wide) = refs[:G], refs[-2:]
    for j in range(out_ref.shape[2] // LANES):
        out_ref[:, :, j * LANES : (j + 1) * LANES] = natural(lax.rem(here_ref[0], G), in_refs, wide, j).astype(BF16)


def join_rows(here, pieces, shape, *tokens):
    depth, rows, cols = shape
    _, count = chunk_tiles(0, cols)
    return call(
        join_kernel,
        0,
        grid=(count,),
        in_specs=[SMEM] + piece_specs(pieces, depth, ROWS * TILE) + [ANY] * len(tokens),
        out_specs=pl.BlockSpec((depth, rows, TILE), lambda i: (0, 0, i)),
        results=value((depth, rows, cols // CHUNKS), BF16),
        scratch_shapes=[wide_tile(depth * rows)],
    )(here, *arrays_of(pieces), *tokens)


def settle_kernel(slabs, count, here_ref, own_ref, above_ref, *refs):
    in_refs, (base_ref, out_ref, wide) = refs[:G], refs[-3:]
    step = pl.program_id(0)
    cols = out_ref.shape[2]
    place = lax.rem(here_ref[0], G)
    last = here_ref[0] == slabs - 1

    @pl.when(last)
    def _():
        pltpu.sync_copy(base_ref.at[:, :, pl.ds(pl.multiple_of(step * cols, cols), cols)], out_ref)

    @pl.when(jnp.logical_not(last) & (step < count) & (place == G - 1))
    def _():
        out_ref[...] = above_ref[...]

    @pl.when(jnp.logical_not(last) & (step < count) & (place != G - 1))
    def _():
        out_ref[...] = own_ref[...]

    @pl.when(jnp.logical_not(last) & (step >= count))
    def _():
        for j in range(cols // LANES):
            out_ref[:, :, j * LANES : (j + 1) * LANES] = natural(place, in_refs, wide, j).astype(BF16)


def settle(here, slabs, own, above, pieces, base, *tokens):
    depth, rows, cols = base.shape
    _, count = chunk_tiles(0, cols)
    block = (depth, rows, TILE)
    early = pl.BlockSpec(block, lambda i: (0, 0, jnp.minimum(i, count - 1)))
    late = [
        pl.BlockSpec((depth, ROWS * TILE), lambda i, at=at: (at, jnp.maximum(i - count, 0))) for _, at in pieces
    ]
    return call(
        functools.partial(settle_kernel, slabs, count),
        0,
        grid=(CHUNKS * count,),
        in_specs=[SMEM, early, early] + late + [ANY] * (len(tokens) + 1),
        out_specs=pl.BlockSpec(block, lambda i: (0, 0, i)),
        results=pltpu.HBM(base.shape, BF16),
        scratch_shapes=[wide_tile(depth * rows)],
    )(here, own, above, *arrays_of(pieces), *tokens, far(base))


def finish_kernel(here_ref, tv_ref, *refs):
    in_refs, (out_ref, wide) = refs[:G], refs[-2:]
    for j in range(out_ref.shape[2] // LANES):
        at = pl.ds(j * LANES, LANES)
        out_ref[:, :, at] = tv_ref[:, :, at] + natural(lax.rem(here_ref[0], G), in_refs, wide, j)


def finish(here, chunk, tv, pieces, *tokens):
    depth, rows, cols = tv.shape
    first, count = chunk_tiles(chunk, cols)
    part = pl.BlockSpec((depth, rows, TILE), lambda i: (0, 0, first + i))
    return call(
        finish_kernel,
        0,
        grid=(count,),
        in_specs=[SMEM, part] + piece_specs(pieces, depth, ROWS * TILE) + [ANY] * len(tokens),
        out_specs=part,
        results=pltpu.HBM(tv.shape, F32),
        input_output_aliases={1: 0},
        scratch_shapes=[wide_tile(depth * rows)],
    )(here, far(tv), *arrays_of(pieces), *tokens)


def band_kernel(slabs, span, here_ref, cover_ref, offset_ref, w_ref, *refs):
    proj_ref, back_ref, turned = refs[-3:]
    side = w_ref.shape[1]
    place = lax.rem(here_ref[0], G)
    first = here_ref[0] - place
    zero = jnp.zeros((side, side), BF16)
    for i in range(w_ref.shape[0]):
        turned[i] = w_ref[i].astype(F32).T.astype(BF16)

    def block(ref, i, j):
        k = j - i
        known, step = jnp.clip(i, 0, slabs - 1), jnp.clip(k, 0, span - 1)
        inside = (i >= 0) & (i < slabs) & (j >= 0) & (j < slabs) & (k >= 0) & (k < span)
        live = inside & (cover_ref[known, step] == 1)
        return jnp.where(live, ref[offset_ref[known, step]], zero)

    def slab(m):
        return first + jnp.bitwise_xor(place, m)

    def group(m):
        to = jnp.bitwise_xor(place, m)
        return first + jnp.where(to == G - 1, -1, to)

    seen = [slab(m) for m in range(G)] + [slab(m) + G for m in range(G)] + [first - 1]
    seeing = [group(m) for m in range(G)] + [group(m) - G for m in range(G)] + [first + G - 1]
    for r in range(G):
        for s in range(2 * G + 1):
            at = (pl.ds(r * side, side), pl.ds(s * side, side))
            proj_ref[at] = block(w_ref, group(r), seen[s])
            back_ref[at] = block(turned, seeing[s], slab(r))


def bands(here, coverage, offsets, weights, *tokens):
    slabs, span = coverage.shape
    side = weights.shape[1]
    shape = (G * side, (2 * G + 1) * side)
    return call(
        functools.partial(band_kernel, slabs, span),
        9,
        in_specs=[SMEM, SMEM, SMEM, pl.BlockSpec(weights.shape, lambda i: (0, 0, 0))] + [ANY] * len(tokens),
        grid=(1,),
        out_specs=[pl.BlockSpec(shape, lambda i: (0, 0))] * 2,
        results=[value(shape, BF16)] * 2,
        scratch_shapes=[pltpu.VMEM(weights.shape, BF16)],
    )(here, coverage, offsets, weights, *tokens)


def project_kernel(groups, here_ref, band_ref, own_ref, high_ref, low_ref, *refs):
    sino_refs, (r_ref, down_ref, *group_refs) = refs[:G], refs[-len(groups) - 2 :]
    side = sino_refs[0].shape[0]
    seen = jnp.concatenate([own_ref[...], high_ref[...], low_ref[...]], axis=0)
    total = jnp.dot(band_ref[...], seen, preferred_element_type=F32)
    resid = [(total[m * side : (m + 1) * side] - ref[...].astype(F32)).astype(BF16) for m, ref in enumerate(sino_refs)]
    for m in range(G):
        r_ref[m * side : (m + 1) * side] = resid[m]
    for group, group_ref in zip(groups, group_refs):
        for n, m in enumerate(group):
            group_ref[n * side : (n + 1) * side] = resid[m]
    down_ref[...] = last_block(here_ref, resid)


def project(here, band, own, high, low, sinos, groups, *tokens):
    n, side = band.shape[0], band.shape[0] // G
    cols = own.shape[1]
    tile = 512
    many, one = pl.BlockSpec((n, tile), lambda i: (0, i)), pl.BlockSpec((side, tile), lambda i: (0, i))
    shapes = [(n, cols), (side, cols)] + [(len(group) * side, cols) for group in groups]
    return call(
        functools.partial(project_kernel, groups),
        3,
        grid=(cols // tile,),
        in_specs=[SMEM, pl.BlockSpec(band.shape, lambda i: (0, 0)), many, many, one]
        + piece_specs(sinos, side, tile)
        + [ANY] * len(tokens),
        out_specs=[across(shape, tile) for shape in shapes],
        results=[value(shape, BF16) for shape in shapes],
    )(here, band, own, high, low, *arrays_of(sinos), *tokens)


def back_kernel(dealing, here_ref, band_ref, own_ref, low_ref, high_ref, *refs):
    out_refs = refs[-G:]
    side = high_ref.shape[0]
    seeing = jnp.concatenate([own_ref[...], low_ref[...], high_ref[...]], axis=0)
    total = jnp.dot(band_ref[...], seeing, preferred_element_type=F32)
    place = lax.rem(here_ref[0], G)
    for m, out_ref in enumerate(out_refs):
        out_ref[:side] = total[m * side : (m + 1) * side].astype(BF16)
        if dealing:
            last = jnp.bitwise_xor(place, m) == G - 1
            out_ref[side:] = jnp.where(last, refs[1][...], refs[0][m * side : (m + 1) * side])


def back(here, band, own, low, high, dealt, *tokens):
    n, side = band.shape[0], band.shape[0] // G
    cols = own.shape[1]
    tile = 512
    many = pl.BlockSpec((n, tile), lambda i: (0, i))
    one = pl.BlockSpec((side, tile), lambda i: (0, i))
    out = ((2 if dealt else 1) * side, cols)
    return call(
        functools.partial(back_kernel, bool(dealt)),
        0,
        grid=(cols // tile,),
        in_specs=[SMEM, pl.BlockSpec(band.shape, lambda i: (0, 0)), many, many, one]
        + ([many, one] if dealt else [])
        + [ANY] * len(tokens),
        out_specs=[across(out, tile)] * G,
        results=[value(out, BF16)] * G,
    )(here, band, own, low, high, *dealt, *tokens)


def tv_flux(cur, above):
    rows, cols = cur.shape
    row = lax.broadcasted_iota(jnp.int32, (rows, cols), 0)
    col = lax.broadcasted_iota(jnp.int32, (rows, cols), 1)
    dz = above - cur
    dy = jnp.where(row == rows - 1, 0.0, pltpu.roll(cur, rows - 1, 0)) - cur
    dx = jnp.where(col == cols - 1, 0.0, pltpu.roll(cur, cols - 1, 1)) - cur
    scale = 0.5 * lax.rsqrt(dz * dz + dy * dy + dx * dx + 0.25)
    return dz * scale, dy * scale, dx * scale


def tv_below(cur, above):
    return tv_flux(cur, above)[0]


def tv_slice(cur, above, below_flux):
    rows, cols = cur.shape
    row = lax.broadcasted_iota(jnp.int32, (rows, cols), 0)
    col = lax.broadcasted_iota(jnp.int32, (rows, cols), 1)
    fz, fy, fx = tv_flux(cur, above)
    sides = 0.5 * cur * lax.rsqrt(cur * cur + 0.25)
    fy_low = jnp.where(row == 0, sides, pltpu.roll(fy, 1, 0))
    fx_low = jnp.where(col == 0, sides, pltpu.roll(fx, 1, 1))
    return (below_flux - fz) + (fy_low - fy) + (fx_low - fx), fz


def tv_kernel(here_ref, near_ref, next_level_ref, far_ref, last_level_ref, next_ref, vol_ref, *refs):
    out_ref, done_ref, flux_ref = refs[-3:]
    step = pl.program_id(0)
    deep, rows, _ = vol_ref.shape
    place = lax.rem(here_ref[0], G)

    @pl.when(step == 0)
    def _():
        inside = jnp.where(place == 2, far_ref[...], near_ref[...])
        low = jnp.where(place == 0, last_level_ref[...], inside)[rows:].astype(F32)
        flux_ref[...] = tv_below(low, vol_ref[0])

    def body(z, flux):
        out_ref[z], flux = tv_slice(vol_ref[z], vol_ref[z + 1], flux)
        return flux

    flux = lax.fori_loop(0, deep - 1, body, flux_ref[...], unroll=5)
    inside = jnp.where(place == 1, far_ref[...], near_ref[...])
    high = jnp.where(place == G - 1, next_level_ref[...], inside)[:rows].astype(F32)
    above = jnp.where(step == pl.num_programs(0) - 1, high, next_ref[0])
    out_ref[deep - 1], flux_ref[...] = tv_slice(vol_ref[deep - 1], above, flux)
    done_ref[...] = flux_ref[:, : done_ref.shape[1]]


def half_tv(here, volume, ends, *tokens):
    depth, rows, cols = volume.shape
    deep = 16
    edges = [pl.BlockSpec((2 * rows, cols), lambda i, last=end.shape[0] // (2 * rows) - 1: (last, 0)) for end in ends]
    body = pl.BlockSpec((deep, rows, cols), lambda i: (i, 0, 0))
    after = pl.BlockSpec((1, rows, cols), lambda i: (jnp.minimum((i + 1) * deep, depth - 1), 0, 0))
    return call(
        tv_kernel,
        0,
        grid=(depth // deep,),
        in_specs=[SMEM] + edges + [after, body] + [ANY] * len(tokens),
        out_specs=[body, pl.BlockSpec((rows, LANES), lambda i: (0, 0))],
        results=[pltpu.HBM(volume.shape, F32), value((rows, LANES), F32)],
        scratch_shapes=[pltpu.VMEM((rows, cols), F32)],
    )(here, *ends, far(volume), far(volume), *tokens)


def local(volume, sinogram, weights, coverage, offsets):
    slabs = lax.axis_size("slab")
    here = lax.axis_index("slab").astype(jnp.int32).reshape(1)
    depth, rows, _ = volume.shape
    single = ((0,), (1,), (2,), (3,))
    paired = ((0,), (1,), (2, 3))

    def tied(array, *others):
        return lax.optimization_barrier((array, *others))[0]

    def beyond(over, *others):
        return swapped(tied(over, *others)[depth:], 1)

    vols0 = cast_rows(here, volume, 0, single, True, None)
    got_vols0 = direct(vols0)
    v0, v1, v23, sent0, sent1 = cast_rows(here, volume, 1, paired, False, sinogram, vols0[1])
    got0 = moved(sent0, G, only=G - 1)
    over = swapped(v23, 2)
    band_p, band_b = bands(here, coverage, offsets, weights, v1)
    got1 = moved(tied(sent1, band_p), G, only=G - 1)
    own0, edge0 = pack(here, [(array, 0) for array in got_vols0], 2 * rows, band_p)
    high0, near = moved(own0, -G), swapped(tied(v1, own0), 1)
    s0, s1, s23, over_beyond = split_rows(here, sinogram, got0, 0, paired, [(over, 1)], near)
    s_near, s_over = swapped(s1, 1), swapped(s23, 2)
    low0 = moved(tied(edge0, s_near), G)
    own1, edge1 = pack(here, [(v0, 0), (near, 0), (over, 0), (swapped(over_beyond, 1), 0)], 0)
    low1, high1 = moved(edge1, G), moved(own1, -G)
    t0, t1, t23 = split_rows(here, sinogram, got1, 1, paired, [], own1)
    sinos0 = [(s0, 0), (s_near, 0), (s_over, 0), (beyond(s_over, t0), 0)]


    resid0, down0, r1, r23 = project(here, band_p, own0, high0, low0, sinos0, paired[1:], low1)
    from_low0, from_high0 = moved(resid0, G), moved(down0, -G)
    t_near, t_over = swapped(t1, 1), swapped(t23, 2)
    r_near, r_over = swapped(tied(r1, t_near), 1), swapped(tied(r23, t_near), 2)
    tv, tv_done = half_tv(here, volume, [got_vols0[1], high0, got_vols0[3], low0], resid0)
    sinos1 = [(t0, 0), (t_near, 0), (t_over, 0), (beyond(t_over, tv_done), 0)]
    resid1, down1 = project(here, band_p, own1, high1, low1, sinos1, (), tv_done, r_near, r_over)
    from_low1, from_high1 = moved(resid1, G), moved(down1, -G)

    backs0 = back(here, band_b, resid0, from_low0, from_high0, [resid1, from_high1])
    got_backs0 = direct(backs0)
    r_pieces = [(resid0, 0), (r_near, 0), (r_over, 0), (beyond(r_over, resid1), 0)]
    natural0 = join_rows(here, r_pieces, sinogram.shape, backs0[0])
    above0 = moved(natural0, -G, only=G - 1)
    r_last, tv = last_group(here, coverage, offsets, weights, volume, sinogram, tv, backs0[0])
    backs1 = back(here, band_b, resid1, from_low1, from_high1, [], far(r_last), natural0)
    got_backs1 = direct(backs1)
    gradient = finish(here, 0, tv, [(array, 0) for array in got_backs0], backs1[0])
    residual = settle(here, slabs, natural0, above0, [(array, 1) for array in got_backs0], r_last, backs1[0])
    gradient = finish(here, 1, gradient, [(array, 0) for array in got_backs1], far(residual))
    return (gradient, residual)


def solution(mesh):
    placed = (P("slab", "grp", None), P("slab", "grp", None), P(), P(), P())
    return jax.shard_map(
        local,
        mesh=mesh,
        in_specs=placed,
        out_specs=(P("slab", "grp", None), P("slab", "grp", None)),
        check_vma=False,
    )
```

```python
import functools

import jax
import jax.numpy as jnp
from jax import lax
from jax.experimental import pallas as pl
from jax.experimental.pallas import tpu as pltpu
from jax.sharding import PartitionSpec as P

G = 4
CHUNKS = 2
ROWS = 2
TILE = 256
F32 = jnp.float32
BF16 = jnp.bfloat16
MIB = 1024 * 1024
LANES = 128
SMEM = pl.BlockSpec(memory_space=pltpu.SMEM)
VMEM = pl.BlockSpec(memory_space=pltpu.VMEM)
ANY = pl.BlockSpec(memory_space=pl.ANY)


def moved(value, steps, only=None):
    count = lax.axis_size("slab")
    first, last = max(0, -steps), min(count, count - steps)
    pairs = [(i, i + steps) for i in range(first, last) if only is None or i % G == only]
    return lax.ppermute(value, "slab", pairs)


def swapped(value, bits):
    count = lax.axis_size("slab")
    return lax.ppermute(value, "slab", [(i, i ^ bits) for i in range(count)])


def direct(arrays):
    return [array if m == 0 else swapped(array, m) for m, array in enumerate(arrays)]


def call(kernel, us, *, results, vmem=16, **how):
    return pl.pallas_call(
        kernel,
        out_shape=results,
        compiler_params=pltpu.CompilerParams(vmem_limit_bytes=vmem * MIB),
        cost_estimate=pl.CostEstimate(flops=int(us * 1.15e9), bytes_accessed=1000, transcendentals=0),
        **how,
    )


def value(shape, dtype):
    return jax.ShapeDtypeStruct(shape, dtype)


def far(array):
    return pltpu.with_memory_space_constraint(array, pltpu.HBM)


def across(shape, tile):
    block = shape[:-1] + (tile,)
    return pl.BlockSpec(block, lambda i: (0,) * (len(shape) - 1) + (i,))


def piece_specs(pieces, side, tile):
    return [pl.BlockSpec((side, tile), lambda i, at=at: (at, i)) for _, at in pieces]


def arrays_of(pieces):
    return [array for array, _ in pieces]


def rows_of(place, m):
    first = ROWS * jnp.bitwise_xor(place, m)
    return [(h * TILE, first + h) for h in range(ROWS)]


def wide_tile(rows_deep):
    return pltpu.VMEM((TILE // LANES, rows_deep, LANES), F32)


def chunk_tiles(chunk, cols):
    count = cols // CHUNKS // TILE
    return chunk * count, count


def cast_kernel(groups, ends, halves, here_ref, *refs):
    parts = TILE // LANES
    vol_refs, end_refs = refs[:parts], refs[parts : parts + ends]
    for half_ref, sent_ref in zip(refs[parts + ends : parts + ends + halves], refs[len(refs) - halves :]):
        sent_ref[...] = half_ref[...]
    out_refs = refs[len(refs) - halves - len(groups) : len(refs) - halves]
    rows = ROWS * G
    depth = vol_refs[0].shape[0] // rows
    place = lax.rem(here_ref[0], G)
    for j, vol_ref in enumerate(vol_refs):
        for group, out_ref in zip(groups, out_refs):
            for n, m in enumerate(group):
                for start, row in rows_of(place, m):
                    at = pl.ds(start + j * LANES, LANES)
                    out_ref[n * depth : (n + 1) * depth, at] = vol_ref[pl.ds(row, depth, stride=rows), :].astype(BF16)
    if ends:
        both = jnp.concatenate([ref[...] for ref in end_refs], axis=0).astype(BF16)
        for group, out_ref in zip(groups, out_refs):
            if group[0] % 2:
                out_ref[depth:, :] = both


def cast_rows(here, volume, chunk, groups, ends, sinogram, *tokens):
    depth, rows, cols = volume.shape
    flat = far(volume.reshape(depth * rows, cols))
    first, count = chunk_tiles(chunk, cols)
    parts, width = TILE // LANES, ROWS * TILE
    shapes = [(len(group) * depth + (2 * rows if ends and group[0] % 2 else 0), cols) for group in groups]
    edges = [pl.BlockSpec((rows, width), lambda i, z=z: (z, i)) for z in (0, depth - 1)] if ends else []
    halves = 0 if sinogram is None else CHUNKS
    block = (depth, rows, TILE)
    return call(
        functools.partial(cast_kernel, groups, len(edges), halves),
        2,
        grid=(count,),
        in_specs=[SMEM]
        + [pl.BlockSpec((depth * rows, LANES), lambda i, j=j: (0, (first + i) * parts + j)) for j in range(parts)]
        + edges
        + [pl.BlockSpec(block, lambda i, c=c: (0, 0, c * count + i)) for c in range(halves)]
        + [ANY] * len(tokens),
        out_specs=[across(shape, width) for shape in shapes] + [pl.BlockSpec(block, lambda i: (0, 0, i))] * halves,
        results=[(pltpu.HBM if group[0] == 0 else value)(shape, BF16) for group, shape in zip(groups, shapes)]
        + [value((depth, rows, cols // CHUNKS), BF16)] * halves,
    )(here, *[flat] * (parts + len(edges)), *[sinogram if halves == 0 else far(sinogram)] * halves, *tokens)


def last_block(here_ref, blocks):
    spot = jnp.bitwise_xor(lax.rem(here_ref[0], G), G - 1)
    last = blocks[0]
    for m in range(1, G):
        last = jnp.where(spot == m, blocks[m], last)
    return last


def pack_kernel(here_ref, *refs):
    in_refs, (all_ref, last_ref) = refs[:G], refs[-2:]
    side = in_refs[0].shape[0]
    for m in range(G):
        all_ref[m * side : (m + 1) * side] = in_refs[m][:side]
    last_ref[:side] = last_block(here_ref, [ref[:side] for ref in in_refs])
    if last_ref.shape[0] > side:
        all_ref[G * side :] = in_refs[G - 1][side:]
        last_ref[side:] = in_refs[G - 1][side:]


def pack(here, pieces, more, *tokens):
    side, cols = pieces[0][0].shape
    tile = 512
    shapes = [(G * side + more, cols), (side + more, cols)]
    specs = [across(array.shape, tile) for array in arrays_of(pieces)] if more else piece_specs(pieces, side, tile)
    return call(
        pack_kernel,
        1,
        grid=(cols // tile,),
        in_specs=[SMEM] + specs + [ANY] * len(tokens),
        out_specs=[across(shape, tile) for shape in shapes],
        results=[value(shape, BF16) for shape in shapes],
    )(here, *arrays_of(pieces), *tokens)


def split_kernel(groups, passing, here_ref, own_ref, got_ref, *refs):
    out_refs, wide = refs[-len(groups) - passing - 1 : -1], refs[-1]
    if passing:
        out_refs[-1][...] = refs[0][...]
    depth, rows, cols = own_ref.shape
    place = lax.rem(here_ref[0], G)

    def fill(ref):
        for j in range(cols // LANES):
            wide[j] = ref[:, :, j * LANES : (j + 1) * LANES].astype(F32).reshape(wide.shape[1:])

    @pl.when(place == G - 1)
    def _():
        fill(got_ref)

    @pl.when(place != G - 1)
    def _():
        fill(own_ref)

    for group, out_ref in zip(groups, out_refs):
        for n, m in enumerate(group):
            for j in range(cols // LANES):
                for start, row in rows_of(place, m):
                    block = wide.at[j][pl.ds(row, depth, stride=rows), :].astype(BF16)
                    out_ref[n * depth : (n + 1) * depth, start + j * LANES : start + (j + 1) * LANES] = block


def split_rows(here, own, got, chunk, groups, passing, *tokens):
    depth, rows, cols = own.shape
    first, count = chunk_tiles(chunk, cols)
    block = pl.BlockSpec((depth, rows, TILE), lambda i: (0, 0, first + i))
    shapes = [(len(group) * depth, cols) for group in groups] + [(depth, cols)] * len(passing)
    return call(
        functools.partial(split_kernel, groups, len(passing)),
        2,
        grid=(count,),
        in_specs=[SMEM, block, pl.BlockSpec((depth, rows, TILE), lambda i: (0, 0, i))]
        + piece_specs(passing, depth, ROWS * TILE) + [ANY] * len(tokens),
        out_specs=[across(shape, ROWS * TILE) for shape in shapes],
        results=[value(shape, BF16) for shape in shapes],
        scratch_shapes=[wide_tile(depth * rows)],
    )(here, far(own), got, *arrays_of(passing), *tokens)


def last_kernel(slabs, here_ref, cover_ref, offset_ref, *refs):
    w_ref, vol_ref, sino_ref, *refs = refs
    r_ref, tv_ref, vol, s, r, wide, tv, sem = refs[-8:]
    depth, rows, cols = sino_ref.shape

    count = cols // LANES

    def columns(j):
        return pl.ds(pl.multiple_of(j * LANES, LANES), LANES)

    def arrival(n, j):
        src, dst = ((vol_ref, vol), (sino_ref, s), (tv_ref, tv))[n]
        return pltpu.make_async_copy(src.at[:, :, columns(j)], dst.at[:, :, columns(j)], sem.at[n, j])

    def departure(n, j):
        src, dst = ((r, r_ref), (tv, tv_ref))[n]
        return pltpu.make_async_copy(src.at[:, :, columns(j)], dst.at[:, :, columns(j)], sem.at[3 + n, j])

    @pl.when(here_ref[0] == slabs - 1)
    def _():
        for j in range(count):
            for n in range(3):
                arrival(n, j).start()
        block = w_ref[offset_ref[slabs - 1, 0]]
        block = jnp.where(cover_ref[slabs - 1, 0] == 1, block, jnp.zeros_like(block))
        turned = block.astype(F32).T.astype(BF16)

        def column(j, _):
            at = columns(j)
            for n in range(3):
                arrival(n, j).wait()
            for n, ref in enumerate((s, tv, vol)):
                wide[n] = ref[:, :, at].astype(F32).reshape(wide.shape[1:])
            for row in range(rows):
                spot = pl.ds(row, depth, stride=rows)
                seen = jnp.dot(block, wide.at[2][spot, :].astype(BF16), preferred_element_type=F32)
                resid = (seen - wide.at[0][spot, :]).astype(BF16)
                wide.at[0][spot, :] = resid.astype(F32)
                wide.at[1][spot, :] += jnp.dot(turned, resid, preferred_element_type=F32)
            r[:, :, at] = wide[0].reshape(depth, rows, LANES).astype(BF16)
            tv[:, :, at] = wide[1].reshape(depth, rows, LANES)
            for n in range(2):
                departure(n, j).start()
            return 0

        lax.fori_loop(0, count, column, 0)
        for j in range(count):
            for n in range(2):
                departure(n, j).wait()


def last_group(here, coverage, offsets, weights, volume, sinogram, tv, *tokens):
    slabs = coverage.shape[0]
    depth, rows, cols = sinogram.shape
    return call(
        functools.partial(last_kernel, slabs),
        0,
        vmem=32,
        grid=(1,),
        in_specs=[SMEM, SMEM, SMEM, pl.BlockSpec(weights.shape, lambda i: (0, 0, 0))] + [ANY] * (3 + len(tokens)),
        out_specs=[ANY, ANY],
        results=[pltpu.HBM(sinogram.shape, BF16), pltpu.HBM(volume.shape, F32)],
        input_output_aliases={6: 1},
        scratch_shapes=[
            pltpu.VMEM(volume.shape, F32),
            pltpu.VMEM(sinogram.shape, BF16),
            pltpu.VMEM(sinogram.shape, BF16),
            pltpu.VMEM((3, depth * rows, LANES), F32),
            pltpu.VMEM(volume.shape, F32),
            pltpu.SemaphoreType.DMA((5, cols // LANES)),
        ],
    )(here, coverage, offsets, weights, far(volume), far(sinogram), far(tv), *tokens)


def natural(place, in_refs, wide, j):
    depth = in_refs[0].shape[0]
    rows = ROWS * len(in_refs)
    for m, ref in enumerate(in_refs):
        for start, row in rows_of(place, m):
            value = ref[:, start + j * LANES : start + (j + 1) * LANES].astype(F32)
            wide.at[j][pl.ds(row, depth, stride=rows), :] = value
    return wide[j].reshape(depth, rows, LANES)


def join_kernel(here_ref, *refs):
    in_refs, (out_ref, wide) = refs[:G], refs[-2:]
    for j in range(out_ref.shape[2] // LANES):
        out_ref[:, :, j * LANES : (j + 1) * LANES] = natural(lax.rem(here_ref[0], G), in_refs, wide, j).astype(BF16)


def join_rows(here, pieces, shape, *tokens):
    depth, rows, cols = shape
    _, count = chunk_tiles(0, cols)
    return call(
        join_kernel,
        0,
        grid=(count,),
        in_specs=[SMEM] + piece_specs(pieces, depth, ROWS * TILE) + [ANY] * len(tokens),
        out_specs=pl.BlockSpec((depth, rows, TILE), lambda i: (0, 0, i)),
        results=value((depth, rows, cols // CHUNKS), BF16),
        scratch_shapes=[wide_tile(depth * rows)],
    )(here, *arrays_of(pieces), *tokens)


def settle_kernel(slabs, count, here_ref, own_ref, above_ref, *refs):
    in_refs, (base_ref, out_ref, wide) = refs[:G], refs[-3:]
    step = pl.program_id(0)
    cols = out_ref.shape[2]
    place = lax.rem(here_ref[0], G)
    last = here_ref[0] == slabs - 1

    @pl.when(last)
    def _():
        pltpu.sync_copy(base_ref.at[:, :, pl.ds(pl.multiple_of(step * cols, cols), cols)], out_ref)

    @pl.when(jnp.logical_not(last) & (step < count) & (place == G - 1))
    def _():
        out_ref[...] = above_ref[...]

    @pl.when(jnp.logical_not(last) & (step < count) & (place != G - 1))
    def _():
        out_ref[...] = own_ref[...]

    @pl.when(jnp.logical_not(last) & (step >= count))
    def _():
        for j in range(cols // LANES):
            out_ref[:, :, j * LANES : (j + 1) * LANES] = natural(place, in_refs, wide, j).astype(BF16)


def settle(here, slabs, own, above, pieces, base, *tokens):
    depth, rows, cols = base.shape
    _, count = chunk_tiles(0, cols)
    block = (depth, rows, TILE)
    early = pl.BlockSpec(block, lambda i: (0, 0, jnp.minimum(i, count - 1)))
    late = [
        pl.BlockSpec((depth, ROWS * TILE), lambda i, at=at: (at, jnp.maximum(i - count, 0))) for _, at in pieces
    ]
    return call(
        functools.partial(settle_kernel, slabs, count),
        0,
        grid=(CHUNKS * count,),
        in_specs=[SMEM, early, early] + late + [ANY] * (len(tokens) + 1),
        out_specs=pl.BlockSpec(block, lambda i: (0, 0, i)),
        results=pltpu.HBM(base.shape, BF16),
        scratch_shapes=[wide_tile(depth * rows)],
    )(here, own, above, *arrays_of(pieces), *tokens, far(base))


def finish_kernel(here_ref, tv_ref, *refs):
    in_refs, (out_ref, wide) = refs[:G], refs[-2:]
    for j in range(out_ref.shape[2] // LANES):
        at = pl.ds(j * LANES, LANES)
        out_ref[:, :, at] = tv_ref[:, :, at] + natural(lax.rem(here_ref[0], G), in_refs, wide, j)


def finish(here, chunk, tv, pieces, *tokens):
    depth, rows, cols = tv.shape
    first, count = chunk_tiles(chunk, cols)
    part = pl.BlockSpec((depth, rows, TILE), lambda i: (0, 0, first + i))
    return call(
        finish_kernel,
        0,
        grid=(count,),
        in_specs=[SMEM, part] + piece_specs(pieces, depth, ROWS * TILE) + [ANY] * len(tokens),
        out_specs=part,
        results=pltpu.HBM(tv.shape, F32),
        input_output_aliases={1: 0},
        scratch_shapes=[wide_tile(depth * rows)],
    )(here, far(tv), *arrays_of(pieces), *tokens)


def band_kernel(slabs, span, here_ref, cover_ref, offset_ref, w_ref, *refs):
    proj_ref, back_ref, turned = refs[-3:]
    side = w_ref.shape[1]
    place = lax.rem(here_ref[0], G)
    first = here_ref[0] - place
    zero = jnp.zeros((side, side), BF16)
    for i in range(w_ref.shape[0]):
        turned[i] = w_ref[i].astype(F32).T.astype(BF16)

    def block(ref, i, j):
        k = j - i
        known, step = jnp.clip(i, 0, slabs - 1), jnp.clip(k, 0, span - 1)
        inside = (i >= 0) & (i < slabs) & (j >= 0) & (j < slabs) & (k >= 0) & (k < span)
        live = inside & (cover_ref[known, step] == 1)
        return jnp.where(live, ref[offset_ref[known, step]], zero)

    def slab(m):
        return first + jnp.bitwise_xor(place, m)

    def group(m):
        to = jnp.bitwise_xor(place, m)
        return first + jnp.where(to == G - 1, -1, to)

    seen = [slab(m) for m in range(G)] + [slab(m) + G for m in range(G)] + [first - 1]
    seeing = [group(m) for m in range(G)] + [group(m) - G for m in range(G)] + [first + G - 1]
    for r in range(G):
        for s in range(2 * G + 1):
            at = (pl.ds(r * side, side), pl.ds(s * side, side))
            proj_ref[at] = block(w_ref, group(r), seen[s])
            back_ref[at] = block(turned, seeing[s], slab(r))


def bands(here, coverage, offsets, weights, *tokens):
    slabs, span = coverage.shape
    side = weights.shape[1]
    shape = (G * side, (2 * G + 1) * side)
    return call(
        functools.partial(band_kernel, slabs, span),
        9,
        in_specs=[SMEM, SMEM, SMEM, pl.BlockSpec(weights.shape, lambda i: (0, 0, 0))] + [ANY] * len(tokens),
        grid=(1,),
        out_specs=[pl.BlockSpec(shape, lambda i: (0, 0))] * 2,
        results=[value(shape, BF16)] * 2,
        scratch_shapes=[pltpu.VMEM(weights.shape, BF16)],
    )(here, coverage, offsets, weights, *tokens)


def project_kernel(groups, here_ref, band_ref, own_ref, high_ref, low_ref, *refs):
    sino_refs, (r_ref, down_ref, *group_refs) = refs[:G], refs[-len(groups) - 2 :]
    side = sino_refs[0].shape[0]
    seen = jnp.concatenate([own_ref[...], high_ref[...], low_ref[...]], axis=0)
    total = jnp.dot(band_ref[...], seen, preferred_element_type=F32)
    resid = [(total[m * side : (m + 1) * side] - ref[...].astype(F32)).astype(BF16) for m, ref in enumerate(sino_refs)]
    for m in range(G):
        r_ref[m * side : (m + 1) * side] = resid[m]
    for group, group_ref in zip(groups, group_refs):
        for n, m in enumerate(group):
            group_ref[n * side : (n + 1) * side] = resid[m]
    down_ref[...] = last_block(here_ref, resid)


def project(here, band, own, high, low, sinos, groups, *tokens):
    n, side = band.shape[0], band.shape[0] // G
    cols = own.shape[1]
    tile = 256
    many, one = pl.BlockSpec((n, tile), lambda i: (0, i)), pl.BlockSpec((side, tile), lambda i: (0, i))
    shapes = [(n, cols), (side, cols)] + [(len(group) * side, cols) for group in groups]
    return call(
        functools.partial(project_kernel, groups),
        3,
        grid=(cols // tile,),
        in_specs=[SMEM, pl.BlockSpec(band.shape, lambda i: (0, 0)), many, many, one]
        + piece_specs(sinos, side, tile)
        + [ANY] * len(tokens),
        out_specs=[across(shape, tile) for shape in shapes],
        results=[value(shape, BF16) for shape in shapes],
    )(here, band, own, high, low, *arrays_of(sinos), *tokens)


def back_kernel(dealing, here_ref, band_ref, own_ref, low_ref, high_ref, *refs):
    out_refs = refs[-G:]
    side = high_ref.shape[0]
    seeing = jnp.concatenate([own_ref[...], low_ref[...], high_ref[...]], axis=0)
    total = jnp.dot(band_ref[...], seeing, preferred_element_type=F32)
    place = lax.rem(here_ref[0], G)
    for m, out_ref in enumerate(out_refs):
        out_ref[:side] = total[m * side : (m + 1) * side].astype(BF16)
        if dealing:
            last = jnp.bitwise_xor(place, m) == G - 1
            out_ref[side:] = jnp.where(last, refs[1][...], refs[0][m * side : (m + 1) * side])


def back(here, band, own, low, high, dealt, *tokens):
    n, side = band.shape[0], band.shape[0] // G
    cols = own.shape[1]
    tile = 256
    many = pl.BlockSpec((n, tile), lambda i: (0, i))
    one = pl.BlockSpec((side, tile), lambda i: (0, i))
    out = ((2 if dealt else 1) * side, cols)
    return call(
        functools.partial(back_kernel, bool(dealt)),
        0,
        grid=(cols // tile,),
        in_specs=[SMEM, pl.BlockSpec(band.shape, lambda i: (0, 0)), many, many, one]
        + ([many, one] if dealt else [])
        + [ANY] * len(tokens),
        out_specs=[across(out, tile)] * G,
        results=[value(out, BF16)] * G,
    )(here, band, own, low, high, *dealt, *tokens)


def tv_flux(cur, above):
    rows, cols = cur.shape
    row = lax.broadcasted_iota(jnp.int32, (rows, cols), 0)
    col = lax.broadcasted_iota(jnp.int32, (rows, cols), 1)
    dz = above - cur
    dy = jnp.where(row == rows - 1, 0.0, pltpu.roll(cur, rows - 1, 0)) - cur
    dx = jnp.where(col == cols - 1, 0.0, pltpu.roll(cur, cols - 1, 1)) - cur
    scale = 0.5 * lax.rsqrt(dz * dz + dy * dy + dx * dx + 0.25)
    return dz * scale, dy * scale, dx * scale


def tv_below(cur, above):
    return tv_flux(cur, above)[0]


def tv_slice(cur, above, below_flux):
    rows, cols = cur.shape
    row = lax.broadcasted_iota(jnp.int32, (rows, cols), 0)
    col = lax.broadcasted_iota(jnp.int32, (rows, cols), 1)
    fz, fy, fx = tv_flux(cur, above)
    sides = 0.5 * cur * lax.rsqrt(cur * cur + 0.25)
    fy_low = jnp.where(row == 0, sides, pltpu.roll(fy, 1, 0))
    fx_low = jnp.where(col == 0, sides, pltpu.roll(fx, 1, 1))
    return (below_flux - fz) + (fy_low - fy) + (fx_low - fx), fz


def tv_kernel(here_ref, near_ref, next_level_ref, far_ref, last_level_ref, next_ref, vol_ref, *refs):
    out_ref, done_ref, flux_ref = refs[-3:]
    step = pl.program_id(0)
    deep, rows, _ = vol_ref.shape
    place = lax.rem(here_ref[0], G)

    @pl.when(step == 0)
    def _():
        inside = jnp.where(place == 2, far_ref[...], near_ref[...])
        low = jnp.where(place == 0, last_level_ref[...], inside)[rows:].astype(F32)
        flux_ref[...] = tv_below(low, vol_ref[0])

    def body(z, flux):
        out_ref[z], flux = tv_slice(vol_ref[z], vol_ref[z + 1], flux)
        return flux

    flux = lax.fori_loop(0, deep - 1, body, flux_ref[...], unroll=5)
    inside = jnp.where(place == 1, far_ref[...], near_ref[...])
    high = jnp.where(place == G - 1, next_level_ref[...], inside)[:rows].astype(F32)
    above = jnp.where(step == pl.num_programs(0) - 1, high, next_ref[0])
    out_ref[deep - 1], flux_ref[...] = tv_slice(vol_ref[deep - 1], above, flux)
    done_ref[...] = flux_ref[:, : done_ref.shape[1]]


def half_tv(here, volume, ends, *tokens):
    depth, rows, cols = volume.shape
    deep = 16
    edges = [pl.BlockSpec((2 * rows, cols), lambda i, last=end.shape[0] // (2 * rows) - 1: (last, 0)) for end in ends]
    body = pl.BlockSpec((deep, rows, cols), lambda i: (i, 0, 0))
    after = pl.BlockSpec((1, rows, cols), lambda i: (jnp.minimum((i + 1) * deep, depth - 1), 0, 0))
    return call(
        tv_kernel,
        0,
        grid=(depth // deep,),
        in_specs=[SMEM] + edges + [after, body] + [ANY] * len(tokens),
        out_specs=[body, pl.BlockSpec((rows, LANES), lambda i: (0, 0))],
        results=[pltpu.HBM(volume.shape, F32), value((rows, LANES), F32)],
        scratch_shapes=[pltpu.VMEM((rows, cols), F32)],
    )(here, *ends, far(volume), far(volume), *tokens)


def local(volume, sinogram, weights, coverage, offsets):
    slabs = lax.axis_size("slab")
    here = lax.axis_index("slab").astype(jnp.int32).reshape(1)
    depth, rows, _ = volume.shape
    single = ((0,), (1,), (2,), (3,))
    paired = ((0,), (1,), (2, 3))

    def tied(array, *others):
        return lax.optimization_barrier((array, *others))[0]

    def beyond(over, *others):
        return swapped(tied(over, *others)[depth:], 1)

    vols0 = cast_rows(here, volume, 0, single, True, None)
    got_vols0 = direct(vols0)
    v0, v1, v23, sent0, sent1 = cast_rows(here, volume, 1, paired, False, sinogram, vols0[1])
    got0 = moved(sent0, G, only=G - 1)
    over = swapped(v23, 2)
    band_p, band_b = bands(here, coverage, offsets, weights, v1)
    got1 = moved(tied(sent1, band_p), G, only=G - 1)
    own0, edge0 = pack(here, [(array, 0) for array in got_vols0], 2 * rows, band_p)
    high0, near = moved(own0, -G), swapped(tied(v1, own0), 1)
    s0, s1, s23, over_beyond = split_rows(here, sinogram, got0, 0, paired, [(over, 1)], near)
    s_near, s_over = swapped(s1, 1), swapped(s23, 2)
    low0 = moved(tied(edge0, s_near), G)
    own1, edge1 = pack(here, [(v0, 0), (near, 0), (over, 0), (swapped(over_beyond, 1), 0)], 0)
    low1, high1 = moved(edge1, G), moved(own1, -G)
    t0, t1, t23 = split_rows(here, sinogram, got1, 1, paired, [], own1)
    sinos0 = [(s0, 0), (s_near, 0), (s_over, 0), (beyond(s_over, t0), 0)]


    resid0, down0, r1, r23 = project(here, band_p, own0, high0, low0, sinos0, paired[1:], low1)
    from_low0, from_high0 = moved(resid0, G), moved(down0, -G)
    t_near, t_over = swapped(t1, 1), swapped(t23, 2)
    r_near, r_over = swapped(tied(r1, t_near), 1), swapped(tied(r23, t_near), 2)
    tv, tv_done = half_tv(here, volume, [got_vols0[1], high0, got_vols0[3], low0], resid0)
    sinos1 = [(t0, 0), (t_near, 0), (t_over, 0), (beyond(t_over, tv_done), 0)]
    resid1, down1 = project(here, band_p, own1, high1, low1, sinos1, (), tv_done, r_near, r_over)
    from_low1, from_high1 = moved(resid1, G), moved(down1, -G)

    backs0 = back(here, band_b, resid0, from_low0, from_high0, [resid1, from_high1])
    got_backs0 = direct(backs0)
    r_pieces = [(resid0, 0), (r_near, 0), (r_over, 0), (beyond(r_over, resid1), 0)]
    natural0 = join_rows(here, r_pieces, sinogram.shape, backs0[0])
    above0 = moved(natural0, -G, only=G - 1)
    r_last, tv = last_group(here, coverage, offsets, weights, volume, sinogram, tv, backs0[0])
    backs1 = back(here, band_b, resid1, from_low1, from_high1, [], far(r_last), natural0)
    got_backs1 = direct(backs1)
    gradient = finish(here, 0, tv, [(array, 0) for array in got_backs0], backs1[0])
    residual = settle(here, slabs, natural0, above0, [(array, 1) for array in got_backs0], r_last, backs1[0])
    gradient = finish(here, 1, gradient, [(array, 0) for array in got_backs1], far(residual))
    return (gradient, residual)


def solution(mesh):
    placed = (P("slab", "grp", None), P("slab", "grp", None), P(), P(), P())
    return jax.shard_map(
        local,
        mesh=mesh,
        in_specs=placed,
        out_specs=(P("slab", "grp", None), P("slab", "grp", None)),
        check_vma=False,
    )
```

```python
import functools

import jax
import jax.numpy as jnp
from jax import lax
from jax.experimental import pallas as pl
from jax.experimental.pallas import tpu as pltpu
from jax.sharding import PartitionSpec as P

G = 4
CHUNKS = 2
ROWS = 2
TILE = 256
F32 = jnp.float32
BF16 = jnp.bfloat16
MIB = 1024 * 1024
LANES = 128
SMEM = pl.BlockSpec(memory_space=pltpu.SMEM)
VMEM = pl.BlockSpec(memory_space=pltpu.VMEM)
ANY = pl.BlockSpec(memory_space=pl.ANY)


def moved(value, steps, only=None):
    count = lax.axis_size("slab")
    first, last = max(0, -steps), min(count, count - steps)
    pairs = [(i, i + steps) for i in range(first, last) if only is None or i % G == only]
    return lax.ppermute(value, "slab", pairs)


def swapped(value, bits):
    count = lax.axis_size("slab")
    return lax.ppermute(value, "slab", [(i, i ^ bits) for i in range(count)])


def direct(arrays):
    return [array if m == 0 else swapped(array, m) for m, array in enumerate(arrays)]


def call(kernel, us, *, results, vmem=16, **how):
    return pl.pallas_call(
        kernel,
        out_shape=results,
        compiler_params=pltpu.CompilerParams(vmem_limit_bytes=vmem * MIB),
        cost_estimate=pl.CostEstimate(flops=int(us * 1.15e9), bytes_accessed=1000, transcendentals=0),
        **how,
    )


def value(shape, dtype):
    return jax.ShapeDtypeStruct(shape, dtype)


def far(array):
    return pltpu.with_memory_space_constraint(array, pltpu.HBM)


def across(shape, tile):
    block = shape[:-1] + (tile,)
    return pl.BlockSpec(block, lambda i: (0,) * (len(shape) - 1) + (i,))


def piece_specs(pieces, side, tile):
    return [pl.BlockSpec((side, tile), lambda i, at=at: (at, i)) for _, at in pieces]


def arrays_of(pieces):
    return [array for array, _ in pieces]


def rows_of(place, m):
    first = ROWS * jnp.bitwise_xor(place, m)
    return [(h * TILE, first + h) for h in range(ROWS)]


def wide_tile(rows_deep):
    return pltpu.VMEM((TILE // LANES, rows_deep, LANES), F32)


def chunk_tiles(chunk, cols):
    count = cols // CHUNKS // TILE
    return chunk * count, count


def cast_kernel(groups, ends, halves, here_ref, *refs):
    parts = TILE // LANES
    vol_refs, end_refs = refs[:parts], refs[parts : parts + ends]
    for half_ref, sent_ref in zip(refs[parts + ends : parts + ends + halves], refs[len(refs) - halves :]):
        sent_ref[...] = half_ref[...]
    out_refs = refs[len(refs) - halves - len(groups) : len(refs) - halves]
    rows = ROWS * G
    depth = vol_refs[0].shape[0] // rows
    place = lax.rem(here_ref[0], G)
    for j, vol_ref in enumerate(vol_refs):
        for group, out_ref in zip(groups, out_refs):
            for n, m in enumerate(group):
                for start, row in rows_of(place, m):
                    at = pl.ds(start + j * LANES, LANES)
                    out_ref[n * depth : (n + 1) * depth, at] = vol_ref[pl.ds(row, depth, stride=rows), :].astype(BF16)
    if ends:
        both = jnp.concatenate([ref[...] for ref in end_refs], axis=0).astype(BF16)
        for group, out_ref in zip(groups, out_refs):
            if group[0] % 2:
                out_ref[depth:, :] = both


def cast_rows(here, volume, chunk, groups, ends, sinogram, *tokens):
    depth, rows, cols = volume.shape
    flat = far(volume.reshape(depth * rows, cols))
    first, count = chunk_tiles(chunk, cols)
    parts, width = TILE // LANES, ROWS * TILE
    shapes = [(len(group) * depth + (2 * rows if ends and group[0] % 2 else 0), cols) for group in groups]
    edges = [pl.BlockSpec((rows, width), lambda i, z=z: (z, i)) for z in (0, depth - 1)] if ends else []
    halves = 0 if sinogram is None else CHUNKS
    block = (depth, rows, TILE)
    return call(
        functools.partial(cast_kernel, groups, len(edges), halves),
        2,
        grid=(count,),
        in_specs=[SMEM]
        + [pl.BlockSpec((depth * rows, LANES), lambda i, j=j: (0, (first + i) * parts + j)) for j in range(parts)]
        + edges
        + [pl.BlockSpec(block, lambda i, c=c: (0, 0, c * count + i)) for c in range(halves)]
        + [ANY] * len(tokens),
        out_specs=[across(shape, width) for shape in shapes] + [pl.BlockSpec(block, lambda i: (0, 0, i))] * halves,
        results=[(pltpu.HBM if group[0] == 0 else value)(shape, BF16) for group, shape in zip(groups, shapes)]
        + [value((depth, rows, cols // CHUNKS), BF16)] * halves,
    )(here, *[flat] * (parts + len(edges)), *[sinogram if halves == 0 else far(sinogram)] * halves, *tokens)


def last_block(here_ref, blocks):
    spot = jnp.bitwise_xor(lax.rem(here_ref[0], G), G - 1)
    last = blocks[0]
    for m in range(1, G):
        last = jnp.where(spot == m, blocks[m], last)
    return last


def pack_kernel(here_ref, *refs):
    in_refs, (all_ref, last_ref) = refs[:G], refs[-2:]
    side = in_refs[0].shape[0]
    for m in range(G):
        all_ref[m * side : (m + 1) * side] = in_refs[m][:side]
    last_ref[:side] = last_block(here_ref, [ref[:side] for ref in in_refs])
    if last_ref.shape[0] > side:
        all_ref[G * side :] = in_refs[G - 1][side:]
        last_ref[side:] = in_refs[G - 1][side:]


def pack(here, pieces, more, *tokens):
    side, cols = pieces[0][0].shape
    tile = 512
    shapes = [(G * side + more, cols), (side + more, cols)]
    specs = [across(array.shape, tile) for array in arrays_of(pieces)] if more else piece_specs(pieces, side, tile)
    return call(
        pack_kernel,
        1,
        grid=(cols // tile,),
        in_specs=[SMEM] + specs + [ANY] * len(tokens),
        out_specs=[across(shape, tile) for shape in shapes],
        results=[value(shape, BF16) for shape in shapes],
    )(here, *arrays_of(pieces), *tokens)


def split_kernel(groups, passing, here_ref, own_ref, got_ref, *refs):
    out_refs, wide = refs[-len(groups) - passing - 1 : -1], refs[-1]
    if passing:
        out_refs[-1][...] = refs[0][...]
    depth, rows, cols = own_ref.shape
    place = lax.rem(here_ref[0], G)

    def fill(ref):
        for j in range(cols // LANES):
            wide[j] = ref[:, :, j * LANES : (j + 1) * LANES].astype(F32).reshape(wide.shape[1:])

    @pl.when(place == G - 1)
    def _():
        fill(got_ref)

    @pl.when(place != G - 1)
    def _():
        fill(own_ref)

    for group, out_ref in zip(groups, out_refs):
        for n, m in enumerate(group):
            for j in range(cols // LANES):
                for start, row in rows_of(place, m):
                    block = wide.at[j][pl.ds(row, depth, stride=rows), :].astype(BF16)
                    out_ref[n * depth : (n + 1) * depth, start + j * LANES : start + (j + 1) * LANES] = block


def split_rows(here, own, got, chunk, groups, passing, *tokens):
    depth, rows, cols = own.shape
    first, count = chunk_tiles(chunk, cols)
    block = pl.BlockSpec((depth, rows, TILE), lambda i: (0, 0, first + i))
    shapes = [(len(group) * depth, cols) for group in groups] + [(depth, cols)] * len(passing)
    return call(
        functools.partial(split_kernel, groups, len(passing)),
        2,
        grid=(count,),
        in_specs=[SMEM, block, pl.BlockSpec((depth, rows, TILE), lambda i: (0, 0, i))]
        + piece_specs(passing, depth, ROWS * TILE) + [ANY] * len(tokens),
        out_specs=[across(shape, ROWS * TILE) for shape in shapes],
        results=[value(shape, BF16) for shape in shapes],
        scratch_shapes=[wide_tile(depth * rows)],
    )(here, far(own), got, *arrays_of(passing), *tokens)


def last_kernel(slabs, here_ref, cover_ref, offset_ref, *refs):
    w_ref, vol_ref, sino_ref, *refs = refs
    r_ref, tv_ref, vol, s, r, wide, tv, sem = refs[-8:]
    depth, rows, cols = sino_ref.shape

    count = cols // LANES

    def columns(j):
        return pl.ds(pl.multiple_of(j * LANES, LANES), LANES)

    def arrival(n, j):
        src, dst = ((vol_ref, vol), (sino_ref, s), (tv_ref, tv))[n]
        return pltpu.make_async_copy(src.at[:, :, columns(j)], dst.at[:, :, columns(j)], sem.at[n, j])

    def departure(n, j):
        src, dst = ((r, r_ref), (tv, tv_ref))[n]
        return pltpu.make_async_copy(src.at[:, :, columns(j)], dst.at[:, :, columns(j)], sem.at[3 + n, j])

    @pl.when(here_ref[0] == slabs - 1)
    def _():
        for j in range(count):
            for n in range(3):
                arrival(n, j).start()
        block = w_ref[offset_ref[slabs - 1, 0]]
        block = jnp.where(cover_ref[slabs - 1, 0] == 1, block, jnp.zeros_like(block))
        turned = block.astype(F32).T.astype(BF16)

        def column(j, _):
            at = columns(j)
            for n in range(3):
                arrival(n, j).wait()
            for n, ref in enumerate((s, tv, vol)):
                wide[n] = ref[:, :, at].astype(F32).reshape(wide.shape[1:])
            for row in range(rows):
                spot = pl.ds(row, depth, stride=rows)
                seen = jnp.dot(block, wide.at[2][spot, :].astype(BF16), preferred_element_type=F32)
                resid = (seen - wide.at[0][spot, :]).astype(BF16)
                wide.at[0][spot, :] = resid.astype(F32)
                wide.at[1][spot, :] += jnp.dot(turned, resid, preferred_element_type=F32)
            r[:, :, at] = wide[0].reshape(depth, rows, LANES).astype(BF16)
            tv[:, :, at] = wide[1].reshape(depth, rows, LANES)
            for n in range(2):
                departure(n, j).start()
            return 0

        lax.fori_loop(0, count, column, 0)
        for j in range(count):
            for n in range(2):
                departure(n, j).wait()


def last_group(here, coverage, offsets, weights, volume, sinogram, tv, *tokens):
    slabs = coverage.shape[0]
    depth, rows, cols = sinogram.shape
    return call(
        functools.partial(last_kernel, slabs),
        0,
        vmem=32,
        grid=(1,),
        in_specs=[SMEM, SMEM, SMEM, pl.BlockSpec(weights.shape, lambda i: (0, 0, 0))] + [ANY] * (3 + len(tokens)),
        out_specs=[ANY, ANY],
        results=[pltpu.HBM(sinogram.shape, BF16), pltpu.HBM(volume.shape, F32)],
        input_output_aliases={6: 1},
        scratch_shapes=[
            pltpu.VMEM(volume.shape, F32),
            pltpu.VMEM(sinogram.shape, BF16),
            pltpu.VMEM(sinogram.shape, BF16),
            pltpu.VMEM((3, depth * rows, LANES), F32),
            pltpu.VMEM(volume.shape, F32),
            pltpu.SemaphoreType.DMA((5, cols // LANES)),
        ],
    )(here, coverage, offsets, weights, far(volume), far(sinogram), far(tv), *tokens)


def natural(place, in_refs, wide, j):
    depth = in_refs[0].shape[0]
    rows = ROWS * len(in_refs)
    for m, ref in enumerate(in_refs):
        for start, row in rows_of(place, m):
            value = ref[:, start + j * LANES : start + (j + 1) * LANES].astype(F32)
            wide.at[j][pl.ds(row, depth, stride=rows), :] = value
    return wide[j].reshape(depth, rows, LANES)


def join_kernel(here_ref, *refs):
    in_refs, (out_ref, wide) = refs[:G], refs[-2:]
    for j in range(out_ref.shape[2] // LANES):
        out_ref[:, :, j * LANES : (j + 1) * LANES] = natural(lax.rem(here_ref[0], G), in_refs, wide, j).astype(BF16)


def join_rows(here, pieces, shape, *tokens):
    depth, rows, cols = shape
    _, count = chunk_tiles(0, cols)
    return call(
        join_kernel,
        0,
        grid=(count,),
        in_specs=[SMEM] + piece_specs(pieces, depth, ROWS * TILE) + [ANY] * len(tokens),
        out_specs=pl.BlockSpec((depth, rows, TILE), lambda i: (0, 0, i)),
        results=value((depth, rows, cols // CHUNKS), BF16),
        scratch_shapes=[wide_tile(depth * rows)],
    )(here, *arrays_of(pieces), *tokens)


def settle_kernel(slabs, count, here_ref, own_ref, above_ref, *refs):
    in_refs, (base_ref, out_ref, wide) = refs[:G], refs[-3:]
    step = pl.program_id(0)
    cols = out_ref.shape[2]
    place = lax.rem(here_ref[0], G)
    last = here_ref[0] == slabs - 1

    @pl.when(last)
    def _():
        pltpu.sync_copy(base_ref.at[:, :, pl.ds(pl.multiple_of(step * cols, cols), cols)], out_ref)

    @pl.when(jnp.logical_not(last) & (step < count) & (place == G - 1))
    def _():
        out_ref[...] = above_ref[...]

    @pl.when(jnp.logical_not(last) & (step < count) & (place != G - 1))
    def _():
        out_ref[...] = own_ref[...]

    @pl.when(jnp.logical_not(last) & (step >= count))
    def _():
        for j in range(cols // LANES):
            out_ref[:, :, j * LANES : (j + 1) * LANES] = natural(place, in_refs, wide, j).astype(BF16)


def settle(here, slabs, own, above, pieces, base, *tokens):
    depth, rows, cols = base.shape
    _, count = chunk_tiles(0, cols)
    block = (depth, rows, TILE)
    early = pl.BlockSpec(block, lambda i: (0, 0, jnp.minimum(i, count - 1)))
    late = [
        pl.BlockSpec((depth, ROWS * TILE), lambda i, at=at: (at, jnp.maximum(i - count, 0))) for _, at in pieces
    ]
    return call(
        functools.partial(settle_kernel, slabs, count),
        0,
        grid=(CHUNKS * count,),
        in_specs=[SMEM, early, early] + late + [ANY] * (len(tokens) + 1),
        out_specs=pl.BlockSpec(block, lambda i: (0, 0, i)),
        results=pltpu.HBM(base.shape, BF16),
        scratch_shapes=[wide_tile(depth * rows)],
    )(here, own, above, *arrays_of(pieces), *tokens, far(base))


def finish_kernel(here_ref, tv_ref, *refs):
    in_refs, (out_ref, wide) = refs[:G], refs[-2:]
    for j in range(out_ref.shape[2] // LANES):
        at = pl.ds(j * LANES, LANES)
        out_ref[:, :, at] = tv_ref[:, :, at] + natural(lax.rem(here_ref[0], G), in_refs, wide, j)


def finish(here, chunk, tv, pieces, *tokens):
    depth, rows, cols = tv.shape
    first, count = chunk_tiles(chunk, cols)
    part = pl.BlockSpec((depth, rows, TILE), lambda i: (0, 0, first + i))
    return call(
        finish_kernel,
        0,
        grid=(count,),
        in_specs=[SMEM, part] + piece_specs(pieces, depth, ROWS * TILE) + [ANY] * len(tokens),
        out_specs=part,
        results=pltpu.HBM(tv.shape, F32),
        input_output_aliases={1: 0},
        scratch_shapes=[wide_tile(depth * rows)],
    )(here, far(tv), *arrays_of(pieces), *tokens)


def band_kernel(slabs, span, here_ref, cover_ref, offset_ref, w_ref, *refs):
    proj_ref, back_ref, turned = refs[-3:]
    side = w_ref.shape[1]
    place = lax.rem(here_ref[0], G)
    first = here_ref[0] - place
    zero = jnp.zeros((side, side), BF16)
    for i in range(w_ref.shape[0]):
        turned[i] = w_ref[i].astype(F32).T.astype(BF16)

    def block(ref, i, j):
        k = j - i
        known, step = jnp.clip(i, 0, slabs - 1), jnp.clip(k, 0, span - 1)
        inside = (i >= 0) & (i < slabs) & (j >= 0) & (j < slabs) & (k >= 0) & (k < span)
        live = inside & (cover_ref[known, step] == 1)
        return jnp.where(live, ref[offset_ref[known, step]], zero)

    def slab(m):
        return first + jnp.bitwise_xor(place, m)

    def group(m):
        to = jnp.bitwise_xor(place, m)
        return first + jnp.where(to == G - 1, -1, to)

    seen = [slab(m) for m in range(G)] + [slab(m) + G for m in range(G)] + [first - 1]
    seeing = [group(m) for m in range(G)] + [group(m) - G for m in range(G)] + [first + G - 1]
    for r in range(G):
        for s in range(2 * G + 1):
            at = (pl.ds(r * side, side), pl.ds(s * side, side))
            proj_ref[at] = block(w_ref, group(r), seen[s])
            back_ref[at] = block(turned, seeing[s], slab(r))


def bands(here, coverage, offsets, weights, *tokens):
    slabs, span = coverage.shape
    side = weights.shape[1]
    shape = (G * side, (2 * G + 1) * side)
    return call(
        functools.partial(band_kernel, slabs, span),
        9,
        in_specs=[SMEM, SMEM, SMEM, pl.BlockSpec(weights.shape, lambda i: (0, 0, 0))] + [ANY] * len(tokens),
        grid=(1,),
        out_specs=[pl.BlockSpec(shape, lambda i: (0, 0))] * 2,
        results=[value(shape, BF16)] * 2,
        scratch_shapes=[pltpu.VMEM(weights.shape, BF16)],
    )(here, coverage, offsets, weights, *tokens)


def project_kernel(groups, here_ref, band_ref, own_ref, high_ref, low_ref, *refs):
    sino_refs, (r_ref, down_ref, *group_refs) = refs[:G], refs[-len(groups) - 2 :]
    side = sino_refs[0].shape[0]
    seen = jnp.concatenate([own_ref[...], high_ref[...], low_ref[...]], axis=0)
    total = jnp.dot(band_ref[...], seen, preferred_element_type=F32)
    resid = [(total[m * side : (m + 1) * side] - ref[...].astype(F32)).astype(BF16) for m, ref in enumerate(sino_refs)]
    for m in range(G):
        r_ref[m * side : (m + 1) * side] = resid[m]
    for group, group_ref in zip(groups, group_refs):
        for n, m in enumerate(group):
            group_ref[n * side : (n + 1) * side] = resid[m]
    down_ref[...] = last_block(here_ref, resid)


def project(here, band, own, high, low, sinos, groups, *tokens):
    n, side = band.shape[0], band.shape[0] // G
    cols = own.shape[1]
    tile = cols
    many, one = pl.BlockSpec((n, tile), lambda i: (0, i)), pl.BlockSpec((side, tile), lambda i: (0, i))
    shapes = [(n, cols), (side, cols)] + [(len(group) * side, cols) for group in groups]
    return call(
        functools.partial(project_kernel, groups),
        3,
        grid=(cols // tile,),
        in_specs=[SMEM, pl.BlockSpec(band.shape, lambda i: (0, 0)), many, many, one]
        + piece_specs(sinos, side, tile)
        + [ANY] * len(tokens),
        out_specs=[across(shape, tile) for shape in shapes],
        results=[value(shape, BF16) for shape in shapes],
    )(here, band, own, high, low, *arrays_of(sinos), *tokens)


def back_kernel(dealing, here_ref, band_ref, own_ref, low_ref, high_ref, *refs):
    out_refs = refs[-G:]
    side = high_ref.shape[0]
    seeing = jnp.concatenate([own_ref[...], low_ref[...], high_ref[...]], axis=0)
    total = jnp.dot(band_ref[...], seeing, preferred_element_type=F32)
    place = lax.rem(here_ref[0], G)
    for m, out_ref in enumerate(out_refs):
        out_ref[:side] = total[m * side : (m + 1) * side].astype(BF16)
        if dealing:
            last = jnp.bitwise_xor(place, m) == G - 1
            out_ref[side:] = jnp.where(last, refs[1][...], refs[0][m * side : (m + 1) * side])


def back(here, band, own, low, high, dealt, *tokens):
    n, side = band.shape[0], band.shape[0] // G
    cols = own.shape[1]
    tile = cols
    many = pl.BlockSpec((n, tile), lambda i: (0, i))
    one = pl.BlockSpec((side, tile), lambda i: (0, i))
    out = ((2 if dealt else 1) * side, cols)
    return call(
        functools.partial(back_kernel, bool(dealt)),
        0,
        grid=(cols // tile,),
        in_specs=[SMEM, pl.BlockSpec(band.shape, lambda i: (0, 0)), many, many, one]
        + ([many, one] if dealt else [])
        + [ANY] * len(tokens),
        out_specs=[across(out, tile)] * G,
        results=[value(out, BF16)] * G,
    )(here, band, own, low, high, *dealt, *tokens)


def tv_flux(cur, above):
    rows, cols = cur.shape
    row = lax.broadcasted_iota(jnp.int32, (rows, cols), 0)
    col = lax.broadcasted_iota(jnp.int32, (rows, cols), 1)
    dz = above - cur
    dy = jnp.where(row == rows - 1, 0.0, pltpu.roll(cur, rows - 1, 0)) - cur
    dx = jnp.where(col == cols - 1, 0.0, pltpu.roll(cur, cols - 1, 1)) - cur
    scale = 0.5 * lax.rsqrt(dz * dz + dy * dy + dx * dx + 0.25)
    return dz * scale, dy * scale, dx * scale


def tv_below(cur, above):
    return tv_flux(cur, above)[0]


def tv_slice(cur, above, below_flux):
    rows, cols = cur.shape
    row = lax.broadcasted_iota(jnp.int32, (rows, cols), 0)
    col = lax.broadcasted_iota(jnp.int32, (rows, cols), 1)
    fz, fy, fx = tv_flux(cur, above)
    sides = 0.5 * cur * lax.rsqrt(cur * cur + 0.25)
    fy_low = jnp.where(row == 0, sides, pltpu.roll(fy, 1, 0))
    fx_low = jnp.where(col == 0, sides, pltpu.roll(fx, 1, 1))
    return (below_flux - fz) + (fy_low - fy) + (fx_low - fx), fz


def tv_kernel(here_ref, near_ref, next_level_ref, far_ref, last_level_ref, next_ref, vol_ref, *refs):
    out_ref, done_ref, flux_ref = refs[-3:]
    step = pl.program_id(0)
    deep, rows, _ = vol_ref.shape
    place = lax.rem(here_ref[0], G)

    @pl.when(step == 0)
    def _():
        inside = jnp.where(place == 2, far_ref[...], near_ref[...])
        low = jnp.where(place == 0, last_level_ref[...], inside)[rows:].astype(F32)
        flux_ref[...] = tv_below(low, vol_ref[0])

    def body(z, flux):
        out_ref[z], flux = tv_slice(vol_ref[z], vol_ref[z + 1], flux)
        return flux

    flux = lax.fori_loop(0, deep - 1, body, flux_ref[...], unroll=5)
    inside = jnp.where(place == 1, far_ref[...], near_ref[...])
    high = jnp.where(place == G - 1, next_level_ref[...], inside)[:rows].astype(F32)
    above = jnp.where(step == pl.num_programs(0) - 1, high, next_ref[0])
    out_ref[deep - 1], flux_ref[...] = tv_slice(vol_ref[deep - 1], above, flux)
    done_ref[...] = flux_ref[:, : done_ref.shape[1]]


def half_tv(here, volume, ends, *tokens):
    depth, rows, cols = volume.shape
    deep = 16
    edges = [pl.BlockSpec((2 * rows, cols), lambda i, last=end.shape[0] // (2 * rows) - 1: (last, 0)) for end in ends]
    body = pl.BlockSpec((deep, rows, cols), lambda i: (i, 0, 0))
    after = pl.BlockSpec((1, rows, cols), lambda i: (jnp.minimum((i + 1) * deep, depth - 1), 0, 0))
    return call(
        tv_kernel,
        0,
        grid=(depth // deep,),
        in_specs=[SMEM] + edges + [after, body] + [ANY] * len(tokens),
        out_specs=[body, pl.BlockSpec((rows, LANES), lambda i: (0, 0))],
        results=[pltpu.HBM(volume.shape, F32), value((rows, LANES), F32)],
        scratch_shapes=[pltpu.VMEM((rows, cols), F32)],
    )(here, *ends, far(volume), far(volume), *tokens)


def local(volume, sinogram, weights, coverage, offsets):
    slabs = lax.axis_size("slab")
    here = lax.axis_index("slab").astype(jnp.int32).reshape(1)
    depth, rows, _ = volume.shape
    single = ((0,), (1,), (2,), (3,))
    paired = ((0,), (1,), (2, 3))

    def tied(array, *others):
        return lax.optimization_barrier((array, *others))[0]

    def beyond(over, *others):
        return swapped(tied(over, *others)[depth:], 1)

    vols0 = cast_rows(here, volume, 0, single, True, None)
    got_vols0 = direct(vols0)
    v0, v1, v23, sent0, sent1 = cast_rows(here, volume, 1, paired, False, sinogram, vols0[1])
    got0 = moved(sent0, G, only=G - 1)
    over = swapped(v23, 2)
    band_p, band_b = bands(here, coverage, offsets, weights, v1)
    got1 = moved(tied(sent1, band_p), G, only=G - 1)
    own0, edge0 = pack(here, [(array, 0) for array in got_vols0], 2 * rows, band_p)
    high0, near = moved(own0, -G), swapped(tied(v1, own0), 1)
    s0, s1, s23, over_beyond = split_rows(here, sinogram, got0, 0, paired, [(over, 1)], near)
    s_near, s_over = swapped(s1, 1), swapped(s23, 2)
    low0 = moved(tied(edge0, s_near), G)
    own1, edge1 = pack(here, [(v0, 0), (near, 0), (over, 0), (swapped(over_beyond, 1), 0)], 0)
    low1, high1 = moved(edge1, G), moved(own1, -G)
    t0, t1, t23 = split_rows(here, sinogram, got1, 1, paired, [], own1)
    sinos0 = [(s0, 0), (s_near, 0), (s_over, 0), (beyond(s_over, t0), 0)]


    resid0, down0, r1, r23 = project(here, band_p, own0, high0, low0, sinos0, paired[1:], low1)
    from_low0, from_high0 = moved(resid0, G), moved(down0, -G)
    t_near, t_over = swapped(t1, 1), swapped(t23, 2)
    r_near, r_over = swapped(tied(r1, t_near), 1), swapped(tied(r23, t_near), 2)
    tv, tv_done = half_tv(here, volume, [got_vols0[1], high0, got_vols0[3], low0], resid0)
    sinos1 = [(t0, 0), (t_near, 0), (t_over, 0), (beyond(t_over, tv_done), 0)]
    resid1, down1 = project(here, band_p, own1, high1, low1, sinos1, (), tv_done, r_near, r_over)
    from_low1, from_high1 = moved(resid1, G), moved(down1, -G)

    backs0 = back(here, band_b, resid0, from_low0, from_high0, [resid1, from_high1])
    got_backs0 = direct(backs0)
    r_pieces = [(resid0, 0), (r_near, 0), (r_over, 0), (beyond(r_over, resid1), 0)]
    natural0 = join_rows(here, r_pieces, sinogram.shape, backs0[0])
    above0 = moved(natural0, -G, only=G - 1)
    r_last, tv = last_group(here, coverage, offsets, weights, volume, sinogram, tv, backs0[0])
    backs1 = back(here, band_b, resid1, from_low1, from_high1, [], far(r_last), natural0)
    got_backs1 = direct(backs1)
    gradient = finish(here, 0, tv, [(array, 0) for array in got_backs0], backs1[0])
    residual = settle(here, slabs, natural0, above0, [(array, 1) for array in got_backs0], r_last, backs1[0])
    gradient = finish(here, 1, gradient, [(array, 0) for array in got_backs1], far(residual))
    return (gradient, residual)


def solution(mesh):
    placed = (P("slab", "grp", None), P("slab", "grp", None), P(), P(), P())
    return jax.shard_map(
        local,
        mesh=mesh,
        in_specs=placed,
        out_specs=(P("slab", "grp", None), P("slab", "grp", None)),
        check_vma=False,
    )
```

```python
import functools

import jax
import jax.numpy as jnp
from jax import lax
from jax.experimental import pallas as pl
from jax.experimental.pallas import tpu as pltpu
from jax.sharding import PartitionSpec as P

G = 4
CHUNKS = 2
ROWS = 2
TILE = 256
F32 = jnp.float32
BF16 = jnp.bfloat16
MIB = 1024 * 1024
LANES = 128
SMEM = pl.BlockSpec(memory_space=pltpu.SMEM)
VMEM = pl.BlockSpec(memory_space=pltpu.VMEM)
ANY = pl.BlockSpec(memory_space=pl.ANY)


def moved(value, steps, only=None):
    count = lax.axis_size("slab")
    first, last = max(0, -steps), min(count, count - steps)
    pairs = [(i, i + steps) for i in range(first, last) if only is None or i % G == only]
    return lax.ppermute(value, "slab", pairs)


def swapped(value, bits):
    count = lax.axis_size("slab")
    return lax.ppermute(value, "slab", [(i, i ^ bits) for i in range(count)])


def direct(arrays):
    return [array if m == 0 else swapped(array, m) for m, array in enumerate(arrays)]


def call(kernel, us, *, results, vmem=16, **how):
    return pl.pallas_call(
        kernel,
        out_shape=results,
        compiler_params=pltpu.CompilerParams(vmem_limit_bytes=vmem * MIB),
        cost_estimate=pl.CostEstimate(flops=int(us * 1.15e9), bytes_accessed=1000, transcendentals=0),
        **how,
    )


def value(shape, dtype):
    return jax.ShapeDtypeStruct(shape, dtype)


def far(array):
    return pltpu.with_memory_space_constraint(array, pltpu.HBM)


def across(shape, tile):
    block = shape[:-1] + (tile,)
    return pl.BlockSpec(block, lambda i: (0,) * (len(shape) - 1) + (i,))


def piece_specs(pieces, side, tile):
    return [pl.BlockSpec((side, tile), lambda i, at=at: (at, i)) for _, at in pieces]


def arrays_of(pieces):
    return [array for array, _ in pieces]


def rows_of(place, m):
    first = ROWS * jnp.bitwise_xor(place, m)
    return [(h * TILE, first + h) for h in range(ROWS)]


def wide_tile(rows_deep):
    return pltpu.VMEM((TILE // LANES, rows_deep, LANES), F32)


def chunk_tiles(chunk, cols):
    count = cols // CHUNKS // TILE
    return chunk * count, count


def cast_kernel(groups, ends, halves, here_ref, *refs):
    parts = TILE // LANES
    vol_refs, end_refs = refs[:parts], refs[parts : parts + ends]
    for half_ref, sent_ref in zip(refs[parts + ends : parts + ends + halves], refs[len(refs) - halves :]):
        sent_ref[...] = half_ref[...]
    out_refs = refs[len(refs) - halves - len(groups) : len(refs) - halves]
    rows = ROWS * G
    depth = vol_refs[0].shape[0] // rows
    place = lax.rem(here_ref[0], G)
    for j, vol_ref in enumerate(vol_refs):
        for group, out_ref in zip(groups, out_refs):
            for n, m in enumerate(group):
                for start, row in rows_of(place, m):
                    at = pl.ds(start + j * LANES, LANES)
                    out_ref[n * depth : (n + 1) * depth, at] = vol_ref[pl.ds(row, depth, stride=rows), :].astype(BF16)
    if ends:
        both = jnp.concatenate([ref[...] for ref in end_refs], axis=0).astype(BF16)
        for group, out_ref in zip(groups, out_refs):
            if group[0] % 2:
                out_ref[depth:, :] = both


def cast_rows(here, volume, chunk, groups, ends, sinogram, *tokens):
    depth, rows, cols = volume.shape
    flat = far(volume.reshape(depth * rows, cols))
    first, count = chunk_tiles(chunk, cols)
    parts, width = TILE // LANES, ROWS * TILE
    shapes = [(len(group) * depth + (2 * rows if ends and group[0] % 2 else 0), cols) for group in groups]
    edges = [pl.BlockSpec((rows, width), lambda i, z=z: (z, i)) for z in (0, depth - 1)] if ends else []
    halves = 0 if sinogram is None else CHUNKS
    block = (depth, rows, TILE)
    return call(
        functools.partial(cast_kernel, groups, len(edges), halves),
        2,
        grid=(count,),
        in_specs=[SMEM]
        + [pl.BlockSpec((depth * rows, LANES), lambda i, j=j: (0, (first + i) * parts + j)) for j in range(parts)]
        + edges
        + [pl.BlockSpec(block, lambda i, c=c: (0, 0, c * count + i)) for c in range(halves)]
        + [ANY] * len(tokens),
        out_specs=[across(shape, width) for shape in shapes] + [pl.BlockSpec(block, lambda i: (0, 0, i))] * halves,
        results=[(pltpu.HBM if group[0] == 0 else value)(shape, BF16) for group, shape in zip(groups, shapes)]
        + [value((depth, rows, cols // CHUNKS), BF16)] * halves,
    )(here, *[flat] * (parts + len(edges)), *[sinogram if halves == 0 else far(sinogram)] * halves, *tokens)


def last_block(here_ref, blocks):
    spot = jnp.bitwise_xor(lax.rem(here_ref[0], G), G - 1)
    last = blocks[0]
    for m in range(1, G):
        last = jnp.where(spot == m, blocks[m], last)
    return last


def pack_kernel(here_ref, *refs):
    in_refs, (all_ref, last_ref) = refs[:G], refs[-2:]
    side = in_refs[0].shape[0]
    for m in range(G):
        all_ref[m * side : (m + 1) * side] = in_refs[m][:side]
    last_ref[:side] = last_block(here_ref, [ref[:side] for ref in in_refs])
    if last_ref.shape[0] > side:
        all_ref[G * side :] = in_refs[G - 1][side:]
        last_ref[side:] = in_refs[G - 1][side:]


def pack(here, pieces, more, *tokens):
    side, cols = pieces[0][0].shape
    tile = cols
    shapes = [(G * side + more, cols), (side + more, cols)]
    specs = [across(array.shape, tile) for array in arrays_of(pieces)] if more else piece_specs(pieces, side, tile)
    return call(
        pack_kernel,
        1,
        grid=(cols // tile,),
        in_specs=[SMEM] + specs + [ANY] * len(tokens),
        out_specs=[across(shape, tile) for shape in shapes],
        results=[value(shape, BF16) for shape in shapes],
    )(here, *arrays_of(pieces), *tokens)


def split_kernel(groups, passing, here_ref, own_ref, got_ref, *refs):
    out_refs, wide = refs[-len(groups) - passing - 1 : -1], refs[-1]
    if passing:
        out_refs[-1][...] = refs[0][...]
    depth, rows, cols = own_ref.shape
    place = lax.rem(here_ref[0], G)

    def fill(ref):
        for j in range(cols // LANES):
            wide[j] = ref[:, :, j * LANES : (j + 1) * LANES].astype(F32).reshape(wide.shape[1:])

    @pl.when(place == G - 1)
    def _():
        fill(got_ref)

    @pl.when(place != G - 1)
    def _():
        fill(own_ref)

    for group, out_ref in zip(groups, out_refs):
        for n, m in enumerate(group):
            for j in range(cols // LANES):
                for start, row in rows_of(place, m):
                    block = wide.at[j][pl.ds(row, depth, stride=rows), :].astype(BF16)
                    out_ref[n * depth : (n + 1) * depth, start + j * LANES : start + (j + 1) * LANES] = block


def split_rows(here, own, got, chunk, groups, passing, *tokens):
    depth, rows, cols = own.shape
    first, count = chunk_tiles(chunk, cols)
    block = pl.BlockSpec((depth, rows, TILE), lambda i: (0, 0, first + i))
    shapes = [(len(group) * depth, cols) for group in groups] + [(depth, cols)] * len(passing)
    return call(
        functools.partial(split_kernel, groups, len(passing)),
        2,
        grid=(count,),
        in_specs=[SMEM, block, pl.BlockSpec((depth, rows, TILE), lambda i: (0, 0, i))]
        + piece_specs(passing, depth, ROWS * TILE) + [ANY] * len(tokens),
        out_specs=[across(shape, ROWS * TILE) for shape in shapes],
        results=[value(shape, BF16) for shape in shapes],
        scratch_shapes=[wide_tile(depth * rows)],
    )(here, far(own), got, *arrays_of(passing), *tokens)


def last_kernel(slabs, here_ref, cover_ref, offset_ref, *refs):
    w_ref, vol_ref, sino_ref, *refs = refs
    r_ref, tv_ref, vol, s, r, wide, tv, sem = refs[-8:]
    depth, rows, cols = sino_ref.shape

    count = cols // LANES

    def columns(j):
        return pl.ds(pl.multiple_of(j * LANES, LANES), LANES)

    def arrival(n, j):
        src, dst = ((vol_ref, vol), (sino_ref, s), (tv_ref, tv))[n]
        return pltpu.make_async_copy(src.at[:, :, columns(j)], dst.at[:, :, columns(j)], sem.at[n, j])

    def departure(n, j):
        src, dst = ((r, r_ref), (tv, tv_ref))[n]
        return pltpu.make_async_copy(src.at[:, :, columns(j)], dst.at[:, :, columns(j)], sem.at[3 + n, j])

    @pl.when(here_ref[0] == slabs - 1)
    def _():
        for j in range(count):
            for n in range(3):
                arrival(n, j).start()
        block = w_ref[offset_ref[slabs - 1, 0]]
        block = jnp.where(cover_ref[slabs - 1, 0] == 1, block, jnp.zeros_like(block))
        turned = block.astype(F32).T.astype(BF16)

        def column(j, _):
            at = columns(j)
            for n in range(3):
                arrival(n, j).wait()
            for n, ref in enumerate((s, tv, vol)):
                wide[n] = ref[:, :, at].astype(F32).reshape(wide.shape[1:])
            for row in range(rows):
                spot = pl.ds(row, depth, stride=rows)
                seen = jnp.dot(block, wide.at[2][spot, :].astype(BF16), preferred_element_type=F32)
                resid = (seen - wide.at[0][spot, :]).astype(BF16)
                wide.at[0][spot, :] = resid.astype(F32)
                wide.at[1][spot, :] += jnp.dot(turned, resid, preferred_element_type=F32)
            r[:, :, at] = wide[0].reshape(depth, rows, LANES).astype(BF16)
            tv[:, :, at] = wide[1].reshape(depth, rows, LANES)
            for n in range(2):
                departure(n, j).start()
            return 0

        lax.fori_loop(0, count, column, 0)
        for j in range(count):
            for n in range(2):
                departure(n, j).wait()


def last_group(here, coverage, offsets, weights, volume, sinogram, tv, *tokens):
    slabs = coverage.shape[0]
    depth, rows, cols = sinogram.shape
    return call(
        functools.partial(last_kernel, slabs),
        0,
        vmem=32,
        grid=(1,),
        in_specs=[SMEM, SMEM, SMEM, pl.BlockSpec(weights.shape, lambda i: (0, 0, 0))] + [ANY] * (3 + len(tokens)),
        out_specs=[ANY, ANY],
        results=[pltpu.HBM(sinogram.shape, BF16), pltpu.HBM(volume.shape, F32)],
        input_output_aliases={6: 1},
        scratch_shapes=[
            pltpu.VMEM(volume.shape, F32),
            pltpu.VMEM(sinogram.shape, BF16),
            pltpu.VMEM(sinogram.shape, BF16),
            pltpu.VMEM((3, depth * rows, LANES), F32),
            pltpu.VMEM(volume.shape, F32),
            pltpu.SemaphoreType.DMA((5, cols // LANES)),
        ],
    )(here, coverage, offsets, weights, far(volume), far(sinogram), far(tv), *tokens)


def natural(place, in_refs, wide, j):
    depth = in_refs[0].shape[0]
    rows = ROWS * len(in_refs)
    for m, ref in enumerate(in_refs):
        for start, row in rows_of(place, m):
            value = ref[:, start + j * LANES : start + (j + 1) * LANES].astype(F32)
            wide.at[j][pl.ds(row, depth, stride=rows), :] = value
    return wide[j].reshape(depth, rows, LANES)


def join_kernel(here_ref, *refs):
    in_refs, (out_ref, wide) = refs[:G], refs[-2:]
    for j in range(out_ref.shape[2] // LANES):
        out_ref[:, :, j * LANES : (j + 1) * LANES] = natural(lax.rem(here_ref[0], G), in_refs, wide, j).astype(BF16)


def join_rows(here, pieces, shape, *tokens):
    depth, rows, cols = shape
    _, count = chunk_tiles(0, cols)
    return call(
        join_kernel,
        0,
        grid=(count,),
        in_specs=[SMEM] + piece_specs(pieces, depth, ROWS * TILE) + [ANY] * len(tokens),
        out_specs=pl.BlockSpec((depth, rows, TILE), lambda i: (0, 0, i)),
        results=value((depth, rows, cols // CHUNKS), BF16),
        scratch_shapes=[wide_tile(depth * rows)],
    )(here, *arrays_of(pieces), *tokens)


def settle_kernel(slabs, count, here_ref, own_ref, above_ref, *refs):
    in_refs, (base_ref, out_ref, wide) = refs[:G], refs[-3:]
    step = pl.program_id(0)
    cols = out_ref.shape[2]
    place = lax.rem(here_ref[0], G)
    last = here_ref[0] == slabs - 1

    @pl.when(last)
    def _():
        pltpu.sync_copy(base_ref.at[:, :, pl.ds(pl.multiple_of(step * cols, cols), cols)], out_ref)

    @pl.when(jnp.logical_not(last) & (step < count) & (place == G - 1))
    def _():
        out_ref[...] = above_ref[...]

    @pl.when(jnp.logical_not(last) & (step < count) & (place != G - 1))
    def _():
        out_ref[...] = own_ref[...]

    @pl.when(jnp.logical_not(last) & (step >= count))
    def _():
        for j in range(cols // LANES):
            out_ref[:, :, j * LANES : (j + 1) * LANES] = natural(place, in_refs, wide, j).astype(BF16)


def settle(here, slabs, own, above, pieces, base, *tokens):
    depth, rows, cols = base.shape
    _, count = chunk_tiles(0, cols)
    block = (depth, rows, TILE)
    early = pl.BlockSpec(block, lambda i: (0, 0, jnp.minimum(i, count - 1)))
    late = [
        pl.BlockSpec((depth, ROWS * TILE), lambda i, at=at: (at, jnp.maximum(i - count, 0))) for _, at in pieces
    ]
    return call(
        functools.partial(settle_kernel, slabs, count),
        0,
        grid=(CHUNKS * count,),
        in_specs=[SMEM, early, early] + late + [ANY] * (len(tokens) + 1),
        out_specs=pl.BlockSpec(block, lambda i: (0, 0, i)),
        results=pltpu.HBM(base.shape, BF16),
        scratch_shapes=[wide_tile(depth * rows)],
    )(here, own, above, *arrays_of(pieces), *tokens, far(base))


def finish_kernel(here_ref, tv_ref, *refs):
    in_refs, (out_ref, wide) = refs[:G], refs[-2:]
    for j in range(out_ref.shape[2] // LANES):
        at = pl.ds(j * LANES, LANES)
        out_ref[:, :, at] = tv_ref[:, :, at] + natural(lax.rem(here_ref[0], G), in_refs, wide, j)


def finish(here, chunk, tv, pieces, *tokens):
    depth, rows, cols = tv.shape
    first, count = chunk_tiles(chunk, cols)
    part = pl.BlockSpec((depth, rows, TILE), lambda i: (0, 0, first + i))
    return call(
        finish_kernel,
        0,
        grid=(count,),
        in_specs=[SMEM, part] + piece_specs(pieces, depth, ROWS * TILE) + [ANY] * len(tokens),
        out_specs=part,
        results=pltpu.HBM(tv.shape, F32),
        input_output_aliases={1: 0},
        scratch_shapes=[wide_tile(depth * rows)],
    )(here, far(tv), *arrays_of(pieces), *tokens)


def band_kernel(slabs, span, here_ref, cover_ref, offset_ref, w_ref, *refs):
    proj_ref, back_ref, turned = refs[-3:]
    side = w_ref.shape[1]
    place = lax.rem(here_ref[0], G)
    first = here_ref[0] - place
    zero = jnp.zeros((side, side), BF16)
    for i in range(w_ref.shape[0]):
        turned[i] = w_ref[i].astype(F32).T.astype(BF16)

    def block(ref, i, j):
        k = j - i
        known, step = jnp.clip(i, 0, slabs - 1), jnp.clip(k, 0, span - 1)
        inside = (i >= 0) & (i < slabs) & (j >= 0) & (j < slabs) & (k >= 0) & (k < span)
        live = inside & (cover_ref[known, step] == 1)
        return jnp.where(live, ref[offset_ref[known, step]], zero)

    def slab(m):
        return first + jnp.bitwise_xor(place, m)

    def group(m):
        to = jnp.bitwise_xor(place, m)
        return first + jnp.where(to == G - 1, -1, to)

    seen = [slab(m) for m in range(G)] + [slab(m) + G for m in range(G)] + [first - 1]
    seeing = [group(m) for m in range(G)] + [group(m) - G for m in range(G)] + [first + G - 1]
    for r in range(G):
        for s in range(2 * G + 1):
            at = (pl.ds(r * side, side), pl.ds(s * side, side))
            proj_ref[at] = block(w_ref, group(r), seen[s])
            back_ref[at] = block(turned, seeing[s], slab(r))


def bands(here, coverage, offsets, weights, *tokens):
    slabs, span = coverage.shape
    side = weights.shape[1]
    shape = (G * side, (2 * G + 1) * side)
    return call(
        functools.partial(band_kernel, slabs, span),
        9,
        in_specs=[SMEM, SMEM, SMEM, pl.BlockSpec(weights.shape, lambda i: (0, 0, 0))] + [ANY] * len(tokens),
        grid=(1,),
        out_specs=[pl.BlockSpec(shape, lambda i: (0, 0))] * 2,
        results=[value(shape, BF16)] * 2,
        scratch_shapes=[pltpu.VMEM(weights.shape, BF16)],
    )(here, coverage, offsets, weights, *tokens)


def project_kernel(groups, here_ref, band_ref, own_ref, high_ref, low_ref, *refs):
    sino_refs, (r_ref, down_ref, *group_refs) = refs[:G], refs[-len(groups) - 2 :]
    side = sino_refs[0].shape[0]
    seen = jnp.concatenate([own_ref[...], high_ref[...], low_ref[...]], axis=0)
    total = jnp.dot(band_ref[...], seen, preferred_element_type=F32)
    resid = [(total[m * side : (m + 1) * side] - ref[...].astype(F32)).astype(BF16) for m, ref in enumerate(sino_refs)]
    for m in range(G):
        r_ref[m * side : (m + 1) * side] = resid[m]
    for group, group_ref in zip(groups, group_refs):
        for n, m in enumerate(group):
            group_ref[n * side : (n + 1) * side] = resid[m]
    down_ref[...] = last_block(here_ref, resid)


def project(here, band, own, high, low, sinos, groups, *tokens):
    n, side = band.shape[0], band.shape[0] // G
    cols = own.shape[1]
    tile = cols
    many, one = pl.BlockSpec((n, tile), lambda i: (0, i)), pl.BlockSpec((side, tile), lambda i: (0, i))
    shapes = [(n, cols), (side, cols)] + [(len(group) * side, cols) for group in groups]
    return call(
        functools.partial(project_kernel, groups),
        3,
        grid=(cols // tile,),
        in_specs=[SMEM, pl.BlockSpec(band.shape, lambda i: (0, 0)), many, many, one]
        + piece_specs(sinos, side, tile)
        + [ANY] * len(tokens),
        out_specs=[across(shape, tile) for shape in shapes],
        results=[value(shape, BF16) for shape in shapes],
    )(here, band, own, high, low, *arrays_of(sinos), *tokens)


def back_kernel(dealing, here_ref, band_ref, own_ref, low_ref, high_ref, *refs):
    out_refs = refs[-G:]
    side = high_ref.shape[0]
    seeing = jnp.concatenate([own_ref[...], low_ref[...], high_ref[...]], axis=0)
    total = jnp.dot(band_ref[...], seeing, preferred_element_type=F32)
    place = lax.rem(here_ref[0], G)
    for m, out_ref in enumerate(out_refs):
        out_ref[:side] = total[m * side : (m + 1) * side].astype(BF16)
        if dealing:
            last = jnp.bitwise_xor(place, m) == G - 1
            out_ref[side:] = jnp.where(last, refs[1][...], refs[0][m * side : (m + 1) * side])


def back(here, band, own, low, high, dealt, *tokens):
    n, side = band.shape[0], band.shape[0] // G
    cols = own.shape[1]
    tile = cols
    many = pl.BlockSpec((n, tile), lambda i: (0, i))
    one = pl.BlockSpec((side, tile), lambda i: (0, i))
    out = ((2 if dealt else 1) * side, cols)
    return call(
        functools.partial(back_kernel, bool(dealt)),
        0,
        grid=(cols // tile,),
        in_specs=[SMEM, pl.BlockSpec(band.shape, lambda i: (0, 0)), many, many, one]
        + ([many, one] if dealt else [])
        + [ANY] * len(tokens),
        out_specs=[across(out, tile)] * G,
        results=[value(out, BF16)] * G,
    )(here, band, own, low, high, *dealt, *tokens)


def tv_flux(cur, above):
    rows, cols = cur.shape
    row = lax.broadcasted_iota(jnp.int32, (rows, cols), 0)
    col = lax.broadcasted_iota(jnp.int32, (rows, cols), 1)
    dz = above - cur
    dy = jnp.where(row == rows - 1, 0.0, pltpu.roll(cur, rows - 1, 0)) - cur
    dx = jnp.where(col == cols - 1, 0.0, pltpu.roll(cur, cols - 1, 1)) - cur
    scale = 0.5 * lax.rsqrt(dz * dz + dy * dy + dx * dx + 0.25)
    return dz * scale, dy * scale, dx * scale


def tv_below(cur, above):
    return tv_flux(cur, above)[0]


def tv_slice(cur, above, below_flux):
    rows, cols = cur.shape
    row = lax.broadcasted_iota(jnp.int32, (rows, cols), 0)
    col = lax.broadcasted_iota(jnp.int32, (rows, cols), 1)
    fz, fy, fx = tv_flux(cur, above)
    sides = 0.5 * cur * lax.rsqrt(cur * cur + 0.25)
    fy_low = jnp.where(row == 0, sides, pltpu.roll(fy, 1, 0))
    fx_low = jnp.where(col == 0, sides, pltpu.roll(fx, 1, 1))
    return (below_flux - fz) + (fy_low - fy) + (fx_low - fx), fz


def tv_kernel(here_ref, near_ref, next_level_ref, far_ref, last_level_ref, next_ref, vol_ref, *refs):
    out_ref, done_ref, flux_ref = refs[-3:]
    step = pl.program_id(0)
    deep, rows, _ = vol_ref.shape
    place = lax.rem(here_ref[0], G)

    @pl.when(step == 0)
    def _():
        inside = jnp.where(place == 2, far_ref[...], near_ref[...])
        low = jnp.where(place == 0, last_level_ref[...], inside)[rows:].astype(F32)
        flux_ref[...] = tv_below(low, vol_ref[0])

    def body(z, flux):
        out_ref[z], flux = tv_slice(vol_ref[z], vol_ref[z + 1], flux)
        return flux

    flux = lax.fori_loop(0, deep - 1, body, flux_ref[...], unroll=5)
    inside = jnp.where(place == 1, far_ref[...], near_ref[...])
    high = jnp.where(place == G - 1, next_level_ref[...], inside)[:rows].astype(F32)
    above = jnp.where(step == pl.num_programs(0) - 1, high, next_ref[0])
    out_ref[deep - 1], flux_ref[...] = tv_slice(vol_ref[deep - 1], above, flux)
    done_ref[...] = flux_ref[:, : done_ref.shape[1]]


def half_tv(here, volume, ends, *tokens):
    depth, rows, cols = volume.shape
    deep = 16
    edges = [pl.BlockSpec((2 * rows, cols), lambda i, last=end.shape[0] // (2 * rows) - 1: (last, 0)) for end in ends]
    body = pl.BlockSpec((deep, rows, cols), lambda i: (i, 0, 0))
    after = pl.BlockSpec((1, rows, cols), lambda i: (jnp.minimum((i + 1) * deep, depth - 1), 0, 0))
    return call(
        tv_kernel,
        0,
        grid=(depth // deep,),
        in_specs=[SMEM] + edges + [after, body] + [ANY] * len(tokens),
        out_specs=[body, pl.BlockSpec((rows, LANES), lambda i: (0, 0))],
        results=[pltpu.HBM(volume.shape, F32), value((rows, LANES), F32)],
        scratch_shapes=[pltpu.VMEM((rows, cols), F32)],
    )(here, *ends, far(volume), far(volume), *tokens)


def local(volume, sinogram, weights, coverage, offsets):
    slabs = lax.axis_size("slab")
    here = lax.axis_index("slab").astype(jnp.int32).reshape(1)
    depth, rows, _ = volume.shape
    single = ((0,), (1,), (2,), (3,))
    paired = ((0,), (1,), (2, 3))

    def tied(array, *others):
        return lax.optimization_barrier((array, *others))[0]

    def beyond(over, *others):
        return swapped(tied(over, *others)[depth:], 1)

    vols0 = cast_rows(here, volume, 0, single, True, None)
    got_vols0 = direct(vols0)
    v0, v1, v23, sent0, sent1 = cast_rows(here, volume, 1, paired, False, sinogram, vols0[1])
    got0 = moved(sent0, G, only=G - 1)
    over = swapped(v23, 2)
    band_p, band_b = bands(here, coverage, offsets, weights, v1)
    got1 = moved(tied(sent1, band_p), G, only=G - 1)
    own0, edge0 = pack(here, [(array, 0) for array in got_vols0], 2 * rows, band_p)
    high0, near = moved(own0, -G), swapped(tied(v1, own0), 1)
    s0, s1, s23, over_beyond = split_rows(here, sinogram, got0, 0, paired, [(over, 1)], near)
    s_near, s_over = swapped(s1, 1), swapped(s23, 2)
    low0 = moved(tied(edge0, s_near), G)
    own1, edge1 = pack(here, [(v0, 0), (near, 0), (over, 0), (swapped(over_beyond, 1), 0)], 0)
    low1, high1 = moved(edge1, G), moved(own1, -G)
    t0, t1, t23 = split_rows(here, sinogram, got1, 1, paired, [], own1)
    sinos0 = [(s0, 0), (s_near, 0), (s_over, 0), (beyond(s_over, t0), 0)]


    resid0, down0, r1, r23 = project(here, band_p, own0, high0, low0, sinos0, paired[1:], low1)
    from_low0, from_high0 = moved(resid0, G), moved(down0, -G)
    t_near, t_over = swapped(t1, 1), swapped(t23, 2)
    r_near, r_over = swapped(tied(r1, t_near), 1), swapped(tied(r23, t_near), 2)
    tv, tv_done = half_tv(here, volume, [got_vols0[1], high0, got_vols0[3], low0], resid0)
    sinos1 = [(t0, 0), (t_near, 0), (t_over, 0), (beyond(t_over, tv_done), 0)]
    resid1, down1 = project(here, band_p, own1, high1, low1, sinos1, (), tv_done, r_near, r_over)
    from_low1, from_high1 = moved(resid1, G), moved(down1, -G)

    backs0 = back(here, band_b, resid0, from_low0, from_high0, [resid1, from_high1])
    got_backs0 = direct(backs0)
    r_pieces = [(resid0, 0), (r_near, 0), (r_over, 0), (beyond(r_over, resid1), 0)]
    natural0 = join_rows(here, r_pieces, sinogram.shape, backs0[0])
    above0 = moved(natural0, -G, only=G - 1)
    r_last, tv = last_group(here, coverage, offsets, weights, volume, sinogram, tv, backs0[0])
    backs1 = back(here, band_b, resid1, from_low1, from_high1, [], far(r_last), natural0)
    got_backs1 = direct(backs1)
    gradient = finish(here, 0, tv, [(array, 0) for array in got_backs0], backs1[0])
    residual = settle(here, slabs, natural0, above0, [(array, 1) for array in got_backs0], r_last, backs1[0])
    gradient = finish(here, 1, gradient, [(array, 0) for array in got_backs1], far(residual))
    return (gradient, residual)


def solution(mesh):
    placed = (P("slab", "grp", None), P("slab", "grp", None), P(), P(), P())
    return jax.shard_map(
        local,
        mesh=mesh,
        in_specs=placed,
        out_specs=(P("slab", "grp", None), P("slab", "grp", None)),
        check_vma=False,
    )
```
